32 devices in a mesh: section: 16 (over z, x, core), row: 2 (over y).
Axes of the slice: x: 2, y: 2, z: 4, core: 2. Of those that a mesh axis runs over, the one named last changes fastest.
Arguments:
- fwd_queue: bfloat16 [16, 3, 8, 32, 320], P('section', None, 'row'), may hold values from -45 to 45
- bwd_queue: bfloat16 [16, 3, 8, 32, 320], P('section', None, 'row'), may hold values from -6 to 6
- mirror_queue: bfloat16 [16, 3, 8, 32, 320], P('section', None, 'row'), may hold values from -45 to 45
- stash: bfloat16 [16, 3, 2, 8, 32, 320], P('section', None, None, 'row'), may hold values from -45 to 45
- weights: bfloat16 [16, 2, 3, 3, 320, 320], P('section', None, None, None, 'row'), may hold values from -0.109375 to 0.109375
- grad_acc: float32 [16, 2, 3, 3, 320, 320], P('section', None, None, None, 'row'), may hold values from -6 to 6
- fwd_slot: int32 [16, 2], replicated, may hold values from 0 to 2
- bwd_slot: int32 [16, 2], replicated, may hold values from 0 to 2
Outputs:
- forward_queue_after: bfloat16 [16, 3, 8, 32, 320], P('section', None, 'row')
- next_grads: bfloat16 [16, 3, 8, 32, 320], P('section', None, 'row')
- next_mirror: bfloat16 [16, 3, 8, 32, 320], P('section', None, 'row')
- next_stash: bfloat16 [16, 3, 2, 8, 32, 320], P('section', None, None, 'row')
- grad_total: float32 [16, 2, 3, 3, 320, 320], P('section', None, None, None, 'row')
- section_outputs: bfloat16 [16, 2, 8, 32, 320], P('section', None, 'row')
The draws below stay inside these ranges and needn't reach their ends.
All inputs are finite; a program needn't handle non-finite values.
Results may differ from the reference program's by a relative error of at most 0.012.
Values may be sent and summed in bfloat16 or wider, within the bound.
No kernel may reach another device: no remote copies, remote signals or barrier semaphores. Data moves between devices by JAX's collectives and lax.ppermute only.
A program may use at most 128 MiB of HBM per device.

```python
import math
import jax
import jax.numpy as jnp
from jax import lax

C = 320
GROUPS = 32
COLS = 32
SLOTS = 3
TICKS = 2
SECTIONS = 16
ROWS = 8
N_ROW = 2


def scaled_field(key, lead_count):
    noise_key, chan_key, cell_key = jax.random.split(key, 3)
    noise_base = jnp.clip(jax.random.normal(noise_key, (lead_count, ROWS, COLS, C), jnp.float32), -4.0, 4.0)
    row_rise = jnp.exp(jnp.arange(ROWS, dtype=jnp.float32) * (math.log(3.0) / max(ROWS - 1, 1))) / math.sqrt(3.0)
    chan_scale = jnp.exp(jax.random.uniform(chan_key, (lead_count, 1, 1, C), jnp.float32, math.log(0.3), math.log(3.0)))
    cell_scale = jnp.exp(jax.random.uniform(cell_key, (lead_count, ROWS, COLS, 1), jnp.float32, math.log(0.5), math.log(2.0)))
    return noise_base * row_rise[None, :, None, None] * chan_scale * cell_scale


def draw_fwd_queue(key, part):
    values = scaled_field(jax.random.fold_in(key, 11), SECTIONS * SLOTS)
    return values.reshape(SECTIONS, SLOTS, ROWS, COLS, C).astype(jnp.bfloat16)


def draw_mirror_queue(key, part):
    values = scaled_field(jax.random.fold_in(key, 12), SECTIONS * SLOTS)
    return values.reshape(SECTIONS, SLOTS, ROWS, COLS, C).astype(jnp.bfloat16)


def draw_stash(key, part):
    values = scaled_field(jax.random.fold_in(key, 13), SECTIONS * SLOTS * 2)
    return values.reshape(SECTIONS, SLOTS, 2, ROWS, COLS, C).astype(jnp.bfloat16)


def place_ends(entries, rng, least, top_value):
    shape = entries.shape
    place = [jax.random.randint(jax.random.fold_in(rng, axis), (), 0, shape[axis]) for axis in range(len(shape))]
    entries = entries.at[tuple(place)].set(least)
    longest = shape.index(max(shape))
    place[longest] = (place[longest] + 1) % shape[longest]
    return entries.at[tuple(place)].set(top_value)


def shard_levels(stream_key, dims, cuts, smallest, high):
    gain = 1.0
    for axis_at, blocks in cuts:
        steps = jax.random.uniform(jax.random.fold_in(jax.random.fold_in(stream_key, 6), axis_at), (blocks,), jnp.float32, smallest / len(cuts), high / len(cuts))
        gain = gain * jnp.repeat(jnp.exp(steps), dims[axis_at] // blocks).reshape((-1,) + (1,) * (len(dims) - 1 - axis_at))
    return gain


def scatter_about(key, extent, scale, most, cuts=(), held_as=jnp.bfloat16):
    values = scale * jax.random.normal(key, extent, jnp.float32)
    if cuts:
        values = values * shard_levels(key, extent, cuts, -0.22, 0.18)
    return jnp.clip(values, -most, most).astype(held_as)


def setup_inputs(seed: int = 0) -> dict:
    key_list = jax.random.split(jax.random.key(seed), 9)
    return {
        "fwd_queue": draw_fwd_queue(jax.random.fold_in(key_list[8], 71), 0),
        "bwd_queue": scatter_about(key_list[1], (SECTIONS, SLOTS, ROWS, COLS, C), 1.0, 6.0, ((0, 16), (2, 2))),
        "mirror_queue": draw_mirror_queue(jax.random.fold_in(key_list[8], 71), 0),
        "stash": draw_stash(jax.random.fold_in(key_list[8], 71), 0),
        "weights": scatter_about(key_list[4], (SECTIONS, 2, 3, 3, C, C), (9 * C) ** -0.5, 0.109375, ((0, 16), (4, 2))),
        "grad_acc": scatter_about(key_list[5], (SECTIONS, 2, 3, 3, C, C), 1.0, 6.0, ((0, 16), (4, 2)), jnp.float32),
        "fwd_slot": place_ends(jax.random.randint(key_list[6], (SECTIONS, TICKS), 0, SLOTS), jax.random.fold_in(key_list[6], 1), 0, SLOTS - 1).astype(jnp.int32),
        "bwd_slot": place_ends(jax.random.randint(key_list[7], (SECTIONS, TICKS), 0, SLOTS), jax.random.fold_in(key_list[7], 1), 0, SLOTS - 1).astype(jnp.int32),
    }


epsilon = 1e-05

def patches(padded, row_tally, col_count):
    widened = jnp.pad(padded, ((0, 0), (1, 1), (0, 0)))
    pieces = [widened[row_offset:row_offset + row_tally, column_offset:column_offset + col_count, :] for row_offset in range(3) for column_offset in range(3)]
    return jnp.concatenate(pieces, axis=2).reshape(row_tally * col_count, -1)

def convolve(tensor, kernel):
    row_tally, col_count = (tensor.shape[0], tensor.shape[1])
    padded = jnp.pad(tensor, ((1, 1), (0, 0), (0, 0)))
    result = jnp.dot(patches(padded, row_tally, col_count), kernel.reshape(-1, kernel.shape[-1]), preferred_element_type=jnp.float32)
    return result.reshape(row_tally, col_count, -1)

def flipped(kernel):
    return jnp.transpose(kernel[::-1, ::-1], (0, 1, 3, 2))

def normalize(tensor):
    values = tensor.astype(jnp.float32).reshape(-1, GROUPS, C // GROUPS)
    number = values.shape[0] * values.shape[2]
    center = lax.optimization_barrier(jnp.sum(values, axis=(0, 2))) / number
    spread = lax.optimization_barrier(jnp.sum(values * values, axis=(0, 2))) / number - center * center
    factor = lax.rsqrt(spread + epsilon)
    return ((values - center[None, :, None]) * factor[None, :, None], factor)

def activate(normed, target_shape):
    return jax.nn.silu(normed).reshape(target_shape).astype(jnp.bfloat16)

def norm_back(normed, factor, upstream):
    upstream = upstream.reshape(normed.shape)
    logistic = jax.nn.sigmoid(normed)
    gated_grad = upstream * logistic * (1.0 + normed * (1.0 - logistic))
    number = normed.shape[0] * normed.shape[2]
    first_mean = lax.optimization_barrier(jnp.sum(gated_grad, axis=(0, 2))) / number
    second_mean = lax.optimization_barrier(jnp.sum(gated_grad * normed, axis=(0, 2))) / number
    return factor[None, :, None] * (gated_grad - first_mean[None, :, None] - normed * second_mean[None, :, None])

def section_tick(packed):
    section_id, inputs_fwd, skip_fwd, grads_bwd, skip_bwd, stash_pair, kernels = packed
    encoder = section_id < SECTIONS // 2
    first_kernel, second_kernel = (kernels[0], kernels[1])
    target_shape = inputs_fwd.shape
    normed, factor = normalize(inputs_fwd)
    conv_first = convolve(activate(normed, target_shape), first_kernel)
    second_in = jnp.where(encoder, conv_first.astype(jnp.bfloat16), skip_fwd)
    normed, factor = normalize(second_in)
    conv_second = convolve(activate(normed, target_shape), second_kernel)
    output = (inputs_fwd.astype(jnp.float32) + conv_second + jnp.where(encoder, 0.0, conv_first)).astype(jnp.bfloat16)
    out_grad = (grads_bwd.astype(jnp.float32) + jnp.where(encoder, skip_bwd.astype(jnp.float32), 0.0)).astype(jnp.bfloat16)
    normed_h, factor_h = normalize(stash_pair[0])
    normed_i, factor_i = normalize(stash_pair[1])
    redo_first = activate(normed_h, target_shape)
    redo_second = activate(normed_i, target_shape)
    back_second = convolve(out_grad, flipped(second_kernel))
    skip_grad = norm_back(normed_i, factor_i, back_second).reshape(target_shape).astype(jnp.bfloat16)
    first_grad = jnp.where(encoder, skip_grad, out_grad)
    back_first = convolve(first_grad, flipped(first_kernel))
    input_grad = (out_grad.astype(jnp.float32) + norm_back(normed_h, factor_h, back_first).reshape(target_shape)).astype(jnp.bfloat16)
    payload = jnp.where(encoder, output, skip_grad)
    return (output, second_in, payload, input_grad, redo_first, first_grad, redo_second, out_grad)

def select_slot(queue, slots):
    return jax.vmap(lambda section_block, slot_index: lax.dynamic_index_in_dim(section_block, slot_index, 0, keepdims=False))(queue, slots)

def write_slot(queue, slots, values):
    return jax.vmap(lambda section_block, slot_index, value_block: lax.dynamic_update_index_in_dim(section_block, value_block, slot_index, 0))(queue, slots, values)

def block_grads(acts, grads):
    grand_total = jnp.zeros((N_ROW, 9 * C, C), jnp.float32)
    for tick_index in range(TICKS):
        padded = jnp.pad(acts[tick_index], ((1, 1), (0, 0), (0, 0)))
        patch_row_group = patches(padded, ROWS, COLS).reshape(N_ROW, -1, 9 * C)
        gradient_block_list = grads[tick_index].reshape(N_ROW, -1, C)
        grand_total = grand_total + jnp.einsum('ylz,yla->yza', patch_row_group.astype(jnp.float32), gradient_block_list.astype(jnp.float32))
    rounded = lax.optimization_barrier(grand_total.astype(jnp.bfloat16))
    return lax.optimization_barrier(jnp.sum(rounded.astype(jnp.float32), axis=0)).reshape(3, 3, C, C)

def section_grads(packed):
    firsts, first_grads, seconds, second_grads = packed
    return jnp.stack([block_grads(firsts, first_grads), block_grads(seconds, second_grads)])

def reference(fwd_queue, bwd_queue, mirror_queue, stash, weights, grad_acc, fwd_slot, bwd_slot):
    section_ids = jnp.arange(SECTIONS, dtype=jnp.int32)
    prior_section = jnp.maximum(section_ids - 1, 0)
    later_section = jnp.minimum(section_ids + 1, SECTIONS - 1)
    partner = (SECTIONS - 1 - section_ids).astype(jnp.int32)
    has_prior = (section_ids > 0)[:, None, None, None]
    has_later = (section_ids < SECTIONS - 1)[:, None, None, None]
    saved_pairs = []
    emitted = []
    for tick_index in range(TICKS):
        fwd_now = fwd_slot[:, tick_index].astype(jnp.int32)
        bwd_now = bwd_slot[:, tick_index].astype(jnp.int32)
        inputs_fwd = select_slot(fwd_queue, fwd_now)
        packed = (section_ids, inputs_fwd, select_slot(mirror_queue, fwd_now), select_slot(bwd_queue, bwd_now), select_slot(mirror_queue, bwd_now), select_slot(stash, bwd_now), weights)
        output, second_in, payload, input_grad, redo_first, first_grad, redo_second, out_grad = lax.map(section_tick, packed)
        arrive_slot = fwd_now[prior_section]
        arrive_value = jnp.where(has_prior, output[prior_section], select_slot(fwd_queue, arrive_slot))
        fwd_queue = write_slot(fwd_queue, arrive_slot, arrive_value)
        return_slot = bwd_now[later_section]
        back_value = jnp.where(has_later, input_grad[later_section], select_slot(bwd_queue, return_slot))
        bwd_queue = write_slot(bwd_queue, return_slot, back_value)
        mirror_slot = jnp.where(section_ids < SECTIONS // 2, bwd_now[partner], fwd_now[partner]).astype(jnp.int32)
        mirror_queue = write_slot(mirror_queue, mirror_slot, payload[partner])
        stash = write_slot(stash, fwd_now, jnp.stack([inputs_fwd, second_in], axis=1))
        saved_pairs.append((redo_first, first_grad, redo_second, out_grad))
        emitted.append(output)
    stacked = tuple((jnp.stack([pair[member] for pair in saved_pairs], axis=1) for member in range(4)))
    grad_total = grad_acc + lax.map(section_grads, stacked)
    return (fwd_queue, bwd_queue, mirror_queue, stash, grad_total, jnp.stack(emitted, axis=1))
```

```python
import functools

import jax
import jax.numpy as jnp
from jax import lax
from jax.experimental import pallas as pl
from jax.experimental.pallas import tpu as pltpu
from jax.sharding import PartitionSpec as P

GROUPS = 32
TICKS = 2
FOLD = 4
EPSILON = 1e-05
BF, F32 = jnp.bfloat16, jnp.float32
VMEM_LIMIT = 24 * 2**20


class Sizes:
    def __init__(self, queue, sections, rows):
        self.sections, self.parts = sections, rows
        self.cols = queue.shape[2]
        self.channels = queue.shape[3]
        self.local = queue.shape[1] * queue.shape[2]
        self.cells = self.local * rows
        self.share = self.channels // rows
        self.group = self.channels // GROUPS
        self.count = self.cells * self.group


def where_am_i():
    return lax.axis_index("section"), lax.axis_index("row")


def share_of(z, value, part):
    value = value.astype(F32)
    out = value[:, : z.share]
    for j in range(1, z.parts):
        out = jnp.where(part == j, value[:, j * z.share : (j + 1) * z.share], out)
    return out


def all_shares(z, own, others, row):
    out = []
    for j in range(z.parts):
        value = own
        for d in range(1, z.parts):
            value = jnp.where(lax.rem(row + z.parts - d, z.parts) == j, others[d - 1], value)
        out.append(value)
    return out


def side_by_side(values):
    return jnp.concatenate([value.astype(F32) for value in values], axis=1)


def fold(z, ref, value):
    rows = value.shape[0] // FOLD
    ref[...] = side_by_side([value[j * rows : (j + 1) * rows] for j in range(FOLD)]).astype(BF)


def unfold(z, ref):
    value = ref[...].astype(F32)
    return jnp.concatenate([value[:, j * z.share : (j + 1) * z.share] for j in range(FOLD)], axis=0)


def source(z, row, d):
    return lax.rem(row + z.parts - d, z.parts)


def target(z, row, d):
    return lax.rem(row + d, z.parts)


def part_rows(z, part):
    return pl.ds(pl.multiple_of(part * z.local, z.local), z.local)


def assemble(z, ref, pieces, row, start, width):
    for d, piece in enumerate(pieces):
        value = piece[...].astype(F32)[:, start : start + width]
        ref[part_rows(z, source(z, row, d)), :] = value.astype(BF)


def group_sums(z, first, second):
    width = first.shape[1]
    line = lax.broadcasted_iota(jnp.int32, (8, width), 0)
    both = jnp.where(line == 0, first, jnp.where(line == 1, second, 0.0))
    across = lax.broadcasted_iota(jnp.int32, (width, width), 1).astype(F32)
    down = lax.broadcasted_iota(jnp.int32, (width, width), 0).astype(F32)
    same = jnp.floor((across + 0.5) * (1.0 / z.group)) == jnp.floor((down + 0.5) * (1.0 / z.group))
    sums = jnp.dot(
        both, same.astype(F32), precision=lax.Precision.HIGHEST, preferred_element_type=F32
    )
    return sums[0:1], sums[1:2]


def normalize(z, x):
    total, square = group_sums(
        z, jnp.sum(x, axis=0, keepdims=True), jnp.sum(x * x, axis=0, keepdims=True)
    )
    center = total / z.count
    factor = lax.rsqrt(square / z.count - center * center + EPSILON)
    return (x - center) * factor, factor


def sigmoid(y):
    return 1.0 / (1.0 + jnp.exp(-y))


def norm_back(z, y, factor, logistic, upstream):
    e = upstream * logistic * (1.0 + y * (1.0 - logistic))
    first, second = group_sums(
        z, jnp.sum(e, axis=0, keepdims=True), jnp.sum(e * y, axis=0, keepdims=True)
    )
    return factor * (e - first / z.count - y * (second / z.count))


def spread(z, x, line_ref, pad_ref):
    cells, cols = z.cells, z.cols
    width = x.shape[1]
    line_ref[8 : 8 + cells, :] = x
    column = lax.rem(lax.broadcasted_iota(jnp.int32, (cells, 1), 0), cols)
    edge = jnp.zeros((cols, width), BF)
    for b in range(3):
        pad_ref[b, :cols, :] = edge
        pad_ref[b, cols + cells :, :] = edge
    pad_ref[1, cols : cols + cells, :] = x.astype(BF)
    left = jnp.where(column > 0, line_ref[7 : 7 + cells, :], 0.0)
    pad_ref[0, cols : cols + cells, :] = left.astype(BF)
    right = jnp.where(column < cols - 1, line_ref[9 : 9 + cells, :], 0.0)
    pad_ref[2, cols : cols + cells, :] = right.astype(BF)


def convolve(z, pad_ref, kernel_ref):
    total = None
    for a in range(3):
        for b in range(3):
            term = jnp.dot(
                pad_ref[b, a * z.cols : a * z.cols + z.cells, :],
                kernel_ref[3 * a + b],
                preferred_element_type=F32,
            )
            total = term if total is None else total + term
    return total


def convolve_back(z, pad_ref, kernel_ref):
    total = None
    for a in range(3):
        for b in range(3):
            term = lax.dot_general(
                pad_ref[b, a * z.cols : a * z.cols + z.cells, :],
                kernel_ref[3 * (2 - a) + 2 - b],
                (((1,), (1,)), ((), ())),
                preferred_element_type=F32,
            )
            total = term if total is None else total + term
    return total


def pad_shapes(z, width):
    return [
        pltpu.VMEM((z.cells + 16, width), F32),
        pltpu.VMEM((3, z.cells + 2 * z.cols, width), BF),
    ]


def call(body, name, scalars, arrays, outs, scratch=(), flops=0):
    moved = sum(x.size * x.dtype.itemsize for x in arrays)
    return pl.pallas_call(
        body,
        name=name,
        out_shape=[jax.ShapeDtypeStruct(shape, dtype) for shape, dtype in outs],
        in_specs=[pl.BlockSpec(memory_space=pltpu.SMEM)] * len(scalars)
        + [pl.BlockSpec(memory_space=pltpu.VMEM)] * len(arrays),
        out_specs=[pl.BlockSpec(memory_space=pltpu.VMEM)] * len(outs),
        scratch_shapes=list(scratch),
        compiler_params=pltpu.CompilerParams(vmem_limit_bytes=VMEM_LIMIT),
        cost_estimate=pl.CostEstimate(flops=flops, bytes_accessed=moved, transcendentals=0),
    )(*scalars, *arrays)


def pack_first(z, fs, bs, fwd, bwd, mir, stash, *outs):
    s, row = where_am_i()
    f, b = fs[0, s], bs[0, s]
    h, i = fwd[f], stash[2 * b + 1]
    g = bwd[b].astype(F32) + jnp.where(s < z.sections // 2, mir[b].astype(F32), 0.0)
    for d, out in enumerate(outs):
        part = target(z, row, d)
        out[...] = side_by_side([share_of(z, h, part), share_of(z, i, part), g]).astype(BF)


def pack_second(z, fs, bs, fwd, bwd, mir, stash, *outs):
    s, row = where_am_i()
    encoder = s < z.sections // 2
    f0, f1, b0, b1 = fs[0, s], fs[1, s], bs[0, s], bs[1, s]
    w = z.share
    halves = (stash[2 * b0], fwd[f1], stash[2 * b1], stash[2 * b1 + 1])
    skip_back, skip_now, skip_before = mir[b1].astype(F32), mir[f1], mir[f0]
    for d, out in enumerate(outs):
        part = target(z, row, d)
        values = [share_of(z, value, part) for value in halves] + [bwd[b1]]
        values.append(jnp.where(encoder, skip_back[:, :w], share_of(z, skip_now, part)))
        values.append(jnp.where(encoder, skip_back[:, w : 2 * w], share_of(z, skip_before, part)))
        if z.parts > 2:
            values.append(skip_back[:, 2 * w :])
        out[...] = side_by_side(values).astype(BF)


def send_partials(z, row, total, own, sends):
    own[...] = share_of(z, total, row)
    for d, send in enumerate(sends, 1):
        fold(z, send, share_of(z, total, target(z, row, d)))


def first_forward(z, *refs):
    n = z.parts
    pieces, kernel, (own, h_out), sends = refs[:n], refs[n], refs[n + 1 : n + 3], refs[n + 3 : 2 * n + 2]
    line, pad = refs[2 * n + 2 :]
    _, row = where_am_i()
    assemble(z, h_out, pieces, row, 0, z.share)
    y, _ = normalize(z, h_out[...].astype(F32))
    spread(z, y * sigmoid(y), line, pad)
    send_partials(z, row, convolve(z, pad, kernel), own, sends)


def later_forward(z, fs, *refs):
    n = z.parts
    arrivals, pieces, kernel = refs[:n], refs[n : 2 * n], refs[2 * n]
    own, h_out, arrived = refs[2 * n + 1 : 2 * n + 4]
    sends = refs[2 * n + 4 : 3 * n + 3]
    line, pad = refs[3 * n + 3 :]
    s, row = where_am_i()
    total = unfold(z, arrivals[0])
    for other in arrivals[1:]:
        total = total + unfold(z, other)
    total = total.astype(BF).astype(F32)
    arrived[...] = total.astype(BF)
    assemble(z, h_out, pieces, row, z.share, z.share)
    prior = jnp.maximum(s - 1, 0)
    taken = jnp.logical_and(s > 0, fs[0, prior] == fs[1, s])
    h = jnp.where(taken, total, h_out[...].astype(F32))
    h_out[...] = h.astype(BF)
    y, _ = normalize(z, h)
    spread(z, y * sigmoid(y), line, pad)
    send_partials(z, row, convolve(z, pad, kernel), own, sends)


def back_through_second(z, i, g, kernel, q_out, q_send, act_out, line, pad):
    y, factor = normalize(z, i.astype(F32))
    logistic = sigmoid(y)
    act_out[...] = (y * logistic).astype(BF)
    spread(z, g, line, pad)
    q = norm_back(z, y, factor, logistic, convolve_back(z, pad, kernel)).astype(BF)
    q_out[...] = q
    fold(z, q_send, q.astype(F32))


def first_backward(z, *refs):
    n = z.parts
    pieces, kernel = refs[:n], refs[n]
    q_out, q_send, g_out, act_out, i_ref, line, pad = refs[n + 1 :]
    _, row = where_am_i()
    assemble(z, i_ref, pieces, row, z.share, z.share)
    assemble(z, g_out, pieces, row, 2 * z.share, z.channels)
    back_through_second(
        z, i_ref[...], g_out[...].astype(F32), kernel, q_out, q_send, act_out, line, pad
    )


def later_backward(z, fs, bs, *refs):
    n = z.parts
    arrivals, mirrors, pieces = refs[:n], refs[n : 2 * n], refs[2 * n : 3 * n]
    i_before, kernel = refs[3 * n : 3 * n + 2]
    q_out, q_send, g_out, act_out, grad_in, skip_in, i_ref, full, line, pad = refs[3 * n + 2 :]
    s, row = where_am_i()
    encoder = s < z.sections // 2
    w = z.share
    for out, parts in ((grad_in, arrivals), (skip_in, mirrors)):
        shares = [unfold(z, part) for part in parts]
        out[...] = side_by_side(all_shares(z, shares[0], shares[1:], row)).astype(BF)
    later = jnp.minimum(s + 1, z.sections - 1)
    partner = z.sections - 1 - s
    grad_taken = jnp.logical_and(s < z.sections - 1, bs[0, later] == bs[1, s])
    skip_taken = bs[0, partner] == bs[1, s]
    assemble(z, full, pieces, row, 4 * w, z.channels)
    g = jnp.where(grad_taken, grad_in[...].astype(F32), full[...].astype(F32))
    assemble(z, full, pieces, row, 4 * w + z.channels, z.channels)
    skip = jnp.where(skip_taken, skip_in[...].astype(F32), full[...].astype(F32))
    g_out[...] = (g + jnp.where(encoder, skip, 0.0)).astype(BF)
    assemble(z, i_ref, pieces, row, 3 * w, w)
    i = jnp.where(fs[0, s] == bs[1, s], i_before[...].astype(F32), i_ref[...].astype(F32))
    back_through_second(
        z, i, g_out[...].astype(F32), kernel, q_out, q_send, act_out, line, pad
    )


def second_convolution(z, encoder, row, own, received, skip, h, kernel, i_out, full, line, pad):
    c0 = own[...]
    for other in received:
        c0 = c0 + unfold(z, other)
    i = jnp.where(encoder, c0, skip.astype(F32)).astype(BF)
    i_out[...] = i
    y, _ = normalize(z, i.astype(F32))
    spread(z, y * sigmoid(y), line, pad)
    total = convolve(z, pad, kernel)
    base = h[...].astype(F32) + jnp.where(encoder, 0.0, c0)
    full[...] = total + side_by_side([jnp.where(row == j, base, 0.0) for j in range(z.parts)])


def second_forward(z, *refs):
    n = z.parts
    own, received, h = refs[0], refs[1:n], refs[n]
    pieces, q, kernel = refs[n + 1 : 2 * n + 1], refs[2 * n + 1], refs[2 * n + 2]
    i_out, full_out = refs[2 * n + 3 : 2 * n + 5]
    sends, mirrors = refs[2 * n + 5 : 3 * n + 5], refs[3 * n + 5 : 4 * n + 5]
    skip, full, line, pad = refs[4 * n + 5 :]
    s, row = where_am_i()
    encoder = s < z.sections // 2
    assemble(z, skip, pieces, row, 5 * z.share + z.channels, z.share)
    second_convolution(
        z, encoder, row, own, received, skip[...], h, kernel, i_out, full, line, pad
    )
    full_out[...] = full[...].astype(BF)
    q_now = q[...].astype(F32)
    for d in range(n):
        piece = share_of(z, full[...], target(z, row, d))
        fold(z, sends[d], piece)
        fold(z, mirrors[d], jnp.where(encoder, piece, q_now))


def last_forward(z, fs, *refs):
    n = z.parts
    own, received, h = refs[0], refs[1:n], refs[n]
    pieces, arrived, kernel = refs[n + 1 : 2 * n + 1], refs[2 * n + 1], refs[2 * n + 2]
    sends = refs[2 * n + 3 : 3 * n + 3]
    i_out, skip, full, line, pad = refs[3 * n + 3 :]
    s, row = where_am_i()
    encoder = s < z.sections // 2
    partner = z.sections - 1 - s
    assemble(z, skip, pieces, row, 4 * z.share + z.channels, z.share)
    now = jnp.where(
        fs[0, partner] == fs[1, s], arrived[...].astype(F32), skip[...].astype(F32)
    )
    second_convolution(z, encoder, row, own, received, now, h, kernel, i_out, full, line, pad)
    for d, send in enumerate(sends):
        at = part_rows(z, target(z, row, d))
        send[...] = side_by_side([full[at, :], i_out[at, :]]).astype(BF)


def back_through_first(z, encoder, row, q, received, g, h, kernel, grad_out, act_out, line, pad):
    shares = all_shares(z, q[...].astype(F32), [unfold(z, other) for other in received], row)
    whole = side_by_side(shares)
    now = jnp.where(encoder, whole, g[...].astype(F32))
    grad_out[...] = now.astype(BF)
    y, factor = normalize(z, h.astype(F32))
    logistic = sigmoid(y)
    act_out[...] = (y * logistic).astype(BF)
    spread(z, now, line, pad)
    back = norm_back(z, y, factor, logistic, convolve_back(z, pad, kernel))
    return share_of(z, g[...], row) + back, whole


def second_backward(z, *refs):
    n = z.parts
    q, received, g, pieces, kernel = refs[0], refs[1:n], refs[n], refs[n + 1 : 2 * n + 1], refs[2 * n + 1]
    send, grad_out, act_out, h, line, pad = refs[2 * n + 2 :]
    s, row = where_am_i()
    assemble(z, h, pieces, row, 0, z.share)
    value, _ = back_through_first(
        z, s < z.sections // 2, row, q, received, g, h[...], kernel, grad_out, act_out, line, pad
    )
    fold(z, send, value)


def last_backward(z, fs, bs, *refs):
    n = z.parts
    q, received, g, pieces = refs[0], refs[1:n], refs[n], refs[n + 1 : 2 * n + 1]
    h_before, kernel = refs[2 * n + 1 : 2 * n + 3]
    sends = refs[2 * n + 3 : 3 * n + 3]
    q_rows, grad_out, act_out, h, value, whole, line, pad = refs[3 * n + 3 :]
    s, row = where_am_i()
    assemble(z, h, pieces, row, 2 * z.share, z.share)
    now = jnp.where(fs[0, s] == bs[1, s], h_before[...], h[...])
    result, entered = back_through_first(
        z, s < z.sections // 2, row, q, received, g, now, kernel, grad_out, act_out, line, pad
    )
    value[...] = result.astype(BF)
    for d, send in enumerate(sends):
        fold(z, send, value[part_rows(z, target(z, row, d)), :])
    whole[...] = entered.astype(BF)
    q_rows[...] = whole[part_rows(z, row), :]


def pack_rows(z, *refs):
    n = z.parts
    full, i, arrived, mirrors = refs[0], refs[1], refs[2], refs[3 : n + 3]
    sends, skip = refs[n + 3 : 2 * n + 3], refs[2 * n + 3]
    _, row = where_am_i()
    total = unfold(z, mirrors[0])
    for other in mirrors[1:]:
        total = total + unfold(z, other)
    skip[...] = total.astype(BF)
    for d, send in enumerate(sends):
        at = part_rows(z, target(z, row, d))
        send[...] = side_by_side([ref[at, :] for ref in (full, i, arrived, skip)]).astype(BF)


def add_rows(z, *refs):
    n = z.parts
    pieces, q_rows = refs[:n], refs[n]
    out, mirror, i_rows = refs[n + 1 :]
    s, row = where_am_i()
    c = z.channels
    values = [piece[...].astype(F32) for piece in pieces]
    total = sum(value[:, :c] for value in values)
    out[...] = total.astype(BF)
    mirror[...] = jnp.where(s < z.sections // 2, total, q_rows[...].astype(F32)).astype(BF)
    shares = all_shares(z, values[0][:, c:], [value[:, c:] for value in values[1:]], row)
    i_rows[...] = side_by_side(shares).astype(BF)


def finish(z, fs, bs, *refs):
    n = z.parts
    fwd, bwd, mir, stash = refs[:4]
    rows0 = refs[4 : n + 4]
    grad_in, skip_in, out1, i1, fwd1, mir1 = refs[n + 4 : n + 10]
    grads1 = refs[n + 10 : 2 * n + 10]
    fwd_out, bwd_out, mir_out, stash_out, emitted = refs[2 * n + 10 :]
    s, row = where_am_i()
    encoder = s < z.sections // 2
    c, w = z.channels, z.share
    prior, later = jnp.maximum(s - 1, 0), jnp.minimum(s + 1, z.sections - 1)
    partner = z.sections - 1 - s
    has_prior, has_later = s > 0, s < z.sections - 1
    mine = part_rows(z, row)

    pieces = [piece[...].astype(F32) for piece in rows0]

    def joined(at):
        shares = [piece[:, at : at + w] for piece in pieces]
        return side_by_side(all_shares(z, shares[0], shares[1:], row))

    total = sum(piece[:, :c] for piece in pieces)
    emitted[0] = total.astype(BF)
    emitted[1] = out1[...]

    i0 = joined(c)
    stash_out[...] = stash[...]
    f0, f1 = fs[0, s], fs[1, s]
    stash_out[2 * f0] = fwd[f0]
    stash_out[2 * f0 + 1] = i0.astype(BF)
    fwd_in = joined(c + w)
    taken = jnp.logical_and(has_prior, fs[0, prior] == f1)
    stash_out[2 * f1] = jnp.where(taken, fwd_in, fwd[f1].astype(F32)).astype(BF)
    stash_out[2 * f1 + 1] = i1[...]

    fwd_out[...] = fwd[...]

    @pl.when(has_prior)
    def _():
        fwd_out[fs[0, prior]] = fwd_in.astype(BF)
        fwd_out[fs[1, prior]] = fwd1[...]

    mir_out[...] = mir[...]
    skip = jnp.where(encoder, skip_in[mine, :].astype(F32), joined(c + 2 * w))
    mir_out[jnp.where(encoder, bs[0, partner], fs[0, partner])] = skip.astype(BF)
    mir_out[jnp.where(encoder, bs[1, partner], fs[1, partner])] = mir1[...]

    bwd_out[...] = bwd[...]
    shares = [unfold(z, piece) for piece in grads1]
    grads = side_by_side(all_shares(z, shares[0], shares[1:], row)).astype(BF)

    @pl.when(has_later)
    def _():
        bwd_out[bs[0, later]] = grad_in[mine, :]
        bwd_out[bs[1, later]] = grads


def kernel_grads(z, acts0, acts1, grads0, grads1, acts2, acts3, grads2, grads3, acc, out, turned, line, pad):
    step = pl.program_id(0)

    def prepare(acts, grads):
        for t in range(TICKS):
            turned[t] = jnp.transpose(acts[t][...].astype(F32)).astype(BF)
            spread(z, grads[t][...].astype(F32), line, pad.at[t])

    @pl.when(step == 0)
    def _():
        prepare((acts0, acts1), (grads0, grads1))

    @pl.when(step == 9)
    def _():
        prepare((acts2, acts3), (grads2, grads3))

    tap = lax.rem(step, 9)
    a, b = lax.div(tap, 3), lax.rem(tap, 3)
    at = pl.ds(pl.multiple_of((2 - a) * z.cols, z.cols), z.cells)
    total = acc[0]
    for t in range(TICKS):
        total = total + jnp.dot(turned[t], pad[t, 2 - b, at, :], preferred_element_type=F32)
    out[0] = total


def per_device(fwd_queue, bwd_queue, mirror_queue, stash, weights, grad_acc, fwd_slot, bwd_slot):
    sections, n = lax.axis_size("section"), lax.axis_size("row")
    z = Sizes(fwd_queue[0], sections, n)
    slots = fwd_queue.shape[1]
    c, w, local, cells = z.channels, z.share, z.local, z.cells
    fwd, bwd, mir = (x.reshape(slots, local, c) for x in (fwd_queue, bwd_queue, mirror_queue))
    kept = stash.reshape(2 * slots, local, c)
    kernels = weights.reshape(2, 9, w, c)
    first_kernel, second_kernel = kernels[0], kernels[1]
    fs, bs = fwd_slot.T, bwd_slot.T
    folded, wide = (cells // FOLD, FOLD * w), (cells, c)
    half = (cells, w)
    flops = 2 * cells * 9 * w * c

    def move(x, d, step):
        route = [
            (s * n + r, step(s) * n + (r + d) % n) for s in range(sections) for r in range(n)
        ]
        return lax.ppermute(x, ("section", "row"), route)

    across = functools.partial(move, step=lambda s: s)
    onward = functools.partial(move, step=lambda s: (s + 1) % sections)
    backward = functools.partial(move, step=lambda s: (s - 1) % sections)
    mirrored = functools.partial(move, step=lambda s: sections - 1 - s)

    def run(body, scalars, arrays, outs, scratch=(), flops=0):
        return call(functools.partial(body, z), body.__name__, scalars, arrays, outs, scratch, flops)

    def exchange(pieces):
        return [pieces[0]] + [across(piece, d) for d, piece in enumerate(pieces[1:], 1)]

    narrow_pad, wide_pad = pad_shapes(z, w), pad_shapes(z, c)
    queues = (fwd, bwd, mir, kept)
    first = exchange(run(pack_first, (fs, bs), queues, [((local, 2 * w + c), BF)] * n))
    second = exchange(run(pack_second, (fs, bs), queues, [((local, 4 * w + 2 * c), BF)] * n))

    own, h0, *sends = run(
        first_forward,
        (),
        (*first, first_kernel),
        [(half, F32), (half, BF)] + [(folded, BF)] * (n - 1),
        narrow_pad,
        flops,
    )
    received = [across(x, d) for d, x in enumerate(sends, 1)]
    q0, q_send, g0, act_i0 = run(
        first_backward,
        (),
        (*first, second_kernel),
        [(half, BF), (folded, BF), (wide, BF), (half, BF)],
        [pltpu.VMEM(half, BF)] + wide_pad,
        flops,
    )
    q_received = [across(q_send, d) for d in range(1, n)]
    i0, full0, *sends = run(
        second_forward,
        (),
        (own, *received, h0, *second, q0, second_kernel),
        [(half, BF), (wide, BF)] + [(folded, BF)] * (2 * n),
        [pltpu.VMEM(half, BF), pltpu.VMEM(wide, F32)] + narrow_pad,
        flops,
    )
    fwd_in = [onward(x, d) for d, x in enumerate(sends[:n])]
    mir_in = [mirrored(x, d) for d, x in enumerate(sends[n:])]
    dh_send, grad0, act_h0 = run(
        second_backward,
        (),
        (q0, *q_received, g0, *second, first_kernel),
        [(folded, BF), (wide, BF), (half, BF)],
        [pltpu.VMEM(half, BF)] + wide_pad,
        flops,
    )
    dh_in = [backward(dh_send, d) for d in range(n)]

    own, h1, arrived, *sends = run(
        later_forward,
        (fs,),
        (*fwd_in, *second, first_kernel),
        [(half, F32), (half, BF), (half, BF)] + [(folded, BF)] * (n - 1),
        narrow_pad,
        flops,
    )
    received = [across(x, d) for d, x in enumerate(sends, 1)]
    q1, q_send, g1, act_i1, grad_in, skip_in = run(
        later_backward,
        (fs, bs),
        (*dh_in, *mir_in, *second, i0, second_kernel),
        [(half, BF), (folded, BF), (wide, BF), (half, BF), (wide, BF), (wide, BF)],
        [pltpu.VMEM(half, BF), pltpu.VMEM(wide, BF)] + wide_pad,
        flops,
    )
    q_received = [across(q_send, d) for d in range(1, n)]
    *sends, skip_arrived = run(
        pack_rows,
        (),
        (full0, i0, arrived, *mir_in),
        [((local, c + 3 * w), BF)] * n + [(half, BF)],
    )
    rows0 = exchange(sends)
    sends = run(
        last_forward,
        (fs,),
        (own, *received, h1, *second, skip_arrived, second_kernel),
        [((local, c + w), BF)] * n,
        [pltpu.VMEM(half, BF), pltpu.VMEM(half, BF), pltpu.VMEM(wide, F32)] + narrow_pad,
        flops,
    )
    rows1 = exchange(sends)
    *dh_sends, q_rows, grad1, act_h1 = run(
        last_backward,
        (fs, bs),
        (q1, *q_received, g1, *second, h0, first_kernel),
        [((local // FOLD, FOLD * w), BF)] * n + [((local, c), BF), (wide, BF), (half, BF)],
        [pltpu.VMEM(half, BF), pltpu.VMEM(half, BF), pltpu.VMEM(wide, BF)] + wide_pad,
        flops,
    )
    dh1_in = [backward(x, d) for d, x in enumerate(dh_sends)]
    out1, mirror1, i1 = run(add_rows, (), (*rows1, q_rows), [((local, c), BF)] * 3)
    fwd1, mir1 = onward(out1, 0), mirrored(mirror1, 0)

    whole = pl.BlockSpec(memory_space=pltpu.VMEM)
    tap = pl.BlockSpec((1, w, c), lambda i: (i, 0, 0))
    grad_total = pl.pallas_call(
        functools.partial(kernel_grads, z),
        name="kernel_grads",
        grid=(18,),
        out_shape=jax.ShapeDtypeStruct((18, w, c), F32),
        in_specs=[whole] * 8 + [tap],
        out_specs=tap,
        scratch_shapes=[
            pltpu.VMEM((TICKS, w, cells), BF),
            pltpu.VMEM((cells + 16, c), F32),
            pltpu.VMEM((TICKS, 3, cells + 2 * z.cols, c), BF),
        ],
        compiler_params=pltpu.CompilerParams(vmem_limit_bytes=VMEM_LIMIT),
        cost_estimate=pl.CostEstimate(
            flops=4 * flops, bytes_accessed=2 * grad_acc.size * 4, transcendentals=0
        ),
    )(act_h0, act_h1, grad0, grad1, act_i0, act_i1, g0, g1, grad_acc.reshape(18, w, c))

    fwd_out, bwd_out, mir_out, stash_out, emitted = run(
        finish,
        (fs, bs),
        (*queues, *rows0, grad_in, skip_in, out1, i1, fwd1, mir1, *dh1_in),
        [((slots, local, c), BF)] * 3 + [((2 * slots, local, c), BF), ((TICKS, local, c), BF)],
    )
    return (
        fwd_out.reshape(fwd_queue.shape),
        bwd_out.reshape(bwd_queue.shape),
        mir_out.reshape(mirror_queue.shape),
        stash_out.reshape(stash.shape),
        grad_total.reshape(grad_acc.shape),
        emitted.reshape((1, TICKS) + fwd_queue.shape[2:]),
    )


def solution(mesh):
    return jax.shard_map(
        per_device,
        mesh=mesh,
        in_specs=(
            P("section", None, "row", None, None),
            P("section", None, "row", None, None),
            P("section", None, "row", None, None),
            P("section", None, None, "row", None, None),
            P("section", None, None, None, "row", None),
            P("section", None, None, None, "row", None),
            P(),
            P(),
        ),
        out_specs=(
            P("section", None, "row", None, None),
            P("section", None, "row", None, None),
            P("section", None, "row", None, None),
            P("section", None, None, "row", None, None),
            P("section", None, None, None, "row", None),
            P("section", None, "row", None, None),
        ),
        check_vma=False,
    )
```

```python
import functools

import jax
import jax.numpy as jnp
from jax import lax
from jax.experimental import pallas as pl
from jax.experimental.pallas import tpu as pltpu
from jax.sharding import PartitionSpec as P

GROUPS = 32
TICKS = 2
FOLD = 4
EPSILON = 1e-05
BF, F32 = jnp.bfloat16, jnp.float32
VMEM_LIMIT = 24 * 2**20


class Sizes:
    def __init__(self, queue, sections, rows):
        self.sections, self.parts = sections, rows
        self.cols = queue.shape[2]
        self.channels = queue.shape[3]
        self.local = queue.shape[1] * queue.shape[2]
        self.cells = self.local * rows
        self.share = self.channels // rows
        self.group = self.channels // GROUPS
        self.count = self.cells * self.group


def where_am_i():
    return lax.axis_index("section"), lax.axis_index("row")


def share_of(z, value, part):
    value = value.astype(F32)
    out = value[:, : z.share]
    for j in range(1, z.parts):
        out = jnp.where(part == j, value[:, j * z.share : (j + 1) * z.share], out)
    return out


def all_shares(z, own, others, row):
    out = []
    for j in range(z.parts):
        value = own
        for d in range(1, z.parts):
            value = jnp.where(lax.rem(row + z.parts - d, z.parts) == j, others[d - 1], value)
        out.append(value)
    return out


def side_by_side(values):
    return jnp.concatenate([value.astype(F32) for value in values], axis=1)


def fold(z, ref, value):
    rows = value.shape[0] // FOLD
    ref[...] = side_by_side([value[j * rows : (j + 1) * rows] for j in range(FOLD)]).astype(BF)


def unfold(z, ref):
    value = ref[...].astype(F32)
    return jnp.concatenate([value[:, j * z.share : (j + 1) * z.share] for j in range(FOLD)], axis=0)


def source(z, row, d):
    return lax.rem(row + z.parts - d, z.parts)


def target(z, row, d):
    return lax.rem(row + d, z.parts)


def part_rows(z, part):
    return pl.ds(pl.multiple_of(part * z.local, z.local), z.local)


def assemble(z, ref, pieces, row, start, width):
    for d, piece in enumerate(pieces):
        value = piece[...].astype(F32)[:, start : start + width]
        ref[part_rows(z, source(z, row, d)), :] = value.astype(BF)


def group_sums(z, first, second):
    width = first.shape[1]
    line = lax.broadcasted_iota(jnp.int32, (8, width), 0)
    both = jnp.where(line == 0, first, jnp.where(line == 1, second, 0.0))
    across = lax.broadcasted_iota(jnp.int32, (width, width), 1).astype(F32)
    down = lax.broadcasted_iota(jnp.int32, (width, width), 0).astype(F32)
    same = jnp.floor((across + 0.5) * (1.0 / z.group)) == jnp.floor((down + 0.5) * (1.0 / z.group))
    sums = jnp.dot(
        both, same.astype(F32), precision=lax.Precision.HIGHEST, preferred_element_type=F32
    )
    return sums[0:1], sums[1:2]


def normalize(z, x):
    total, square = group_sums(
        z, jnp.sum(x, axis=0, keepdims=True), jnp.sum(x * x, axis=0, keepdims=True)
    )
    center = total / z.count
    factor = lax.rsqrt(square / z.count - center * center + EPSILON)
    return (x - center) * factor, factor


def sigmoid(y):
    return 1.0 / (1.0 + jnp.exp(-y))


def norm_back(z, y, factor, logistic, upstream):
    e = upstream * logistic * (1.0 + y * (1.0 - logistic))
    first, second = group_sums(
        z, jnp.sum(e, axis=0, keepdims=True), jnp.sum(e * y, axis=0, keepdims=True)
    )
    return factor * (e - first / z.count - y * (second / z.count))


def spread(z, x, line_ref, pad_ref):
    cells, cols = z.cells, z.cols
    width = x.shape[1]
    line_ref[8 : 8 + cells, :] = x
    column = lax.rem(lax.broadcasted_iota(jnp.int32, (cells, 1), 0), cols)
    edge = jnp.zeros((cols, width), BF)
    for b in range(3):
        pad_ref[b, :cols, :] = edge
        pad_ref[b, cols + cells :, :] = edge
    pad_ref[1, cols : cols + cells, :] = x.astype(BF)
    left = jnp.where(column > 0, line_ref[7 : 7 + cells, :], 0.0)
    pad_ref[0, cols : cols + cells, :] = left.astype(BF)
    right = jnp.where(column < cols - 1, line_ref[9 : 9 + cells, :], 0.0)
    pad_ref[2, cols : cols + cells, :] = right.astype(BF)


def convolve(z, pad_ref, kernel_ref, which):
    total = None
    for a in range(3):
        for b in range(3):
            term = jnp.dot(
                pad_ref[b, a * z.cols : a * z.cols + z.cells, :],
                kernel_ref[9 * which + 3 * a + b],
                preferred_element_type=F32,
            )
            total = term if total is None else total + term
    return total


def convolve_back(z, pad_ref, kernel_ref, which):
    total = None
    for a in range(3):
        for b in range(3):
            term = lax.dot_general(
                pad_ref[b, a * z.cols : a * z.cols + z.cells, :],
                kernel_ref[9 * which + 3 * (2 - a) + 2 - b],
                (((1,), (1,)), ((), ())),
                preferred_element_type=F32,
            )
            total = term if total is None else total + term
    return total


def pad_shapes(z, width):
    return [
        pltpu.VMEM((z.cells + 16, width), F32),
        pltpu.VMEM((3, z.cells + 2 * z.cols, width), BF),
    ]


def call(body, name, scalars, arrays, outs, scratch=(), after=(), remote=0, far_outs=0, aliases=None):
    near, far = pl.BlockSpec(memory_space=pltpu.VMEM), pl.BlockSpec(memory_space=pltpu.HBM)

    def inner(*refs):
        given = len(scalars) + len(arrays)
        body(*refs[:given], *refs[given + len(after) :])

    arrays = [
        pltpu.with_memory_space_constraint(x, pltpu.HBM) if j < remote else x
        for j, x in enumerate(arrays)
    ]
    near_outs = len(outs) - far_outs
    return pl.pallas_call(
        inner,
        name=name,
        out_shape=[
            jax.ShapeDtypeStruct(shape, dtype) if j < near_outs else pltpu.HBM(shape, dtype)
            for j, (shape, dtype) in enumerate(outs)
        ],
        in_specs=[pl.BlockSpec(memory_space=pltpu.SMEM)] * len(scalars)
        + [far] * remote
        + [near] * (len(arrays) - remote)
        + [pl.BlockSpec(memory_space=pl.ANY)] * len(after),
        out_specs=[near] * near_outs + [far] * far_outs,
        scratch_shapes=list(scratch),
        input_output_aliases=aliases or {},
        compiler_params=pltpu.CompilerParams(vmem_limit_bytes=VMEM_LIMIT),
        cost_estimate=pl.CostEstimate(flops=1, bytes_accessed=1, transcendentals=0),
    )(*scalars, *arrays, *after)


def held_until(values, earlier):
    return lax.optimization_barrier((tuple(values), earlier))[0]


def fetch(pairs, sems):
    copies = [pltpu.make_async_copy(a, b, sems.at[j]) for j, (a, b) in enumerate(pairs)]
    for copy in copies:
        copy.start()
    for copy in copies:
        copy.wait()


def pack_first(z, fs_far, bs_far, fwd_far, bwd_far, mir_far, stash_far, *refs):
    outs = refs[: z.parts]
    fs, bs, fwd, bwd, mir, stash, sems = refs[z.parts :]
    fetch(
        [
            (fs_far, fs),
            (bs_far, bs),
            (fwd_far, fwd),
            (bwd_far, bwd),
            (mir_far, mir),
            (stash_far, stash),
        ],
        sems,
    )
    s, row = where_am_i()
    f, b = fs[0, s], bs[0, s]
    h, i = fwd[f], stash[2 * b + 1]
    g = bwd[b].astype(F32) + jnp.where(s < z.sections // 2, mir[b].astype(F32), 0.0)
    for d, out in enumerate(outs):
        part = target(z, row, d)
        out[...] = side_by_side([share_of(z, h, part), share_of(z, i, part), g]).astype(BF)


def taken_back(z, bs, s):
    later, partner = jnp.minimum(s + 1, z.sections - 1), z.sections - 1 - s
    return (
        jnp.logical_and(s < z.sections - 1, bs[0, later] == bs[1, s]),
        jnp.logical_and(s < z.sections // 2, bs[0, partner] == bs[1, s]),
    )


def pack_second(z, fs_far, bs_far, mir_far, stash_far, *outs):
    *outs, fs, bs, held, sems = outs
    fetch([(fs_far, fs), (bs_far, bs)], sems)
    s, row = where_am_i()
    fetch([(stash_far.at[2 * bs[0, s]], held.at[0]), (mir_far.at[fs[0, s]], held.at[1])], sems)
    for d, out in enumerate(outs):
        part = target(z, row, d)
        out[...] = side_by_side([share_of(z, held[j], part) for j in (0, 1)]).astype(BF)


def pack_third(z, fs_far, bs_far, fwd_far, bwd_far, mir_far, stash_far, *outs):
    *outs, fs, bs, held, sems = outs
    fetch([(fs_far, fs), (bs_far, bs)], sems)
    s, row = where_am_i()
    f1, b1 = fs[1, s], bs[1, s]
    places = (
        fwd_far.at[f1],
        stash_far.at[2 * b1],
        stash_far.at[2 * b1 + 1],
        bwd_far.at[b1],
        mir_far.at[b1],
        mir_far.at[f1],
    )
    fetch([(place, held.at[j]) for j, place in enumerate(places)], sems)
    grad_taken, skip_taken = taken_back(z, bs, s)
    skip_kept = jnp.logical_and(s < z.sections // 2, jnp.logical_not(skip_taken))
    kept = jnp.where(grad_taken, 0.0, held[3].astype(F32))
    kept = kept + jnp.where(skip_kept, held[4].astype(F32), 0.0)
    for d, out in enumerate(outs):
        part = target(z, row, d)
        values = [share_of(z, held[j], part) for j in (0, 1, 2)] + [kept]
        out[...] = side_by_side(values + [share_of(z, held[5], part)]).astype(BF)


def send_partials(z, row, total, own, sends):
    own[...] = share_of(z, total, row)
    for d, send in enumerate(sends, 1):
        fold(z, send, share_of(z, total, target(z, row, d)))


def first_forward(z, *refs):
    n = z.parts
    pieces, kernel, (own, h_out), sends = refs[:n], refs[n], refs[n + 1 : n + 3], refs[n + 3 : 2 * n + 2]
    line, pad = refs[2 * n + 2 :]
    _, row = where_am_i()
    assemble(z, h_out, pieces, row, 0, z.share)
    y, _ = normalize(z, h_out[...].astype(F32))
    spread(z, y * sigmoid(y), line, pad)
    send_partials(z, row, convolve(z, pad, kernel, 0), own, sends)


def later_forward(z, fs, *refs):
    n = z.parts
    arrivals, pieces, kernel = refs[:n], refs[n : 2 * n], refs[2 * n]
    own, h_out, arrived = refs[2 * n + 1 : 2 * n + 4]
    sends = refs[2 * n + 4 : 3 * n + 3]
    line, pad = refs[3 * n + 3 :]
    s, row = where_am_i()
    total = unfold(z, arrivals[0])
    for other in arrivals[1:]:
        total = total + unfold(z, other)
    total = total.astype(BF).astype(F32)
    arrived[...] = total.astype(BF)
    assemble(z, h_out, pieces, row, 0, z.share)
    prior = jnp.maximum(s - 1, 0)
    taken = jnp.logical_and(s > 0, fs[0, prior] == fs[1, s])
    h = jnp.where(taken, total, h_out[...].astype(F32))
    h_out[...] = h.astype(BF)
    y, _ = normalize(z, h)
    spread(z, y * sigmoid(y), line, pad)
    send_partials(z, row, convolve(z, pad, kernel, 0), own, sends)


def back_through_second(z, i, g, kernel, q_out, q_send, act_out, pad, line):
    y, factor = normalize(z, i.astype(F32))
    logistic = sigmoid(y)
    act_out[...] = (y * logistic).astype(BF)
    spread(z, g, line, pad)
    q = norm_back(z, y, factor, logistic, convolve_back(z, pad, kernel, 1)).astype(BF)
    q_out[...] = q
    fold(z, q_send, q.astype(F32))


def first_backward(z, *refs):
    n = z.parts
    pieces, kernel = refs[:n], refs[n]
    q_out, q_send, pad, act_out, i_ref, g_ref, line = refs[n + 1 :]
    _, row = where_am_i()
    assemble(z, i_ref, pieces, row, z.share, z.share)
    assemble(z, g_ref, pieces, row, 2 * z.share, z.channels)
    back_through_second(
        z, i_ref[...], g_ref[...].astype(F32), kernel, q_out, q_send, act_out, pad, line
    )


def later_backward(z, fs, bs, *refs):
    n = z.parts
    arrivals, mirrors, pieces = refs[:n], refs[n : 2 * n], refs[2 * n : 3 * n]
    i_before, kernel = refs[3 * n : 3 * n + 2]
    q_out, q_send, pad, act_out, grad_in, skip_in, i_ref, full, line = refs[3 * n + 2 :]
    s, row = where_am_i()
    w = z.share
    for out, parts in ((grad_in, arrivals), (skip_in, mirrors)):
        shares = [unfold(z, part) for part in parts]
        out[...] = side_by_side(all_shares(z, shares[0], shares[1:], row)).astype(BF)
    grad_taken, skip_taken = taken_back(z, bs, s)
    assemble(z, full, pieces, row, 3 * w, z.channels)
    g = full[...].astype(F32) + jnp.where(grad_taken, grad_in[...].astype(F32), 0.0)
    g = g + jnp.where(skip_taken, skip_in[...].astype(F32), 0.0)
    g = g.astype(BF).astype(F32)
    assemble(z, i_ref, pieces, row, 2 * w, w)
    i = jnp.where(fs[0, s] == bs[1, s], i_before[...].astype(F32), i_ref[...].astype(F32))
    back_through_second(z, i, g, kernel, q_out, q_send, act_out, pad, line)


def second_convolution(z, encoder, row, own, received, skip, h, kernel, i_out, full, line, pad):
    c0 = own[...]
    for other in received:
        c0 = c0 + unfold(z, other)
    i = jnp.where(encoder, c0, skip.astype(F32)).astype(BF)
    i_out[...] = i
    y, _ = normalize(z, i.astype(F32))
    spread(z, y * sigmoid(y), line, pad)
    total = convolve(z, pad, kernel, 1)
    base = h[...].astype(F32) + jnp.where(encoder, 0.0, c0)
    full[...] = total + side_by_side([jnp.where(row == j, base, 0.0) for j in range(z.parts)])


def middle(z, pad):
    return pad[1, z.cols : z.cols + z.cells, :].astype(F32)


def second_forward(z, *refs):
    n = z.parts
    own, received, h = refs[0], refs[1:n], refs[n]
    pieces, q, kernel = refs[n + 1 : 2 * n + 1], refs[2 * n + 1], refs[2 * n + 2]
    i_out, full_out = refs[2 * n + 3 : 2 * n + 5]
    sends, mirrors = refs[2 * n + 5 : 3 * n + 5], refs[3 * n + 5 : 4 * n + 5]
    skip, full, line, pad = refs[4 * n + 5 :]
    s, row = where_am_i()
    encoder = s < z.sections // 2
    assemble(z, skip, pieces, row, z.share, z.share)
    second_convolution(
        z, encoder, row, own, received, skip[...], h, kernel, i_out, full, line, pad
    )
    full_out[...] = full[...].astype(BF)
    q_now = q[...].astype(F32)
    for d in range(n):
        piece = share_of(z, full[...], target(z, row, d))
        fold(z, sends[d], piece)
        fold(z, mirrors[d], jnp.where(encoder, piece, q_now))


def last_forward(z, fs, *refs):
    n = z.parts
    own, received, h = refs[0], refs[1:n], refs[n]
    pieces, arrived, kernel = refs[n + 1 : 2 * n + 1], refs[2 * n + 1], refs[2 * n + 2]
    sends = refs[2 * n + 3 : 3 * n + 3]
    i_out, skip, full, line, pad = refs[3 * n + 3 :]
    s, row = where_am_i()
    encoder = s < z.sections // 2
    partner = z.sections - 1 - s
    assemble(z, skip, pieces, row, 3 * z.share + z.channels, z.share)
    now = jnp.where(
        fs[0, partner] == fs[1, s], arrived[...].astype(F32), skip[...].astype(F32)
    )
    second_convolution(z, encoder, row, own, received, now, h, kernel, i_out, full, line, pad)
    for d, send in enumerate(sends):
        at = part_rows(z, target(z, row, d))
        send[...] = side_by_side([full[at, :], i_out[at, :]]).astype(BF)


def back_through_first(z, encoder, row, q, received, g_pad, h, kernel, act_out, pad, line):
    g = middle(z, g_pad)
    shares = all_shares(z, q[...].astype(F32), [unfold(z, other) for other in received], row)
    whole = side_by_side(shares)
    now = jnp.where(encoder, whole, g)
    y, factor = normalize(z, h.astype(F32))
    logistic = sigmoid(y)
    act_out[...] = (y * logistic).astype(BF)
    spread(z, now, line, pad)
    back = norm_back(z, y, factor, logistic, convolve_back(z, pad, kernel, 0))
    return share_of(z, g, row) + back, whole


def second_backward(z, *refs):
    n = z.parts
    q, received, g, pieces, kernel = refs[0], refs[1:n], refs[n], refs[n + 1 : 2 * n + 1], refs[2 * n + 1]
    send, pad, act_out, h, line = refs[2 * n + 2 :]
    s, row = where_am_i()
    assemble(z, h, pieces, row, 0, z.share)
    value, _ = back_through_first(
        z, s < z.sections // 2, row, q, received, g, h[...], kernel, act_out, pad, line
    )
    fold(z, send, value)


def last_backward(z, fs, bs, *refs):
    n = z.parts
    q, received, g, pieces = refs[0], refs[1:n], refs[n], refs[n + 1 : 2 * n + 1]
    h_before, kernel = refs[2 * n + 1 : 2 * n + 3]
    sends = refs[2 * n + 3 : 3 * n + 3]
    q_rows, pad, act_out, h, value, whole, line = refs[3 * n + 3 :]
    s, row = where_am_i()
    assemble(z, h, pieces, row, z.share, z.share)
    now = jnp.where(fs[0, s] == bs[1, s], h_before[...], h[...])
    result, entered = back_through_first(
        z, s < z.sections // 2, row, q, received, g, now, kernel, act_out, pad, line
    )
    value[...] = result.astype(BF)
    for d, send in enumerate(sends):
        fold(z, send, value[part_rows(z, target(z, row, d)), :])
    whole[...] = entered.astype(BF)
    q_rows[...] = whole[part_rows(z, row), :]


def pack_rows(z, *refs):
    n = z.parts
    full, i, arrived, mirrors = refs[0], refs[1], refs[2], refs[3 : n + 3]
    sends, skip = refs[n + 3 : 2 * n + 3], refs[2 * n + 3]
    _, row = where_am_i()
    total = unfold(z, mirrors[0])
    for other in mirrors[1:]:
        total = total + unfold(z, other)
    skip[...] = total.astype(BF)
    for d, send in enumerate(sends):
        at = part_rows(z, target(z, row, d))
        send[...] = side_by_side([ref[at, :] for ref in (full, i, arrived, skip)]).astype(BF)


def add_rows(z, *refs):
    n = z.parts
    pieces, q_rows = refs[:n], refs[n]
    out, mirror, i_rows = refs[n + 1 :]
    s, row = where_am_i()
    c = z.channels
    values = [piece[...].astype(F32) for piece in pieces]
    total = sum(value[:, :c] for value in values)
    out[...] = total.astype(BF)
    mirror[...] = jnp.where(s < z.sections // 2, total, q_rows[...].astype(F32)).astype(BF)
    shares = all_shares(z, values[0][:, c:], [value[:, c:] for value in values[1:]], row)
    i_rows[...] = side_by_side(shares).astype(BF)


def finish_first(z, fs, bs, fwd, bwd, mir, stash, *refs):
    n = z.parts
    rows0, (grad_in, skip_in) = refs[:n], refs[n : n + 2]
    fwd_out, bwd_out, mir_out, stash_out, emitted = refs[n + 2 : n + 7]
    out0, fwd_in, i0, skip, grads, sems = refs[n + 7 :]
    s, row = where_am_i()
    encoder = s < z.sections // 2
    c, w = z.channels, z.share
    prior, later = jnp.maximum(s - 1, 0), jnp.minimum(s + 1, z.sections - 1)
    partner = z.sections - 1 - s
    f0, f1 = fs[0, s], fs[1, s]
    has_prior, has_later = s > 0, s < z.sections - 1
    mine = part_rows(z, row)
    whole = [
        pltpu.make_async_copy(a, b, sems.at[j])
        for j, (a, b) in enumerate(
            ((fwd, fwd_out), (bwd, bwd_out), (mir, mir_out), (stash, stash_out))
        )
    ]
    for copy in whole:
        copy.start()

    pieces = [piece[...].astype(F32) for piece in rows0]

    def joined(at):
        shares = [piece[:, at : at + w] for piece in pieces]
        return side_by_side(all_shares(z, shares[0], shares[1:], row))

    out0[...] = sum(piece[:, :c] for piece in pieces).astype(BF)
    i0[...] = joined(c).astype(BF)
    fwd_in[...] = joined(c + w).astype(BF)
    skip[...] = jnp.where(encoder, skip_in[mine, :].astype(F32), joined(c + 2 * w)).astype(BF)
    grads[...] = grad_in[mine, :]
    for copy in whole:
        copy.wait()

    def put(source, place, j):
        return pltpu.make_async_copy(source, place, sems.at[j])

    always = [
        put(out0, emitted.at[0], 4),
        put(i0, stash_out.at[2 * f0 + 1], 5),
        put(fwd.at[f0], stash_out.at[2 * f0], 6),
        put(skip, mir_out.at[jnp.where(encoder, bs[0, partner], fs[0, partner])], 7),
    ]
    for copy in always:
        copy.start()
    onward, back = put(fwd_in, fwd_out.at[fs[0, prior]], 8), put(grads, bwd_out.at[bs[0, later]], 9)
    pl.when(has_prior)(onward.start)
    pl.when(has_later)(back.start)
    for copy in always:
        copy.wait()
    taken = jnp.logical_and(has_prior, fs[0, prior] == f1)
    moved, same = put(fwd_in, stash_out.at[2 * f1], 10), put(fwd.at[f1], stash_out.at[2 * f1], 11)
    pl.when(taken)(moved.start)
    pl.when(jnp.logical_not(taken))(same.start)
    pl.when(has_prior)(onward.wait)
    pl.when(has_later)(back.wait)
    pl.when(taken)(moved.wait)
    pl.when(jnp.logical_not(taken))(same.wait)


def finish_last(z, fs, bs, *refs):
    n = z.parts
    out1, i1, fwd1, mir1 = refs[5:9]
    grads1 = refs[9 : n + 9]
    fwd_out, bwd_out, mir_out, stash_out, emitted, grads, sems = refs[n + 9 :]
    s, row = where_am_i()
    prior, later = jnp.maximum(s - 1, 0), jnp.minimum(s + 1, z.sections - 1)
    partner = z.sections - 1 - s
    has_prior, has_later = s > 0, s < z.sections - 1
    slot = jnp.where(s < z.sections // 2, bs[1, partner], fs[1, partner])

    def put(source, place, j):
        return pltpu.make_async_copy(source, place, sems.at[j])

    always = [
        put(out1, emitted.at[1], 0),
        put(i1, stash_out.at[2 * fs[1, s] + 1], 1),
        put(mir1, mir_out.at[slot], 2),
    ]
    for copy in always:
        copy.start()
    onward, back = put(fwd1, fwd_out.at[fs[1, prior]], 3), put(grads, bwd_out.at[bs[1, later]], 4)
    pl.when(has_prior)(onward.start)
    shares = [unfold(z, piece) for piece in grads1]
    grads[...] = side_by_side(all_shares(z, shares[0], shares[1:], row)).astype(BF)
    pl.when(has_later)(back.start)
    for copy in always:
        copy.wait()
    pl.when(has_prior)(onward.wait)
    pl.when(has_later)(back.wait)


def add_taps(z, act, pad, before, store):
    turned = jnp.transpose(act[...].astype(F32)).astype(BF)
    for tap in range(9):
        a, b = divmod(tap, 3)
        at = (2 - a) * z.cols
        moved = pad[2 - b, at : at + z.cells, :]
        store(tap, before(tap) + jnp.dot(turned, moved, preferred_element_type=F32))


def kernel_grads_first(z, which, acc, act, pad, out, held, sems):
    copies = [
        pltpu.make_async_copy(acc.at[9 * which + tap], held.at[tap], sems.at[tap]) for tap in range(9)
    ]
    for copy in copies:
        copy.start()

    def before(tap):
        copies[tap].wait()
        return held[tap]

    def store(tap, value):
        out[tap] = value

    add_taps(z, act, pad, before, store)


def kernel_grads_last(z, which, *refs):
    total, act, pad, token, out, held, sems = refs[-7:]
    token[...] = jnp.zeros_like(token)
    copies = [
        pltpu.make_async_copy(held.at[tap], out.at[9 * which + tap], sems.at[tap]) for tap in range(9)
    ]

    def store(tap, value):
        held[tap] = value
        copies[tap].start()

    add_taps(z, act, pad, lambda tap: total[tap], store)
    for copy in copies:
        copy.wait()


def per_device(fwd_queue, bwd_queue, mirror_queue, stash, weights, grad_acc, fwd_slot, bwd_slot):
    sections, n = lax.axis_size("section"), lax.axis_size("row")
    z = Sizes(fwd_queue[0], sections, n)
    slots = fwd_queue.shape[1]
    c, w, local, cells = z.channels, z.share, z.local, z.cells
    fwd, bwd, mir = (x.reshape(slots, local, c) for x in (fwd_queue, bwd_queue, mirror_queue))
    kept = stash.reshape(2 * slots, local, c)
    kernels = weights.reshape(18, w, c)
    acc = grad_acc.reshape(18, w, c)
    fs, bs = fwd_slot.T, bwd_slot.T
    folded, wide = (cells // FOLD, FOLD * w), (cells, c)
    half = (cells, w)
    padded = (3, cells + 2 * z.cols, c)

    def move(x, d, step):
        route = [
            (s * n + r, step(s) * n + (r + d) % n) for s in range(sections) for r in range(n)
        ]
        return lax.ppermute(x, ("section", "row"), route)

    across = functools.partial(move, step=lambda s: s)
    onward = functools.partial(move, step=lambda s: (s + 1) % sections)
    backward = functools.partial(move, step=lambda s: (s - 1) % sections)
    mirrored = functools.partial(move, step=lambda s: sections - 1 - s)

    def run(body, scalars, arrays, outs, scratch=(), **options):
        return call(
            functools.partial(body, z), body.__name__, scalars, arrays, outs, scratch, **options
        )

    def exchange(pieces):
        return [pieces[0]] + [across(piece, d) for d, piece in enumerate(pieces[1:], 1)]

    narrow_pad = pad_shapes(z, w)
    wide_line = pltpu.VMEM((cells + 16, c), F32)
    queues = (fwd, bwd, mir, kept)
    rows = (local, c)
    sems = pltpu.SemaphoreType.DMA
    first = exchange(
        run(
            pack_first,
            (),
            (fs, bs, *queues),
            [((local, 2 * w + c), BF)] * n,
            [pltpu.SMEM(fs.shape, jnp.int32)] * 2
            + [pltpu.VMEM(x.shape, BF) for x in queues]
            + [sems((6,))],
            remote=6,
        )
    )
    soon = exchange(
        run(
            pack_second,
            (),
            (fs, bs, mir, kept),
            [((local, 2 * w), BF)] * n,
            [pltpu.SMEM(fs.shape, jnp.int32)] * 2 + [pltpu.VMEM((2, local, c), BF), sems((2,))],
            remote=4,
            after=(first[0],),
        )
    )
    packed = run(
        pack_third,
        (),
        (fs, bs, *queues),
        [((local, 4 * w + c), BF)] * n,
        [pltpu.SMEM(fs.shape, jnp.int32)] * 2 + [pltpu.VMEM((6, local, c), BF), sems((6,))],
        remote=6,
        after=(soon[0],),
    )
    late = exchange(held_until(packed, first[1]))

    own, h0, *sends = run(
        first_forward,
        (),
        (*first, kernels),
        [(half, F32), (half, BF)] + [(folded, BF)] * (n - 1),
        narrow_pad,
        after=(packed[0],),
    )
    received = [across(x, d) for d, x in enumerate(sends, 1)]
    q0, q_send, g_pad0, act_i0 = run(
        first_backward,
        (),
        (*first, kernels),
        [(half, BF), (folded, BF), (padded, BF), (half, BF)],
        [pltpu.VMEM(half, BF), pltpu.VMEM(wide, BF), wide_line],
        after=(own,),
    )
    q_received = [across(q_send, d) for d in range(1, n)]

    def start_grads(which, act, pad, after):
        [out] = call(
            functools.partial(kernel_grads_first, z, which),
            f"kernel_grads_first_{which}",
            (),
            (acc, act, pad),
            [((9, w, c), F32)],
            [pltpu.VMEM((9, w, c), F32), sems((9,))],
            remote=1,
            after=after,
        )
        return out

    def end_grads(which, earlier, total, act, pad, after):
        token, out = call(
            functools.partial(kernel_grads_last, z, which),
            f"kernel_grads_last_{which}",
            (),
            (*earlier, total, act, pad),
            [((8, 128), F32), ((18, w, c), F32)],
            [pltpu.VMEM((9, w, c), F32), sems((9,))],
            remote=len(earlier),
            far_outs=1,
            after=after,
            aliases={0: 1} if earlier else None,
        )
        return token, out

    sum_i = start_grads(1, act_i0, g_pad0, (q_send,))
    i0, full0, *sends = run(
        second_forward,
        (),
        (own, *received, h0, *soon, q0, kernels),
        [(half, BF), (wide, BF)] + [(folded, BF)] * (2 * n),
        [pltpu.VMEM(half, BF), pltpu.VMEM(wide, F32)] + narrow_pad,
        after=(sum_i,),
    )
    fwd_in = [onward(x, d) for d, x in enumerate(sends[:n])]
    mir_in = [mirrored(x, d) for d, x in enumerate(sends[n:])]
    dh_send, f_pad0, act_h0 = run(
        second_backward,
        (),
        (q0, *q_received, g_pad0, *soon, kernels),
        [(folded, BF), (padded, BF), (half, BF)],
        [pltpu.VMEM(half, BF), wide_line],
        after=(i0,),
    )
    dh_in = [backward(dh_send, d) for d in range(n)]

    own, h1, arrived, *sends = run(
        later_forward,
        (fs,),
        (*fwd_in, *late, kernels),
        [(half, F32), (half, BF), (half, BF)] + [(folded, BF)] * (n - 1),
        narrow_pad,
        after=(dh_send,),
    )
    received = [across(x, d) for d, x in enumerate(sends, 1)]
    sum_h = start_grads(0, act_h0, f_pad0, (own,))
    q1, q_send, g_pad1, act_i1, grad_in, skip_in = run(
        later_backward,
        (fs, bs),
        (*dh_in, *mir_in, *late, i0, kernels),
        [(half, BF), (folded, BF), (padded, BF), (half, BF), (wide, BF), (wide, BF)],
        [pltpu.VMEM(half, BF), pltpu.VMEM(wide, BF), wide_line],
        after=(sum_h,),
    )
    q_received = [across(q_send, d) for d in range(1, n)]
    *sends, skip_arrived = run(
        pack_rows,
        (),
        (full0, i0, arrived, *mir_in),
        [((local, c + 3 * w), BF)] * n + [(half, BF)],
        after=(q_send,),
    )
    rows0 = exchange(sends)
    sends = run(
        last_forward,
        (fs,),
        (own, *received, h1, *late, skip_arrived, kernels),
        [((local, c + w), BF)] * n,
        [pltpu.VMEM(half, BF), pltpu.VMEM(half, BF), pltpu.VMEM(wide, F32)] + narrow_pad,
    )
    rows1 = exchange(sends)
    token, part_i = end_grads(1, (), sum_i, act_i1, g_pad1, (sends[0],))
    *dh_sends, q_rows, f_pad1, act_h1 = run(
        last_backward,
        (fs, bs),
        (q1, *q_received, g_pad1, *late, h0, kernels),
        [((local // FOLD, FOLD * w), BF)] * n + [(rows, BF), (padded, BF), (half, BF)],
        [pltpu.VMEM(half, BF), pltpu.VMEM(half, BF), pltpu.VMEM(wide, BF), wide_line],
        after=(token,),
    )
    dh1_in = [backward(x, d) for d, x in enumerate(dh_sends)]
    out1, mirror1, i1 = run(add_rows, (), (*rows1, q_rows), [(rows, BF)] * 3)
    fwd1, mir1 = onward(out1, 0), mirrored(mirror1, 0)
    _, grad_total = end_grads(0, (part_i,), sum_h, act_h1, f_pad1, (out1,))
    written = [(x.shape, BF) for x in queues] + [((TICKS, local, c), BF)]
    early = run(
        finish_first,
        (fs, bs),
        (*queues, *rows0, grad_in, skip_in),
        written,
        [pltpu.VMEM(rows, BF)] * 5 + [sems((12,))],
        remote=4,
        far_outs=5,
        after=(out1,),
    )
    fwd_out, bwd_out, mir_out, stash_out, emitted = run(
        finish_last,
        (fs, bs),
        (*early, out1, i1, fwd1, mir1, *dh1_in),
        written,
        [pltpu.VMEM(rows, BF), sems((5,))],
        remote=5,
        far_outs=5,
        aliases={j + 2: j for j in range(5)},
    )
    return (
        fwd_out.reshape(fwd_queue.shape),
        bwd_out.reshape(bwd_queue.shape),
        mir_out.reshape(mirror_queue.shape),
        stash_out.reshape(stash.shape),
        grad_total.reshape(grad_acc.shape),
        emitted.reshape((1, TICKS) + fwd_queue.shape[2:]),
    )


def solution(mesh):
    return jax.shard_map(
        per_device,
        mesh=mesh,
        in_specs=(
            P("section", None, "row", None, None),
            P("section", None, "row", None, None),
            P("section", None, "row", None, None),
            P("section", None, None, "row", None, None),
            P("section", None, None, None, "row", None),
            P("section", None, None, None, "row", None),
            P(),
            P(),
        ),
        out_specs=(
            P("section", None, "row", None, None),
            P("section", None, "row", None, None),
            P("section", None, "row", None, None),
            P("section", None, None, "row", None, None),
            P("section", None, None, None, "row", None),
            P("section", None, "row", None, None),
        ),
        check_vma=False,
    )
```

```python
import functools

import jax
import jax.numpy as jnp
from jax import lax
from jax.experimental import pallas as pl
from jax.experimental.pallas import tpu as pltpu
from jax.sharding import PartitionSpec as P

GROUPS = 32
TICKS = 2
FOLD = 4
EPSILON = 1e-05
BF, F32 = jnp.bfloat16, jnp.float32
VMEM_LIMIT = 24 * 2**20


class Sizes:
    def __init__(self, queue, sections, rows):
        self.sections, self.parts = sections, rows
        self.cols = queue.shape[2]
        self.channels = queue.shape[3]
        self.local = queue.shape[1] * queue.shape[2]
        self.cells = self.local * rows
        self.share = self.channels // rows
        self.group = self.channels // GROUPS
        self.count = self.cells * self.group


def where_am_i():
    return lax.axis_index("section"), lax.axis_index("row")


def share_of(z, value, part):
    value = value.astype(F32)
    out = value[:, : z.share]
    for j in range(1, z.parts):
        out = jnp.where(part == j, value[:, j * z.share : (j + 1) * z.share], out)
    return out


def all_shares(z, own, others, row):
    out = []
    for j in range(z.parts):
        value = own
        for d in range(1, z.parts):
            value = jnp.where(lax.rem(row + z.parts - d, z.parts) == j, others[d - 1], value)
        out.append(value)
    return out


def side_by_side(values):
    return jnp.concatenate([value.astype(F32) for value in values], axis=1)


def folded(value, blocks):
    rows = value.shape[0] // blocks
    return side_by_side([value[j * rows : (j + 1) * rows] for j in range(blocks)])


def unfolded(value, blocks):
    value, width = value.astype(F32), value.shape[1] // blocks
    return jnp.concatenate([value[:, j * width : (j + 1) * width] for j in range(blocks)], axis=0)


def fold(z, ref, value):
    ref[...] = folded(value, FOLD).astype(BF)


def unfold(z, ref):
    return unfolded(ref[...], FOLD)


def source(z, row, d):
    return lax.rem(row + z.parts - d, z.parts)


def target(z, row, d):
    return lax.rem(row + d, z.parts)


def part_rows(z, part):
    return pl.ds(pl.multiple_of(part * z.local, z.local), z.local)


def assemble(z, ref, pieces, row, start, width):
    for d, piece in enumerate(pieces):
        value = (piece if isinstance(piece, jax.Array) else piece[...]).astype(F32)
        value = value[:, start : start + width]
        ref[part_rows(z, source(z, row, d)), :] = value.astype(BF)


def group_sums(z, first, second):
    width = first.shape[1]
    line = lax.broadcasted_iota(jnp.int32, (8, width), 0)
    both = jnp.where(line == 0, first, jnp.where(line == 1, second, 0.0))
    across = lax.broadcasted_iota(jnp.int32, (width, width), 1).astype(F32)
    down = lax.broadcasted_iota(jnp.int32, (width, width), 0).astype(F32)
    same = jnp.floor((across + 0.5) * (1.0 / z.group)) == jnp.floor((down + 0.5) * (1.0 / z.group))
    sums = jnp.dot(
        both, same.astype(F32), precision=lax.Precision.HIGHEST, preferred_element_type=F32
    )
    return sums[0:1], sums[1:2]


def normalize(z, x):
    total, square = group_sums(
        z, jnp.sum(x, axis=0, keepdims=True), jnp.sum(x * x, axis=0, keepdims=True)
    )
    center = total / z.count
    factor = lax.rsqrt(square / z.count - center * center + EPSILON)
    return (x - center) * factor, factor


def sigmoid(y):
    return 1.0 / (1.0 + jnp.exp(-y))


def norm_back(z, y, factor, logistic, upstream):
    e = upstream * logistic * (1.0 + y * (1.0 - logistic))
    first, second = group_sums(
        z, jnp.sum(e, axis=0, keepdims=True), jnp.sum(e * y, axis=0, keepdims=True)
    )
    return factor * (e - first / z.count - y * (second / z.count))


def spread(z, x, line_ref, pad_ref):
    cells, cols = z.cells, z.cols
    width = x.shape[1]
    line_ref[8 : 8 + cells, :] = x
    column = lax.rem(lax.broadcasted_iota(jnp.int32, (cells, 1), 0), cols)
    edge = jnp.zeros((cols, width), BF)
    for b in range(3):
        pad_ref[b, :cols, :] = edge
        pad_ref[b, cols + cells :, :] = edge
    pad_ref[1, cols : cols + cells, :] = x.astype(BF)
    left = jnp.where(column > 0, line_ref[7 : 7 + cells, :], 0.0)
    pad_ref[0, cols : cols + cells, :] = left.astype(BF)
    right = jnp.where(column < cols - 1, line_ref[9 : 9 + cells, :], 0.0)
    pad_ref[2, cols : cols + cells, :] = right.astype(BF)


def convolve(z, pad_ref, kernel_ref, which):
    total = None
    for a in range(3):
        for b in range(3):
            term = jnp.dot(
                pad_ref[b, a * z.cols : a * z.cols + z.cells, :],
                kernel_ref[9 * which + 3 * a + b],
                preferred_element_type=F32,
            )
            total = term if total is None else total + term
    return total


def convolve_back(z, pad_ref, kernel_ref, which):
    total = None
    for a in range(3):
        for b in range(3):
            term = lax.dot_general(
                pad_ref[b, a * z.cols : a * z.cols + z.cells, :],
                kernel_ref[9 * which + 3 * (2 - a) + 2 - b],
                (((1,), (1,)), ((), ())),
                preferred_element_type=F32,
            )
            total = term if total is None else total + term
    return total


def pad_shapes(z, width):
    return [
        pltpu.VMEM((z.cells + 16, width), F32),
        pltpu.VMEM((3, z.cells + 2 * z.cols, width), BF),
    ]


def call(body, name, scalars, arrays, outs, scratch=(), after=(), remote=0, far_outs=0, aliases=None):
    near, far = pl.BlockSpec(memory_space=pltpu.VMEM), pl.BlockSpec(memory_space=pltpu.HBM)

    def inner(*refs):
        given = len(scalars) + len(arrays)
        body(*refs[:given], *refs[given + len(after) :])

    arrays = [
        pltpu.with_memory_space_constraint(x, pltpu.HBM) if j < remote else x
        for j, x in enumerate(arrays)
    ]
    near_outs = len(outs) - far_outs
    return pl.pallas_call(
        inner,
        name=name,
        out_shape=[
            jax.ShapeDtypeStruct(shape, dtype) if j < near_outs else pltpu.HBM(shape, dtype)
            for j, (shape, dtype) in enumerate(outs)
        ],
        in_specs=[pl.BlockSpec(memory_space=pltpu.SMEM)] * len(scalars)
        + [far] * remote
        + [near] * (len(arrays) - remote)
        + [pl.BlockSpec(memory_space=pl.ANY)] * len(after),
        out_specs=[near] * near_outs + [far] * far_outs,
        scratch_shapes=list(scratch),
        input_output_aliases=aliases or {},
        compiler_params=pltpu.CompilerParams(vmem_limit_bytes=VMEM_LIMIT),
        cost_estimate=pl.CostEstimate(flops=1, bytes_accessed=1, transcendentals=0),
    )(*scalars, *arrays, *after)


def held_until(values, earlier):
    return lax.optimization_barrier((tuple(values), earlier))[0]


def fetch(pairs, sems):
    copies = [pltpu.make_async_copy(a, b, sems.at[j]) for j, (a, b) in enumerate(pairs)]
    for copy in copies:
        copy.start()
    for copy in copies:
        copy.wait()


def pack_first(z, fs_far, bs_far, fwd_far, bwd_far, mir_far, stash_far, *refs):
    outs = refs[: z.parts]
    fs, bs, fwd, bwd, mir, stash, sems = refs[z.parts :]
    fetch(
        [
            (fs_far, fs),
            (bs_far, bs),
            (fwd_far, fwd),
            (bwd_far, bwd),
            (mir_far, mir),
            (stash_far, stash),
        ],
        sems,
    )
    s, row = where_am_i()
    f, b = fs[0, s], bs[0, s]
    h, i = fwd[f], stash[2 * b + 1]
    g = bwd[b].astype(F32) + jnp.where(s < z.sections // 2, mir[b].astype(F32), 0.0)
    for d, out in enumerate(outs):
        part = target(z, row, d)
        out[...] = side_by_side([share_of(z, h, part), share_of(z, i, part), g]).astype(BF)


def taken_back(z, bs, s):
    later, partner = jnp.minimum(s + 1, z.sections - 1), z.sections - 1 - s
    return (
        jnp.logical_and(s < z.sections - 1, bs[0, later] == bs[1, s]),
        jnp.logical_and(s < z.sections // 2, bs[0, partner] == bs[1, s]),
    )


def pack_later(z, fs_far, bs_far, fwd_far, bwd_far, mir_far, stash_far, *refs):
    n = z.parts
    soon, late = refs[:n], refs[n : 2 * n]
    fs, bs, held, sems = refs[2 * n :]
    fetch([(fs_far, fs), (bs_far, bs)], sems)
    s, row = where_am_i()
    f1, b1 = fs[1, s], bs[1, s]
    places = (
        stash_far.at[2 * bs[0, s]],
        mir_far.at[fs[0, s]],
        fwd_far.at[f1],
        stash_far.at[2 * b1],
        stash_far.at[2 * b1 + 1],
        mir_far.at[f1],
        bwd_far.at[b1],
        mir_far.at[b1],
    )
    fetch([(place, held.at[j]) for j, place in enumerate(places)], sems)
    grad_taken, skip_taken = taken_back(z, bs, s)
    skip_kept = jnp.logical_and(s < z.sections // 2, jnp.logical_not(skip_taken))
    kept = jnp.where(grad_taken, 0.0, held[6].astype(F32))
    kept = kept + jnp.where(skip_kept, held[7].astype(F32), 0.0)
    for d in range(n):
        shares = [share_of(z, held[j], target(z, row, d)) for j in range(6)]
        soon[d][...] = folded(side_by_side(shares[:2]), 2).astype(BF)
        late[d][...] = side_by_side(shares[2:] + [kept]).astype(BF)


def send_partials(z, row, total, own, sends, extra=None):
    own[...] = share_of(z, total, row)
    for d, send in enumerate(sends, 1):
        part = folded(share_of(z, total, target(z, row, d)), FOLD).astype(BF)
        send[: part.shape[0], :] = part
        if extra:
            send[part.shape[0] :, :] = extra[d][...]


def first_forward(z, *refs):
    n = z.parts
    pieces, soon, kernel = refs[:n], refs[n : 2 * n], refs[2 * n]
    own, h_out = refs[2 * n + 1 : 2 * n + 3]
    sends, (line, pad) = refs[2 * n + 3 : 3 * n + 2], refs[3 * n + 2 :]
    _, row = where_am_i()
    assemble(z, h_out, pieces, row, 0, z.share)
    y, _ = normalize(z, h_out[...].astype(F32))
    spread(z, y * sigmoid(y), line, pad)
    send_partials(z, row, convolve(z, pad, kernel, 0), own, sends, soon)


def later_forward(z, fs, *refs):
    n = z.parts
    arrivals, pieces, kernel = refs[:n], refs[n : 2 * n], refs[2 * n]
    own, h_out, arrived = refs[2 * n + 1 : 2 * n + 4]
    sends = refs[2 * n + 4 : 3 * n + 3]
    line, pad = refs[3 * n + 3 :]
    s, row = where_am_i()
    total = unfold(z, arrivals[0])
    for other in arrivals[1:]:
        total = total + unfold(z, other)
    total = total.astype(BF).astype(F32)
    arrived[...] = total.astype(BF)
    assemble(z, h_out, pieces, row, 0, z.share)
    prior = jnp.maximum(s - 1, 0)
    taken = jnp.logical_and(s > 0, fs[0, prior] == fs[1, s])
    h = jnp.where(taken, total, h_out[...].astype(F32))
    h_out[...] = h.astype(BF)
    y, _ = normalize(z, h)
    spread(z, y * sigmoid(y), line, pad)
    send_partials(z, row, convolve(z, pad, kernel, 0), own, sends)


def back_through_second(z, i, g, kernel, q_out, q_send, act_out, pad, line):
    y, factor = normalize(z, i.astype(F32))
    logistic = sigmoid(y)
    act_out[...] = (y * logistic).astype(BF)
    spread(z, g, line, pad)
    q = norm_back(z, y, factor, logistic, convolve_back(z, pad, kernel, 1)).astype(BF)
    q_out[...] = q
    fold(z, q_send, q.astype(F32))


def first_backward(z, *refs):
    n = z.parts
    pieces, kernel = refs[:n], refs[n]
    q_out, q_send, pad, act_out, i_ref, g_ref, line = refs[n + 1 :]
    _, row = where_am_i()
    assemble(z, i_ref, pieces, row, z.share, z.share)
    assemble(z, g_ref, pieces, row, 2 * z.share, z.channels)
    back_through_second(
        z, i_ref[...], g_ref[...].astype(F32), kernel, q_out, q_send, act_out, pad, line
    )


def later_backward(z, fs, bs, *refs):
    n = z.parts
    arrivals, mirror, pieces = refs[:n], refs[n], refs[n + 1 : 2 * n + 1]
    i_before, kernel = refs[2 * n + 1 : 2 * n + 3]
    q_out, pad, act_out, grad_in, skip_in, skip_own = refs[2 * n + 3 : 2 * n + 9]
    sends = refs[2 * n + 9 : 3 * n + 8]
    q_send, i_ref, full, line = refs[3 * n + 8 :]
    s, row = where_am_i()
    w, rows = z.share, z.cells // FOLD
    shares = [unfold(z, part) for part in arrivals]
    grad = side_by_side(all_shares(z, shares[0], shares[1:], row))
    grad_in[...] = grad.astype(BF)
    skip = unfolded(mirror[...], 2)
    skip_in[...] = skip.astype(BF)
    skip_own[...] = share_of(z, skip, row)
    for d, send in enumerate(sends, 1):
        send[rows:, :] = folded(share_of(z, skip, target(z, row, d)), FOLD).astype(BF)
    grad_taken, skip_taken = taken_back(z, bs, s)
    assemble(z, full, pieces, row, 4 * w, z.channels)
    g = full[...].astype(F32) + jnp.where(grad_taken, grad, 0.0)
    g = g + jnp.where(skip_taken, skip, 0.0)
    g = g.astype(BF).astype(F32)
    assemble(z, i_ref, pieces, row, 2 * w, w)
    i = jnp.where(fs[0, s] == bs[1, s], i_before[...].astype(F32), i_ref[...].astype(F32))
    back_through_second(z, i, g, kernel, q_out, q_send, act_out, pad, line)
    for send in sends:
        send[:rows, :] = q_send[...]


def second_convolution(z, encoder, row, own, received, skip, h, kernel, i_out, full, line, pad):
    c0 = own[...]
    for other in received:
        c0 = c0 + unfolded(other[: z.cells // FOLD, :], FOLD)
    i = jnp.where(encoder, c0, skip.astype(F32)).astype(BF)
    i_out[...] = i
    y, _ = normalize(z, i.astype(F32))
    spread(z, y * sigmoid(y), line, pad)
    total = convolve(z, pad, kernel, 1)
    base = h[...].astype(F32) + jnp.where(encoder, 0.0, c0)
    full[...] = total + side_by_side([jnp.where(row == j, base, 0.0) for j in range(z.parts)])


def middle(z, pad):
    return pad[1, z.cols : z.cols + z.cells, :].astype(F32)


def soon_pieces(z, soon, received):
    return [unfolded(soon[...], 2)] + [unfolded(x[z.cells // FOLD :, :], 2) for x in received]


def second_forward(z, *refs):
    n = z.parts
    own, received, h, soon, kernel = refs[0], refs[1:n], refs[n], refs[n + 1], refs[n + 2]
    i_out, full_out = refs[n + 3 : n + 5]
    sends = refs[n + 5 : 2 * n + 5]
    skip, full, line, pad = refs[2 * n + 5 :]
    s, row = where_am_i()
    encoder = s < z.sections // 2
    assemble(z, skip, soon_pieces(z, soon, received), row, z.share, z.share)
    second_convolution(
        z, encoder, row, own, received, skip[...], h, kernel, i_out, full, line, pad
    )
    full_out[...] = full[...].astype(BF)
    for d in range(n):
        fold(z, sends[d], share_of(z, full[...], target(z, row, d)))


def last_forward(z, fs, *refs):
    n = z.parts
    own, received, h = refs[0], refs[1:n], refs[n]
    pieces, arrived, kernel = refs[n + 1 : 2 * n + 1], refs[2 * n + 1], refs[2 * n + 2]
    sends = refs[2 * n + 3 : 3 * n + 3]
    i_out, skip, full, line, pad = refs[3 * n + 3 :]
    s, row = where_am_i()
    encoder = s < z.sections // 2
    partner = z.sections - 1 - s
    assemble(z, skip, pieces, row, 3 * z.share, z.share)
    now = jnp.where(
        fs[0, partner] == fs[1, s], arrived[...].astype(F32), skip[...].astype(F32)
    )
    second_convolution(z, encoder, row, own, received, now, h, kernel, i_out, full, line, pad)
    for d, send in enumerate(sends):
        at = part_rows(z, target(z, row, d))
        send[...] = side_by_side([full[at, :], i_out[at, :]]).astype(BF)


def joined_shares(z, own, received, row):
    others = [unfolded(other[: z.cells // FOLD, :], FOLD) for other in received]
    return side_by_side(all_shares(z, own[...].astype(F32), others, row))


def back_through_first(z, encoder, row, q, received, g_pad, h, kernel, act_out, pad, line):
    g = middle(z, g_pad)
    whole = joined_shares(z, q, received, row)
    now = jnp.where(encoder, whole, g)
    y, factor = normalize(z, h.astype(F32))
    logistic = sigmoid(y)
    act_out[...] = (y * logistic).astype(BF)
    spread(z, now, line, pad)
    back = norm_back(z, y, factor, logistic, convolve_back(z, pad, kernel, 0))
    return share_of(z, g, row) + back, whole


def second_backward(z, *refs):
    n = z.parts
    q, q_received, g, soon, received = refs[0], refs[1:n], refs[n], refs[n + 1], refs[n + 2 : 2 * n + 1]
    forward, kernel = refs[2 * n + 1 : 2 * n + 3]
    send, mirror, pad, act_out, h, line = refs[2 * n + 3 :]
    s, row = where_am_i()
    encoder = s < z.sections // 2
    assemble(z, h, soon_pieces(z, soon, received), row, 0, z.share)
    value, entered = back_through_first(
        z, encoder, row, q, q_received, g, h[...], kernel, act_out, pad, line
    )
    fold(z, send, value)
    mirror[...] = folded(jnp.where(encoder, forward[...].astype(F32), entered), 2).astype(BF)


def last_backward(z, fs, bs, *refs):
    n = z.parts
    q, received, g, pieces = refs[0], refs[1:n], refs[n], refs[n + 1 : 2 * n + 1]
    h_before, kernel = refs[2 * n + 1 : 2 * n + 3]
    sends = refs[2 * n + 3 : 3 * n + 3]
    pad, act_out, h, value, line = refs[3 * n + 3 :]
    s, row = where_am_i()
    assemble(z, h, pieces, row, z.share, z.share)
    now = jnp.where(fs[0, s] == bs[1, s], h_before[...], h[...])
    result, _ = back_through_first(
        z, s < z.sections // 2, row, q, received, g, now, kernel, act_out, pad, line
    )
    value[...] = result.astype(BF)
    for d, send in enumerate(sends):
        fold(z, send, value[part_rows(z, target(z, row, d)), :])


def pack_rows(z, *refs):
    n = z.parts
    full, i, arrived, skip_own = refs[:4]
    received, sends, skip = refs[4 : n + 3], refs[n + 3 : 2 * n + 3], refs[2 * n + 3]
    _, row = where_am_i()
    total = skip_own[...]
    for other in received:
        total = total + unfolded(other[z.cells // FOLD :, :], FOLD)
    skip[...] = total.astype(BF)
    for d, send in enumerate(sends):
        at = part_rows(z, target(z, row, d))
        send[...] = side_by_side([ref[at, :] for ref in (full, i, arrived, skip)]).astype(BF)


def add_rows(z, *refs):
    n = z.parts
    pieces, q, received = refs[:n], refs[n], refs[n + 1 : 2 * n]
    out, mirror, i_rows, whole = refs[2 * n :]
    s, row = where_am_i()
    c = z.channels
    whole[...] = joined_shares(z, q, received, row)
    values = [piece[...].astype(F32) for piece in pieces]
    total = sum(value[:, :c] for value in values)
    out[...] = total.astype(BF)
    mine = whole[part_rows(z, row), :]
    mirror[...] = jnp.where(s < z.sections // 2, total, mine).astype(BF)
    shares = all_shares(z, values[0][:, c:], [value[:, c:] for value in values[1:]], row)
    i_rows[...] = side_by_side(shares).astype(BF)


def finish_first(z, fs, bs, fwd, bwd, mir, stash, *refs):
    n = z.parts
    rows0, (grad_in, skip_in) = refs[:n], refs[n : n + 2]
    fwd_out, bwd_out, mir_out, stash_out, emitted = refs[n + 2 : n + 7]
    out0, fwd_in, i0, skip, grads, sems = refs[n + 7 :]
    s, row = where_am_i()
    encoder = s < z.sections // 2
    c, w = z.channels, z.share
    prior, later = jnp.maximum(s - 1, 0), jnp.minimum(s + 1, z.sections - 1)
    partner = z.sections - 1 - s
    f0, f1 = fs[0, s], fs[1, s]
    has_prior, has_later = s > 0, s < z.sections - 1
    mine = part_rows(z, row)
    whole = [
        pltpu.make_async_copy(a, b, sems.at[j])
        for j, (a, b) in enumerate(
            ((fwd, fwd_out), (bwd, bwd_out), (mir, mir_out), (stash, stash_out))
        )
    ]
    for copy in whole:
        copy.start()

    pieces = [piece[...].astype(F32) for piece in rows0]

    def joined(at):
        shares = [piece[:, at : at + w] for piece in pieces]
        return side_by_side(all_shares(z, shares[0], shares[1:], row))

    out0[...] = sum(piece[:, :c] for piece in pieces).astype(BF)
    i0[...] = joined(c).astype(BF)
    fwd_in[...] = joined(c + w).astype(BF)
    skip[...] = jnp.where(encoder, skip_in[mine, :].astype(F32), joined(c + 2 * w)).astype(BF)
    grads[...] = grad_in[mine, :]
    for copy in whole:
        copy.wait()

    def put(source, place, j):
        return pltpu.make_async_copy(source, place, sems.at[j])

    always = [
        put(out0, emitted.at[0], 4),
        put(i0, stash_out.at[2 * f0 + 1], 5),
        put(fwd.at[f0], stash_out.at[2 * f0], 6),
        put(skip, mir_out.at[jnp.where(encoder, bs[0, partner], fs[0, partner])], 7),
    ]
    for copy in always:
        copy.start()
    onward, back = put(fwd_in, fwd_out.at[fs[0, prior]], 8), put(grads, bwd_out.at[bs[0, later]], 9)
    pl.when(has_prior)(onward.start)
    pl.when(has_later)(back.start)
    for copy in always:
        copy.wait()
    taken = jnp.logical_and(has_prior, fs[0, prior] == f1)
    moved, same = put(fwd_in, stash_out.at[2 * f1], 10), put(fwd.at[f1], stash_out.at[2 * f1], 11)
    pl.when(taken)(moved.start)
    pl.when(jnp.logical_not(taken))(same.start)
    pl.when(has_prior)(onward.wait)
    pl.when(has_later)(back.wait)
    pl.when(taken)(moved.wait)
    pl.when(jnp.logical_not(taken))(same.wait)


def finish_last(z, fs, bs, *refs):
    n = z.parts
    out1, i1, fwd1, mir1 = refs[5:9]
    grads1 = refs[9 : n + 9]
    fwd_out, bwd_out, mir_out, stash_out, emitted, grads, sems = refs[n + 9 :]
    s, row = where_am_i()
    prior, later = jnp.maximum(s - 1, 0), jnp.minimum(s + 1, z.sections - 1)
    partner = z.sections - 1 - s
    has_prior, has_later = s > 0, s < z.sections - 1
    slot = jnp.where(s < z.sections // 2, bs[1, partner], fs[1, partner])

    def put(source, place, j):
        return pltpu.make_async_copy(source, place, sems.at[j])

    always = [
        put(out1, emitted.at[1], 0),
        put(i1, stash_out.at[2 * fs[1, s] + 1], 1),
        put(mir1, mir_out.at[slot], 2),
    ]
    for copy in always:
        copy.start()
    onward, back = put(fwd1, fwd_out.at[fs[1, prior]], 3), put(grads, bwd_out.at[bs[1, later]], 4)
    pl.when(has_prior)(onward.start)
    shares = [unfold(z, piece) for piece in grads1]
    grads[...] = side_by_side(all_shares(z, shares[0], shares[1:], row)).astype(BF)
    pl.when(has_later)(back.start)
    for copy in always:
        copy.wait()
    pl.when(has_prior)(onward.wait)
    pl.when(has_later)(back.wait)


def add_taps(z, act, pad, before, store):
    turned = jnp.transpose(act[...].astype(F32)).astype(BF)
    for tap in range(9):
        a, b = divmod(tap, 3)
        at = (2 - a) * z.cols
        moved = pad[2 - b, at : at + z.cells, :]
        store(tap, before(tap) + jnp.dot(turned, moved, preferred_element_type=F32))


def kernel_grads_first(z, which, acc, act, pad, out):
    def store(tap, value):
        out[tap] = value

    add_taps(z, act, pad, lambda tap: acc[9 * which + tap], store)


def kernel_grads_last(z, which, *refs):
    total, act, pad, token, out, held, sems = refs[-7:]
    token[...] = jnp.zeros_like(token)
    copies = [
        pltpu.make_async_copy(held.at[tap], out.at[9 * which + tap], sems.at[tap]) for tap in range(9)
    ]

    def store(tap, value):
        held[tap] = value
        copies[tap].start()

    add_taps(z, act, pad, lambda tap: total[tap], store)
    for copy in copies:
        copy.wait()


def per_device(fwd_queue, bwd_queue, mirror_queue, stash, weights, grad_acc, fwd_slot, bwd_slot):
    sections, n = lax.axis_size("section"), lax.axis_size("row")
    z = Sizes(fwd_queue[0], sections, n)
    slots = fwd_queue.shape[1]
    c, w, local, cells = z.channels, z.share, z.local, z.cells
    fwd, bwd, mir = (x.reshape(slots, local, c) for x in (fwd_queue, bwd_queue, mirror_queue))
    kept = stash.reshape(2 * slots, local, c)
    kernels = weights.reshape(18, w, c)
    acc = grad_acc.reshape(18, w, c)
    fs, bs = fwd_slot.T, bwd_slot.T
    fold_shape, wide = (cells // FOLD, FOLD * w), (cells, c)
    half = (cells, w)
    padded = (3, cells + 2 * z.cols, c)

    def move(x, d, step):
        route = [
            (s * n + r, step(s) * n + (r + d) % n) for s in range(sections) for r in range(n)
        ]
        return lax.ppermute(x, ("section", "row"), route)

    across = functools.partial(move, step=lambda s: s)
    onward = functools.partial(move, step=lambda s: (s + 1) % sections)
    backward = functools.partial(move, step=lambda s: (s - 1) % sections)
    mirrored = functools.partial(move, step=lambda s: sections - 1 - s)

    def run(body, scalars, arrays, outs, scratch=(), **options):
        return call(
            functools.partial(body, z), body.__name__, scalars, arrays, outs, scratch, **options
        )

    def exchange(pieces):
        return [pieces[0]] + [across(piece, d) for d, piece in enumerate(pieces[1:], 1)]

    narrow_pad = pad_shapes(z, w)
    wide_line = pltpu.VMEM((cells + 16, c), F32)
    queues = (fwd, bwd, mir, kept)
    rows = (local, c)
    sems = pltpu.SemaphoreType.DMA
    first = exchange(
        run(
            pack_first,
            (),
            (fs, bs, *queues),
            [((local, 2 * w + c), BF)] * n,
            [pltpu.SMEM(fs.shape, jnp.int32)] * 2
            + [pltpu.VMEM(x.shape, BF) for x in queues]
            + [sems((6,))],
            remote=6,
        )
    )
    packed = run(
        pack_later,
        (),
        (fs, bs, *queues),
        [((local // 2, 4 * w), BF)] * n + [((local, 4 * w + c), BF)] * n,
        [pltpu.SMEM(fs.shape, jnp.int32)] * 2 + [pltpu.VMEM((8, local, c), BF), sems((8,))],
        remote=6,
        after=(first[0],),
    )
    soon, late = packed[:n], packed[n:]

    own, h0, *sends = run(
        first_forward,
        (),
        (*first, *soon, kernels),
        [(half, F32), (half, BF)] + [((cells // FOLD + local // 2, FOLD * w), BF)] * (n - 1),
        narrow_pad,
    )
    received = [across(x, d) for d, x in enumerate(sends, 1)]
    q0, q_send, g_pad0, act_i0 = run(
        first_backward,
        (),
        (*first, kernels),
        [(half, BF), (fold_shape, BF), (padded, BF), (half, BF)],
        [pltpu.VMEM(half, BF), pltpu.VMEM(wide, BF), wide_line],
        after=(own,),
    )
    q_received = [across(q_send, d) for d in range(1, n)]

    def start_grads(which, act, pad, after):
        [out] = call(
            functools.partial(kernel_grads_first, z, which),
            f"kernel_grads_first_{which}",
            (),
            (acc, act, pad),
            [((9, w, c), F32)],
            after=after,
        )
        return out

    def end_grads(which, earlier, total, act, pad, after):
        token, out = call(
            functools.partial(kernel_grads_last, z, which),
            f"kernel_grads_last_{which}",
            (),
            (*earlier, total, act, pad),
            [((8, 128), F32), ((18, w, c), F32)],
            [pltpu.VMEM((9, w, c), F32), sems((9,))],
            remote=len(earlier),
            far_outs=1,
            after=after,
            aliases={0: 1} if earlier else None,
        )
        return token, out

    sum_i = start_grads(1, act_i0, g_pad0, (q_send,))
    late = exchange(held_until(late, (received, q_received, sum_i)))
    i0, full0, *sends = run(
        second_forward,
        (),
        (own, *received, h0, soon[0], kernels),
        [(half, BF), (wide, BF)] + [(fold_shape, BF)] * n,
        [pltpu.VMEM(half, BF), pltpu.VMEM(wide, F32)] + narrow_pad,
        after=(sum_i,),
    )
    fwd_in = [onward(x, d) for d, x in enumerate(sends)]
    dh_send, mir_send, f_pad0, act_h0 = run(
        second_backward,
        (),
        (q0, *q_received, g_pad0, soon[0], *received, full0, kernels),
        [(fold_shape, BF), ((cells // 2, 2 * c), BF), (padded, BF), (half, BF)],
        [pltpu.VMEM(half, BF), wide_line],
    )
    dh_in = [backward(dh_send, d) for d in range(n)]
    mir_in = mirrored(held_until([mir_send], fwd_in)[0], 0)

    own, h1, arrived, *sends = run(
        later_forward,
        (fs,),
        (*fwd_in, *late, kernels),
        [(half, F32), (half, BF), (half, BF)] + [(fold_shape, BF)] * (n - 1),
        narrow_pad,
        after=(dh_send,),
    )
    received = [across(x, d) for d, x in enumerate(sends, 1)]
    sum_h = start_grads(0, act_h0, f_pad0, (own,))
    q1, g_pad1, act_i1, grad_in, skip_in, skip_own, *sends = run(
        later_backward,
        (fs, bs),
        (*dh_in, mir_in, *late, *held_until([i0], received), kernels),
        [(half, BF), (padded, BF), (half, BF), (wide, BF), (wide, BF), (half, F32)]
        + [((2 * (cells // FOLD), FOLD * w), BF)] * (n - 1),
        [pltpu.VMEM(fold_shape, BF), pltpu.VMEM(half, BF), pltpu.VMEM(wide, BF), wide_line],
        after=(sum_h,),
    )
    q_received = [across(x, d) for d, x in enumerate(sends, 1)]
    token, part_i = end_grads(1, (), sum_i, act_i1, g_pad1, ())
    *sends, skip_arrived = run(
        pack_rows,
        (),
        (full0, i0, arrived, skip_own, *q_received),
        [((local, c + 3 * w), BF)] * n + [(half, BF)],
        after=(token,),
    )
    rows0 = exchange(sends)
    sends = run(
        last_forward,
        (fs,),
        (own, *received, h1, *late, skip_arrived, kernels),
        [((local, c + w), BF)] * n,
        [pltpu.VMEM(half, BF), pltpu.VMEM(half, BF), pltpu.VMEM(wide, F32)] + narrow_pad,
    )
    rows1 = exchange(sends)
    *dh_sends, f_pad1, act_h1 = run(
        last_backward,
        (fs, bs),
        (q1, *q_received, g_pad1, *late, h0, kernels),
        [((local // FOLD, FOLD * w), BF)] * n + [(padded, BF), (half, BF)],
        [pltpu.VMEM(half, BF), pltpu.VMEM(half, BF), wide_line],
        after=(rows1[0],),
    )
    dh1_in = [backward(x, d) for d, x in enumerate(dh_sends)]
    out1, mirror1, i1 = run(
        add_rows,
        (),
        (*rows1, q1, *q_received),
        [(rows, BF)] * 3,
        [pltpu.VMEM(wide, F32)],
        after=(act_h1,),
    )
    fwd1, mir1 = onward(out1, 0), mirrored(mirror1, 0)
    token, grad_total = end_grads(0, (part_i,), sum_h, act_h1, f_pad1, (out1,))
    written = [(x.shape, BF) for x in queues] + [((TICKS, local, c), BF)]
    early = run(
        finish_first,
        (fs, bs),
        (*queues, *rows0, grad_in, skip_in),
        written,
        [pltpu.VMEM(rows, BF)] * 5 + [sems((12,))],
        far_outs=5,
        after=(token,),
    )
    fwd_out, bwd_out, mir_out, stash_out, emitted = run(
        finish_last,
        (fs, bs),
        (*early, out1, i1, fwd1, mir1, *dh1_in),
        written,
        [pltpu.VMEM(rows, BF), sems((5,))],
        remote=5,
        far_outs=5,
        aliases={j + 2: j for j in range(5)},
    )
    return (
        fwd_out.reshape(fwd_queue.shape),
        bwd_out.reshape(bwd_queue.shape),
        mir_out.reshape(mirror_queue.shape),
        stash_out.reshape(stash.shape),
        grad_total.reshape(grad_acc.shape),
        emitted.reshape((1, TICKS) + fwd_queue.shape[2:]),
    )


def solution(mesh):
    return jax.shard_map(
        per_device,
        mesh=mesh,
        in_specs=(
            P("section", None, "row", None, None),
            P("section", None, "row", None, None),
            P("section", None, "row", None, None),
            P("section", None, None, "row", None, None),
            P("section", None, None, None, "row", None),
            P("section", None, None, None, "row", None),
            P(),
            P(),
        ),
        out_specs=(
            P("section", None, "row", None, None),
            P("section", None, "row", None, None),
            P("section", None, "row", None, None),
            P("section", None, None, "row", None, None),
            P("section", None, None, None, "row", None),
            P("section", None, "row", None, None),
        ),
        check_vma=False,
    )
```

```python
import functools

import jax
import jax.numpy as jnp
from jax import lax
from jax.experimental import pallas as pl
from jax.experimental.pallas import tpu as pltpu
from jax.sharding import PartitionSpec as P

GROUPS = 32
TICKS = 2
FOLD = 4
EPSILON = 1e-05
BF, F32 = jnp.bfloat16, jnp.float32
VMEM_LIMIT = 24 * 2**20


class Sizes:
    def __init__(self, queue, sections, rows):
        self.sections, self.parts = sections, rows
        self.cols = queue.shape[2]
        self.channels = queue.shape[3]
        self.local = queue.shape[1] * queue.shape[2]
        self.cells = self.local * rows
        self.share = self.channels // rows
        self.group = self.channels // GROUPS
        self.count = self.cells * self.group


def where_am_i():
    return lax.axis_index("section"), lax.axis_index("row")


def share_of(z, value, part):
    value = value.astype(F32)
    out = value[:, : z.share]
    for j in range(1, z.parts):
        out = jnp.where(part == j, value[:, j * z.share : (j + 1) * z.share], out)
    return out


def all_shares(z, own, others, row):
    out = []
    for j in range(z.parts):
        value = own
        for d in range(1, z.parts):
            value = jnp.where(lax.rem(row + z.parts - d, z.parts) == j, others[d - 1], value)
        out.append(value)
    return out


def side_by_side(values):
    return jnp.concatenate([value.astype(F32) for value in values], axis=1)


def folded(value, blocks):
    rows = value.shape[0] // blocks
    return side_by_side([value[j * rows : (j + 1) * rows] for j in range(blocks)])


def unfolded(value, blocks):
    value, width = value.astype(F32), value.shape[1] // blocks
    return jnp.concatenate([value[:, j * width : (j + 1) * width] for j in range(blocks)], axis=0)


def fold(z, ref, value):
    ref[...] = folded(value, FOLD).astype(BF)


def unfold(z, ref):
    return unfolded(ref[...], FOLD)


def source(z, row, d):
    return lax.rem(row + z.parts - d, z.parts)


def target(z, row, d):
    return lax.rem(row + d, z.parts)


def part_rows(z, part):
    return pl.ds(pl.multiple_of(part * z.local, z.local), z.local)


def assemble(z, ref, pieces, row, start, width):
    for d, piece in enumerate(pieces):
        value = (piece if isinstance(piece, jax.Array) else piece[...]).astype(F32)
        value = value[:, start : start + width]
        ref[part_rows(z, source(z, row, d)), :] = value.astype(BF)


def group_sums(z, first, second):
    width = first.shape[1]
    line = lax.broadcasted_iota(jnp.int32, (8, width), 0)
    both = jnp.where(line == 0, first, jnp.where(line == 1, second, 0.0))
    across = lax.broadcasted_iota(jnp.int32, (width, width), 1).astype(F32)
    down = lax.broadcasted_iota(jnp.int32, (width, width), 0).astype(F32)
    same = jnp.floor((across + 0.5) * (1.0 / z.group)) == jnp.floor((down + 0.5) * (1.0 / z.group))
    sums = jnp.dot(
        both, same.astype(F32), precision=lax.Precision.HIGHEST, preferred_element_type=F32
    )
    return sums[0:1], sums[1:2]


def normalize(z, x):
    total, square = group_sums(
        z, jnp.sum(x, axis=0, keepdims=True), jnp.sum(x * x, axis=0, keepdims=True)
    )
    center = total / z.count
    factor = lax.rsqrt(square / z.count - center * center + EPSILON)
    return (x - center) * factor, factor


def sigmoid(y):
    return 1.0 / (1.0 + jnp.exp(-y))


def norm_back(z, y, factor, logistic, upstream):
    e = upstream * logistic * (1.0 + y * (1.0 - logistic))
    first, second = group_sums(
        z, jnp.sum(e, axis=0, keepdims=True), jnp.sum(e * y, axis=0, keepdims=True)
    )
    return factor * (e - first / z.count - y * (second / z.count))


def spread(z, x, line_ref, pad_ref):
    cells, cols = z.cells, z.cols
    width = x.shape[1]
    line_ref[8 : 8 + cells, :] = x
    column = lax.rem(lax.broadcasted_iota(jnp.int32, (cells, 1), 0), cols)
    edge = jnp.zeros((cols, width), BF)
    for b in range(3):
        pad_ref[b, :cols, :] = edge
        pad_ref[b, cols + cells :, :] = edge
    pad_ref[1, cols : cols + cells, :] = x.astype(BF)
    left = jnp.where(column > 0, line_ref[7 : 7 + cells, :], 0.0)
    pad_ref[0, cols : cols + cells, :] = left.astype(BF)
    right = jnp.where(column < cols - 1, line_ref[9 : 9 + cells, :], 0.0)
    pad_ref[2, cols : cols + cells, :] = right.astype(BF)


def convolve(z, pad_ref, kernel_ref, which):
    total = None
    for a in range(3):
        for b in range(3):
            term = jnp.dot(
                pad_ref[b, a * z.cols : a * z.cols + z.cells, :],
                kernel_ref[9 * which + 3 * a + b],
                preferred_element_type=F32,
            )
            total = term if total is None else total + term
    return total


def convolve_back(z, pad_ref, kernel_ref, which):
    total = None
    for a in range(3):
        for b in range(3):
            term = lax.dot_general(
                pad_ref[b, a * z.cols : a * z.cols + z.cells, :],
                kernel_ref[9 * which + 3 * (2 - a) + 2 - b],
                (((1,), (1,)), ((), ())),
                preferred_element_type=F32,
            )
            total = term if total is None else total + term
    return total


def pad_shapes(z, width):
    return [
        pltpu.VMEM((z.cells + 16, width), F32),
        pltpu.VMEM((3, z.cells + 2 * z.cols, width), BF),
    ]


def call(body, name, scalars, arrays, outs, scratch=(), after=(), remote=0, far_outs=0, aliases=None):
    near, far = pl.BlockSpec(memory_space=pltpu.VMEM), pl.BlockSpec(memory_space=pltpu.HBM)

    def inner(*refs):
        given = len(scalars) + len(arrays)
        body(*refs[:given], *refs[given + len(after) :])

    arrays = [
        pltpu.with_memory_space_constraint(x, pltpu.HBM) if j < remote else x
        for j, x in enumerate(arrays)
    ]
    near_outs = len(outs) - far_outs
    return pl.pallas_call(
        inner,
        name=name,
        out_shape=[
            jax.ShapeDtypeStruct(shape, dtype) if j < near_outs else pltpu.HBM(shape, dtype)
            for j, (shape, dtype) in enumerate(outs)
        ],
        in_specs=[pl.BlockSpec(memory_space=pltpu.SMEM)] * len(scalars)
        + [far] * remote
        + [near] * (len(arrays) - remote)
        + [pl.BlockSpec(memory_space=pl.ANY)] * len(after),
        out_specs=[near] * near_outs + [far] * far_outs,
        scratch_shapes=list(scratch),
        input_output_aliases=aliases or {},
        compiler_params=pltpu.CompilerParams(vmem_limit_bytes=VMEM_LIMIT),
        cost_estimate=pl.CostEstimate(flops=1, bytes_accessed=1, transcendentals=0),
    )(*scalars, *arrays, *after)


def held_until(values, earlier):
    return lax.optimization_barrier((tuple(values), earlier))[0]


def fetch(pairs, sems):
    copies = [pltpu.make_async_copy(a, b, sems.at[j]) for j, (a, b) in enumerate(pairs)]
    for copy in copies:
        copy.start()
    for copy in copies:
        copy.wait()


def pack_first(z, fs_far, bs_far, fwd_far, bwd_far, mir_far, stash_far, *refs):
    outs = refs[: z.parts]
    fs, bs, fwd, bwd, mir, stash, sems = refs[z.parts :]
    fetch(
        [
            (fs_far, fs),
            (bs_far, bs),
            (fwd_far, fwd),
            (bwd_far, bwd),
            (mir_far, mir),
            (stash_far, stash),
        ],
        sems,
    )
    s, row = where_am_i()
    f, b = fs[0, s], bs[0, s]
    h, i = fwd[f], stash[2 * b + 1]
    g = bwd[b].astype(F32) + jnp.where(s < z.sections // 2, mir[b].astype(F32), 0.0)
    for d, out in enumerate(outs):
        part = target(z, row, d)
        out[...] = side_by_side([share_of(z, h, part), share_of(z, i, part), g]).astype(BF)


def taken_back(z, bs, s):
    later, partner = jnp.minimum(s + 1, z.sections - 1), z.sections - 1 - s
    return (
        jnp.logical_and(s < z.sections - 1, bs[0, later] == bs[1, s]),
        jnp.logical_and(s < z.sections // 2, bs[0, partner] == bs[1, s]),
    )


def pack_later(z, fs_far, bs_far, fwd_far, bwd_far, mir_far, stash_far, *refs):
    n = z.parts
    skips, heads, late = refs[:n], refs[n : 2 * n], refs[2 * n : 3 * n]
    fs, bs, held, sems = refs[3 * n :]
    fetch([(fs_far, fs), (bs_far, bs)], sems)
    s, row = where_am_i()
    f1, b1 = fs[1, s], bs[1, s]
    places = (
        mir_far.at[fs[0, s]],
        stash_far.at[2 * bs[0, s]],
        fwd_far.at[f1],
        stash_far.at[2 * b1],
        stash_far.at[2 * b1 + 1],
        mir_far.at[f1],
        bwd_far.at[b1],
        mir_far.at[b1],
    )
    fetch([(place, held.at[j]) for j, place in enumerate(places)], sems)
    grad_taken, skip_taken = taken_back(z, bs, s)
    skip_kept = jnp.logical_and(s < z.sections // 2, jnp.logical_not(skip_taken))
    kept = jnp.where(grad_taken, 0.0, held[6].astype(F32))
    kept = kept + jnp.where(skip_kept, held[7].astype(F32), 0.0)
    for d in range(n):
        shares = [share_of(z, held[j], target(z, row, d)) for j in range(6)]
        fold(z, skips[d], shares[0])
        heads[d][...] = folded(side_by_side(shares[1:3]), 2).astype(BF)
        late[d][...] = side_by_side(shares[3:] + [kept]).astype(BF)


def copy_queues(z, *refs):
    ins, token, outs, held, sems = refs[:4], refs[4], refs[5:9], refs[10:14], refs[14]
    token[...] = jnp.zeros_like(token)
    fetch(list(zip(ins, held)), sems)
    fetch(list(zip(held, outs)), sems)


def send_partials(z, row, total, own, sends, extra=None):
    own[...] = share_of(z, total, row)
    for d, send in enumerate(sends, 1):
        part = folded(share_of(z, total, target(z, row, d)), FOLD).astype(BF)
        send[: part.shape[0], :] = part
        if extra:
            rows = send.shape[0] - part.shape[0]
            send[part.shape[0] :, :] = extra[d][:rows, :]


def first_forward(z, *refs):
    n = z.parts
    pieces, skips, kernel = refs[:n], refs[n : 2 * n], refs[2 * n]
    own, h_out = refs[2 * n + 1 : 2 * n + 3]
    sends, (line, pad) = refs[2 * n + 3 : 3 * n + 2], refs[3 * n + 2 :]
    _, row = where_am_i()
    assemble(z, h_out, pieces, row, 0, z.share)
    y, _ = normalize(z, h_out[...].astype(F32))
    spread(z, y * sigmoid(y), line, pad)
    send_partials(z, row, convolve(z, pad, kernel, 0), own, sends, skips)


def heads_pieces(z, heads, received):
    return [unfolded(heads[...], 2)] + [unfolded(x[z.cells // FOLD :, :], 2) for x in received]


def later_forward(z, fs, *refs):
    n = z.parts
    arrivals, heads, received = refs[:n], refs[n], refs[n + 1 : 2 * n]
    mirror, kernel = refs[2 * n : 2 * n + 2]
    own, h_out, arrived, onward = refs[2 * n + 2 : 2 * n + 6]
    sends = refs[2 * n + 6 : 3 * n + 5]
    line, pad = refs[3 * n + 5 :]
    s, row = where_am_i()
    total = unfold(z, arrivals[0])
    for other in arrivals[1:]:
        total = total + unfold(z, other)
    total = total.astype(BF).astype(F32)
    arrived[...] = total.astype(BF)
    fold(z, onward, total)
    assemble(z, h_out, heads_pieces(z, heads, received), row, z.share, z.share)
    prior = jnp.maximum(s - 1, 0)
    taken = jnp.logical_and(s > 0, fs[0, prior] == fs[1, s])
    h = jnp.where(taken, total, h_out[...].astype(F32))
    h_out[...] = h.astype(BF)
    y, _ = normalize(z, h)
    spread(z, y * sigmoid(y), line, pad)
    send_partials(z, row, convolve(z, pad, kernel, 0), own, sends, [mirror] * n)


def back_through_second(z, i, g, kernel, q_out, q_send, act_out, pad, line):
    y, factor = normalize(z, i.astype(F32))
    logistic = sigmoid(y)
    act_out[...] = (y * logistic).astype(BF)
    spread(z, g, line, pad)
    q = norm_back(z, y, factor, logistic, convolve_back(z, pad, kernel, 1)).astype(BF)
    q_out[...] = q
    fold(z, q_send, q.astype(F32))


def first_backward(z, *refs):
    n = z.parts
    pieces, heads, kernel = refs[:n], refs[n : 2 * n], refs[2 * n]
    q_out, mirror, pad, act_out = refs[2 * n + 1 : 2 * n + 5]
    sends, (q_send, i_ref, g_ref, line) = refs[2 * n + 5 : 3 * n + 4], refs[3 * n + 4 :]
    _, row = where_am_i()
    assemble(z, i_ref, pieces, row, z.share, z.share)
    assemble(z, g_ref, pieces, row, 2 * z.share, z.channels)
    back_through_second(
        z, i_ref[...], g_ref[...].astype(F32), kernel, q_out, q_send, act_out, pad, line
    )
    rows = z.cells // FOLD
    mirror[:rows, :] = q_send[...]
    mirror[rows:, :] = q_send[:16, :]
    for d, send in enumerate(sends, 1):
        send[:rows, :] = q_send[...]
        send[rows:, :] = heads[d][...]


def later_backward(z, fs, bs, *refs):
    n = z.parts
    arrivals, mirror, received = refs[:n], refs[n], refs[n + 1 : 2 * n]
    pieces, (i_before, arrived, kernel) = refs[2 * n : 3 * n], refs[3 * n : 3 * n + 3]
    q_out, pad, act_out, grad_in, skip_in = refs[3 * n + 3 : 3 * n + 8]
    rows_own, sends = refs[3 * n + 8], refs[3 * n + 9 : 4 * n + 8]
    q_send, i_ref, full, line = refs[4 * n + 8 :]
    s, row = where_am_i()
    w = z.share
    shares = [unfold(z, part) for part in arrivals]
    grad = side_by_side(all_shares(z, shares[0], shares[1:], row))
    grad_in[...] = grad.astype(BF)
    shares = [unfolded(x[z.cells // FOLD :, :], FOLD) for x in received]
    skip = side_by_side(all_shares(z, unfolded(mirror[: z.cells // FOLD, :], FOLD), shares, row))
    skip_in[...] = skip.astype(BF)
    grad_taken, skip_taken = taken_back(z, bs, s)
    assemble(z, full, pieces, row, 3 * w, z.channels)
    g = full[...].astype(F32) + jnp.where(grad_taken, grad, 0.0)
    g = g + jnp.where(skip_taken, skip, 0.0)
    g = g.astype(BF).astype(F32)
    assemble(z, i_ref, pieces, row, w, w)
    i = jnp.where(fs[0, s] == bs[1, s], i_before[...].astype(F32), i_ref[...].astype(F32))
    back_through_second(z, i, g, kernel, q_out, q_send, act_out, pad, line)
    for d, out in enumerate([rows_own, *sends]):
        at = part_rows(z, target(z, row, d))
        part = folded(side_by_side([i_before[at, :], arrived[at, :]]), 2).astype(BF)
        out[out.shape[0] - part.shape[0] :, :] = part
    for send in sends:
        send[: q_send.shape[0], :] = q_send[...]


def second_convolution(z, encoder, row, own, received, skip, h, kernel, i_out, full, line, pad):
    c0 = own[...]
    for other in received:
        c0 = c0 + unfolded(other[: z.cells // FOLD, :], FOLD)
    i = jnp.where(encoder, c0, skip.astype(F32)).astype(BF)
    i_out[...] = i
    y, _ = normalize(z, i.astype(F32))
    spread(z, y * sigmoid(y), line, pad)
    total = convolve(z, pad, kernel, 1)
    base = h[...].astype(F32) + jnp.where(encoder, 0.0, c0)
    full[...] = total + side_by_side([jnp.where(row == j, base, 0.0) for j in range(z.parts)])


def middle(z, pad):
    return pad[1, z.cols : z.cols + z.cells, :].astype(F32)


def second_forward(z, *refs):
    n = z.parts
    own, received, h, skip_own, kernel = refs[0], refs[1:n], refs[n], refs[n + 1], refs[n + 2]
    i_out, full_out = refs[n + 3 : n + 5]
    sends = refs[n + 5 : 2 * n + 5]
    skip, full, line, pad = refs[2 * n + 5 :]
    s, row = where_am_i()
    encoder = s < z.sections // 2
    skips = [unfold(z, skip_own)]
    skips += [unfolded(other[z.cells // FOLD :, :], FOLD) for other in received]
    assemble(z, skip, skips, row, 0, z.share)
    second_convolution(
        z, encoder, row, own, received, skip[...], h, kernel, i_out, full, line, pad
    )
    full_out[...] = full[...].astype(BF)
    for d in range(n):
        fold(z, sends[d], share_of(z, full[...], target(z, row, d)))


def last_forward(z, fs, *refs):
    n = z.parts
    own, received, h = refs[0], refs[1:n], refs[n]
    pieces, arrived, kernel = refs[n + 1 : 2 * n + 1], refs[2 * n + 1], refs[2 * n + 2]
    sends = refs[2 * n + 3 : 3 * n + 3]
    i_out, skip, full, line, pad = refs[3 * n + 3 :]
    s, row = where_am_i()
    encoder = s < z.sections // 2
    partner = z.sections - 1 - s
    assemble(z, skip, pieces, row, 2 * z.share, z.share)
    now = jnp.where(
        fs[0, partner] == fs[1, s], unfold(z, arrived), skip[...].astype(F32)
    )
    second_convolution(z, encoder, row, own, received, now, h, kernel, i_out, full, line, pad)
    for d, send in enumerate(sends):
        at = part_rows(z, target(z, row, d))
        send[...] = side_by_side([full[at, :], i_out[at, :]]).astype(BF)


def joined_shares(z, own, received, row):
    others = [unfolded(other[: z.cells // FOLD, :], FOLD) for other in received]
    return side_by_side(all_shares(z, own[...].astype(F32), others, row))


def back_through_first(z, encoder, row, q, received, g_pad, h, kernel, act_out, pad, line):
    g = middle(z, g_pad)
    whole = joined_shares(z, q, received, row)
    now = jnp.where(encoder, whole, g)
    y, factor = normalize(z, h.astype(F32))
    logistic = sigmoid(y)
    act_out[...] = (y * logistic).astype(BF)
    spread(z, now, line, pad)
    back = norm_back(z, y, factor, logistic, convolve_back(z, pad, kernel, 0))
    return share_of(z, g, row) + back, whole


def second_backward(z, *refs):
    n = z.parts
    q, received, g, heads, kernel = refs[0], refs[1:n], refs[n], refs[n + 1], refs[n + 2]
    send, pad, act_out, h, line = refs[n + 3 :]
    s, row = where_am_i()
    assemble(z, h, heads_pieces(z, heads, received), row, 0, z.share)
    value, _ = back_through_first(
        z, s < z.sections // 2, row, q, received, g, h[...], kernel, act_out, pad, line
    )
    fold(z, send, value)


def last_backward(z, fs, bs, *refs):
    n = z.parts
    q, received, g, pieces = refs[0], refs[1:n], refs[n], refs[n + 1 : 2 * n + 1]
    h_before, kernel = refs[2 * n + 1 : 2 * n + 3]
    sends = refs[2 * n + 3 : 3 * n + 3]
    pad, act_out, h, value, line = refs[3 * n + 3 :]
    s, row = where_am_i()
    assemble(z, h, pieces, row, 0, z.share)
    now = jnp.where(fs[0, s] == bs[1, s], h_before[...], h[...])
    result, _ = back_through_first(
        z, s < z.sections // 2, row, q, received, g, now, kernel, act_out, pad, line
    )
    value[...] = result.astype(BF)
    for d, send in enumerate(sends):
        fold(z, send, value[part_rows(z, target(z, row, d)), :])


def pack_rows(z, *refs):
    n = z.parts
    full, mirror = refs[:2]
    sends, skip = refs[2 : n + 2], refs[n + 2]
    _, row = where_am_i()
    skip[...] = unfold(z, mirror).astype(BF)
    for d, send in enumerate(sends):
        at = part_rows(z, target(z, row, d))
        send[...] = side_by_side([ref[at, :] for ref in (full, skip)]).astype(BF)


def add_rows(z, *refs):
    n = z.parts
    pieces, q, received = refs[:n], refs[n], refs[n + 1 : 2 * n]
    out, mirror, i_rows, whole = refs[2 * n :]
    s, row = where_am_i()
    c = z.channels
    whole[...] = joined_shares(z, q, received, row)
    values = [piece[...].astype(F32) for piece in pieces]
    total = sum(value[:, :c] for value in values)
    out[...] = total.astype(BF)
    mine = whole[part_rows(z, row), :]
    mirror[...] = jnp.where(s < z.sections // 2, total, mine).astype(BF)
    shares = all_shares(z, values[0][:, c:], [value[:, c:] for value in values[1:]], row)
    i_rows[...] = side_by_side(shares).astype(BF)


def finish_first(z, fs, bs, *refs):
    n = z.parts
    fwd, rows0, (grad_in, skip_in) = refs[5], refs[6 : n + 6], refs[n + 6 : n + 8]
    others = refs[n + 8 : 2 * n + 8]
    fwd_out, bwd_out, mir_out, stash_out, emitted = refs[2 * n + 8 : 2 * n + 13]
    out0, fwd_in, i0, skip, grads, h0, h1, sems = refs[2 * n + 13 :]
    s, row = where_am_i()
    encoder = s < z.sections // 2
    c, w = z.channels, z.share
    prior, later = jnp.maximum(s - 1, 0), jnp.minimum(s + 1, z.sections - 1)
    partner = z.sections - 1 - s
    f0, f1 = fs[0, s], fs[1, s]
    has_prior, has_later = s > 0, s < z.sections - 1
    mine = part_rows(z, row)
    loads = [
        pltpu.make_async_copy(fwd.at[f0], h0, sems.at[0]),
        pltpu.make_async_copy(fwd.at[f1], h1, sems.at[1]),
    ]
    for copy in loads:
        copy.start()

    pieces = [piece[...].astype(F32) for piece in rows0]

    others = [unfolded(other[other.shape[0] - z.local // 2 :, :], 2) for other in others]

    def joined(pieces, at):
        shares = [piece[:, at : at + w] for piece in pieces]
        return side_by_side(all_shares(z, shares[0], shares[1:], row))

    out0[...] = sum(piece[:, :c] for piece in pieces).astype(BF)
    i0[...] = joined(others, 0).astype(BF)
    fwd_in[...] = joined(others, w).astype(BF)
    skip[...] = jnp.where(encoder, skip_in[mine, :].astype(F32), joined(pieces, c)).astype(BF)
    grads[...] = grad_in[mine, :]
    for copy in loads:
        copy.wait()

    def put(source, place, j):
        return pltpu.make_async_copy(source, place, sems.at[j])

    always = [
        put(out0, emitted.at[0], 4),
        put(i0, stash_out.at[2 * f0 + 1], 5),
        put(h0, stash_out.at[2 * f0], 6),
        put(skip, mir_out.at[jnp.where(encoder, bs[0, partner], fs[0, partner])], 7),
    ]
    for copy in always:
        copy.start()
    onward, back = put(fwd_in, fwd_out.at[fs[0, prior]], 8), put(grads, bwd_out.at[bs[0, later]], 9)
    pl.when(has_prior)(onward.start)
    pl.when(has_later)(back.start)
    for copy in always:
        copy.wait()
    taken = jnp.logical_and(has_prior, fs[0, prior] == f1)
    moved, same = put(fwd_in, stash_out.at[2 * f1], 10), put(h1, stash_out.at[2 * f1], 11)
    pl.when(taken)(moved.start)
    pl.when(jnp.logical_not(taken))(same.start)
    pl.when(has_prior)(onward.wait)
    pl.when(has_later)(back.wait)
    pl.when(taken)(moved.wait)
    pl.when(jnp.logical_not(taken))(same.wait)


def finish_last(z, fs, bs, *refs):
    n = z.parts
    out1, i1, fwd1, mir1 = refs[5:9]
    grads1 = refs[9 : n + 9]
    fwd_out, bwd_out, mir_out, stash_out, emitted, grads, sems = refs[n + 9 :]
    s, row = where_am_i()
    prior, later = jnp.maximum(s - 1, 0), jnp.minimum(s + 1, z.sections - 1)
    partner = z.sections - 1 - s
    has_prior, has_later = s > 0, s < z.sections - 1
    slot = jnp.where(s < z.sections // 2, bs[1, partner], fs[1, partner])

    def put(source, place, j):
        return pltpu.make_async_copy(source, place, sems.at[j])

    always = [
        put(out1, emitted.at[1], 0),
        put(i1, stash_out.at[2 * fs[1, s] + 1], 1),
        put(mir1, mir_out.at[slot], 2),
    ]
    for copy in always:
        copy.start()
    onward, back = put(fwd1, fwd_out.at[fs[1, prior]], 3), put(grads, bwd_out.at[bs[1, later]], 4)
    pl.when(has_prior)(onward.start)
    shares = [unfold(z, piece) for piece in grads1]
    grads[...] = side_by_side(all_shares(z, shares[0], shares[1:], row)).astype(BF)
    pl.when(has_later)(back.start)
    for copy in always:
        copy.wait()
    pl.when(has_prior)(onward.wait)
    pl.when(has_later)(back.wait)


def add_taps(z, act, pad, before, store):
    turned = jnp.transpose(act[...].astype(F32)).astype(BF)
    for tap in range(9):
        a, b = divmod(tap, 3)
        at = (2 - a) * z.cols
        moved = pad[2 - b, at : at + z.cells, :]
        store(tap, before(tap) + jnp.dot(turned, moved, preferred_element_type=F32))


def kernel_grads_first(z, which, acc, act, pad, out):
    def store(tap, value):
        out[tap] = value

    add_taps(z, act, pad, lambda tap: acc[9 * which + tap], store)


def kernel_grads_last(z, which, *refs):
    total, act, pad, token, out, held, sems = refs[-7:]
    token[...] = jnp.zeros_like(token)
    copies = [
        pltpu.make_async_copy(held.at[tap], out.at[9 * which + tap], sems.at[tap]) for tap in range(9)
    ]

    def store(tap, value):
        held[tap] = value
        copies[tap].start()

    add_taps(z, act, pad, lambda tap: total[tap], store)
    for copy in copies:
        copy.wait()


def per_device(fwd_queue, bwd_queue, mirror_queue, stash, weights, grad_acc, fwd_slot, bwd_slot):
    sections, n = lax.axis_size("section"), lax.axis_size("row")
    z = Sizes(fwd_queue[0], sections, n)
    slots = fwd_queue.shape[1]
    c, w, local, cells = z.channels, z.share, z.local, z.cells
    fwd, bwd, mir = (x.reshape(slots, local, c) for x in (fwd_queue, bwd_queue, mirror_queue))
    kept = stash.reshape(2 * slots, local, c)
    kernels = weights.reshape(18, w, c)
    acc = grad_acc.reshape(18, w, c)
    fs, bs = fwd_slot.T, bwd_slot.T
    fold_shape, wide = (cells // FOLD, FOLD * w), (cells, c)
    half = (cells, w)
    padded = (3, cells + 2 * z.cols, c)

    def move(x, d, step):
        route = [
            (s * n + r, step(s) * n + (r + d) % n) for s in range(sections) for r in range(n)
        ]
        return lax.ppermute(x, ("section", "row"), route)

    across = functools.partial(move, step=lambda s: s)
    onward = functools.partial(move, step=lambda s: (s + 1) % sections)
    backward = functools.partial(move, step=lambda s: (s - 1) % sections)
    crossed = functools.partial(move, step=lambda s: (sections - s) % sections)
    mirrored = functools.partial(move, step=lambda s: sections - 1 - s)

    def run(body, scalars, arrays, outs, scratch=(), **options):
        return call(
            functools.partial(body, z), body.__name__, scalars, arrays, outs, scratch, **options
        )

    def exchange(pieces):
        return [pieces[0]] + [across(piece, d) for d, piece in enumerate(pieces[1:], 1)]

    narrow_pad = pad_shapes(z, w)
    wide_line = pltpu.VMEM((cells + 16, c), F32)
    queues = (fwd, bwd, mir, kept)
    rows = (local, c)
    sems = pltpu.SemaphoreType.DMA
    first = exchange(
        run(
            pack_first,
            (),
            (fs, bs, *queues),
            [((local, 2 * w + c), BF)] * n,
            [pltpu.SMEM(fs.shape, jnp.int32)] * 2
            + [pltpu.VMEM(x.shape, BF) for x in queues]
            + [sems((6,))],
            remote=6,
        )
    )
    packed = run(
        pack_later,
        (),
        (fs, bs, *queues),
        [((local // FOLD, FOLD * w), BF)] * n
        + [((local // 2, 4 * w), BF)] * n
        + [((local, 3 * w + c), BF)] * n,
        [pltpu.SMEM(fs.shape, jnp.int32)] * 2 + [pltpu.VMEM((8, local, c), BF), sems((8,))],
        remote=6,
        after=(first[0],),
    )
    skips, heads, late = packed[:n], packed[n : 2 * n], packed[2 * n :]

    own, h0, *sends = run(
        first_forward,
        (),
        (*first, *skips, kernels),
        [(half, F32), (half, BF)] + [(((cells + local) // FOLD, FOLD * w), BF)] * (n - 1),
        narrow_pad,
    )
    received = [across(x, d) for d, x in enumerate(sends, 1)]
    q0, mirror_send, g_pad0, act_i0, *sends = run(
        first_backward,
        (),
        (*first, *heads, kernels),
        [(half, BF), ((cells // FOLD + 16, FOLD * w), BF), (padded, BF), (half, BF)]
        + [((cells // FOLD + local // 2, FOLD * w), BF)] * (n - 1),
        [pltpu.VMEM(fold_shape, BF), pltpu.VMEM(half, BF), pltpu.VMEM(wide, BF), wide_line],
        after=(own,),
    )
    q_received = [across(x, d) for d, x in enumerate(sends, 1)]
    skip_in = mirrored(mirror_send, 0)

    def start_grads(which, act, pad, after):
        [out] = call(
            functools.partial(kernel_grads_first, z, which),
            f"kernel_grads_first_{which}",
            (),
            (acc, act, pad),
            [((9, w, c), F32)],
            after=after,
        )
        return out

    def end_grads(which, earlier, total, act, pad, after):
        token, out = call(
            functools.partial(kernel_grads_last, z, which),
            f"kernel_grads_last_{which}",
            (),
            (*earlier, total, act, pad),
            [((8, 128), F32), ((18, w, c), F32)],
            [pltpu.VMEM((9, w, c), F32), sems((9,))],
            remote=len(earlier),
            far_outs=1,
            after=after,
            aliases={0: 1} if earlier else None,
        )
        return token, out

    sum_i = start_grads(1, act_i0, g_pad0, (q0,))
    written = [(x.shape, BF) for x in queues] + [((TICKS, local, c), BF)]
    token, *copies = run(
        copy_queues,
        (),
        queues,
        [((8, 128), F32)] + written,
        [pltpu.VMEM(x.shape, BF) for x in queues] + [sems((4,))],
        remote=4,
        far_outs=5,
        after=(sum_i,),
    )
    i0, full0, *sends = run(
        second_forward,
        (),
        (own, *received, h0, skips[0], kernels),
        [(half, BF), (wide, BF)] + [(fold_shape, BF)] * n,
        [pltpu.VMEM(half, BF), pltpu.VMEM(wide, F32)] + narrow_pad,
        after=(token,),
    )
    fwd_in = [onward(x, d) for d, x in enumerate(sends)]
    dh_send, f_pad0, act_h0 = run(
        second_backward,
        (),
        (*held_until([q0], skip_in), *q_received, g_pad0, heads[0], kernels),
        [(fold_shape, BF), (padded, BF), (half, BF)],
        [pltpu.VMEM(half, BF), wide_line],
        after=(i0,),
    )
    late = exchange(held_until(late, (fwd_in, act_h0)))
    dh_in = [backward(dh_send, d) for d in range(n)]

    own, h1, arrived, turned, *sends = run(
        later_forward,
        (fs,),
        (*fwd_in, heads[0], *q_received, skip_in, kernels),
        [(half, F32), (half, BF), (half, BF), (fold_shape, BF)]
        + [((2 * (cells // FOLD), FOLD * w), BF)] * (n - 1),
        narrow_pad,
        after=(dh_send,),
    )
    received = [across(x, d) for d, x in enumerate(sends, 1)]
    mir_in = crossed(turned, 0)
    sum_h = start_grads(0, act_h0, f_pad0, (own,))
    q1, g_pad1, act_i1, grad_in, skip_in, rows_own, *sends = run(
        later_backward,
        (fs, bs),
        (*dh_in, skip_in, *received, *late, i0, arrived, kernels),
        [(half, BF), (padded, BF), (half, BF), (wide, BF), (wide, BF), ((local // 2, 4 * w), BF)]
        + [((cells // FOLD + local // 2, FOLD * w), BF)] * (n - 1),
        [pltpu.VMEM(fold_shape, BF), pltpu.VMEM(half, BF), pltpu.VMEM(wide, BF), wide_line],
        after=(sum_h,),
    )
    q_received = [across(x, d) for d, x in enumerate(sends, 1)]
    sends = run(
        last_forward,
        (fs,),
        (own, *received, h1, *late, mir_in, kernels),
        [((local, c + w), BF)] * n,
        [pltpu.VMEM(half, BF), pltpu.VMEM(half, BF), pltpu.VMEM(wide, F32)] + narrow_pad,
        after=(q1,),
    )
    rows1 = exchange(sends)
    token, part_i = end_grads(1, (), sum_i, act_i1, g_pad1, (sends[0],))
    rows0 = run(
        pack_rows,
        (),
        (full0, mir_in),
        [((local, c + w), BF)] * n,
        [pltpu.VMEM(half, BF)],
        after=(token,),
    )
    rows0 = exchange(held_until(rows0, (rows1, q_received)))
    out1, mirror1, i1 = run(
        add_rows,
        (),
        (*rows1, q1, *q_received),
        [(rows, BF)] * 3,
        [pltpu.VMEM(wide, F32)],
        after=(rows0[0],),
    )
    fwd1, mir1 = onward(out1, 0), mirrored(mirror1, 0)
    *dh_sends, f_pad1, act_h1 = run(
        last_backward,
        (fs, bs),
        (q1, *q_received, g_pad1, *late, h0, kernels),
        [((local // FOLD, FOLD * w), BF)] * n + [(padded, BF), (half, BF)],
        [pltpu.VMEM(half, BF), pltpu.VMEM(half, BF), wide_line],
        after=(out1,),
    )
    dh1_in = [backward(x, d) for d, x in enumerate(dh_sends)]
    token, grad_total = end_grads(0, (part_i,), sum_h, act_h1, f_pad1, ())
    early = run(
        finish_first,
        (fs, bs),
        (*copies, fwd, *rows0, grad_in, skip_in, rows_own, *q_received),
        written,
        [pltpu.VMEM(rows, BF)] * 7 + [sems((12,))],
        remote=6,
        far_outs=5,
        aliases={j + 2: j for j in range(5)},
        after=(token,),
    )
    fwd_out, bwd_out, mir_out, stash_out, emitted = run(
        finish_last,
        (fs, bs),
        (*early, out1, i1, fwd1, mir1, *dh1_in),
        written,
        [pltpu.VMEM(rows, BF), sems((5,))],
        remote=5,
        far_outs=5,
        aliases={j + 2: j for j in range(5)},
    )
    return (
        fwd_out.reshape(fwd_queue.shape),
        bwd_out.reshape(bwd_queue.shape),
        mir_out.reshape(mirror_queue.shape),
        stash_out.reshape(stash.shape),
        grad_total.reshape(grad_acc.shape),
        emitted.reshape((1, TICKS) + fwd_queue.shape[2:]),
    )


def solution(mesh):
    return jax.shard_map(
        per_device,
        mesh=mesh,
        in_specs=(
            P("section", None, "row", None, None),
            P("section", None, "row", None, None),
            P("section", None, "row", None, None),
            P("section", None, None, "row", None, None),
            P("section", None, None, None, "row", None),
            P("section", None, None, None, "row", None),
            P(),
            P(),
        ),
        out_specs=(
            P("section", None, "row", None, None),
            P("section", None, "row", None, None),
            P("section", None, "row", None, None),
            P("section", None, None, "row", None, None),
            P("section", None, None, None, "row", None),
            P("section", None, "row", None, None),
        ),
        check_vma=False,
    )
```

```python
import functools

import jax
import jax.numpy as jnp
from jax import lax
from jax.experimental import pallas as pl
from jax.experimental.pallas import tpu as pltpu
from jax.sharding import PartitionSpec as P

GROUPS = 32
TICKS = 2
FOLD = 4
EPSILON = 1e-05
BF, F32 = jnp.bfloat16, jnp.float32
VMEM_LIMIT = 24 * 2**20


class Sizes:
    def __init__(self, queue, sections, rows):
        self.sections, self.parts = sections, rows
        self.cols = queue.shape[2]
        self.channels = queue.shape[3]
        self.local = queue.shape[1] * queue.shape[2]
        self.cells = self.local * rows
        self.share = self.channels // rows
        self.group = self.channels // GROUPS
        self.count = self.cells * self.group


def where_am_i():
    return lax.axis_index("section"), lax.axis_index("row")


def share_of(z, value, part):
    value = value.astype(F32)
    out = value[:, : z.share]
    for j in range(1, z.parts):
        out = jnp.where(part == j, value[:, j * z.share : (j + 1) * z.share], out)
    return out


def all_shares(z, own, others, row):
    out = []
    for j in range(z.parts):
        value = own
        for d in range(1, z.parts):
            value = jnp.where(lax.rem(row + z.parts - d, z.parts) == j, others[d - 1], value)
        out.append(value)
    return out


def side_by_side(values):
    return jnp.concatenate([value.astype(F32) for value in values], axis=1)


def folded(value, blocks):
    rows = value.shape[0] // blocks
    return side_by_side([value[j * rows : (j + 1) * rows] for j in range(blocks)])


def unfolded(value, blocks):
    value, width = value.astype(F32), value.shape[1] // blocks
    return jnp.concatenate([value[:, j * width : (j + 1) * width] for j in range(blocks)], axis=0)


def fold(z, ref, value):
    ref[...] = folded(value, FOLD).astype(BF)


def unfold(z, ref):
    return unfolded(ref[...], FOLD)


def source(z, row, d):
    return lax.rem(row + z.parts - d, z.parts)


def target(z, row, d):
    return lax.rem(row + d, z.parts)


def part_rows(z, part):
    return pl.ds(pl.multiple_of(part * z.local, z.local), z.local)


def assemble(z, ref, pieces, row, start, width):
    for d, piece in enumerate(pieces):
        value = (piece if isinstance(piece, jax.Array) else piece[...]).astype(F32)
        value = value[:, start : start + width]
        ref[part_rows(z, source(z, row, d)), :] = value.astype(BF)


def group_sums(z, first, second):
    width = first.shape[1]
    line = lax.broadcasted_iota(jnp.int32, (8, width), 0)
    both = jnp.where(line == 0, first, jnp.where(line == 1, second, 0.0))
    across = lax.broadcasted_iota(jnp.int32, (width, width), 1).astype(F32)
    down = lax.broadcasted_iota(jnp.int32, (width, width), 0).astype(F32)
    same = jnp.floor((across + 0.5) * (1.0 / z.group)) == jnp.floor((down + 0.5) * (1.0 / z.group))
    sums = jnp.dot(
        both, same.astype(F32), precision=lax.Precision.HIGHEST, preferred_element_type=F32
    )
    return sums[0:1], sums[1:2]


def normalize(z, x):
    total, square = group_sums(
        z, jnp.sum(x, axis=0, keepdims=True), jnp.sum(x * x, axis=0, keepdims=True)
    )
    center = total / z.count
    factor = lax.rsqrt(square / z.count - center * center + EPSILON)
    return (x - center) * factor, factor


def sigmoid(y):
    return 1.0 / (1.0 + jnp.exp(-y))


def norm_back(z, y, factor, logistic, upstream):
    e = upstream * logistic * (1.0 + y * (1.0 - logistic))
    first, second = group_sums(
        z, jnp.sum(e, axis=0, keepdims=True), jnp.sum(e * y, axis=0, keepdims=True)
    )
    return factor * (e - first / z.count - y * (second / z.count))


def spread(z, x, line_ref, pad_ref):
    cells, cols = z.cells, z.cols
    width = x.shape[1]
    line_ref[8 : 8 + cells, :] = x
    column = lax.rem(lax.broadcasted_iota(jnp.int32, (cells, 1), 0), cols)
    edge = jnp.zeros((cols, width), BF)
    for b in range(3):
        pad_ref[b, :cols, :] = edge
        pad_ref[b, cols + cells :, :] = edge
    pad_ref[1, cols : cols + cells, :] = x.astype(BF)
    left = jnp.where(column > 0, line_ref[7 : 7 + cells, :], 0.0)
    pad_ref[0, cols : cols + cells, :] = left.astype(BF)
    right = jnp.where(column < cols - 1, line_ref[9 : 9 + cells, :], 0.0)
    pad_ref[2, cols : cols + cells, :] = right.astype(BF)


def convolve(z, pad_ref, kernel_ref, which):
    total = None
    for a in range(3):
        for b in range(3):
            term = jnp.dot(
                pad_ref[b, a * z.cols : a * z.cols + z.cells, :],
                kernel_ref[9 * which + 3 * a + b],
                preferred_element_type=F32,
            )
            total = term if total is None else total + term
    return total


def convolve_back(z, pad_ref, kernel_ref, which):
    total = None
    for a in range(3):
        for b in range(3):
            term = lax.dot_general(
                pad_ref[b, a * z.cols : a * z.cols + z.cells, :],
                kernel_ref[9 * which + 3 * (2 - a) + 2 - b],
                (((1,), (1,)), ((), ())),
                preferred_element_type=F32,
            )
            total = term if total is None else total + term
    return total


def pad_shapes(z, width):
    return [
        pltpu.VMEM((z.cells + 16, width), F32),
        pltpu.VMEM((3, z.cells + 2 * z.cols, width), BF),
    ]


def call(body, name, scalars, arrays, outs, scratch=(), after=(), remote=0, far_outs=0, aliases=None):
    near, far = pl.BlockSpec(memory_space=pltpu.VMEM), pl.BlockSpec(memory_space=pltpu.HBM)

    def inner(*refs):
        given = len(scalars) + len(arrays)
        body(*refs[:given], *refs[given + len(after) :])

    arrays = [
        pltpu.with_memory_space_constraint(x, pltpu.HBM) if j < remote else x
        for j, x in enumerate(arrays)
    ]
    near_outs = len(outs) - far_outs
    return pl.pallas_call(
        inner,
        name=name,
        out_shape=[
            jax.ShapeDtypeStruct(shape, dtype) if j < near_outs else pltpu.HBM(shape, dtype)
            for j, (shape, dtype) in enumerate(outs)
        ],
        in_specs=[pl.BlockSpec(memory_space=pltpu.SMEM)] * len(scalars)
        + [far] * remote
        + [near] * (len(arrays) - remote)
        + [pl.BlockSpec(memory_space=pl.ANY)] * len(after),
        out_specs=[near] * near_outs + [far] * far_outs,
        scratch_shapes=list(scratch),
        input_output_aliases=aliases or {},
        compiler_params=pltpu.CompilerParams(vmem_limit_bytes=VMEM_LIMIT),
        cost_estimate=pl.CostEstimate(flops=1, bytes_accessed=1, transcendentals=0),
    )(*scalars, *arrays, *after)


def held_until(values, earlier):
    return lax.optimization_barrier((tuple(values), earlier))[0]


def fetch(pairs, sems):
    copies = [pltpu.make_async_copy(a, b, sems.at[j]) for j, (a, b) in enumerate(pairs)]
    for copy in copies:
        copy.start()
    for copy in copies:
        copy.wait()


def pack_first(z, fs_far, bs_far, fwd_far, bwd_far, mir_far, stash_far, *refs):
    n = z.parts
    heads, pieces = refs[:n], refs[n : 2 * n]
    fwd, bwd, mir, stash, fs, bs, sems = refs[2 * n :]
    fetch(
        [
            (fs_far, fs),
            (bs_far, bs),
            (fwd_far, fwd),
            (bwd_far, bwd),
            (mir_far, mir),
            (stash_far, stash),
        ],
        sems,
    )
    s, row = where_am_i()
    f, b = fs[0, s], bs[0, s]
    h, i, skip = fwd[f], stash[2 * b + 1], mir[f]
    g = bwd[b].astype(F32) + jnp.where(s < z.sections // 2, mir[b].astype(F32), 0.0)
    for d in range(n):
        part = target(z, row, d)
        fold(z, heads[d], share_of(z, h, part))
        shares = [share_of(z, i, part), share_of(z, skip, part), g]
        pieces[d][...] = side_by_side(shares).astype(BF)


def taken_back(z, bs, s):
    later, partner = jnp.minimum(s + 1, z.sections - 1), z.sections - 1 - s
    return (
        jnp.logical_and(s < z.sections - 1, bs[0, later] == bs[1, s]),
        jnp.logical_and(s < z.sections // 2, bs[0, partner] == bs[1, s]),
    )


def pack_later(z, fs_far, bs_far, fwd, bwd, mir, stash, *refs):
    n = z.parts
    groups = [refs[j * n : (j + 1) * n] for j in range(4)]
    fs, bs, sems = refs[4 * n :]
    fetch([(fs_far, fs), (bs_far, bs)], sems)
    s, row = where_am_i()
    f1, b1 = fs[1, s], bs[1, s]
    grad_taken, skip_taken = taken_back(z, bs, s)
    skip_kept = jnp.logical_and(s < z.sections // 2, jnp.logical_not(skip_taken))
    kept = jnp.where(grad_taken, 0.0, bwd[b1].astype(F32))
    kept = kept + jnp.where(skip_kept, mir[b1].astype(F32), 0.0)
    values = [stash[2 * bs[0, s]], stash[2 * b1], fwd[f1], stash[2 * b1 + 1], mir[f1]]
    rows = z.local // FOLD
    for d in range(n):
        shares = [share_of(z, value, target(z, row, d)) for value in values]
        grads = [kept[:, j * z.share : (j + 1) * z.share] for j in range(n)]
        for outs, parts in zip(groups, (shares[:2], shares[2:4], grads, shares[4:])):
            for j, value in enumerate(parts):
                outs[d][j * rows : (j + 1) * rows, :] = folded(value, FOLD).astype(BF)


def send_partials(z, row, total, own, sends, extra):
    own[...] = share_of(z, total, row)
    for d, send in enumerate(sends, 1):
        part = folded(share_of(z, total, target(z, row, d)), FOLD).astype(BF)
        send[: part.shape[0], :] = part
        send[part.shape[0] :, :] = extra[d][...]


def first_forward(z, *refs):
    n = z.parts
    pieces, extra, kernel = refs[:n], refs[n : 2 * n], refs[2 * n]
    own, h_out = refs[2 * n + 1 : 2 * n + 3]
    sends, (line, pad) = refs[2 * n + 3 : 3 * n + 2], refs[3 * n + 2 :]
    _, row = where_am_i()
    assemble(z, h_out, [unfold(z, piece) for piece in pieces], row, 0, z.share)
    y, _ = normalize(z, h_out[...].astype(F32))
    spread(z, y * sigmoid(y), line, pad)
    send_partials(z, row, convolve(z, pad, kernel, 0), own, sends, extra)


def enclosed(z, own, received, j):
    rows, base = z.local // FOLD, z.cells // FOLD
    at, there = slice(j * rows, (j + 1) * rows), slice(base + j * rows, base + (j + 1) * rows)
    return [unfolded(own[at, :], FOLD)] + [unfolded(x[there, :], FOLD) for x in received]


def later_forward(z, fs, *refs):
    n = z.parts
    arrivals, nexts, received = refs[:n], refs[n], refs[n + 1 : 2 * n]
    lasts, kernel = refs[2 * n : 3 * n], refs[3 * n]
    own, h_out, arrived, onward = refs[3 * n + 1 : 3 * n + 5]
    sends = refs[3 * n + 5 : 4 * n + 4]
    line, pad = refs[4 * n + 4 :]
    s, row = where_am_i()
    total = unfold(z, arrivals[0])
    for other in arrivals[1:]:
        total = total + unfold(z, other)
    total = total.astype(BF).astype(F32)
    arrived[...] = total.astype(BF)
    fold(z, onward, total)
    assemble(z, h_out, enclosed(z, nexts, received, 0), row, 0, z.share)
    prior = jnp.maximum(s - 1, 0)
    taken = jnp.logical_and(s > 0, fs[0, prior] == fs[1, s])
    h = jnp.where(taken, total, h_out[...].astype(F32))
    h_out[...] = h.astype(BF)
    y, _ = normalize(z, h)
    spread(z, y * sigmoid(y), line, pad)
    send_partials(z, row, convolve(z, pad, kernel, 0), own, sends, lasts)


def back_through_second(z, i, g, kernel, q_out, q_send, act_out, pad, line):
    y, factor = normalize(z, i.astype(F32))
    logistic = sigmoid(y)
    act_out[...] = (y * logistic).astype(BF)
    spread(z, g, line, pad)
    q = norm_back(z, y, factor, logistic, convolve_back(z, pad, kernel, 1)).astype(BF)
    q_out[...] = q
    fold(z, q_send, q.astype(F32))


def first_backward(z, *refs):
    n = z.parts
    pieces, heads, kernel = refs[:n], refs[n : 2 * n], refs[2 * n]
    q_out, q_send, pad, act_out = refs[2 * n + 1 : 2 * n + 5]
    sends, (i_ref, g_ref, line) = refs[2 * n + 5 : 3 * n + 4], refs[3 * n + 4 :]
    _, row = where_am_i()
    assemble(z, i_ref, pieces, row, 0, z.share)
    assemble(z, g_ref, pieces, row, 2 * z.share, z.channels)
    back_through_second(
        z, i_ref[...], g_ref[...].astype(F32), kernel, q_out, q_send, act_out, pad, line
    )
    rows = z.cells // FOLD
    for d, send in enumerate(sends, 1):
        send[:rows, :] = q_send[...]
        send[rows:, :] = heads[d][...]


def later_backward(z, fs, bs, *refs):
    n = z.parts
    arrivals, mirror, received, kept = refs[:n], refs[n], refs[n + 1 : 2 * n], refs[2 * n]
    nexts, others = refs[2 * n + 1], refs[2 * n + 2 : 3 * n + 1]
    i_before, arrived, kernel = refs[3 * n + 1 : 3 * n + 4]
    q_out, pad, act_out, grad_in, skip_in = refs[3 * n + 4 : 3 * n + 9]
    rows_own, sends = refs[3 * n + 9], refs[3 * n + 10 : 4 * n + 9]
    q_send, i_ref, full, line = refs[4 * n + 9 :]
    s, row = where_am_i()
    w = z.share
    shares = [unfold(z, part) for part in arrivals]
    grad = side_by_side(all_shares(z, shares[0], shares[1:], row))
    grad_in[...] = grad.astype(BF)
    shares = [unfolded(x[: z.cells // FOLD, :], FOLD) for x in received]
    skip = side_by_side(all_shares(z, unfold(z, mirror), shares, row))
    skip_in[...] = skip.astype(BF)
    grad_taken, skip_taken = taken_back(z, bs, s)
    for j in range(n):
        assemble(z, full.at[j], enclosed(z, kept, received, j), row, 0, w)
    g = side_by_side([full[j] for j in range(n)]) + jnp.where(grad_taken, grad, 0.0)
    g = g + jnp.where(skip_taken, skip, 0.0)
    g = g.astype(BF).astype(F32)
    assemble(z, i_ref, enclosed(z, nexts, others, 1), row, 0, w)
    i = jnp.where(fs[0, s] == bs[1, s], i_before[...].astype(F32), i_ref[...].astype(F32))
    back_through_second(z, i, g, kernel, q_out, q_send, act_out, pad, line)
    for d, out in enumerate([rows_own, *sends]):
        at = part_rows(z, target(z, row, d))
        part = folded(side_by_side([i_before[at, :], arrived[at, :]]), 2).astype(BF)
        out[out.shape[0] - part.shape[0] :, :] = part
    for send in sends:
        send[: q_send.shape[0], :] = q_send[...]


def second_convolution(z, encoder, row, own, received, skip, h, kernel, i_out, full, line, pad):
    c0 = own[...]
    for other in received:
        c0 = c0 + unfolded(other[: z.cells // FOLD, :], FOLD)
    i = jnp.where(encoder, c0, skip.astype(F32)).astype(BF)
    i_out[...] = i
    y, _ = normalize(z, i.astype(F32))
    spread(z, y * sigmoid(y), line, pad)
    total = convolve(z, pad, kernel, 1)
    base = h[...].astype(F32) + jnp.where(encoder, 0.0, c0)
    full[...] = total + side_by_side([jnp.where(row == j, base, 0.0) for j in range(z.parts)])


def middle(z, pad):
    return pad[1, z.cols : z.cols + z.cells, :].astype(F32)


def second_forward(z, *refs):
    n = z.parts
    own, received, h, pieces, kernel = refs[0], refs[1:n], refs[n], refs[n + 1 : 2 * n + 1], refs[2 * n + 1]
    i_out, full_out = refs[2 * n + 2 : 2 * n + 4]
    sends = refs[2 * n + 4 : 3 * n + 4]
    skip, full, line, pad = refs[3 * n + 4 :]
    s, row = where_am_i()
    encoder = s < z.sections // 2
    assemble(z, skip, pieces, row, z.share, z.share)
    second_convolution(
        z, encoder, row, own, received, skip[...], h, kernel, i_out, full, line, pad
    )
    full_out[...] = full[...].astype(BF)
    for d in range(n):
        fold(z, sends[d], share_of(z, full[...], target(z, row, d)))


def last_forward(z, fs, *refs):
    n = z.parts
    own, received, h = refs[0], refs[1:n], refs[n]
    lasts, arrived, kernel = refs[n + 1 : n + 4]
    sends = refs[n + 4 : 2 * n + 4]
    i_out, skip, full, line, pad = refs[2 * n + 4 :]
    s, row = where_am_i()
    encoder = s < z.sections // 2
    partner = z.sections - 1 - s
    assemble(z, skip, enclosed(z, lasts, received, 0), row, 0, z.share)
    now = jnp.where(
        fs[0, partner] == fs[1, s], unfold(z, arrived), skip[...].astype(F32)
    )
    second_convolution(z, encoder, row, own, received, now, h, kernel, i_out, full, line, pad)
    for d, send in enumerate(sends):
        at = part_rows(z, target(z, row, d))
        send[...] = side_by_side([full[at, :], i_out[at, :]]).astype(BF)


def joined_shares(z, own, received, row):
    others = [unfolded(other[: z.cells // FOLD, :], FOLD) for other in received]
    return side_by_side(all_shares(z, own[...].astype(F32), others, row))


def back_through_first(z, encoder, row, q, received, g_pad, h, kernel, act_out, pad, line):
    g = middle(z, g_pad)
    whole = joined_shares(z, q, received, row)
    now = jnp.where(encoder, whole, g)
    y, factor = normalize(z, h.astype(F32))
    logistic = sigmoid(y)
    act_out[...] = (y * logistic).astype(BF)
    spread(z, now, line, pad)
    back = norm_back(z, y, factor, logistic, convolve_back(z, pad, kernel, 0))
    return share_of(z, g, row) + back, whole


def second_backward(z, *refs):
    n = z.parts
    q, received, g = refs[0], refs[1:n], refs[n]
    heads, others, mirror = refs[n + 1], refs[n + 2 : 2 * n + 1], refs[2 * n + 1]
    grads, kernel = refs[2 * n + 2 : 3 * n + 2], refs[3 * n + 2]
    send, pad, act_out = refs[3 * n + 3 : 3 * n + 6]
    relays, (h, line) = refs[3 * n + 6 : 4 * n + 5], refs[4 * n + 5 :]
    s, row = where_am_i()
    for d, relay in enumerate(relays, 1):
        relay[: z.cells // FOLD, :] = mirror[...]
        relay[z.cells // FOLD :, :] = grads[d][...]
    assemble(z, h, enclosed(z, heads, others, 0), row, 0, z.share)
    value, _ = back_through_first(
        z, s < z.sections // 2, row, q, received, g, h[...], kernel, act_out, pad, line
    )
    fold(z, send, value)


def last_backward(z, fs, bs, *refs):
    n = z.parts
    q, received, g = refs[0], refs[1:n], refs[n]
    heads, others = refs[n + 1], refs[n + 2 : 2 * n + 1]
    h_before, kernel = refs[2 * n + 1 : 2 * n + 3]
    sends = refs[2 * n + 3 : 3 * n + 3]
    pad, act_out, h, value, line = refs[3 * n + 3 :]
    s, row = where_am_i()
    assemble(z, h, enclosed(z, heads, others, 1), row, 0, z.share)
    now = jnp.where(fs[0, s] == bs[1, s], h_before[...], h[...])
    result, _ = back_through_first(
        z, s < z.sections // 2, row, q, received, g, now, kernel, act_out, pad, line
    )
    value[...] = result.astype(BF)
    for d, send in enumerate(sends):
        fold(z, send, value[part_rows(z, target(z, row, d)), :])


def pack_rows(z, *refs):
    n = z.parts
    full, mirror = refs[:2]
    sends, skip = refs[2 : n + 2], refs[n + 2]
    _, row = where_am_i()
    skip[...] = unfold(z, mirror).astype(BF)
    for d, send in enumerate(sends):
        at = part_rows(z, target(z, row, d))
        send[...] = side_by_side([ref[at, :] for ref in (full, skip)]).astype(BF)


def add_rows(z, *refs):
    n = z.parts
    pieces, q, received = refs[:n], refs[n], refs[n + 1 : 2 * n]
    out, mirror, i_rows, whole = refs[2 * n :]
    s, row = where_am_i()
    c = z.channels
    whole[...] = joined_shares(z, q, received, row)
    values = [piece[...].astype(F32) for piece in pieces]
    total = sum(value[:, :c] for value in values)
    out[...] = total.astype(BF)
    mine = whole[part_rows(z, row), :]
    mirror[...] = jnp.where(s < z.sections // 2, total, mine).astype(BF)
    shares = all_shares(z, values[0][:, c:], [value[:, c:] for value in values[1:]], row)
    i_rows[...] = side_by_side(shares).astype(BF)


def write_queues(z, fs, bs, *refs):
    n = z.parts
    fwd, bwd, mir, stash, grad_in, skip_in = refs[:6]
    pieces = refs[6 : n + 6]
    outs, held, sems = refs[n + 6 : n + 10], refs[n + 10 : n + 14], refs[n + 14]
    s, row = where_am_i()
    w = z.share
    prior, later = jnp.maximum(s - 1, 0), jnp.minimum(s + 1, z.sections - 1)
    partner = z.sections - 1 - s
    f0, f1 = fs[0, s], fs[1, s]
    mine = part_rows(z, row)
    copies = [pltpu.make_async_copy(a, b, sems.at[j]) for j, (a, b) in enumerate(zip(held, outs))]
    for ref, queue in zip(held, (fwd, bwd, mir, stash)):
        ref[...] = queue[...]

    @pl.when(s < z.sections - 1)
    def _():
        held[1][bs[0, later]] = grad_in[mine, :]

    copies[1].start()

    @pl.when(s < z.sections // 2)
    def _():
        held[2][bs[0, partner]] = skip_in[mine, :]

    copies[2].start()
    values = [unfolded(piece[piece.shape[0] - z.local // 2 :, :], 2) for piece in pieces]

    def joined(at):
        shares = [value[:, at : at + w] for value in values]
        return side_by_side(all_shares(z, shares[0], shares[1:], row)).astype(BF)

    fwd_in = joined(w)

    @pl.when(s > 0)
    def _():
        held[0][fs[0, prior]] = fwd_in

    copies[0].start()
    held[3][2 * f0] = fwd[f0]
    held[3][2 * f0 + 1] = joined(0)
    held[3][2 * f1] = fwd[f1]

    @pl.when(jnp.logical_and(s > 0, fs[0, prior] == f1))
    def _():
        held[3][2 * f1] = fwd_in

    copies[3].start()
    for copy in copies:
        copy.wait()


def finish(z, fs, bs, *refs):
    n = z.parts
    out1, i1, fwd1, mir1 = refs[4:8]
    rows0, grads1 = refs[8 : n + 8], refs[n + 8 : 2 * n + 8]
    fwd_out, bwd_out, mir_out, stash_out, emitted = refs[2 * n + 8 : 2 * n + 13]
    out0, skip, grads, sems = refs[2 * n + 13 :]
    s, row = where_am_i()
    c = z.channels
    prior, later = jnp.maximum(s - 1, 0), jnp.minimum(s + 1, z.sections - 1)
    partner = z.sections - 1 - s
    encoder, has_prior, has_later = s < z.sections // 2, s > 0, s < z.sections - 1
    first = jnp.where(encoder, bs[0, partner], fs[0, partner])
    second = jnp.where(encoder, bs[1, partner], fs[1, partner])
    skip_stays = jnp.logical_and(jnp.logical_not(encoder), first != second)

    def put(source, place, j):
        return pltpu.make_async_copy(source, place, sems.at[j])

    always = [
        put(out1, emitted.at[1], 0),
        put(i1, stash_out.at[2 * fs[1, s] + 1], 1),
        put(mir1, mir_out.at[second], 2),
        put(out0, emitted.at[0], 3),
    ]
    for copy in always[:3]:
        copy.start()
    onward, back = put(fwd1, fwd_out.at[fs[1, prior]], 4), put(grads, bwd_out.at[bs[1, later]], 5)
    aside = put(skip, mir_out.at[first], 6)
    pl.when(has_prior)(onward.start)
    pieces = [unfold(z, piece) for piece in grads1]
    grads[...] = side_by_side(all_shares(z, pieces[0], pieces[1:], row)).astype(BF)
    pl.when(has_later)(back.start)
    pieces = [piece[...].astype(F32) for piece in rows0]
    out0[...] = sum(piece[:, :c] for piece in pieces).astype(BF)
    always[3].start()
    shares = [piece[:, c:] for piece in pieces]
    skip[...] = side_by_side(all_shares(z, shares[0], shares[1:], row)).astype(BF)
    pl.when(skip_stays)(aside.start)
    for copy in always:
        copy.wait()
    pl.when(has_prior)(onward.wait)
    pl.when(has_later)(back.wait)
    pl.when(skip_stays)(aside.wait)


def add_taps(z, act, pad, before, store):
    turned = jnp.transpose(act[...].astype(F32)).astype(BF)
    for tap in range(9):
        a, b = divmod(tap, 3)
        at = (2 - a) * z.cols
        moved = pad[2 - b, at : at + z.cells, :]
        store(tap, before(tap) + jnp.dot(turned, moved, preferred_element_type=F32))


def kernel_grads_first(z, which, acc, act, pad, out):
    def store(tap, value):
        out[tap] = value

    add_taps(z, act, pad, lambda tap: acc[9 * which + tap], store)


def kernel_grads_last(z, which, *refs):
    total, act, pad, token, out, held, sems = refs[-7:]
    token[...] = jnp.zeros_like(token)
    copies = [
        pltpu.make_async_copy(held.at[tap], out.at[9 * which + tap], sems.at[tap]) for tap in range(9)
    ]

    def store(tap, value):
        held[tap] = value
        copies[tap].start()

    add_taps(z, act, pad, lambda tap: total[tap], store)
    for copy in copies:
        copy.wait()


def per_device(fwd_queue, bwd_queue, mirror_queue, stash, weights, grad_acc, fwd_slot, bwd_slot):
    sections, n = lax.axis_size("section"), lax.axis_size("row")
    z = Sizes(fwd_queue[0], sections, n)
    slots = fwd_queue.shape[1]
    c, w, local, cells = z.channels, z.share, z.local, z.cells
    fwd, bwd, mir = (x.reshape(slots, local, c) for x in (fwd_queue, bwd_queue, mirror_queue))
    kept = stash.reshape(2 * slots, local, c)
    kernels = weights.reshape(18, w, c)
    acc = grad_acc.reshape(18, w, c)
    fs, bs = fwd_slot.T, bwd_slot.T
    fold_shape, wide = (cells // FOLD, FOLD * w), (cells, c)
    half = (cells, w)

    def with_shares(k):
        return ((cells + k * local) // FOLD, FOLD * w)

    padded = (3, cells + 2 * z.cols, c)

    def move(x, d, step):
        route = [
            (s * n + r, step(s) * n + (r + d) % n) for s in range(sections) for r in range(n)
        ]
        return lax.ppermute(x, ("section", "row"), route)

    across = functools.partial(move, step=lambda s: s)
    onward = functools.partial(move, step=lambda s: (s + 1) % sections)
    backward = functools.partial(move, step=lambda s: (s - 1) % sections)
    crossed = functools.partial(move, step=lambda s: (sections - s) % sections)
    mirrored = functools.partial(move, step=lambda s: sections - 1 - s)

    def run(body, scalars, arrays, outs, scratch=(), **options):
        return call(
            functools.partial(body, z), body.__name__, scalars, arrays, outs, scratch, **options
        )

    def exchange(pieces):
        return [pieces[0]] + [across(piece, d) for d, piece in enumerate(pieces[1:], 1)]

    narrow_pad = pad_shapes(z, w)
    wide_line = pltpu.VMEM((cells + 16, c), F32)
    queues = (fwd, bwd, mir, kept)
    rows = (local, c)
    sems = pltpu.SemaphoreType.DMA
    packed = run(
        pack_first,
        (),
        (fs, bs, *queues),
        [((local // FOLD, FOLD * w), BF)] * n
        + [((local, 2 * w + c), BF)] * n
        + [(x.shape, BF) for x in queues],
        [pltpu.SMEM(fs.shape, jnp.int32)] * 2 + [sems((6,))],
        remote=6,
    )
    inputs, held = exchange(packed[:n]), packed[2 * n :]
    first = exchange(held_until(packed[n : 2 * n], inputs))

    packed = run(
        pack_later,
        (),
        (fs, bs, *held),
        [((k * (local // FOLD), FOLD * w), BF) for k in (2, 2, n, 1) for _ in range(n)],
        [pltpu.SMEM(fs.shape, jnp.int32)] * 2 + [sems((2,))],
        remote=2,
        after=(inputs[0],),
    )
    heads, nexts, grads, lasts = (packed[j * n : (j + 1) * n] for j in range(4))

    own, h0, *sends = run(
        first_forward,
        (),
        (*inputs, *heads, kernels),
        [(half, F32), (half, BF)] + [(with_shares(2), BF)] * (n - 1),
        narrow_pad,
    )
    sums = [across(x, d) for d, x in enumerate(sends, 1)]
    q0, q_send, g_pad0, act_i0, *sends = run(
        first_backward,
        (),
        (*first, *nexts, kernels),
        [(half, BF), (fold_shape, BF), (padded, BF), (half, BF)]
        + [(with_shares(2), BF)] * (n - 1),
        [pltpu.VMEM(half, BF), pltpu.VMEM(wide, BF), wide_line],
        after=(own,),
    )
    q_received = [across(x, d) for d, x in enumerate(sends, 1)]
    skip_in = mirrored(q_send, 0)

    def start_grads(which, act, pad, after):
        [out] = call(
            functools.partial(kernel_grads_first, z, which),
            f"kernel_grads_first_{which}",
            (),
            (acc, act, pad),
            [((9, w, c), F32)],
            after=after,
        )
        return out

    def end_grads(which, earlier, total, act, pad, after):
        token, out = call(
            functools.partial(kernel_grads_last, z, which),
            f"kernel_grads_last_{which}",
            (),
            (*earlier, total, act, pad),
            [((8, 128), F32), ((18, w, c), F32)],
            [pltpu.VMEM((9, w, c), F32), sems((9,))],
            remote=len(earlier),
            far_outs=1,
            after=after,
            aliases={0: 1} if earlier else None,
        )
        return token, out

    sum_i = start_grads(1, act_i0, g_pad0, (q0,))
    i0, full0, *sends = run(
        second_forward,
        (),
        (own, *sums, h0, *first, kernels),
        [(half, BF), (wide, BF)] + [(fold_shape, BF)] * n,
        [pltpu.VMEM(half, BF), pltpu.VMEM(wide, F32)] + narrow_pad,
        after=(sum_i,),
    )
    fwd_in = [onward(x, d) for d, x in enumerate(sends)]
    dh_send, f_pad0, act_h0, *relays = run(
        second_backward,
        (),
        (q0, *q_received, g_pad0, heads[0], *sums, skip_in, *grads, kernels),
        [(fold_shape, BF), (padded, BF), (half, BF)] + [(with_shares(n), BF)] * (n - 1),
        [pltpu.VMEM(half, BF), wide_line],
        after=(i0,),
    )
    dh_in = [backward(dh_send, d) for d in range(n)]
    relayed = [across(x, d) for d, x in enumerate(relays, 1)]

    own, h1, arrived, turned, *sends = run(
        later_forward,
        (fs,),
        (*fwd_in, nexts[0], *q_received, *lasts, kernels),
        [(half, F32), (half, BF), (half, BF), (fold_shape, BF)]
        + [(with_shares(1), BF)] * (n - 1),
        narrow_pad,
        after=(dh_send,),
    )
    received = [across(x, d) for d, x in enumerate(sends, 1)]
    mir_in = crossed(turned, 0)
    sum_h = start_grads(0, act_h0, f_pad0, (own,))
    q1, g_pad1, act_i1, grad_in, skip_full, rows_own, *sends = run(
        later_backward,
        (fs, bs),
        (*dh_in, skip_in, *relayed, grads[0], nexts[0], *q_received, i0, arrived, kernels),
        [(half, BF), (padded, BF), (half, BF), (wide, BF), (wide, BF), ((local // 2, 4 * w), BF)]
        + [((cells // FOLD + local // 2, FOLD * w), BF)] * (n - 1),
        [pltpu.VMEM(fold_shape, BF), pltpu.VMEM(half, BF), pltpu.VMEM((n, *half), BF), wide_line],
        after=(sum_h,),
    )
    q_received = [across(x, d) for d, x in enumerate(sends, 1)]
    sends = run(
        last_forward,
        (fs,),
        (own, *received, h1, lasts[0], mir_in, kernels),
        [((local, c + w), BF)] * n,
        [pltpu.VMEM(half, BF), pltpu.VMEM(half, BF), pltpu.VMEM(wide, F32)] + narrow_pad,
        after=(q1,),
    )
    rows1 = exchange(sends)
    token, part_i = end_grads(1, (), sum_i, act_i1, g_pad1, (sends[0],))
    packed = run(
        pack_rows,
        (),
        (full0, mir_in),
        [((local, c + w), BF)] * n,
        [pltpu.VMEM(half, BF)],
        after=(token,),
    )
    written = run(
        write_queues,
        (fs, bs),
        (*held, grad_in, skip_full, rows_own, *q_received),
        [(x.shape, BF) for x in queues],
        [pltpu.VMEM(x.shape, BF) for x in queues] + [sems((4,))],
        far_outs=4,
        after=(packed[0],),
    )
    rows0 = exchange(held_until(packed, (rows1, written[0])))
    out1, mirror1, i1 = run(
        add_rows,
        (),
        (*rows1, q1, *q_received),
        [(rows, BF)] * 3,
        [pltpu.VMEM(wide, F32)],
        after=(written[0],),
    )
    fwd1, mir1 = onward(out1, 0), mirrored(mirror1, 0)
    *dh_sends, f_pad1, act_h1 = run(
        last_backward,
        (fs, bs),
        (q1, *q_received, g_pad1, heads[0], *sums, h0, kernels),
        [((local // FOLD, FOLD * w), BF)] * n + [(padded, BF), (half, BF)],
        [pltpu.VMEM(half, BF), pltpu.VMEM(half, BF), wide_line],
        after=(out1,),
    )
    dh1_in = [backward(x, d) for d, x in enumerate(dh_sends)]
    token, grad_total = end_grads(0, (part_i,), sum_h, act_h1, f_pad1, ())
    fwd_out, bwd_out, mir_out, stash_out, emitted = run(
        finish,
        (fs, bs),
        (*written, out1, i1, fwd1, mir1, *rows0, *dh1_in),
        [(x.shape, BF) for x in queues] + [((TICKS, local, c), BF)],
        [pltpu.VMEM(rows, BF)] * 3 + [sems((7,))],
        remote=4,
        far_outs=5,
        aliases={j + 2: j for j in range(4)},
        after=(token,),
    )
    return (
        fwd_out.reshape(fwd_queue.shape),
        bwd_out.reshape(bwd_queue.shape),
        mir_out.reshape(mirror_queue.shape),
        stash_out.reshape(stash.shape),
        grad_total.reshape(grad_acc.shape),
        emitted.reshape((1, TICKS) + fwd_queue.shape[2:]),
    )


def solution(mesh):
    return jax.shard_map(
        per_device,
        mesh=mesh,
        in_specs=(
            P("section", None, "row", None, None),
            P("section", None, "row", None, None),
            P("section", None, "row", None, None),
            P("section", None, None, "row", None, None),
            P("section", None, None, None, "row", None),
            P("section", None, None, None, "row", None),
            P(),
            P(),
        ),
        out_specs=(
            P("section", None, "row", None, None),
            P("section", None, "row", None, None),
            P("section", None, "row", None, None),
            P("section", None, None, "row", None, None),
            P("section", None, None, None, "row", None),
            P("section", None, "row", None, None),
        ),
        check_vma=False,
    )
```

```python
import functools

import jax
import jax.numpy as jnp
from jax import lax
from jax.experimental import pallas as pl
from jax.experimental.pallas import tpu as pltpu
from jax.sharding import PartitionSpec as P

GROUPS = 32
TICKS = 2
FOLD = 4
EPSILON = 1e-05
BF, F32 = jnp.bfloat16, jnp.float32
VMEM_LIMIT = 24 * 2**20


class Sizes:
    def __init__(self, queue, sections, rows):
        self.sections, self.parts = sections, rows
        self.cols = queue.shape[2]
        self.channels = queue.shape[3]
        self.local = queue.shape[1] * queue.shape[2]
        self.cells = self.local * rows
        self.share = self.channels // rows
        self.group = self.channels // GROUPS
        self.count = self.cells * self.group


def where_am_i():
    return lax.axis_index("section"), lax.axis_index("row")


def share_of(z, value, part):
    value = value.astype(F32)
    out = value[:, : z.share]
    for j in range(1, z.parts):
        out = jnp.where(part == j, value[:, j * z.share : (j + 1) * z.share], out)
    return out


def all_shares(z, own, others, row):
    out = []
    for j in range(z.parts):
        value = own
        for d in range(1, z.parts):
            value = jnp.where(lax.rem(row + z.parts - d, z.parts) == j, others[d - 1], value)
        out.append(value)
    return out


def side_by_side(values):
    return jnp.concatenate([value.astype(F32) for value in values], axis=1)


def folded(value, blocks):
    rows = value.shape[0] // blocks
    return side_by_side([value[j * rows : (j + 1) * rows] for j in range(blocks)])


def unfolded(value, blocks):
    value, width = value.astype(F32), value.shape[1] // blocks
    return jnp.concatenate([value[:, j * width : (j + 1) * width] for j in range(blocks)], axis=0)


def fold(z, ref, value):
    ref[...] = folded(value, FOLD).astype(BF)


def unfold(z, ref):
    return unfolded(ref[...], FOLD)


def source(z, row, d):
    return lax.rem(row + z.parts - d, z.parts)


def target(z, row, d):
    return lax.rem(row + d, z.parts)


def part_rows(z, part):
    return pl.ds(pl.multiple_of(part * z.local, z.local), z.local)


def assemble(z, ref, pieces, row, start, width):
    for d, piece in enumerate(pieces):
        value = (piece if isinstance(piece, jax.Array) else piece[...]).astype(F32)
        value = value[:, start : start + width]
        ref[part_rows(z, source(z, row, d)), :] = value.astype(BF)


def group_sums(z, first, second):
    width = first.shape[1]
    line = lax.broadcasted_iota(jnp.int32, (8, width), 0)
    both = jnp.where(line == 0, first, jnp.where(line == 1, second, 0.0))
    across = lax.broadcasted_iota(jnp.int32, (width, width), 1).astype(F32)
    down = lax.broadcasted_iota(jnp.int32, (width, width), 0).astype(F32)
    same = jnp.floor((across + 0.5) * (1.0 / z.group)) == jnp.floor((down + 0.5) * (1.0 / z.group))
    sums = jnp.dot(
        both, same.astype(F32), precision=lax.Precision.HIGHEST, preferred_element_type=F32
    )
    return sums[0:1], sums[1:2]


def normalize(z, x):
    total, square = group_sums(
        z, jnp.sum(x, axis=0, keepdims=True), jnp.sum(x * x, axis=0, keepdims=True)
    )
    center = total / z.count
    factor = lax.rsqrt(square / z.count - center * center + EPSILON)
    return (x - center) * factor, factor


def sigmoid(y):
    return 1.0 / (1.0 + jnp.exp(-y))


def norm_back(z, y, factor, logistic, upstream):
    e = upstream * logistic * (1.0 + y * (1.0 - logistic))
    first, second = group_sums(
        z, jnp.sum(e, axis=0, keepdims=True), jnp.sum(e * y, axis=0, keepdims=True)
    )
    return factor * (e - first / z.count - y * (second / z.count))


def spread(z, x, line_ref, pad_ref):
    cells, cols = z.cells, z.cols
    width = x.shape[1]
    line_ref[8 : 8 + cells, :] = x
    column = lax.rem(lax.broadcasted_iota(jnp.int32, (cells, 1), 0), cols)
    edge = jnp.zeros((cols, width), BF)
    for b in range(3):
        pad_ref[b, :cols, :] = edge
        pad_ref[b, cols + cells :, :] = edge
    pad_ref[1, cols : cols + cells, :] = x.astype(BF)
    left = jnp.where(column > 0, line_ref[7 : 7 + cells, :], 0.0)
    pad_ref[0, cols : cols + cells, :] = left.astype(BF)
    right = jnp.where(column < cols - 1, line_ref[9 : 9 + cells, :], 0.0)
    pad_ref[2, cols : cols + cells, :] = right.astype(BF)


def convolve(z, pad_ref, kernel_ref, which):
    total = None
    for a in range(3):
        for b in range(3):
            term = jnp.dot(
                pad_ref[b, a * z.cols : a * z.cols + z.cells, :],
                kernel_ref[9 * which + 3 * a + b],
                preferred_element_type=F32,
            )
            total = term if total is None else total + term
    return total


def convolve_back(z, pad_ref, kernel_ref, which):
    total = None
    for a in range(3):
        for b in range(3):
            term = lax.dot_general(
                pad_ref[b, a * z.cols : a * z.cols + z.cells, :],
                kernel_ref[9 * which + 3 * (2 - a) + 2 - b],
                (((1,), (1,)), ((), ())),
                preferred_element_type=F32,
            )
            total = term if total is None else total + term
    return total


def pad_shapes(z, width):
    return [
        pltpu.VMEM((z.cells + 16, width), F32),
        pltpu.VMEM((3, z.cells + 2 * z.cols, width), BF),
    ]


def call(body, name, scalars, arrays, outs, scratch=(), after=(), remote=0, far_outs=0, aliases=None):
    near, far = pl.BlockSpec(memory_space=pltpu.VMEM), pl.BlockSpec(memory_space=pltpu.HBM)

    def inner(*refs):
        given = len(scalars) + len(arrays)
        body(*refs[:given], *refs[given + len(after) :])

    arrays = [
        pltpu.with_memory_space_constraint(x, pltpu.HBM) if j < remote else x
        for j, x in enumerate(arrays)
    ]
    near_outs = len(outs) - far_outs
    return pl.pallas_call(
        inner,
        name=name,
        out_shape=[
            jax.ShapeDtypeStruct(shape, dtype) if j < near_outs else pltpu.HBM(shape, dtype)
            for j, (shape, dtype) in enumerate(outs)
        ],
        in_specs=[pl.BlockSpec(memory_space=pltpu.SMEM)] * len(scalars)
        + [far] * remote
        + [near] * (len(arrays) - remote)
        + [pl.BlockSpec(memory_space=pl.ANY)] * len(after),
        out_specs=[near] * near_outs + [far] * far_outs,
        scratch_shapes=list(scratch),
        input_output_aliases=aliases or {},
        compiler_params=pltpu.CompilerParams(vmem_limit_bytes=VMEM_LIMIT),
        cost_estimate=pl.CostEstimate(flops=1, bytes_accessed=1, transcendentals=0),
    )(*scalars, *arrays, *after)


def held_until(values, earlier):
    return lax.optimization_barrier((tuple(values), earlier))[0]


def fetch(pairs, sems):
    copies = [pltpu.make_async_copy(a, b, sems.at[j]) for j, (a, b) in enumerate(pairs)]
    for copy in copies:
        copy.start()
    for copy in copies:
        copy.wait()


def pack_first(z, fs_far, bs_far, fwd_far, bwd_far, mir_far, stash_far, *refs):
    n = z.parts
    heads, pieces = refs[:n], refs[n : 2 * n]
    fwd, bwd, mir, stash, fs, bs, sems = refs[2 * n :]
    fetch(
        [
            (fs_far, fs),
            (bs_far, bs),
            (fwd_far, fwd),
            (bwd_far, bwd),
            (mir_far, mir),
            (stash_far, stash),
        ],
        sems,
    )
    s, row = where_am_i()
    f, b = fs[0, s], bs[0, s]
    h, i, skip = fwd[f], stash[2 * b + 1], mir[f]
    g = bwd[b].astype(F32) + jnp.where(s < z.sections // 2, mir[b].astype(F32), 0.0)
    for d in range(n):
        part = target(z, row, d)
        fold(z, heads[d], share_of(z, h, part))
        shares = [share_of(z, i, part), share_of(z, skip, part), g]
        pieces[d][...] = side_by_side(shares).astype(BF)


def taken_back(z, bs, s):
    later, partner = jnp.minimum(s + 1, z.sections - 1), z.sections - 1 - s
    return (
        jnp.logical_and(s < z.sections - 1, bs[0, later] == bs[1, s]),
        jnp.logical_and(s < z.sections // 2, bs[0, partner] == bs[1, s]),
    )


def pack_later(z, fs_far, bs_far, fwd, bwd, mir, stash, *refs):
    n = z.parts
    groups = [refs[j * n : (j + 1) * n] for j in range(4)]
    fs, bs, sems = refs[4 * n :]
    fetch([(fs_far, fs), (bs_far, bs)], sems)
    s, row = where_am_i()
    f1, b1 = fs[1, s], bs[1, s]
    grad_taken, skip_taken = taken_back(z, bs, s)
    skip_kept = jnp.logical_and(s < z.sections // 2, jnp.logical_not(skip_taken))
    kept = jnp.where(grad_taken, 0.0, bwd[b1].astype(F32))
    kept = kept + jnp.where(skip_kept, mir[b1].astype(F32), 0.0)
    values = [stash[2 * bs[0, s]], stash[2 * b1], fwd[f1], stash[2 * b1 + 1], mir[f1]]
    rows = z.local // FOLD
    for d in range(n):
        shares = [share_of(z, value, target(z, row, d)) for value in values]
        grads = [kept[:, j * z.share : (j + 1) * z.share] for j in range(n)]
        for outs, parts in zip(groups, (shares[:2], shares[2:4], grads, shares[4:])):
            for j, value in enumerate(parts):
                outs[d][j * rows : (j + 1) * rows, :] = folded(value, FOLD).astype(BF)


def send_partials(z, row, total, own, sends, extra):
    own[...] = share_of(z, total, row)
    for d, send in enumerate(sends, 1):
        part = folded(share_of(z, total, target(z, row, d)), FOLD).astype(BF)
        send[: part.shape[0], :] = part
        send[part.shape[0] :, :] = extra[d][...]


def first_forward(z, *refs):
    n = z.parts
    pieces, extra, kernel = refs[:n], refs[n : 2 * n], refs[2 * n]
    own, h_out = refs[2 * n + 1 : 2 * n + 3]
    sends, (line, pad) = refs[2 * n + 3 : 3 * n + 2], refs[3 * n + 2 :]
    _, row = where_am_i()
    assemble(z, h_out, [unfold(z, piece) for piece in pieces], row, 0, z.share)
    y, _ = normalize(z, h_out[...].astype(F32))
    spread(z, y * sigmoid(y), line, pad)
    send_partials(z, row, convolve(z, pad, kernel, 0), own, sends, extra)


def enclosed(z, own, received, j):
    rows, base = z.local // FOLD, z.cells // FOLD
    at, there = slice(j * rows, (j + 1) * rows), slice(base + j * rows, base + (j + 1) * rows)
    return [unfolded(own[at, :], FOLD)] + [unfolded(x[there, :], FOLD) for x in received]


def later_forward(z, fs, *refs):
    n = z.parts
    arrivals, nexts, received = refs[:n], refs[n], refs[n + 1 : 2 * n]
    lasts, kernel = refs[2 * n : 3 * n], refs[3 * n]
    own, h_out, arrived, onward = refs[3 * n + 1 : 3 * n + 5]
    sends = refs[3 * n + 5 : 4 * n + 4]
    line, pad = refs[4 * n + 4 :]
    s, row = where_am_i()
    total = unfold(z, arrivals[0])
    for other in arrivals[1:]:
        total = total + unfold(z, other)
    total = total.astype(BF).astype(F32)
    arrived[...] = total.astype(BF)
    fold(z, onward, total)
    assemble(z, h_out, enclosed(z, nexts, received, 0), row, 0, z.share)
    prior = jnp.maximum(s - 1, 0)
    taken = jnp.logical_and(s > 0, fs[0, prior] == fs[1, s])
    h = jnp.where(taken, total, h_out[...].astype(F32))
    h_out[...] = h.astype(BF)
    y, _ = normalize(z, h)
    spread(z, y * sigmoid(y), line, pad)
    send_partials(z, row, convolve(z, pad, kernel, 0), own, sends, lasts)


def back_through_second(z, i, g, kernel, q_out, q_send, act_out, pad, line):
    y, factor = normalize(z, i.astype(F32))
    logistic = sigmoid(y)
    act_out[...] = (y * logistic).astype(BF)
    spread(z, g, line, pad)
    q = norm_back(z, y, factor, logistic, convolve_back(z, pad, kernel, 1)).astype(BF)
    q_out[...] = q
    fold(z, q_send, q.astype(F32))


def first_backward(z, *refs):
    n = z.parts
    pieces, heads, kernel = refs[:n], refs[n : 2 * n], refs[2 * n]
    q_out, q_send, pad, act_out = refs[2 * n + 1 : 2 * n + 5]
    sends, (i_ref, g_ref, line) = refs[2 * n + 5 : 3 * n + 4], refs[3 * n + 4 :]
    _, row = where_am_i()
    assemble(z, i_ref, pieces, row, 0, z.share)
    assemble(z, g_ref, pieces, row, 2 * z.share, z.channels)
    back_through_second(
        z, i_ref[...], g_ref[...].astype(F32), kernel, q_out, q_send, act_out, pad, line
    )
    rows = z.cells // FOLD
    for d, send in enumerate(sends, 1):
        send[:rows, :] = q_send[...]
        send[rows:, :] = heads[d][...]


def later_backward(z, fs, bs, *refs):
    n = z.parts
    arrivals, mirror, received, kept = refs[:n], refs[n], refs[n + 1 : 2 * n], refs[2 * n]
    nexts, others = refs[2 * n + 1], refs[2 * n + 2 : 3 * n + 1]
    i_before, arrived, kernel = refs[3 * n + 1 : 3 * n + 4]
    q_out, pad, act_out, grad_in, skip_in = refs[3 * n + 4 : 3 * n + 9]
    rows_own, sends = refs[3 * n + 9], refs[3 * n + 10 : 4 * n + 9]
    q_send, i_ref, full, line = refs[4 * n + 9 :]
    s, row = where_am_i()
    w = z.share
    shares = [unfold(z, part) for part in arrivals]
    grad = side_by_side(all_shares(z, shares[0], shares[1:], row))
    grad_in[...] = grad.astype(BF)
    shares = [unfolded(x[: z.cells // FOLD, :], FOLD) for x in received]
    skip = side_by_side(all_shares(z, unfold(z, mirror.at[partner_place(z, s)]), shares, row))
    skip_in[...] = skip.astype(BF)
    grad_taken, skip_taken = taken_back(z, bs, s)
    for j in range(n):
        assemble(z, full.at[j], enclosed(z, kept, received, j), row, 0, w)
    g = side_by_side([full[j] for j in range(n)]) + jnp.where(grad_taken, grad, 0.0)
    g = g + jnp.where(skip_taken, skip, 0.0)
    g = g.astype(BF).astype(F32)
    assemble(z, i_ref, enclosed(z, nexts, others, 1), row, 0, w)
    i = jnp.where(fs[0, s] == bs[1, s], i_before[...].astype(F32), i_ref[...].astype(F32))
    back_through_second(z, i, g, kernel, q_out, q_send, act_out, pad, line)
    for d, out in enumerate([rows_own, *sends]):
        at = part_rows(z, target(z, row, d))
        part = folded(side_by_side([i_before[at, :], arrived[at, :]]), 2).astype(BF)
        out[out.shape[0] - part.shape[0] :, :] = part
    for send in sends:
        send[: q_send.shape[0], :] = q_send[...]


def second_convolution(z, encoder, row, own, received, skip, h, kernel, i_out, full, line, pad):
    c0 = own[...]
    for other in received:
        c0 = c0 + unfolded(other[: z.cells // FOLD, :], FOLD)
    i = jnp.where(encoder, c0, skip.astype(F32)).astype(BF)
    i_out[...] = i
    y, _ = normalize(z, i.astype(F32))
    spread(z, y * sigmoid(y), line, pad)
    total = convolve(z, pad, kernel, 1)
    base = h[...].astype(F32) + jnp.where(encoder, 0.0, c0)
    full[...] = total + side_by_side([jnp.where(row == j, base, 0.0) for j in range(z.parts)])


def middle(z, pad):
    return pad[1, z.cols : z.cols + z.cells, :].astype(F32)


def second_forward(z, *refs):
    n = z.parts
    own, received, h, pieces, kernel = refs[0], refs[1:n], refs[n], refs[n + 1 : 2 * n + 1], refs[2 * n + 1]
    i_out, full_out = refs[2 * n + 2 : 2 * n + 4]
    sends = refs[2 * n + 4 : 3 * n + 4]
    skip, full, line, pad = refs[3 * n + 4 :]
    s, row = where_am_i()
    encoder = s < z.sections // 2
    assemble(z, skip, pieces, row, z.share, z.share)
    second_convolution(
        z, encoder, row, own, received, skip[...], h, kernel, i_out, full, line, pad
    )
    full_out[...] = full[...].astype(BF)
    for d in range(n):
        fold(z, sends[d], share_of(z, full[...], target(z, row, d)))


def last_forward(z, fs, *refs):
    n = z.parts
    own, received, h = refs[0], refs[1:n], refs[n]
    lasts, arrived, kernel = refs[n + 1 : n + 4]
    sends = refs[n + 4 : 2 * n + 4]
    i_out, skip, full, line, pad = refs[2 * n + 4 :]
    s, row = where_am_i()
    encoder = s < z.sections // 2
    partner = z.sections - 1 - s
    assemble(z, skip, enclosed(z, lasts, received, 0), row, 0, z.share)
    now = jnp.where(
        fs[0, partner] == fs[1, s], partner_output(z, arrived, s), skip[...].astype(F32)
    )
    second_convolution(z, encoder, row, own, received, now, h, kernel, i_out, full, line, pad)
    for d, send in enumerate(sends):
        at = part_rows(z, target(z, row, d))
        send[...] = side_by_side([full[at, :], i_out[at, :]]).astype(BF)


def joined_shares(z, own, received, row):
    others = [unfolded(other[: z.cells // FOLD, :], FOLD) for other in received]
    return side_by_side(all_shares(z, own[...].astype(F32), others, row))


def partner_place(z, s):
    return jnp.where(s < z.sections // 2, 1, 0)


def partner_output(z, pair, s):
    return unfold(z, pair.at[jnp.where(s == z.sections // 2, 1, 0)])


def back_through_first(z, encoder, row, q, received, g_pad, h, kernel, act_out, pad, line):
    g = middle(z, g_pad)
    whole = joined_shares(z, q, received, row)
    now = jnp.where(encoder, whole, g)
    y, factor = normalize(z, h.astype(F32))
    logistic = sigmoid(y)
    act_out[...] = (y * logistic).astype(BF)
    spread(z, now, line, pad)
    back = norm_back(z, y, factor, logistic, convolve_back(z, pad, kernel, 0))
    return share_of(z, g, row) + back, whole


def second_backward(z, *refs):
    n = z.parts
    q, received, g = refs[0], refs[1:n], refs[n]
    heads, others, mirror = refs[n + 1], refs[n + 2 : 2 * n + 1], refs[2 * n + 1]
    grads, kernel = refs[2 * n + 2 : 3 * n + 2], refs[3 * n + 2]
    send, pad, act_out = refs[3 * n + 3 : 3 * n + 6]
    relays, (h, line) = refs[3 * n + 6 : 4 * n + 5], refs[4 * n + 5 :]
    s, row = where_am_i()
    for d, relay in enumerate(relays, 1):
        relay[: z.cells // FOLD, :] = mirror[partner_place(z, s)]
        relay[z.cells // FOLD :, :] = grads[d][...]
    assemble(z, h, enclosed(z, heads, others, 0), row, 0, z.share)
    value, _ = back_through_first(
        z, s < z.sections // 2, row, q, received, g, h[...], kernel, act_out, pad, line
    )
    fold(z, send, value)


def last_backward(z, fs, bs, *refs):
    n = z.parts
    q, received, g = refs[0], refs[1:n], refs[n]
    heads, others = refs[n + 1], refs[n + 2 : 2 * n + 1]
    h_before, kernel = refs[2 * n + 1 : 2 * n + 3]
    sends = refs[2 * n + 3 : 3 * n + 3]
    pad, act_out, h, value, line = refs[3 * n + 3 :]
    s, row = where_am_i()
    assemble(z, h, enclosed(z, heads, others, 1), row, 0, z.share)
    now = jnp.where(fs[0, s] == bs[1, s], h_before[...], h[...])
    result, _ = back_through_first(
        z, s < z.sections // 2, row, q, received, g, now, kernel, act_out, pad, line
    )
    value[...] = result.astype(BF)
    for d, send in enumerate(sends):
        fold(z, send, value[part_rows(z, target(z, row, d)), :])


def pack_rows(z, *refs):
    n = z.parts
    full, mirror = refs[:2]
    sends, skip = refs[2 : n + 2], refs[n + 2]
    s, row = where_am_i()
    skip[...] = partner_output(z, mirror, s).astype(BF)
    for d, send in enumerate(sends):
        at = part_rows(z, target(z, row, d))
        send[...] = side_by_side([ref[at, :] for ref in (full, skip)]).astype(BF)


def add_rows(z, *refs):
    n = z.parts
    pieces, q, received = refs[:n], refs[n], refs[n + 1 : 2 * n]
    out, mirror, i_rows, whole = refs[2 * n :]
    s, row = where_am_i()
    c = z.channels
    whole[...] = joined_shares(z, q, received, row)
    values = [piece[...].astype(F32) for piece in pieces]
    total = sum(value[:, :c] for value in values)
    out[...] = total.astype(BF)
    mine = whole[part_rows(z, row), :]
    mirror[...] = jnp.where(s < z.sections // 2, total, mine).astype(BF)
    shares = all_shares(z, values[0][:, c:], [value[:, c:] for value in values[1:]], row)
    i_rows[...] = side_by_side(shares).astype(BF)


def write_queues(z, fs, bs, *refs):
    n = z.parts
    fwd, bwd, mir, stash, grad_in, skip_in = refs[:6]
    pieces = refs[6 : n + 6]
    token, outs, held = refs[n + 6], refs[n + 7 : n + 11], refs[n + 11 : n + 15]
    sems = refs[n + 15]
    token[...] = jnp.zeros_like(token)
    s, row = where_am_i()
    w = z.share
    prior, later = jnp.maximum(s - 1, 0), jnp.minimum(s + 1, z.sections - 1)
    partner = z.sections - 1 - s
    f0, f1 = fs[0, s], fs[1, s]
    mine = part_rows(z, row)
    copies = [pltpu.make_async_copy(a, b, sems.at[j]) for j, (a, b) in enumerate(zip(held, outs))]
    for ref, queue in zip(held, (fwd, bwd, mir, stash)):
        ref[...] = queue[...]

    @pl.when(s < z.sections - 1)
    def _():
        held[1][bs[0, later]] = grad_in[mine, :]

    copies[1].start()

    @pl.when(s < z.sections // 2)
    def _():
        held[2][bs[0, partner]] = skip_in[mine, :]

    copies[2].start()
    values = [unfolded(piece[piece.shape[0] - z.local // 2 :, :], 2) for piece in pieces]

    def joined(at):
        shares = [value[:, at : at + w] for value in values]
        return side_by_side(all_shares(z, shares[0], shares[1:], row)).astype(BF)

    fwd_in = joined(w)

    @pl.when(s > 0)
    def _():
        held[0][fs[0, prior]] = fwd_in

    copies[0].start()
    held[3][2 * f0] = fwd[f0]
    held[3][2 * f0 + 1] = joined(0)
    held[3][2 * f1] = fwd[f1]

    @pl.when(jnp.logical_and(s > 0, fs[0, prior] == f1))
    def _():
        held[3][2 * f1] = fwd_in

    copies[3].start()
    for copy in copies:
        copy.wait()


def finish(z, fs, bs, *refs):
    n = z.parts
    out1, i1, fwd1, mir1 = refs[4:8]
    rows0, grads1 = refs[8 : n + 8], refs[n + 8 : 2 * n + 8]
    fwd_out, bwd_out, mir_out, stash_out, emitted = refs[2 * n + 8 : 2 * n + 13]
    out0, skip, grads, sems = refs[2 * n + 13 :]
    s, row = where_am_i()
    c = z.channels
    prior, later = jnp.maximum(s - 1, 0), jnp.minimum(s + 1, z.sections - 1)
    partner = z.sections - 1 - s
    encoder, has_prior, has_later = s < z.sections // 2, s > 0, s < z.sections - 1
    first = jnp.where(encoder, bs[0, partner], fs[0, partner])
    second = jnp.where(encoder, bs[1, partner], fs[1, partner])
    skip_stays = jnp.logical_and(jnp.logical_not(encoder), first != second)

    def put(source, place, j):
        return pltpu.make_async_copy(source, place, sems.at[j])

    always = [
        put(out1, emitted.at[1], 0),
        put(i1, stash_out.at[2 * fs[1, s] + 1], 1),
        put(mir1, mir_out.at[second], 2),
        put(out0, emitted.at[0], 3),
    ]
    for copy in always[:3]:
        copy.start()
    onward, back = put(fwd1, fwd_out.at[fs[1, prior]], 4), put(grads, bwd_out.at[bs[1, later]], 5)
    aside = put(skip, mir_out.at[first], 6)
    pl.when(has_prior)(onward.start)
    pieces = [unfold(z, piece) for piece in grads1]
    grads[...] = side_by_side(all_shares(z, pieces[0], pieces[1:], row)).astype(BF)
    pl.when(has_later)(back.start)
    pieces = [piece[...].astype(F32) for piece in rows0]
    out0[...] = sum(piece[:, :c] for piece in pieces).astype(BF)
    always[3].start()
    shares = [piece[:, c:] for piece in pieces]
    skip[...] = side_by_side(all_shares(z, shares[0], shares[1:], row)).astype(BF)
    pl.when(skip_stays)(aside.start)
    for copy in always:
        copy.wait()
    pl.when(has_prior)(onward.wait)
    pl.when(has_later)(back.wait)
    pl.when(skip_stays)(aside.wait)


def add_taps(z, act, pad, before, store):
    turned = jnp.transpose(act[...].astype(F32)).astype(BF)
    for tap in range(9):
        a, b = divmod(tap, 3)
        at = (2 - a) * z.cols
        moved = pad[2 - b, at : at + z.cells, :]
        store(tap, before(tap) + jnp.dot(turned, moved, preferred_element_type=F32))


def kernel_grads_first(z, which, acc, act, pad, out):
    def store(tap, value):
        out[tap] = value

    add_taps(z, act, pad, lambda tap: acc[9 * which + tap], store)


def kernel_grads_last(z, which, *refs):
    total, act, pad, token, out, held, sems = refs[-7:]
    token[...] = jnp.zeros_like(token)
    copies = [
        pltpu.make_async_copy(held.at[tap], out.at[9 * which + tap], sems.at[tap]) for tap in range(9)
    ]

    def store(tap, value):
        held[tap] = value
        copies[tap].start()

    add_taps(z, act, pad, lambda tap: total[tap], store)
    for copy in copies:
        copy.wait()


def per_device(fwd_queue, bwd_queue, mirror_queue, stash, weights, grad_acc, fwd_slot, bwd_slot):
    sections, n = lax.axis_size("section"), lax.axis_size("row")
    z = Sizes(fwd_queue[0], sections, n)
    slots = fwd_queue.shape[1]
    c, w, local, cells = z.channels, z.share, z.local, z.cells
    fwd, bwd, mir = (x.reshape(slots, local, c) for x in (fwd_queue, bwd_queue, mirror_queue))
    kept = stash.reshape(2 * slots, local, c)
    kernels = weights.reshape(18, w, c)
    acc = grad_acc.reshape(18, w, c)
    fs, bs = fwd_slot.T, bwd_slot.T
    fold_shape, wide = (cells // FOLD, FOLD * w), (cells, c)
    half = (cells, w)

    def with_shares(k):
        return ((cells + k * local) // FOLD, FOLD * w)

    padded = (3, cells + 2 * z.cols, c)

    def move(x, d, step):
        route = [
            (s * n + r, step(s) * n + (r + d) % n) for s in range(sections) for r in range(n)
        ]
        return lax.ppermute(x, ("section", "row"), route)

    def swapped(x, other):
        pairs = [[s, other(s)] for s in range(sections) if s < other(s)]
        return lax.all_gather(x, "section", axis_index_groups=pairs)

    across = functools.partial(move, step=lambda s: s)
    onward = functools.partial(move, step=lambda s: (s + 1) % sections)
    backward = functools.partial(move, step=lambda s: (s - 1) % sections)
    mirrored = functools.partial(move, step=lambda s: sections - 1 - s)

    def run(body, scalars, arrays, outs, scratch=(), **options):
        return call(
            functools.partial(body, z), body.__name__, scalars, arrays, outs, scratch, **options
        )

    def exchange(pieces):
        return [pieces[0]] + [across(piece, d) for d, piece in enumerate(pieces[1:], 1)]

    narrow_pad = pad_shapes(z, w)
    wide_line = pltpu.VMEM((cells + 16, c), F32)
    queues = (fwd, bwd, mir, kept)
    rows = (local, c)
    sems = pltpu.SemaphoreType.DMA
    packed = run(
        pack_first,
        (),
        (fs, bs, *queues),
        [((local // FOLD, FOLD * w), BF)] * n
        + [((local, 2 * w + c), BF)] * n
        + [(x.shape, BF) for x in queues],
        [pltpu.SMEM(fs.shape, jnp.int32)] * 2 + [sems((6,))],
        remote=6,
    )
    inputs, held = exchange(packed[:n]), packed[2 * n :]
    first = exchange(held_until(packed[n : 2 * n], inputs))

    packed = run(
        pack_later,
        (),
        (fs, bs, *held),
        [((k * (local // FOLD), FOLD * w), BF) for k in (2, 2, n, 1) for _ in range(n)],
        [pltpu.SMEM(fs.shape, jnp.int32)] * 2 + [sems((2,))],
        remote=2,
        after=(inputs[0],),
    )
    heads, nexts, grads, lasts = (packed[j * n : (j + 1) * n] for j in range(4))

    own, h0, *sends = run(
        first_forward,
        (),
        (*inputs, *heads, kernels),
        [(half, F32), (half, BF)] + [(with_shares(2), BF)] * (n - 1),
        narrow_pad,
    )
    sums = [across(x, d) for d, x in enumerate(sends, 1)]
    q0, q_send, g_pad0, act_i0, *sends = run(
        first_backward,
        (),
        (*first, *nexts, kernels),
        [(half, BF), (fold_shape, BF), (padded, BF), (half, BF)]
        + [(with_shares(2), BF)] * (n - 1),
        [pltpu.VMEM(half, BF), pltpu.VMEM(wide, BF), wide_line],
        after=(own,),
    )
    q_received = [across(x, d) for d, x in enumerate(sends, 1)]
    skip_in = swapped(q_send, lambda s: sections - 1 - s)

    def start_grads(which, act, pad, after):
        [out] = call(
            functools.partial(kernel_grads_first, z, which),
            f"kernel_grads_first_{which}",
            (),
            (acc, act, pad),
            [((9, w, c), F32)],
            after=after,
        )
        return out

    def end_grads(which, earlier, total, act, pad, after):
        token, out = call(
            functools.partial(kernel_grads_last, z, which),
            f"kernel_grads_last_{which}",
            (),
            (*earlier, total, act, pad),
            [((8, 128), F32), ((18, w, c), F32)],
            [pltpu.VMEM((9, w, c), F32), sems((9,))],
            remote=len(earlier),
            far_outs=1,
            after=after,
            aliases={0: 1} if earlier else None,
        )
        return token, out

    sum_i = start_grads(1, act_i0, g_pad0, (q0,))
    i0, full0, *sends = run(
        second_forward,
        (),
        (own, *sums, h0, *first, kernels),
        [(half, BF), (wide, BF)] + [(fold_shape, BF)] * n,
        [pltpu.VMEM(half, BF), pltpu.VMEM(wide, F32)] + narrow_pad,
        after=(sum_i,),
    )
    fwd_in = [onward(x, d) for d, x in enumerate(sends)]
    dh_send, f_pad0, act_h0, *relays = run(
        second_backward,
        (),
        (q0, *q_received, g_pad0, heads[0], *sums, skip_in, *grads, kernels),
        [(fold_shape, BF), (padded, BF), (half, BF)] + [(with_shares(n), BF)] * (n - 1),
        [pltpu.VMEM(half, BF), wide_line],
        after=(i0,),
    )
    dh_in = [backward(dh_send, d) for d in range(n)]
    relayed = [across(x, d) for d, x in enumerate(relays, 1)]

    own, h1, arrived, turned, *sends = run(
        later_forward,
        (fs,),
        (*fwd_in, nexts[0], *q_received, *lasts, kernels),
        [(half, F32), (half, BF), (half, BF), (fold_shape, BF)]
        + [(with_shares(1), BF)] * (n - 1),
        narrow_pad,
        after=(dh_send,),
    )
    received = [across(x, d) for d, x in enumerate(sends, 1)]
    middle_pair = {0: sections // 2, sections // 2: 0}
    mir_in = swapped(turned, lambda s: middle_pair.get(s, sections - s))
    sum_h = start_grads(0, act_h0, f_pad0, (own,))
    q1, g_pad1, act_i1, grad_in, skip_full, rows_own, *sends = run(
        later_backward,
        (fs, bs),
        (*dh_in, skip_in, *relayed, grads[0], nexts[0], *q_received, i0, arrived, kernels),
        [(half, BF), (padded, BF), (half, BF), (wide, BF), (wide, BF), ((local // 2, 4 * w), BF)]
        + [((cells // FOLD + local // 2, FOLD * w), BF)] * (n - 1),
        [pltpu.VMEM(fold_shape, BF), pltpu.VMEM(half, BF), pltpu.VMEM((n, *half), BF), wide_line],
        after=(sum_h,),
    )
    q_received = [across(x, d) for d, x in enumerate(sends, 1)]
    sends = run(
        last_forward,
        (fs,),
        (own, *received, h1, lasts[0], mir_in, kernels),
        [((local, c + w), BF)] * n,
        [pltpu.VMEM(half, BF), pltpu.VMEM(half, BF), pltpu.VMEM(wide, F32)] + narrow_pad,
        after=(q1,),
    )
    rows1 = exchange(sends)
    token, part_i = end_grads(1, (), sum_i, act_i1, g_pad1, (sends[0],))
    packed = run(
        pack_rows,
        (),
        (full0, mir_in),
        [((local, c + w), BF)] * n,
        [pltpu.VMEM(half, BF)],
        after=(token,),
    )
    token, *written = run(
        write_queues,
        (fs, bs),
        (*held, grad_in, skip_full, rows_own, *q_received),
        [((8, 128), F32)] + [(x.shape, BF) for x in queues],
        [pltpu.VMEM(x.shape, BF) for x in queues] + [sems((4,))],
        far_outs=4,
        after=(packed[0],),
    )
    rows0 = exchange(held_until(packed, (rows1, token)))
    out1, mirror1, i1 = run(
        add_rows,
        (),
        (*rows1, q1, *q_received),
        [(rows, BF)] * 3,
        [pltpu.VMEM(wide, F32)],
        after=(token,),
    )
    fwd1, mir1 = onward(out1, 0), mirrored(mirror1, 0)
    *dh_sends, f_pad1, act_h1 = run(
        last_backward,
        (fs, bs),
        (q1, *q_received, g_pad1, heads[0], *sums, h0, kernels),
        [((local // FOLD, FOLD * w), BF)] * n + [(padded, BF), (half, BF)],
        [pltpu.VMEM(half, BF), pltpu.VMEM(half, BF), wide_line],
        after=(out1,),
    )
    dh1_in = [backward(x, d) for d, x in enumerate(dh_sends)]
    token, grad_total = end_grads(0, (part_i,), sum_h, act_h1, f_pad1, ())
    fwd_out, bwd_out, mir_out, stash_out, emitted = run(
        finish,
        (fs, bs),
        (*written, out1, i1, fwd1, mir1, *rows0, *dh1_in),
        [(x.shape, BF) for x in queues] + [((TICKS, local, c), BF)],
        [pltpu.VMEM(rows, BF)] * 3 + [sems((7,))],
        remote=4,
        far_outs=5,
        aliases={j + 2: j for j in range(4)},
        after=(token,),
    )
    return (
        fwd_out.reshape(fwd_queue.shape),
        bwd_out.reshape(bwd_queue.shape),
        mir_out.reshape(mirror_queue.shape),
        stash_out.reshape(stash.shape),
        grad_total.reshape(grad_acc.shape),
        emitted.reshape((1, TICKS) + fwd_queue.shape[2:]),
    )


def solution(mesh):
    return jax.shard_map(
        per_device,
        mesh=mesh,
        in_specs=(
            P("section", None, "row", None, None),
            P("section", None, "row", None, None),
            P("section", None, "row", None, None),
            P("section", None, None, "row", None, None),
            P("section", None, None, None, "row", None),
            P("section", None, None, None, "row", None),
            P(),
            P(),
        ),
        out_specs=(
            P("section", None, "row", None, None),
            P("section", None, "row", None, None),
            P("section", None, "row", None, None),
            P("section", None, None, "row", None, None),
            P("section", None, None, None, "row", None),
            P("section", None, "row", None, None),
        ),
        check_vma=False,
    )
```

```python
import functools

import jax
import jax.numpy as jnp
from jax import lax
from jax.experimental import pallas as pl
from jax.experimental.pallas import tpu as pltpu
from jax.sharding import PartitionSpec as P

GROUPS = 32
TICKS = 2
FOLD = 4
EPSILON = 1e-05
BF, F32 = jnp.bfloat16, jnp.float32
VMEM_LIMIT = 24 * 2**20


class Sizes:
    def __init__(self, queue, sections, rows):
        self.sections, self.parts = sections, rows
        self.cols = queue.shape[2]
        self.channels = queue.shape[3]
        self.local = queue.shape[1] * queue.shape[2]
        self.cells = self.local * rows
        self.share = self.channels // rows
        self.group = self.channels // GROUPS
        self.count = self.cells * self.group


def where_am_i():
    return lax.axis_index("section"), lax.axis_index("row")


def share_of(z, value, part):
    value = value.astype(F32)
    out = value[:, : z.share]
    for j in range(1, z.parts):
        out = jnp.where(part == j, value[:, j * z.share : (j + 1) * z.share], out)
    return out


def all_shares(z, own, others, row):
    out = []
    for j in range(z.parts):
        value = own
        for d in range(1, z.parts):
            value = jnp.where(lax.rem(row + z.parts - d, z.parts) == j, others[d - 1], value)
        out.append(value)
    return out


def side_by_side(values):
    return jnp.concatenate([value.astype(F32) for value in values], axis=1)


def folded(value, blocks):
    rows = value.shape[0] // blocks
    return side_by_side([value[j * rows : (j + 1) * rows] for j in range(blocks)])


def unfolded(value, blocks):
    value, width = value.astype(F32), value.shape[1] // blocks
    return jnp.concatenate([value[:, j * width : (j + 1) * width] for j in range(blocks)], axis=0)


def fold(z, ref, value):
    ref[...] = folded(value, FOLD).astype(BF)


def unfold(z, ref):
    return unfolded(ref[...], FOLD)


def source(z, row, d):
    return lax.rem(row + z.parts - d, z.parts)


def target(z, row, d):
    return lax.rem(row + d, z.parts)


def part_rows(z, part):
    return pl.ds(pl.multiple_of(part * z.local, z.local), z.local)


def assemble(z, ref, pieces, row, start, width):
    for d, piece in enumerate(pieces):
        value = (piece if isinstance(piece, jax.Array) else piece[...]).astype(F32)
        value = value[:, start : start + width]
        ref[part_rows(z, source(z, row, d)), :] = value.astype(BF)


def group_sums(z, first, second):
    width = first.shape[1]
    line = lax.broadcasted_iota(jnp.int32, (8, width), 0)
    both = jnp.where(line == 0, first, jnp.where(line == 1, second, 0.0))
    across = lax.broadcasted_iota(jnp.int32, (width, width), 1).astype(F32)
    down = lax.broadcasted_iota(jnp.int32, (width, width), 0).astype(F32)
    same = jnp.floor((across + 0.5) * (1.0 / z.group)) == jnp.floor((down + 0.5) * (1.0 / z.group))
    sums = jnp.dot(
        both, same.astype(F32), precision=lax.Precision.HIGHEST, preferred_element_type=F32
    )
    return sums[0:1], sums[1:2]


def normalize(z, x):
    total, square = group_sums(
        z, jnp.sum(x, axis=0, keepdims=True), jnp.sum(x * x, axis=0, keepdims=True)
    )
    center = total / z.count
    factor = lax.rsqrt(square / z.count - center * center + EPSILON)
    return (x - center) * factor, factor


def sigmoid(y):
    return 1.0 / (1.0 + jnp.exp(-y))


def norm_back(z, y, factor, logistic, upstream):
    e = upstream * logistic * (1.0 + y * (1.0 - logistic))
    first, second = group_sums(
        z, jnp.sum(e, axis=0, keepdims=True), jnp.sum(e * y, axis=0, keepdims=True)
    )
    return factor * (e - first / z.count - y * (second / z.count))


def spread(z, x, line_ref, pad_ref):
    cells, cols = z.cells, z.cols
    width = x.shape[1]
    line_ref[8 : 8 + cells, :] = x
    column = lax.rem(lax.broadcasted_iota(jnp.int32, (cells, 1), 0), cols)
    edge = jnp.zeros((cols, width), BF)
    for b in range(3):
        pad_ref[b, :cols, :] = edge
        pad_ref[b, cols + cells :, :] = edge
    pad_ref[1, cols : cols + cells, :] = x.astype(BF)
    left = jnp.where(column > 0, line_ref[7 : 7 + cells, :], 0.0)
    pad_ref[0, cols : cols + cells, :] = left.astype(BF)
    right = jnp.where(column < cols - 1, line_ref[9 : 9 + cells, :], 0.0)
    pad_ref[2, cols : cols + cells, :] = right.astype(BF)


def convolve(z, pad_ref, kernel_ref, which):
    total = None
    for a in range(3):
        for b in range(3):
            term = jnp.dot(
                pad_ref[b, a * z.cols : a * z.cols + z.cells, :],
                kernel_ref[9 * which + 3 * a + b],
                preferred_element_type=F32,
            )
            total = term if total is None else total + term
    return total


def convolve_back(z, pad_ref, kernel_ref, which):
    total = None
    for a in range(3):
        for b in range(3):
            term = lax.dot_general(
                pad_ref[b, a * z.cols : a * z.cols + z.cells, :],
                kernel_ref[9 * which + 3 * (2 - a) + 2 - b],
                (((1,), (1,)), ((), ())),
                preferred_element_type=F32,
            )
            total = term if total is None else total + term
    return total


def pad_shapes(z, width):
    return [
        pltpu.VMEM((z.cells + 16, width), F32),
        pltpu.VMEM((3, z.cells + 2 * z.cols, width), BF),
    ]


def call(body, name, scalars, arrays, outs, scratch=(), after=(), remote=0, far_outs=0, aliases=None):
    near, far = pl.BlockSpec(memory_space=pltpu.VMEM), pl.BlockSpec(memory_space=pltpu.HBM)

    def inner(*refs):
        given = len(scalars) + len(arrays)
        body(*refs[:given], *refs[given + len(after) :])

    arrays = [
        pltpu.with_memory_space_constraint(x, pltpu.HBM) if j < remote else x
        for j, x in enumerate(arrays)
    ]
    near_outs = len(outs) - far_outs
    return pl.pallas_call(
        inner,
        name=name,
        out_shape=[
            jax.ShapeDtypeStruct(shape, dtype) if j < near_outs else pltpu.HBM(shape, dtype)
            for j, (shape, dtype) in enumerate(outs)
        ],
        in_specs=[pl.BlockSpec(memory_space=pltpu.SMEM)] * len(scalars)
        + [far] * remote
        + [near] * (len(arrays) - remote)
        + [pl.BlockSpec(memory_space=pl.ANY)] * len(after),
        out_specs=[near] * near_outs + [far] * far_outs,
        scratch_shapes=list(scratch),
        input_output_aliases=aliases or {},
        compiler_params=pltpu.CompilerParams(vmem_limit_bytes=VMEM_LIMIT),
        cost_estimate=pl.CostEstimate(flops=1, bytes_accessed=1, transcendentals=0),
    )(*scalars, *arrays, *after)


def held_until(values, earlier):
    return lax.optimization_barrier((tuple(values), earlier))[0]


def fetch(pairs, sems):
    copies = [pltpu.make_async_copy(a, b, sems.at[j]) for j, (a, b) in enumerate(pairs)]
    for copy in copies:
        copy.start()
    for copy in copies:
        copy.wait()


def pack_first(z, fs_far, bs_far, fwd_far, bwd_far, mir_far, stash_far, *refs):
    n = z.parts
    heads = refs[:n]
    fwd, bwd, mir, stash, fs, bs, sems = refs[n:]
    fetch(
        [
            (fs_far, fs),
            (bs_far, bs),
            (fwd_far, fwd),
            (bwd_far, bwd),
            (mir_far, mir),
            (stash_far, stash),
        ],
        sems,
    )
    s, row = where_am_i()
    h = fwd[fs[0, s]]
    for d in range(n):
        fold(z, heads[d], share_of(z, h, target(z, row, d)))


def taken_back(z, bs, s):
    later, partner = jnp.minimum(s + 1, z.sections - 1), z.sections - 1 - s
    return (
        jnp.logical_and(s < z.sections - 1, bs[0, later] == bs[1, s]),
        jnp.logical_and(s < z.sections // 2, bs[0, partner] == bs[1, s]),
    )


def pack_later(z, fs_far, bs_far, fwd, bwd, mir, stash, *refs):
    n = z.parts
    pieces, groups = refs[:n], [refs[j * n : (j + 1) * n] for j in range(1, 3)]
    fs, bs, sems = refs[3 * n :]
    fetch([(fs_far, fs), (bs_far, bs)], sems)
    s, row = where_am_i()
    f1, b1 = fs[1, s], bs[1, s]
    grad_taken, skip_taken = taken_back(z, bs, s)
    skip_kept = jnp.logical_and(s < z.sections // 2, jnp.logical_not(skip_taken))
    kept = jnp.where(grad_taken, 0.0, bwd[b1].astype(F32))
    kept = kept + jnp.where(skip_kept, mir[b1].astype(F32), 0.0)
    f0, b0 = fs[0, s], bs[0, s]
    g = bwd[b0].astype(F32) + jnp.where(s < z.sections // 2, mir[b0].astype(F32), 0.0)
    for d, piece in enumerate(pieces):
        part = target(z, row, d)
        shares = [share_of(z, stash[2 * b0 + 1], part), share_of(z, mir[f0], part)]
        piece[...] = side_by_side(shares + [g]).astype(BF)
    values = [stash[2 * b0], stash[2 * b1], stash[2 * b1 + 1], mir[f1], fwd[f1]]
    rows = z.local // FOLD
    for d in range(n):
        shares = [share_of(z, value, target(z, row, d)) for value in values]
        grads = [kept[:, j * z.share : (j + 1) * z.share] for j in range(n)]
        for outs, parts in zip(groups, (shares[:4], shares[4:] + grads)):
            for j, value in enumerate(parts):
                outs[d][j * rows : (j + 1) * rows, :] = folded(value, FOLD).astype(BF)


def send_partials(z, row, total, own, sends, extra=None):
    own[...] = share_of(z, total, row)
    for d, send in enumerate(sends, 1):
        part = folded(share_of(z, total, target(z, row, d)), FOLD).astype(BF)
        send[: part.shape[0], :] = part
        if extra:
            send[part.shape[0] :, :] = extra[d][...]


def first_forward(z, *refs):
    n = z.parts
    pieces, extra, kernel = refs[:n], refs[n : 2 * n], refs[2 * n]
    own, h_out = refs[2 * n + 1 : 2 * n + 3]
    sends, (line, pad) = refs[2 * n + 3 : 3 * n + 2], refs[3 * n + 2 :]
    _, row = where_am_i()
    assemble(z, h_out, [unfold(z, piece) for piece in pieces], row, 0, z.share)
    y, _ = normalize(z, h_out[...].astype(F32))
    spread(z, y * sigmoid(y), line, pad)
    send_partials(z, row, convolve(z, pad, kernel, 0), own, sends, extra)


def enclosed(z, own, received, j):
    rows, base = z.local // FOLD, z.cells // FOLD
    at, there = slice(j * rows, (j + 1) * rows), slice(base + j * rows, base + (j + 1) * rows)
    return [unfolded(own[at, :], FOLD)] + [unfolded(x[there, :], FOLD) for x in received]


def later_forward(z, fs, *refs):
    n = z.parts
    arrivals, nexts, received, kernel = refs[:n], refs[n], refs[n + 1 : 2 * n], refs[2 * n]
    own, h_out, arrived, onward = refs[2 * n + 1 : 2 * n + 5]
    sends = refs[2 * n + 5 : 3 * n + 4]
    line, pad = refs[3 * n + 4 :]
    s, row = where_am_i()
    total = unfold(z, arrivals[0])
    for other in arrivals[1:]:
        total = total + unfold(z, other)
    total = total.astype(BF).astype(F32)
    arrived[...] = total.astype(BF)
    fold(z, onward, total)
    assemble(z, h_out, enclosed(z, nexts, received, 0), row, 0, z.share)
    prior = jnp.maximum(s - 1, 0)
    taken = jnp.logical_and(s > 0, fs[0, prior] == fs[1, s])
    h = jnp.where(taken, total, h_out[...].astype(F32))
    h_out[...] = h.astype(BF)
    y, _ = normalize(z, h)
    spread(z, y * sigmoid(y), line, pad)
    send_partials(z, row, convolve(z, pad, kernel, 0), own, sends)


def back_through_second(z, i, g, kernel, q_out, q_send, act_out, pad, line):
    y, factor = normalize(z, i.astype(F32))
    logistic = sigmoid(y)
    act_out[...] = (y * logistic).astype(BF)
    spread(z, g, line, pad)
    q = norm_back(z, y, factor, logistic, convolve_back(z, pad, kernel, 1)).astype(BF)
    q_out[...] = q
    fold(z, q_send, q.astype(F32))


def first_backward(z, *refs):
    n = z.parts
    pieces, heads, kernel = refs[:n], refs[n : 2 * n], refs[2 * n]
    q_out, q_send, pad, act_out = refs[2 * n + 1 : 2 * n + 5]
    sends, (i_ref, g_ref, line) = refs[2 * n + 5 : 3 * n + 4], refs[3 * n + 4 :]
    _, row = where_am_i()
    assemble(z, i_ref, pieces, row, 0, z.share)
    assemble(z, g_ref, pieces, row, 2 * z.share, z.channels)
    back_through_second(
        z, i_ref[...], g_ref[...].astype(F32), kernel, q_out, q_send, act_out, pad, line
    )
    rows = z.cells // FOLD
    for d, send in enumerate(sends, 1):
        send[:rows, :] = q_send[...]
        send[rows:, :] = heads[d][...]


def later_backward(z, fs, bs, *refs):
    n = z.parts
    arrivals, mirror, received = refs[:n], refs[n], refs[n + 1 : 2 * n]
    heads, sums = refs[2 * n], refs[2 * n + 1 : 3 * n]
    nexts, others = refs[3 * n], refs[3 * n + 1 : 4 * n]
    i_before, arrived, output, kernel = refs[4 * n : 4 * n + 4]
    q_out, pad, act_out, grad_in, skip_in = refs[4 * n + 4 : 4 * n + 9]
    rows_own, sends = refs[4 * n + 9], refs[4 * n + 10 : 5 * n + 9]
    q_send, i_ref, full, line = refs[5 * n + 9 :]
    s, row = where_am_i()
    w = z.share
    shares = [unfold(z, part) for part in arrivals]
    grad = side_by_side(all_shares(z, shares[0], shares[1:], row))
    grad_in[...] = grad.astype(BF)
    shares = [unfolded(x[: z.cells // FOLD, :], FOLD) for x in received]
    skip = side_by_side(all_shares(z, unfold(z, mirror), shares, row))
    skip_in[...] = skip.astype(BF)
    grad_taken, skip_taken = taken_back(z, bs, s)
    for j in range(n):
        assemble(z, full.at[j], enclosed(z, nexts, others, 1 + j), row, 0, w)
    g = side_by_side([full[j] for j in range(n)]) + jnp.where(grad_taken, grad, 0.0)
    g = g + jnp.where(skip_taken, skip, 0.0)
    g = g.astype(BF).astype(F32)
    assemble(z, i_ref, enclosed(z, heads, sums, 2), row, 0, w)
    i = jnp.where(fs[0, s] == bs[1, s], i_before[...].astype(F32), i_ref[...].astype(F32))
    back_through_second(z, i, g, kernel, q_out, q_send, act_out, pad, line)
    rows = z.local // FOLD
    for d, out in enumerate([rows_own, *sends]):
        at = part_rows(z, target(z, row, d))
        base = out.shape[0] - (2 + n) * rows
        whole = output[at, :].astype(F32)
        values = [i_before[at, :], arrived[at, :]]
        values += [whole[:, j * w : (j + 1) * w] for j in range(n)]
        for j, value in enumerate(values):
            at = slice(base + j * rows, base + (j + 1) * rows)
            out[at, :] = folded(value.astype(F32), FOLD).astype(BF)
    for send in sends:
        send[: q_send.shape[0], :] = q_send[...]


def second_convolution(z, encoder, row, own, received, skip, h, kernel, i_out, full, line, pad):
    c0 = own[...]
    for other in received:
        c0 = c0 + unfolded(other[: z.cells // FOLD, :], FOLD)
    i = jnp.where(encoder, c0, skip.astype(F32)).astype(BF)
    i_out[...] = i
    y, _ = normalize(z, i.astype(F32))
    spread(z, y * sigmoid(y), line, pad)
    total = convolve(z, pad, kernel, 1)
    base = h[...].astype(F32) + jnp.where(encoder, 0.0, c0)
    full[...] = total + side_by_side([jnp.where(row == j, base, 0.0) for j in range(z.parts)])


def middle(z, pad):
    return pad[1, z.cols : z.cols + z.cells, :].astype(F32)


def second_forward(z, *refs):
    n = z.parts
    own, received, h, pieces, kernel = refs[0], refs[1:n], refs[n], refs[n + 1 : 2 * n + 1], refs[2 * n + 1]
    i_out, full_out = refs[2 * n + 2 : 2 * n + 4]
    sends = refs[2 * n + 4 : 3 * n + 4]
    skip, full, line, pad = refs[3 * n + 4 :]
    s, row = where_am_i()
    encoder = s < z.sections // 2
    assemble(z, skip, pieces, row, z.share, z.share)
    second_convolution(
        z, encoder, row, own, received, skip[...], h, kernel, i_out, full, line, pad
    )
    full_out[...] = full[...].astype(BF)
    for d in range(n):
        fold(z, sends[d], share_of(z, full[...], target(z, row, d)))


def last_forward(z, fs, *refs):
    n = z.parts
    own, received, h = refs[0], refs[1:n], refs[n]
    heads, others = refs[n + 1], refs[n + 2 : 2 * n + 1]
    arrived, kernel = refs[2 * n + 1 : 2 * n + 3]
    sends = refs[2 * n + 3 : 3 * n + 3]
    i_out, skip, full, line, pad = refs[3 * n + 3 :]
    skip_in = unfold(z, arrived)
    s, row = where_am_i()
    encoder = s < z.sections // 2
    partner = z.sections - 1 - s
    assemble(z, skip, enclosed(z, heads, others, 3), row, 0, z.share)
    now = jnp.where(
        fs[0, partner] == fs[1, s], skip_in, skip[...].astype(F32)
    )
    second_convolution(z, encoder, row, own, received, now, h, kernel, i_out, full, line, pad)
    skip[...] = skip_in.astype(BF)
    for d, send in enumerate(sends):
        at = part_rows(z, target(z, row, d))
        send[...] = side_by_side([full[at, :], i_out[at, :], skip[at, :]]).astype(BF)


def joined_shares(z, own, received, row):
    others = [unfolded(other[: z.cells // FOLD, :], FOLD) for other in received]
    return side_by_side(all_shares(z, own[...].astype(F32), others, row))


def back_through_first(z, encoder, row, q, received, g_pad, h, kernel, act_out, pad, line):
    g = middle(z, g_pad)
    whole = joined_shares(z, q, received, row)
    now = jnp.where(encoder, whole, g)
    y, factor = normalize(z, h.astype(F32))
    logistic = sigmoid(y)
    act_out[...] = (y * logistic).astype(BF)
    spread(z, now, line, pad)
    back = norm_back(z, y, factor, logistic, convolve_back(z, pad, kernel, 0))
    return share_of(z, g, row) + back, whole


def second_backward(z, *refs):
    n = z.parts
    q, received, g = refs[0], refs[1:n], refs[n]
    heads, others, kernel = refs[n + 1], refs[n + 2 : 2 * n + 1], refs[2 * n + 1]
    send, pad, act_out, h, line = refs[2 * n + 2 :]
    s, row = where_am_i()
    assemble(z, h, enclosed(z, heads, others, 0), row, 0, z.share)
    value, _ = back_through_first(
        z, s < z.sections // 2, row, q, received, g, h[...], kernel, act_out, pad, line
    )
    fold(z, send, value)


def last_backward(z, fs, bs, *refs):
    n = z.parts
    q, received, g = refs[0], refs[1:n], refs[n]
    heads, others = refs[n + 1], refs[n + 2 : 2 * n + 1]
    h_before, kernel = refs[2 * n + 1 : 2 * n + 3]
    sends = refs[2 * n + 3 : 3 * n + 3]
    pad, act_out, h, value, line = refs[3 * n + 3 :]
    s, row = where_am_i()
    assemble(z, h, enclosed(z, heads, others, 1), row, 0, z.share)
    now = jnp.where(fs[0, s] == bs[1, s], h_before[...], h[...])
    result, _ = back_through_first(
        z, s < z.sections // 2, row, q, received, g, now, kernel, act_out, pad, line
    )
    value[...] = result.astype(BF)
    for d, send in enumerate(sends):
        fold(z, send, value[part_rows(z, target(z, row, d)), :])


def add_rows(z, *refs):
    n = z.parts
    pieces, q, received = refs[:n], refs[n], refs[n + 1 : 2 * n]
    out, mirror, i_rows, skip_rows, whole = refs[2 * n :]
    s, row = where_am_i()
    c = z.channels
    whole[...] = joined_shares(z, q, received, row)
    values = [piece[...].astype(F32) for piece in pieces]
    total = sum(value[:, :c] for value in values)
    out[...] = total.astype(BF)
    mine = whole[part_rows(z, row), :]
    mirror[...] = jnp.where(s < z.sections // 2, total, mine).astype(BF)
    for ref, at in ((i_rows, c), (skip_rows, c + z.share)):
        shares = [value[:, at : at + z.share] for value in values]
        ref[...] = side_by_side(all_shares(z, shares[0], shares[1:], row)).astype(BF)


def write_queues(z, fs, bs, *refs):
    n = z.parts
    fwd, bwd, mir, stash, grad_in, skip_in = refs[:6]
    pieces = refs[6 : n + 6]
    token, out0, outs, held = refs[n + 6], refs[n + 7], refs[n + 8 : n + 12], refs[n + 12 : n + 16]
    sems = refs[n + 16]
    token[...] = jnp.zeros_like(token)
    s, row = where_am_i()
    prior, later = jnp.maximum(s - 1, 0), jnp.minimum(s + 1, z.sections - 1)
    partner = z.sections - 1 - s
    f0, f1 = fs[0, s], fs[1, s]
    mine = part_rows(z, row)
    copies = [pltpu.make_async_copy(a, b, sems.at[j]) for j, (a, b) in enumerate(zip(held, outs))]
    for ref, queue in zip(held, (fwd, bwd, mir, stash)):
        ref[...] = queue[...]

    @pl.when(s < z.sections - 1)
    def _():
        held[1][bs[0, later]] = grad_in[mine, :]

    copies[1].start()

    @pl.when(s < z.sections // 2)
    def _():
        held[2][bs[0, partner]] = skip_in[mine, :]

    copies[2].start()
    rows = z.local // FOLD

    def value(piece, j):
        at = piece.shape[0] - (2 + n) * rows + j * rows
        return unfolded(piece[at : at + rows, :], FOLD)

    def joined(j):
        shares = [value(piece, j) for piece in pieces]
        return side_by_side(all_shares(z, shares[0], shares[1:], row)).astype(BF)

    out0[...] = side_by_side(
        [sum(value(piece, 2 + j) for piece in pieces) for j in range(n)]
    ).astype(BF)
    fwd_in = joined(1)

    @pl.when(s > 0)
    def _():
        held[0][fs[0, prior]] = fwd_in

    copies[0].start()
    held[3][2 * f0] = fwd[f0]
    held[3][2 * f0 + 1] = joined(0)
    held[3][2 * f1] = fwd[f1]

    @pl.when(jnp.logical_and(s > 0, fs[0, prior] == f1))
    def _():
        held[3][2 * f1] = fwd_in

    copies[3].start()
    for copy in copies:
        copy.wait()


def finish(z, fs, bs, *refs):
    n = z.parts
    out0, out1, i1, skip, fwd1, mir1 = refs[4:10]
    grads1 = refs[10 : n + 10]
    fwd_out, bwd_out, mir_out, stash_out, emitted = refs[n + 10 : n + 15]
    grads, sems = refs[n + 15 :]
    s, row = where_am_i()
    prior, later = jnp.maximum(s - 1, 0), jnp.minimum(s + 1, z.sections - 1)
    partner = z.sections - 1 - s
    encoder, has_prior, has_later = s < z.sections // 2, s > 0, s < z.sections - 1
    first = jnp.where(encoder, bs[0, partner], fs[0, partner])
    second = jnp.where(encoder, bs[1, partner], fs[1, partner])
    skip_stays = jnp.logical_and(jnp.logical_not(encoder), first != second)

    def put(source, place, j):
        return pltpu.make_async_copy(source, place, sems.at[j])

    always = [
        put(out1, emitted.at[1], 0),
        put(i1, stash_out.at[2 * fs[1, s] + 1], 1),
        put(mir1, mir_out.at[second], 2),
        put(out0, emitted.at[0], 3),
    ]
    for copy in always:
        copy.start()
    onward, back = put(fwd1, fwd_out.at[fs[1, prior]], 4), put(grads, bwd_out.at[bs[1, later]], 5)
    aside = put(skip, mir_out.at[first], 6)
    pl.when(has_prior)(onward.start)
    pl.when(skip_stays)(aside.start)
    pieces = [unfold(z, piece) for piece in grads1]
    grads[...] = side_by_side(all_shares(z, pieces[0], pieces[1:], row)).astype(BF)
    pl.when(has_later)(back.start)
    for copy in always:
        copy.wait()
    pl.when(has_prior)(onward.wait)
    pl.when(has_later)(back.wait)
    pl.when(skip_stays)(aside.wait)


def add_taps(z, act, pad, before, store):
    turned = jnp.transpose(act[...].astype(F32)).astype(BF)
    for tap in range(9):
        a, b = divmod(tap, 3)
        at = (2 - a) * z.cols
        moved = pad[2 - b, at : at + z.cells, :]
        store(tap, before(tap) + jnp.dot(turned, moved, preferred_element_type=F32))


def kernel_grads_add(z, start, acc, act, pad, out):
    def store(tap, value):
        out[tap] = value

    add_taps(z, act, pad, lambda tap: acc[start + tap], store)


def kernel_grads_last(z, total, other, act, pad, token, out, held, sems):
    token[...] = jnp.zeros_like(token)
    copies = [pltpu.make_async_copy(other, out.at[9:], sems.at[9])]
    copies[0].start()

    def store(tap, value):
        held[tap] = value
        copies.append(pltpu.make_async_copy(held.at[tap], out.at[tap], sems.at[tap]))
        copies[-1].start()

    add_taps(z, act, pad, lambda tap: total[tap], store)
    for copy in copies:
        copy.wait()


def per_device(fwd_queue, bwd_queue, mirror_queue, stash, weights, grad_acc, fwd_slot, bwd_slot):
    sections, n = lax.axis_size("section"), lax.axis_size("row")
    z = Sizes(fwd_queue[0], sections, n)
    slots = fwd_queue.shape[1]
    c, w, local, cells = z.channels, z.share, z.local, z.cells
    fwd, bwd, mir = (x.reshape(slots, local, c) for x in (fwd_queue, bwd_queue, mirror_queue))
    kept = stash.reshape(2 * slots, local, c)
    kernels = weights.reshape(18, w, c)
    acc = grad_acc.reshape(18, w, c)
    fs, bs = fwd_slot.T, bwd_slot.T
    fold_shape, wide = (cells // FOLD, FOLD * w), (cells, c)
    half = (cells, w)

    def with_shares(k):
        return ((cells + k * local) // FOLD, FOLD * w)

    padded = (3, cells + 2 * z.cols, c)

    def move(x, d, step):
        route = [
            (s * n + r, step(s) * n + (r + d) % n) for s in range(sections) for r in range(n)
        ]
        return lax.ppermute(x, ("section", "row"), route)

    across = functools.partial(move, step=lambda s: s)
    onward = functools.partial(move, step=lambda s: (s + 1) % sections)
    backward = functools.partial(move, step=lambda s: (s - 1) % sections)
    crossed = functools.partial(move, step=lambda s: (sections - s) % sections)
    mirrored = functools.partial(move, step=lambda s: sections - 1 - s)

    def run(body, scalars, arrays, outs, scratch=(), **options):
        return call(
            functools.partial(body, z), body.__name__, scalars, arrays, outs, scratch, **options
        )

    def exchange(pieces):
        return [pieces[0]] + [across(piece, d) for d, piece in enumerate(pieces[1:], 1)]

    narrow_pad = pad_shapes(z, w)
    wide_line = pltpu.VMEM((cells + 16, c), F32)
    queues = (fwd, bwd, mir, kept)
    rows = (local, c)
    sems = pltpu.SemaphoreType.DMA
    packed = run(
        pack_first,
        (),
        (fs, bs, *queues),
        [((local // FOLD, FOLD * w), BF)] * n
        + [(x.shape, BF) for x in queues],
        [pltpu.SMEM(fs.shape, jnp.int32)] * 2 + [sems((6,))],
        remote=6,
    )
    inputs, held = exchange(packed[:n]), packed[n:]

    packed = run(
        pack_later,
        (),
        (fs, bs, *held),
        [((local, 2 * w + c), BF)] * n
        + [((k * (local // FOLD), FOLD * w), BF) for k in (4, 1 + n) for _ in range(n)],
        [pltpu.SMEM(fs.shape, jnp.int32)] * 2 + [sems((2,))],
        remote=2,
        after=(inputs[0],),
    )
    pieces, heads, nexts = (packed[j * n : (j + 1) * n] for j in range(3))
    first = exchange(held_until(pieces, inputs))

    own, h0, *sends = run(
        first_forward,
        (),
        (*inputs, *heads, kernels),
        [(half, F32), (half, BF)] + [(with_shares(4), BF)] * (n - 1),
        narrow_pad,
    )
    sums = [across(x, d) for d, x in enumerate(sends, 1)]
    q0, q_send, g_pad0, act_i0, *sends = run(
        first_backward,
        (),
        (*first, *nexts, kernels),
        [(half, BF), (fold_shape, BF), (padded, BF), (half, BF)]
        + [(with_shares(1 + n), BF)] * (n - 1),
        [pltpu.VMEM(half, BF), pltpu.VMEM(wide, BF), wide_line],
        after=(own,),
    )
    q_received = [across(x, d) for d, x in enumerate(sends, 1)]
    skip_in = mirrored(q_send, 0)

    def add_grads(start, total, act, pad, after):
        [out] = call(
            functools.partial(kernel_grads_add, z, start),
            f"kernel_grads_add_{start}",
            (),
            (total, act, pad),
            [((9, w, c), F32)],
            after=after,
        )
        return out

    sum_i = add_grads(9, acc, act_i0, g_pad0, (q0,))
    i0, full0, *sends = run(
        second_forward,
        (),
        (own, *sums, h0, *first, kernels),
        [(half, BF), (wide, BF)] + [(fold_shape, BF)] * n,
        [pltpu.VMEM(half, BF), pltpu.VMEM(wide, F32)] + narrow_pad,
        after=(sum_i,),
    )
    fwd_in = [onward(x, d) for d, x in enumerate(sends)]
    dh_send, f_pad0, act_h0 = run(
        second_backward,
        (),
        (*held_until([q0], skip_in), *q_received, g_pad0, heads[0], *sums, kernels),
        [(fold_shape, BF), (padded, BF), (half, BF)],
        [pltpu.VMEM(half, BF), wide_line],
        after=(i0,),
    )
    dh_in = [backward(dh_send, d) for d in range(n)]
    relayed = [across(skip_in, d) for d in range(1, n)]

    own, h1, arrived, turned, *sends = run(
        later_forward,
        (fs,),
        (*fwd_in, nexts[0], *q_received, kernels),
        [(half, F32), (half, BF), (half, BF), (fold_shape, BF)]
        + [(fold_shape, BF)] * (n - 1),
        narrow_pad,
        after=(dh_send,),
    )
    received = [across(x, d) for d, x in enumerate(sends, 1)]
    mir_in = crossed(turned, 0)
    sum_h = add_grads(0, acc, act_h0, f_pad0, (own,))
    q1, g_pad1, act_i1, grad_in, skip_full, rows_own, *sends = run(
        later_backward,
        (fs, bs),
        (*dh_in, skip_in, *relayed, heads[0], *sums, nexts[0], *q_received, i0, arrived, full0, kernels),
        [(half, BF), (padded, BF), (half, BF), (wide, BF), (wide, BF), (((2 + n) * (local // FOLD), FOLD * w), BF)]
        + [(with_shares(2 + n), BF)] * (n - 1),
        [pltpu.VMEM(fold_shape, BF), pltpu.VMEM(half, BF), pltpu.VMEM((n, *half), BF), wide_line],
        after=(sum_h,),
    )
    q_received = [across(x, d) for d, x in enumerate(sends, 1)]
    sends = run(
        last_forward,
        (fs,),
        (own, *received, h1, heads[0], *sums, mir_in, kernels),
        [((local, c + 2 * w), BF)] * n,
        [pltpu.VMEM(half, BF), pltpu.VMEM(half, BF), pltpu.VMEM(wide, F32)] + narrow_pad,
        after=(q1,),
    )
    rows1 = exchange(sends)
    part_i = add_grads(0, sum_i, act_i1, g_pad1, (sends[0],))
    token, out0, *written = run(
        write_queues,
        (fs, bs),
        (*held, grad_in, skip_full, rows_own, *q_received),
        [((8, 128), F32), (rows, BF)] + [(x.shape, BF) for x in queues],
        [pltpu.VMEM(x.shape, BF) for x in queues] + [sems((4,))],
        far_outs=4,
        after=(part_i,),
    )
    out1, mirror1, i1, skip1 = run(
        add_rows,
        (),
        (*rows1, q1, *q_received),
        [(rows, BF)] * 4,
        [pltpu.VMEM(wide, F32)],
        after=(token,),
    )
    fwd1, mir1 = onward(out1, 0), mirrored(mirror1, 0)
    *dh_sends, f_pad1, act_h1 = run(
        last_backward,
        (fs, bs),
        (q1, *q_received, g_pad1, heads[0], *sums, h0, kernels),
        [((local // FOLD, FOLD * w), BF)] * n + [(padded, BF), (half, BF)],
        [pltpu.VMEM(half, BF), pltpu.VMEM(half, BF), wide_line],
        after=(out1,),
    )
    dh1_in = [backward(x, d) for d, x in enumerate(dh_sends)]
    token, grad_total = run(
        kernel_grads_last,
        (),
        (sum_h, part_i, act_h1, f_pad1),
        [((8, 128), F32), ((18, w, c), F32)],
        [pltpu.VMEM((9, w, c), F32), sems((10,))],
        far_outs=1,
    )
    fwd_out, bwd_out, mir_out, stash_out, emitted = run(
        finish,
        (fs, bs),
        (*written, out0, out1, i1, skip1, fwd1, mir1, *dh1_in),
        [(x.shape, BF) for x in queues] + [((TICKS, local, c), BF)],
        [pltpu.VMEM(rows, BF), sems((7,))],
        remote=4,
        far_outs=5,
        aliases={j + 2: j for j in range(4)},
        after=(token,),
    )
    return (
        fwd_out.reshape(fwd_queue.shape),
        bwd_out.reshape(bwd_queue.shape),
        mir_out.reshape(mirror_queue.shape),
        stash_out.reshape(stash.shape),
        grad_total.reshape(grad_acc.shape),
        emitted.reshape((1, TICKS) + fwd_queue.shape[2:]),
    )


def solution(mesh):
    return jax.shard_map(
        per_device,
        mesh=mesh,
        in_specs=(
            P("section", None, "row", None, None),
            P("section", None, "row", None, None),
            P("section", None, "row", None, None),
            P("section", None, None, "row", None, None),
            P("section", None, None, None, "row", None),
            P("section", None, None, None, "row", None),
            P(),
            P(),
        ),
        out_specs=(
            P("section", None, "row", None, None),
            P("section", None, "row", None, None),
            P("section", None, "row", None, None),
            P("section", None, None, "row", None, None),
            P("section", None, None, None, "row", None),
            P("section", None, "row", None, None),
        ),
        check_vma=False,
    )
```

```python
import functools

import jax
import jax.numpy as jnp
from jax import lax
from jax.experimental import pallas as pl
from jax.experimental.pallas import tpu as pltpu
from jax.sharding import PartitionSpec as P

GROUPS = 32
TICKS = 2
FOLD = 4
EPSILON = 1e-05
BF, F32 = jnp.bfloat16, jnp.float32
VMEM_LIMIT = 24 * 2**20


class Sizes:
    def __init__(self, queue, sections, rows):
        self.sections, self.parts = sections, rows
        self.cols = queue.shape[2]
        self.channels = queue.shape[3]
        self.local = queue.shape[1] * queue.shape[2]
        self.cells = self.local * rows
        self.share = self.channels // rows
        self.group = self.channels // GROUPS
        self.count = self.cells * self.group


def where_am_i():
    return lax.axis_index("section"), lax.axis_index("row")


def share_of(z, value, part):
    value = value.astype(F32)
    out = value[:, : z.share]
    for j in range(1, z.parts):
        out = jnp.where(part == j, value[:, j * z.share : (j + 1) * z.share], out)
    return out


def all_shares(z, own, others, row):
    out = []
    for j in range(z.parts):
        value = own
        for d in range(1, z.parts):
            value = jnp.where(lax.rem(row + z.parts - d, z.parts) == j, others[d - 1], value)
        out.append(value)
    return out


def side_by_side(values):
    return jnp.concatenate([value.astype(F32) for value in values], axis=1)


def folded(value, blocks):
    rows = value.shape[0] // blocks
    return side_by_side([value[j * rows : (j + 1) * rows] for j in range(blocks)])


def unfolded(value, blocks):
    value, width = value.astype(F32), value.shape[1] // blocks
    return jnp.concatenate([value[:, j * width : (j + 1) * width] for j in range(blocks)], axis=0)


def fold(z, ref, value):
    ref[...] = folded(value, FOLD).astype(BF)


def unfold(z, ref):
    return unfolded(ref[...], FOLD)


def source(z, row, d):
    return lax.rem(row + z.parts - d, z.parts)


def target(z, row, d):
    return lax.rem(row + d, z.parts)


def part_rows(z, part):
    return pl.ds(pl.multiple_of(part * z.local, z.local), z.local)


def assemble(z, ref, pieces, row, start, width):
    for d, piece in enumerate(pieces):
        value = (piece if isinstance(piece, jax.Array) else piece[...]).astype(F32)
        value = value[:, start : start + width]
        ref[part_rows(z, source(z, row, d)), :] = value.astype(BF)


def group_sums(z, first, second):
    width = first.shape[1]
    line = lax.broadcasted_iota(jnp.int32, (8, width), 0)
    both = jnp.where(line == 0, first, jnp.where(line == 1, second, 0.0))
    across = lax.broadcasted_iota(jnp.int32, (width, width), 1).astype(F32)
    down = lax.broadcasted_iota(jnp.int32, (width, width), 0).astype(F32)
    same = jnp.floor((across + 0.5) * (1.0 / z.group)) == jnp.floor((down + 0.5) * (1.0 / z.group))
    sums = jnp.dot(
        both, same.astype(F32), precision=lax.Precision.HIGHEST, preferred_element_type=F32
    )
    return sums[0:1], sums[1:2]


def normalize(z, x):
    total, square = group_sums(
        z, jnp.sum(x, axis=0, keepdims=True), jnp.sum(x * x, axis=0, keepdims=True)
    )
    center = total / z.count
    factor = lax.rsqrt(square / z.count - center * center + EPSILON)
    return (x - center) * factor, factor


def sigmoid(y):
    return 1.0 / (1.0 + jnp.exp(-y))


def norm_back(z, y, factor, logistic, upstream):
    e = upstream * logistic * (1.0 + y * (1.0 - logistic))
    first, second = group_sums(
        z, jnp.sum(e, axis=0, keepdims=True), jnp.sum(e * y, axis=0, keepdims=True)
    )
    return factor * (e - first / z.count - y * (second / z.count))


def spread(z, x, line_ref, pad_ref):
    cells, cols = z.cells, z.cols
    width = x.shape[1]
    line_ref[8 : 8 + cells, :] = x
    column = lax.rem(lax.broadcasted_iota(jnp.int32, (cells, 1), 0), cols)
    edge = jnp.zeros((cols, width), BF)
    for b in range(3):
        pad_ref[b, :cols, :] = edge
        pad_ref[b, cols + cells :, :] = edge
    pad_ref[1, cols : cols + cells, :] = x.astype(BF)
    left = jnp.where(column > 0, line_ref[7 : 7 + cells, :], 0.0)
    pad_ref[0, cols : cols + cells, :] = left.astype(BF)
    right = jnp.where(column < cols - 1, line_ref[9 : 9 + cells, :], 0.0)
    pad_ref[2, cols : cols + cells, :] = right.astype(BF)


def convolve(z, pad_ref, kernel_ref, which):
    total = None
    for a in range(3):
        for b in range(3):
            term = jnp.dot(
                pad_ref[b, a * z.cols : a * z.cols + z.cells, :],
                kernel_ref[9 * which + 3 * a + b],
                preferred_element_type=F32,
            )
            total = term if total is None else total + term
    return total


def convolve_back(z, pad_ref, kernel_ref, which):
    total = None
    for a in range(3):
        for b in range(3):
            term = lax.dot_general(
                pad_ref[b, a * z.cols : a * z.cols + z.cells, :],
                kernel_ref[9 * which + 3 * (2 - a) + 2 - b],
                (((1,), (1,)), ((), ())),
                preferred_element_type=F32,
            )
            total = term if total is None else total + term
    return total


def pad_shapes(z, width):
    return [
        pltpu.VMEM((z.cells + 16, width), F32),
        pltpu.VMEM((3, z.cells + 2 * z.cols, width), BF),
    ]


def call(body, name, scalars, arrays, outs, scratch=(), after=(), remote=0, far_outs=0, aliases=None):
    near, far = pl.BlockSpec(memory_space=pltpu.VMEM), pl.BlockSpec(memory_space=pltpu.HBM)

    def inner(*refs):
        given = len(scalars) + len(arrays)
        body(*refs[:given], *refs[given + len(after) :])

    arrays = [
        pltpu.with_memory_space_constraint(x, pltpu.HBM) if j < remote else x
        for j, x in enumerate(arrays)
    ]
    near_outs = len(outs) - far_outs
    return pl.pallas_call(
        inner,
        name=name,
        out_shape=[
            jax.ShapeDtypeStruct(shape, dtype) if j < near_outs else pltpu.HBM(shape, dtype)
            for j, (shape, dtype) in enumerate(outs)
        ],
        in_specs=[pl.BlockSpec(memory_space=pltpu.SMEM)] * len(scalars)
        + [far] * remote
        + [near] * (len(arrays) - remote)
        + [pl.BlockSpec(memory_space=pl.ANY)] * len(after),
        out_specs=[near] * near_outs + [far] * far_outs,
        scratch_shapes=list(scratch),
        input_output_aliases=aliases or {},
        compiler_params=pltpu.CompilerParams(vmem_limit_bytes=VMEM_LIMIT),
        cost_estimate=pl.CostEstimate(flops=1, bytes_accessed=1, transcendentals=0),
    )(*scalars, *arrays, *after)


def held_until(values, earlier):
    return lax.optimization_barrier((tuple(values), earlier))[0]


def fetch(pairs, sems):
    copies = [pltpu.make_async_copy(a, b, sems.at[j]) for j, (a, b) in enumerate(pairs)]
    for copy in copies:
        copy.start()
    for copy in copies:
        copy.wait()


def pack_first(z, fs_far, bs_far, fwd_far, bwd_far, mir_far, stash_far, *refs):
    n = z.parts
    heads = refs[:n]
    fwd, bwd, mir, stash, fs, bs, sems = refs[n:]
    fetch(
        [
            (fs_far, fs),
            (bs_far, bs),
            (fwd_far, fwd),
            (bwd_far, bwd),
            (mir_far, mir),
            (stash_far, stash),
        ],
        sems,
    )
    s, row = where_am_i()
    h = fwd[fs[0, s]]
    for d in range(n):
        fold(z, heads[d], share_of(z, h, target(z, row, d)))


def taken_back(z, bs, s):
    later, partner = jnp.minimum(s + 1, z.sections - 1), z.sections - 1 - s
    return (
        jnp.logical_and(s < z.sections - 1, bs[0, later] == bs[1, s]),
        jnp.logical_and(s < z.sections // 2, bs[0, partner] == bs[1, s]),
    )


def pack_later(z, fs_far, bs_far, fwd, bwd, mir, stash, *refs):
    n = z.parts
    pieces, groups = refs[:n], [refs[j * n : (j + 1) * n] for j in range(1, 5)]
    fs, bs, sems = refs[5 * n :]
    fetch([(fs_far, fs), (bs_far, bs)], sems)
    s, row = where_am_i()
    f1, b1 = fs[1, s], bs[1, s]
    grad_taken, skip_taken = taken_back(z, bs, s)
    skip_kept = jnp.logical_and(s < z.sections // 2, jnp.logical_not(skip_taken))
    kept = jnp.where(grad_taken, 0.0, bwd[b1].astype(F32))
    kept = kept + jnp.where(skip_kept, mir[b1].astype(F32), 0.0)
    f0, b0 = fs[0, s], bs[0, s]
    g = bwd[b0].astype(F32) + jnp.where(s < z.sections // 2, mir[b0].astype(F32), 0.0)
    for d, piece in enumerate(pieces):
        part = target(z, row, d)
        shares = [share_of(z, stash[2 * b0 + 1], part), share_of(z, mir[f0], part)]
        piece[...] = side_by_side(shares + [g]).astype(BF)
    values = [stash[2 * b0], stash[2 * b1], fwd[f1], stash[2 * b1 + 1], mir[f1]]
    rows = z.local // FOLD
    for d in range(n):
        shares = [share_of(z, value, target(z, row, d)) for value in values]
        grads = [kept[:, j * z.share : (j + 1) * z.share] for j in range(n)]
        for outs, parts in zip(groups, (shares[:2], shares[2:4], grads, shares[4:])):
            for j, value in enumerate(parts):
                outs[d][j * rows : (j + 1) * rows, :] = folded(value, FOLD).astype(BF)


def send_partials(z, row, total, own, sends, extra):
    own[...] = share_of(z, total, row)
    for d, send in enumerate(sends, 1):
        part = folded(share_of(z, total, target(z, row, d)), FOLD).astype(BF)
        send[: part.shape[0], :] = part
        send[part.shape[0] :, :] = extra[d][...]


def first_forward(z, *refs):
    n = z.parts
    pieces, extra, kernel = refs[:n], refs[n : 2 * n], refs[2 * n]
    own, h_out = refs[2 * n + 1 : 2 * n + 3]
    sends, (line, pad) = refs[2 * n + 3 : 3 * n + 2], refs[3 * n + 2 :]
    _, row = where_am_i()
    assemble(z, h_out, [unfold(z, piece) for piece in pieces], row, 0, z.share)
    y, _ = normalize(z, h_out[...].astype(F32))
    spread(z, y * sigmoid(y), line, pad)
    send_partials(z, row, convolve(z, pad, kernel, 0), own, sends, extra)


def enclosed(z, own, received, j):
    rows, base = z.local // FOLD, z.cells // FOLD
    at, there = slice(j * rows, (j + 1) * rows), slice(base + j * rows, base + (j + 1) * rows)
    return [unfolded(own[at, :], FOLD)] + [unfolded(x[there, :], FOLD) for x in received]


def later_forward(z, fs, *refs):
    n = z.parts
    arrivals, nexts, received = refs[:n], refs[n], refs[n + 1 : 2 * n]
    lasts, kernel = refs[2 * n : 3 * n], refs[3 * n]
    own, h_out, arrived, onward = refs[3 * n + 1 : 3 * n + 5]
    sends = refs[3 * n + 5 : 4 * n + 4]
    line, pad = refs[4 * n + 4 :]
    s, row = where_am_i()
    total = unfold(z, arrivals[0])
    for other in arrivals[1:]:
        total = total + unfold(z, other)
    total = total.astype(BF).astype(F32)
    arrived[...] = total.astype(BF)
    fold(z, onward, total)
    assemble(z, h_out, enclosed(z, nexts, received, 0), row, 0, z.share)
    prior = jnp.maximum(s - 1, 0)
    taken = jnp.logical_and(s > 0, fs[0, prior] == fs[1, s])
    h = jnp.where(taken, total, h_out[...].astype(F32))
    h_out[...] = h.astype(BF)
    y, _ = normalize(z, h)
    spread(z, y * sigmoid(y), line, pad)
    send_partials(z, row, convolve(z, pad, kernel, 0), own, sends, lasts)


def back_through_second(z, i, g, kernel, q_out, q_send, act_out, pad, line):
    y, factor = normalize(z, i.astype(F32))
    logistic = sigmoid(y)
    act_out[...] = (y * logistic).astype(BF)
    spread(z, g, line, pad)
    q = norm_back(z, y, factor, logistic, convolve_back(z, pad, kernel, 1)).astype(BF)
    q_out[...] = q
    fold(z, q_send, q.astype(F32))


def first_backward(z, *refs):
    n = z.parts
    pieces, heads, kernel = refs[:n], refs[n : 2 * n], refs[2 * n]
    q_out, q_send, pad, act_out = refs[2 * n + 1 : 2 * n + 5]
    sends, (i_ref, g_ref, line) = refs[2 * n + 5 : 3 * n + 4], refs[3 * n + 4 :]
    _, row = where_am_i()
    assemble(z, i_ref, pieces, row, 0, z.share)
    assemble(z, g_ref, pieces, row, 2 * z.share, z.channels)
    back_through_second(
        z, i_ref[...], g_ref[...].astype(F32), kernel, q_out, q_send, act_out, pad, line
    )
    rows = z.cells // FOLD
    for d, send in enumerate(sends, 1):
        send[:rows, :] = q_send[...]
        send[rows:, :] = heads[d][...]


def later_backward(z, fs, bs, *refs):
    n = z.parts
    arrivals, mirror, received, kept = refs[:n], refs[n], refs[n + 1 : 2 * n], refs[2 * n]
    nexts, others = refs[2 * n + 1], refs[2 * n + 2 : 3 * n + 1]
    i_before, arrived, kernel = refs[3 * n + 1 : 3 * n + 4]
    q_out, pad, act_out, grad_in, skip_in = refs[3 * n + 4 : 3 * n + 9]
    rows_own, sends = refs[3 * n + 9], refs[3 * n + 10 : 4 * n + 9]
    q_send, i_ref, full, line = refs[4 * n + 9 :]
    s, row = where_am_i()
    w = z.share
    shares = [unfold(z, part) for part in arrivals]
    grad = side_by_side(all_shares(z, shares[0], shares[1:], row))
    grad_in[...] = grad.astype(BF)
    shares = [unfolded(x[: z.cells // FOLD, :], FOLD) for x in received]
    skip = side_by_side(all_shares(z, unfold(z, mirror), shares, row))
    skip_in[...] = skip.astype(BF)
    grad_taken, skip_taken = taken_back(z, bs, s)
    for j in range(n):
        assemble(z, full.at[j], enclosed(z, kept, received, j), row, 0, w)
    g = side_by_side([full[j] for j in range(n)]) + jnp.where(grad_taken, grad, 0.0)
    g = g + jnp.where(skip_taken, skip, 0.0)
    g = g.astype(BF).astype(F32)
    assemble(z, i_ref, enclosed(z, nexts, others, 1), row, 0, w)
    i = jnp.where(fs[0, s] == bs[1, s], i_before[...].astype(F32), i_ref[...].astype(F32))
    back_through_second(z, i, g, kernel, q_out, q_send, act_out, pad, line)
    for d, out in enumerate([rows_own, *sends]):
        at = part_rows(z, target(z, row, d))
        part = folded(side_by_side([i_before[at, :], arrived[at, :]]), 2).astype(BF)
        out[out.shape[0] - part.shape[0] :, :] = part
    for send in sends:
        send[: q_send.shape[0], :] = q_send[...]


def second_convolution(z, encoder, row, own, received, skip, h, kernel, i_out, full, line, pad):
    c0 = own[...]
    for other in received:
        c0 = c0 + unfolded(other[: z.cells // FOLD, :], FOLD)
    i = jnp.where(encoder, c0, skip.astype(F32)).astype(BF)
    i_out[...] = i
    y, _ = normalize(z, i.astype(F32))
    spread(z, y * sigmoid(y), line, pad)
    total = convolve(z, pad, kernel, 1)
    base = h[...].astype(F32) + jnp.where(encoder, 0.0, c0)
    full[...] = total + side_by_side([jnp.where(row == j, base, 0.0) for j in range(z.parts)])


def middle(z, pad):
    return pad[1, z.cols : z.cols + z.cells, :].astype(F32)


def second_forward(z, *refs):
    n = z.parts
    own, received, h, pieces, kernel = refs[0], refs[1:n], refs[n], refs[n + 1 : 2 * n + 1], refs[2 * n + 1]
    i_out, full_out = refs[2 * n + 2 : 2 * n + 4]
    sends = refs[2 * n + 4 : 3 * n + 4]
    skip, full, line, pad = refs[3 * n + 4 :]
    s, row = where_am_i()
    encoder = s < z.sections // 2
    assemble(z, skip, pieces, row, z.share, z.share)
    second_convolution(
        z, encoder, row, own, received, skip[...], h, kernel, i_out, full, line, pad
    )
    full_out[...] = full[...].astype(BF)
    for d in range(n):
        fold(z, sends[d], share_of(z, full[...], target(z, row, d)))


def last_forward(z, fs, *refs):
    n = z.parts
    own, received, h = refs[0], refs[1:n], refs[n]
    lasts, arrived, kernel = refs[n + 1 : n + 4]
    sends = refs[n + 4 : 2 * n + 4]
    i_out, skip, full, line, pad = refs[2 * n + 4 :]
    s, row = where_am_i()
    encoder = s < z.sections // 2
    partner = z.sections - 1 - s
    assemble(z, skip, enclosed(z, lasts, received, 0), row, 0, z.share)
    now = jnp.where(
        fs[0, partner] == fs[1, s], unfold(z, arrived), skip[...].astype(F32)
    )
    second_convolution(z, encoder, row, own, received, now, h, kernel, i_out, full, line, pad)
    for d, send in enumerate(sends):
        at = part_rows(z, target(z, row, d))
        send[...] = side_by_side([full[at, :], i_out[at, :]]).astype(BF)


def joined_shares(z, own, received, row):
    others = [unfolded(other[: z.cells // FOLD, :], FOLD) for other in received]
    return side_by_side(all_shares(z, own[...].astype(F32), others, row))


def back_through_first(z, encoder, row, q, received, g_pad, h, kernel, act_out, pad, line):
    g = middle(z, g_pad)
    whole = joined_shares(z, q, received, row)
    now = jnp.where(encoder, whole, g)
    y, factor = normalize(z, h.astype(F32))
    logistic = sigmoid(y)
    act_out[...] = (y * logistic).astype(BF)
    spread(z, now, line, pad)
    back = norm_back(z, y, factor, logistic, convolve_back(z, pad, kernel, 0))
    return share_of(z, g, row) + back, whole


def second_backward(z, *refs):
    n = z.parts
    q, received, g = refs[0], refs[1:n], refs[n]
    heads, others, mirror = refs[n + 1], refs[n + 2 : 2 * n + 1], refs[2 * n + 1]
    grads, kernel = refs[2 * n + 2 : 3 * n + 2], refs[3 * n + 2]
    send, pad, act_out = refs[3 * n + 3 : 3 * n + 6]
    relays, (h, line) = refs[3 * n + 6 : 4 * n + 5], refs[4 * n + 5 :]
    s, row = where_am_i()
    for d, relay in enumerate(relays, 1):
        relay[: z.cells // FOLD, :] = mirror[...]
        relay[z.cells // FOLD :, :] = grads[d][...]
    assemble(z, h, enclosed(z, heads, others, 0), row, 0, z.share)
    value, _ = back_through_first(
        z, s < z.sections // 2, row, q, received, g, h[...], kernel, act_out, pad, line
    )
    fold(z, send, value)


def last_backward(z, fs, bs, *refs):
    n = z.parts
    q, received, g = refs[0], refs[1:n], refs[n]
    heads, others = refs[n + 1], refs[n + 2 : 2 * n + 1]
    h_before, kernel = refs[2 * n + 1 : 2 * n + 3]
    sends = refs[2 * n + 3 : 3 * n + 3]
    pad, act_out, h, value, line = refs[3 * n + 3 :]
    s, row = where_am_i()
    assemble(z, h, enclosed(z, heads, others, 1), row, 0, z.share)
    now = jnp.where(fs[0, s] == bs[1, s], h_before[...], h[...])
    result, _ = back_through_first(
        z, s < z.sections // 2, row, q, received, g, now, kernel, act_out, pad, line
    )
    value[...] = result.astype(BF)
    for d, send in enumerate(sends):
        fold(z, send, value[part_rows(z, target(z, row, d)), :])


def pack_rows(z, *refs):
    n = z.parts
    full, mirror = refs[:2]
    sends, skip = refs[2 : n + 2], refs[n + 2]
    _, row = where_am_i()
    skip[...] = unfold(z, mirror).astype(BF)
    for d, send in enumerate(sends):
        at = part_rows(z, target(z, row, d))
        send[...] = side_by_side([ref[at, :] for ref in (full, skip)]).astype(BF)


def add_rows(z, *refs):
    n = z.parts
    pieces, q, received = refs[:n], refs[n], refs[n + 1 : 2 * n]
    out, mirror, i_rows, whole = refs[2 * n :]
    s, row = where_am_i()
    c = z.channels
    whole[...] = joined_shares(z, q, received, row)
    values = [piece[...].astype(F32) for piece in pieces]
    total = sum(value[:, :c] for value in values)
    out[...] = total.astype(BF)
    mine = whole[part_rows(z, row), :]
    mirror[...] = jnp.where(s < z.sections // 2, total, mine).astype(BF)
    shares = all_shares(z, values[0][:, c:], [value[:, c:] for value in values[1:]], row)
    i_rows[...] = side_by_side(shares).astype(BF)


def write_queues(z, fs, bs, *refs):
    n = z.parts
    fwd, bwd, mir, stash, grad_in, skip_in = refs[:6]
    pieces = refs[6 : n + 6]
    token, outs, held = refs[n + 6], refs[n + 7 : n + 11], refs[n + 11 : n + 15]
    sems = refs[n + 15]
    token[...] = jnp.zeros_like(token)
    s, row = where_am_i()
    w = z.share
    prior, later = jnp.maximum(s - 1, 0), jnp.minimum(s + 1, z.sections - 1)
    partner = z.sections - 1 - s
    f0, f1 = fs[0, s], fs[1, s]
    mine = part_rows(z, row)
    copies = [pltpu.make_async_copy(a, b, sems.at[j]) for j, (a, b) in enumerate(zip(held, outs))]
    for ref, queue in zip(held, (fwd, bwd, mir, stash)):
        ref[...] = queue[...]

    @pl.when(s < z.sections - 1)
    def _():
        held[1][bs[0, later]] = grad_in[mine, :]

    copies[1].start()

    @pl.when(s < z.sections // 2)
    def _():
        held[2][bs[0, partner]] = skip_in[mine, :]

    copies[2].start()
    values = [unfolded(piece[piece.shape[0] - z.local // 2 :, :], 2) for piece in pieces]

    def joined(at):
        shares = [value[:, at : at + w] for value in values]
        return side_by_side(all_shares(z, shares[0], shares[1:], row)).astype(BF)

    fwd_in = joined(w)

    @pl.when(s > 0)
    def _():
        held[0][fs[0, prior]] = fwd_in

    copies[0].start()
    held[3][2 * f0] = fwd[f0]
    held[3][2 * f0 + 1] = joined(0)
    held[3][2 * f1] = fwd[f1]

    @pl.when(jnp.logical_and(s > 0, fs[0, prior] == f1))
    def _():
        held[3][2 * f1] = fwd_in

    copies[3].start()
    for copy in copies:
        copy.wait()


def finish(z, fs, bs, *refs):
    n = z.parts
    out1, i1, fwd1, mir1 = refs[4:8]
    rows0, grads1 = refs[8 : n + 8], refs[n + 8 : 2 * n + 8]
    fwd_out, bwd_out, mir_out, stash_out, emitted = refs[2 * n + 8 : 2 * n + 13]
    out0, skip, grads, sems = refs[2 * n + 13 :]
    s, row = where_am_i()
    c = z.channels
    prior, later = jnp.maximum(s - 1, 0), jnp.minimum(s + 1, z.sections - 1)
    partner = z.sections - 1 - s
    encoder, has_prior, has_later = s < z.sections // 2, s > 0, s < z.sections - 1
    first = jnp.where(encoder, bs[0, partner], fs[0, partner])
    second = jnp.where(encoder, bs[1, partner], fs[1, partner])
    skip_stays = jnp.logical_and(jnp.logical_not(encoder), first != second)

    def put(source, place, j):
        return pltpu.make_async_copy(source, place, sems.at[j])

    always = [
        put(out1, emitted.at[1], 0),
        put(i1, stash_out.at[2 * fs[1, s] + 1], 1),
        put(mir1, mir_out.at[second], 2),
        put(out0, emitted.at[0], 3),
    ]
    for copy in always[:3]:
        copy.start()
    onward, back = put(fwd1, fwd_out.at[fs[1, prior]], 4), put(grads, bwd_out.at[bs[1, later]], 5)
    aside = put(skip, mir_out.at[first], 6)
    pl.when(has_prior)(onward.start)
    pieces = [unfold(z, piece) for piece in grads1]
    grads[...] = side_by_side(all_shares(z, pieces[0], pieces[1:], row)).astype(BF)
    pl.when(has_later)(back.start)
    pieces = [piece[...].astype(F32) for piece in rows0]
    out0[...] = sum(piece[:, :c] for piece in pieces).astype(BF)
    always[3].start()
    shares = [piece[:, c:] for piece in pieces]
    skip[...] = side_by_side(all_shares(z, shares[0], shares[1:], row)).astype(BF)
    pl.when(skip_stays)(aside.start)
    for copy in always:
        copy.wait()
    pl.when(has_prior)(onward.wait)
    pl.when(has_later)(back.wait)
    pl.when(skip_stays)(aside.wait)


def add_taps(z, act, pad, before, store):
    turned = jnp.transpose(act[...].astype(F32)).astype(BF)
    for tap in range(9):
        a, b = divmod(tap, 3)
        at = (2 - a) * z.cols
        moved = pad[2 - b, at : at + z.cells, :]
        store(tap, before(tap) + jnp.dot(turned, moved, preferred_element_type=F32))


def kernel_grads_add(z, start, acc, act, pad, out):
    def store(tap, value):
        out[tap] = value

    add_taps(z, act, pad, lambda tap: acc[start + tap], store)


def kernel_grads_last(z, total, other, act, pad, token, out, held, sems):
    token[...] = jnp.zeros_like(token)
    copies = [pltpu.make_async_copy(other, out.at[9:], sems.at[9])]
    copies[0].start()

    def store(tap, value):
        held[tap] = value
        copies.append(pltpu.make_async_copy(held.at[tap], out.at[tap], sems.at[tap]))
        copies[-1].start()

    add_taps(z, act, pad, lambda tap: total[tap], store)
    for copy in copies:
        copy.wait()


def per_device(fwd_queue, bwd_queue, mirror_queue, stash, weights, grad_acc, fwd_slot, bwd_slot):
    sections, n = lax.axis_size("section"), lax.axis_size("row")
    z = Sizes(fwd_queue[0], sections, n)
    slots = fwd_queue.shape[1]
    c, w, local, cells = z.channels, z.share, z.local, z.cells
    fwd, bwd, mir = (x.reshape(slots, local, c) for x in (fwd_queue, bwd_queue, mirror_queue))
    kept = stash.reshape(2 * slots, local, c)
    kernels = weights.reshape(18, w, c)
    acc = grad_acc.reshape(18, w, c)
    fs, bs = fwd_slot.T, bwd_slot.T
    fold_shape, wide = (cells // FOLD, FOLD * w), (cells, c)
    half = (cells, w)

    def with_shares(k):
        return ((cells + k * local) // FOLD, FOLD * w)

    padded = (3, cells + 2 * z.cols, c)

    def move(x, d, step):
        route = [
            (s * n + r, step(s) * n + (r + d) % n) for s in range(sections) for r in range(n)
        ]
        return lax.ppermute(x, ("section", "row"), route)

    across = functools.partial(move, step=lambda s: s)
    onward = functools.partial(move, step=lambda s: (s + 1) % sections)
    backward = functools.partial(move, step=lambda s: (s - 1) % sections)
    crossed = functools.partial(move, step=lambda s: (sections - s) % sections)
    mirrored = functools.partial(move, step=lambda s: sections - 1 - s)

    def run(body, scalars, arrays, outs, scratch=(), **options):
        return call(
            functools.partial(body, z), body.__name__, scalars, arrays, outs, scratch, **options
        )

    def exchange(pieces):
        return [pieces[0]] + [across(piece, d) for d, piece in enumerate(pieces[1:], 1)]

    narrow_pad = pad_shapes(z, w)
    wide_line = pltpu.VMEM((cells + 16, c), F32)
    queues = (fwd, bwd, mir, kept)
    rows = (local, c)
    sems = pltpu.SemaphoreType.DMA
    packed = run(
        pack_first,
        (),
        (fs, bs, *queues),
        [((local // FOLD, FOLD * w), BF)] * n
        + [(x.shape, BF) for x in queues],
        [pltpu.SMEM(fs.shape, jnp.int32)] * 2 + [sems((6,))],
        remote=6,
    )
    inputs, held = exchange(packed[:n]), packed[n:]

    packed = run(
        pack_later,
        (),
        (fs, bs, *held),
        [((local, 2 * w + c), BF)] * n
        + [((k * (local // FOLD), FOLD * w), BF) for k in (2, 2, n, 1) for _ in range(n)],
        [pltpu.SMEM(fs.shape, jnp.int32)] * 2 + [sems((2,))],
        remote=2,
        after=(inputs[0],),
    )
    pieces, heads, nexts, grads, lasts = (packed[j * n : (j + 1) * n] for j in range(5))
    first = exchange(held_until(pieces, inputs))

    own, h0, *sends = run(
        first_forward,
        (),
        (*inputs, *heads, kernels),
        [(half, F32), (half, BF)] + [(with_shares(2), BF)] * (n - 1),
        narrow_pad,
    )
    sums = [across(x, d) for d, x in enumerate(sends, 1)]
    q0, q_send, g_pad0, act_i0, *sends = run(
        first_backward,
        (),
        (*first, *nexts, kernels),
        [(half, BF), (fold_shape, BF), (padded, BF), (half, BF)]
        + [(with_shares(2), BF)] * (n - 1),
        [pltpu.VMEM(half, BF), pltpu.VMEM(wide, BF), wide_line],
        after=(own,),
    )
    q_received = [across(x, d) for d, x in enumerate(sends, 1)]
    skip_in = mirrored(q_send, 0)

    def add_grads(start, total, act, pad, after):
        [out] = call(
            functools.partial(kernel_grads_add, z, start),
            f"kernel_grads_add_{start}",
            (),
            (total, act, pad),
            [((9, w, c), F32)],
            after=after,
        )
        return out

    sum_i = add_grads(9, acc, act_i0, g_pad0, (q0,))
    i0, full0, *sends = run(
        second_forward,
        (),
        (own, *sums, h0, *first, kernels),
        [(half, BF), (wide, BF)] + [(fold_shape, BF)] * n,
        [pltpu.VMEM(half, BF), pltpu.VMEM(wide, F32)] + narrow_pad,
        after=(sum_i,),
    )
    fwd_in = [onward(x, d) for d, x in enumerate(sends)]
    dh_send, f_pad0, act_h0, *relays = run(
        second_backward,
        (),
        (q0, *q_received, g_pad0, heads[0], *sums, skip_in, *grads, kernels),
        [(fold_shape, BF), (padded, BF), (half, BF)] + [(with_shares(n), BF)] * (n - 1),
        [pltpu.VMEM(half, BF), wide_line],
        after=(i0,),
    )
    dh_in = [backward(dh_send, d) for d in range(n)]
    relayed = [across(x, d) for d, x in enumerate(relays, 1)]

    own, h1, arrived, turned, *sends = run(
        later_forward,
        (fs,),
        (*fwd_in, nexts[0], *q_received, *lasts, kernels),
        [(half, F32), (half, BF), (half, BF), (fold_shape, BF)]
        + [(with_shares(1), BF)] * (n - 1),
        narrow_pad,
        after=(dh_send,),
    )
    received = [across(x, d) for d, x in enumerate(sends, 1)]
    mir_in = crossed(turned, 0)
    sum_h = add_grads(0, acc, act_h0, f_pad0, (own,))
    q1, g_pad1, act_i1, grad_in, skip_full, rows_own, *sends = run(
        later_backward,
        (fs, bs),
        (*dh_in, skip_in, *relayed, grads[0], nexts[0], *q_received, i0, arrived, kernels),
        [(half, BF), (padded, BF), (half, BF), (wide, BF), (wide, BF), ((local // 2, 4 * w), BF)]
        + [((cells // FOLD + local // 2, FOLD * w), BF)] * (n - 1),
        [pltpu.VMEM(fold_shape, BF), pltpu.VMEM(half, BF), pltpu.VMEM((n, *half), BF), wide_line],
        after=(sum_h,),
    )
    q_received = [across(x, d) for d, x in enumerate(sends, 1)]
    sends = run(
        last_forward,
        (fs,),
        (own, *received, h1, lasts[0], mir_in, kernels),
        [((local, c + w), BF)] * n,
        [pltpu.VMEM(half, BF), pltpu.VMEM(half, BF), pltpu.VMEM(wide, F32)] + narrow_pad,
        after=(q1,),
    )
    rows1 = exchange(sends)
    part_i = add_grads(0, sum_i, act_i1, g_pad1, (sends[0],))
    packed = run(
        pack_rows,
        (),
        (full0, mir_in),
        [((local, c + w), BF)] * n,
        [pltpu.VMEM(half, BF)],
        after=(part_i,),
    )
    token, *written = run(
        write_queues,
        (fs, bs),
        (*held, grad_in, skip_full, rows_own, *q_received),
        [((8, 128), F32)] + [(x.shape, BF) for x in queues],
        [pltpu.VMEM(x.shape, BF) for x in queues] + [sems((4,))],
        far_outs=4,
        after=(packed[0],),
    )
    rows0 = exchange(held_until(packed, (rows1, token)))
    out1, mirror1, i1 = run(
        add_rows,
        (),
        (*rows1, q1, *q_received),
        [(rows, BF)] * 3,
        [pltpu.VMEM(wide, F32)],
        after=(token,),
    )
    fwd1, mir1 = onward(out1, 0), mirrored(mirror1, 0)
    *dh_sends, f_pad1, act_h1 = run(
        last_backward,
        (fs, bs),
        (q1, *q_received, g_pad1, heads[0], *sums, h0, kernels),
        [((local // FOLD, FOLD * w), BF)] * n + [(padded, BF), (half, BF)],
        [pltpu.VMEM(half, BF), pltpu.VMEM(half, BF), wide_line],
        after=(out1,),
    )
    dh1_in = [backward(x, d) for d, x in enumerate(dh_sends)]
    token, grad_total = run(
        kernel_grads_last,
        (),
        (sum_h, part_i, act_h1, f_pad1),
        [((8, 128), F32), ((18, w, c), F32)],
        [pltpu.VMEM((9, w, c), F32), sems((10,))],
        far_outs=1,
    )
    fwd_out, bwd_out, mir_out, stash_out, emitted = run(
        finish,
        (fs, bs),
        (*written, out1, i1, fwd1, mir1, *rows0, *dh1_in),
        [(x.shape, BF) for x in queues] + [((TICKS, local, c), BF)],
        [pltpu.VMEM(rows, BF)] * 3 + [sems((7,))],
        remote=4,
        far_outs=5,
        aliases={j + 2: j for j in range(4)},
        after=(token,),
    )
    return (
        fwd_out.reshape(fwd_queue.shape),
        bwd_out.reshape(bwd_queue.shape),
        mir_out.reshape(mirror_queue.shape),
        stash_out.reshape(stash.shape),
        grad_total.reshape(grad_acc.shape),
        emitted.reshape((1, TICKS) + fwd_queue.shape[2:]),
    )


def solution(mesh):
    return jax.shard_map(
        per_device,
        mesh=mesh,
        in_specs=(
            P("section", None, "row", None, None),
            P("section", None, "row", None, None),
            P("section", None, "row", None, None),
            P("section", None, None, "row", None, None),
            P("section", None, None, None, "row", None),
            P("section", None, None, None, "row", None),
            P(),
            P(),
        ),
        out_specs=(
            P("section", None, "row", None, None),
            P("section", None, "row", None, None),
            P("section", None, "row", None, None),
            P("section", None, None, "row", None, None),
            P("section", None, None, None, "row", None),
            P("section", None, "row", None, None),
        ),
        check_vma=False,
    )
```

```python
import functools

import jax
import jax.numpy as jnp
from jax import lax
from jax.experimental import pallas as pl
from jax.experimental.pallas import tpu as pltpu
from jax.sharding import PartitionSpec as P

GROUPS = 32
TICKS = 2
FOLD = 4
EPSILON = 1e-05
BF, F32 = jnp.bfloat16, jnp.float32
VMEM_LIMIT = 24 * 2**20


class Sizes:
    def __init__(self, queue, sections, rows):
        self.sections, self.parts = sections, rows
        self.cols = queue.shape[2]
        self.channels = queue.shape[3]
        self.local = queue.shape[1] * queue.shape[2]
        self.cells = self.local * rows
        self.share = self.channels // rows
        self.group = self.channels // GROUPS
        self.count = self.cells * self.group


def where_am_i():
    return lax.axis_index("section"), lax.axis_index("row")


def share_of(z, value, part):
    value = value.astype(F32)
    out = value[:, : z.share]
    for j in range(1, z.parts):
        out = jnp.where(part == j, value[:, j * z.share : (j + 1) * z.share], out)
    return out


def all_shares(z, own, others, row):
    out = []
    for j in range(z.parts):
        value = own
        for d in range(1, z.parts):
            value = jnp.where(lax.rem(row + z.parts - d, z.parts) == j, others[d - 1], value)
        out.append(value)
    return out


def side_by_side(values):
    return jnp.concatenate([value.astype(F32) for value in values], axis=1)


def folded(value, blocks):
    rows = value.shape[0] // blocks
    return side_by_side([value[j * rows : (j + 1) * rows] for j in range(blocks)])


def unfolded(value, blocks):
    value, width = value.astype(F32), value.shape[1] // blocks
    return jnp.concatenate([value[:, j * width : (j + 1) * width] for j in range(blocks)], axis=0)


def fold(z, ref, value):
    ref[...] = folded(value, FOLD).astype(BF)


def unfold(z, ref):
    return unfolded(ref[...], FOLD)


def source(z, row, d):
    return lax.rem(row + z.parts - d, z.parts)


def target(z, row, d):
    return lax.rem(row + d, z.parts)


def part_rows(z, part):
    return pl.ds(pl.multiple_of(part * z.local, z.local), z.local)


def assemble(z, ref, pieces, row, start, width):
    for d, piece in enumerate(pieces):
        value = (piece if isinstance(piece, jax.Array) else piece[...]).astype(F32)
        value = value[:, start : start + width]
        ref[part_rows(z, source(z, row, d)), :] = value.astype(BF)


def group_sums(z, first, second):
    width = first.shape[1]
    line = lax.broadcasted_iota(jnp.int32, (8, width), 0)
    both = jnp.where(line == 0, first, jnp.where(line == 1, second, 0.0))
    across = lax.broadcasted_iota(jnp.int32, (width, width), 1).astype(F32)
    down = lax.broadcasted_iota(jnp.int32, (width, width), 0).astype(F32)
    same = jnp.floor((across + 0.5) * (1.0 / z.group)) == jnp.floor((down + 0.5) * (1.0 / z.group))
    sums = jnp.dot(
        both, same.astype(F32), precision=lax.Precision.HIGHEST, preferred_element_type=F32
    )
    return sums[0:1], sums[1:2]


def normalize(z, x):
    total, square = group_sums(
        z, jnp.sum(x, axis=0, keepdims=True), jnp.sum(x * x, axis=0, keepdims=True)
    )
    center = total / z.count
    factor = lax.rsqrt(square / z.count - center * center + EPSILON)
    return (x - center) * factor, factor


def sigmoid(y):
    return 1.0 / (1.0 + jnp.exp(-y))


def norm_back(z, y, factor, logistic, upstream):
    e = upstream * logistic * (1.0 + y * (1.0 - logistic))
    first, second = group_sums(
        z, jnp.sum(e, axis=0, keepdims=True), jnp.sum(e * y, axis=0, keepdims=True)
    )
    return factor * (e - first / z.count - y * (second / z.count))


def spread(z, x, line_ref, pad_ref):
    cells, cols = z.cells, z.cols
    width = x.shape[1]
    line_ref[8 : 8 + cells, :] = x
    column = lax.rem(lax.broadcasted_iota(jnp.int32, (cells, 1), 0), cols)
    edge = jnp.zeros((cols, width), BF)
    for b in range(3):
        pad_ref[b, :cols, :] = edge
        pad_ref[b, cols + cells :, :] = edge
    pad_ref[1, cols : cols + cells, :] = x.astype(BF)
    left = jnp.where(column > 0, line_ref[7 : 7 + cells, :], 0.0)
    pad_ref[0, cols : cols + cells, :] = left.astype(BF)
    right = jnp.where(column < cols - 1, line_ref[9 : 9 + cells, :], 0.0)
    pad_ref[2, cols : cols + cells, :] = right.astype(BF)


def spread_wide(z, x, line_ref, pad_ref):
    cells, cols = z.cells, z.cols
    line_ref[8 : 8 + cells, :] = x
    column = lax.rem(lax.broadcasted_iota(jnp.int32, (cells, 1), 0), cols)
    edge = jnp.zeros((cols, 3 * z.share), BF)
    pad_ref[:cols, :] = edge
    pad_ref[cols + cells :, :] = edge
    left = jnp.where(column > 0, line_ref[7 : 7 + cells, :], 0.0)
    right = jnp.where(column < cols - 1, line_ref[9 : 9 + cells, :], 0.0)
    pad_ref[cols : cols + cells, :] = side_by_side([left, x, right]).astype(BF)


def convolve(z, pad_ref, kernel_ref, which):
    total = None
    for a in range(3):
        first = (9 * which + 3 * a) * z.share
        term = jnp.dot(
            pad_ref[a * z.cols : a * z.cols + z.cells, :],
            kernel_ref[first : first + 3 * z.share, :],
            preferred_element_type=F32,
        )
        total = term if total is None else total + term
    return total


def convolve_back(z, pad_ref, kernel_ref, which, line_ref):
    cells, cols, w = z.cells, z.cols, z.share
    total = None
    for a in range(3):
        first = (9 * which + 3 * (2 - a)) * w
        term = lax.dot_general(
            pad_ref[1, a * cols : a * cols + cells, :],
            kernel_ref[first : first + 3 * w, :],
            (((1,), (1,)), ((), ())),
            preferred_element_type=F32,
        )
        total = term if total is None else total + term
    column = lax.rem(lax.broadcasted_iota(jnp.int32, (cells, 1), 0), cols)
    line_ref[8 : 8 + cells, :w] = total[:, :w]
    out = total[:, w : 2 * w]
    out = out + jnp.where(column < cols - 1, line_ref[9 : 9 + cells, :w], 0.0)
    line_ref[8 : 8 + cells, :w] = total[:, 2 * w :]
    return out + jnp.where(column > 0, line_ref[7 : 7 + cells, :w], 0.0)


def pad_shapes(z, width):
    return [
        pltpu.VMEM((z.cells + 16, width), F32),
        pltpu.VMEM((z.cells + 2 * z.cols, 3 * width), BF),
    ]


def call(body, name, scalars, arrays, outs, scratch=(), after=(), remote=0, far_outs=0, aliases=None):
    near, far = pl.BlockSpec(memory_space=pltpu.VMEM), pl.BlockSpec(memory_space=pltpu.HBM)

    def inner(*refs):
        given = len(scalars) + len(arrays)
        body(*refs[:given], *refs[given + len(after) :])

    arrays = [
        pltpu.with_memory_space_constraint(x, pltpu.HBM) if j < remote else x
        for j, x in enumerate(arrays)
    ]
    near_outs = len(outs) - far_outs
    return pl.pallas_call(
        inner,
        name=name,
        out_shape=[
            jax.ShapeDtypeStruct(shape, dtype) if j < near_outs else pltpu.HBM(shape, dtype)
            for j, (shape, dtype) in enumerate(outs)
        ],
        in_specs=[pl.BlockSpec(memory_space=pltpu.SMEM)] * len(scalars)
        + [far] * remote
        + [near] * (len(arrays) - remote)
        + [pl.BlockSpec(memory_space=pl.ANY)] * len(after),
        out_specs=[near] * near_outs + [far] * far_outs,
        scratch_shapes=list(scratch),
        input_output_aliases=aliases or {},
        compiler_params=pltpu.CompilerParams(vmem_limit_bytes=VMEM_LIMIT),
        cost_estimate=pl.CostEstimate(flops=1, bytes_accessed=1, transcendentals=0),
    )(*scalars, *arrays, *after)


def held_until(values, earlier):
    return lax.optimization_barrier((tuple(values), earlier))[0]


def fetch(pairs, sems):
    copies = [pltpu.make_async_copy(a, b, sems.at[j]) for j, (a, b) in enumerate(pairs)]
    for copy in copies:
        copy.start()
    for copy in copies:
        copy.wait()


def pack_first(z, fs_far, bs_far, fwd_far, bwd_far, mir_far, stash_far, *refs):
    n = z.parts
    heads = refs[:n]
    fwd, bwd, mir, stash, fs, bs, sems = refs[n:]
    fetch(
        [
            (fs_far, fs),
            (bs_far, bs),
            (fwd_far, fwd),
            (bwd_far, bwd),
            (mir_far, mir),
            (stash_far, stash),
        ],
        sems,
    )
    s, row = where_am_i()
    h = fwd[fs[0, s]]
    for d in range(n):
        fold(z, heads[d], share_of(z, h, target(z, row, d)))


def taken_back(z, bs, s):
    later, partner = jnp.minimum(s + 1, z.sections - 1), z.sections - 1 - s
    return (
        jnp.logical_and(s < z.sections - 1, bs[0, later] == bs[1, s]),
        jnp.logical_and(s < z.sections // 2, bs[0, partner] == bs[1, s]),
    )


def pack_later(z, fs_far, bs_far, fwd, bwd, mir, stash, *refs):
    n = z.parts
    pieces, groups = refs[:n], [refs[j * n : (j + 1) * n] for j in range(1, 5)]
    fs, bs, sems = refs[5 * n :]
    fetch([(fs_far, fs), (bs_far, bs)], sems)
    s, row = where_am_i()
    f1, b1 = fs[1, s], bs[1, s]
    grad_taken, skip_taken = taken_back(z, bs, s)
    skip_kept = jnp.logical_and(s < z.sections // 2, jnp.logical_not(skip_taken))
    kept = jnp.where(grad_taken, 0.0, bwd[b1].astype(F32))
    kept = kept + jnp.where(skip_kept, mir[b1].astype(F32), 0.0)
    f0, b0 = fs[0, s], bs[0, s]
    g = bwd[b0].astype(F32) + jnp.where(s < z.sections // 2, mir[b0].astype(F32), 0.0)
    for d, piece in enumerate(pieces):
        part = target(z, row, d)
        shares = [share_of(z, stash[2 * b0 + 1], part), share_of(z, mir[f0], part)]
        piece[...] = side_by_side(shares + [g]).astype(BF)
    values = [stash[2 * b0], stash[2 * b1], fwd[f1], stash[2 * b1 + 1], mir[f1]]
    rows = z.local // FOLD
    for d in range(n):
        shares = [share_of(z, value, target(z, row, d)) for value in values]
        grads = [kept[:, j * z.share : (j + 1) * z.share] for j in range(n)]
        for outs, parts in zip(groups, (shares[:2], shares[2:4], grads, shares[4:])):
            for j, value in enumerate(parts):
                outs[d][j * rows : (j + 1) * rows, :] = folded(value, FOLD).astype(BF)


def send_partials(z, row, total, own, sends, extra):
    own[...] = share_of(z, total, row)
    for d, send in enumerate(sends, 1):
        part = folded(share_of(z, total, target(z, row, d)), FOLD).astype(BF)
        send[: part.shape[0], :] = part
        send[part.shape[0] :, :] = extra[d][...]


def first_forward(z, *refs):
    n = z.parts
    pieces, extra, kernel = refs[:n], refs[n : 2 * n], refs[2 * n]
    own, h_out = refs[2 * n + 1 : 2 * n + 3]
    sends, (line, pad) = refs[2 * n + 3 : 3 * n + 2], refs[3 * n + 2 :]
    _, row = where_am_i()
    assemble(z, h_out, [unfold(z, piece) for piece in pieces], row, 0, z.share)
    y, _ = normalize(z, h_out[...].astype(F32))
    spread_wide(z, y * sigmoid(y), line, pad)
    send_partials(z, row, convolve(z, pad, kernel, 0), own, sends, extra)


def enclosed(z, own, received, j):
    rows, base = z.local // FOLD, z.cells // FOLD
    at, there = slice(j * rows, (j + 1) * rows), slice(base + j * rows, base + (j + 1) * rows)
    return [unfolded(own[at, :], FOLD)] + [unfolded(x[there, :], FOLD) for x in received]


def later_forward(z, fs, *refs):
    n = z.parts
    arrivals, nexts, received = refs[:n], refs[n], refs[n + 1 : 2 * n]
    lasts, kernel = refs[2 * n : 3 * n], refs[3 * n]
    own, h_out, arrived, onward = refs[3 * n + 1 : 3 * n + 5]
    sends = refs[3 * n + 5 : 4 * n + 4]
    line, pad = refs[4 * n + 4 :]
    s, row = where_am_i()
    total = unfold(z, arrivals[0])
    for other in arrivals[1:]:
        total = total + unfold(z, other)
    total = total.astype(BF).astype(F32)
    arrived[...] = total.astype(BF)
    fold(z, onward, total)
    assemble(z, h_out, enclosed(z, nexts, received, 0), row, 0, z.share)
    prior = jnp.maximum(s - 1, 0)
    taken = jnp.logical_and(s > 0, fs[0, prior] == fs[1, s])
    h = jnp.where(taken, total, h_out[...].astype(F32))
    h_out[...] = h.astype(BF)
    y, _ = normalize(z, h)
    spread_wide(z, y * sigmoid(y), line, pad)
    send_partials(z, row, convolve(z, pad, kernel, 0), own, sends, lasts)


def back_through_second(z, i, g, kernel, q_out, q_send, act_out, pad, line):
    y, factor = normalize(z, i.astype(F32))
    logistic = sigmoid(y)
    act_out[...] = (y * logistic).astype(BF)
    spread(z, g, line, pad)
    q = norm_back(z, y, factor, logistic, convolve_back(z, pad, kernel, 1, line)).astype(BF)
    q_out[...] = q
    fold(z, q_send, q.astype(F32))


def first_backward(z, *refs):
    n = z.parts
    pieces, heads, kernel = refs[:n], refs[n : 2 * n], refs[2 * n]
    q_out, q_send, pad, act_out = refs[2 * n + 1 : 2 * n + 5]
    sends, (i_ref, g_ref, line) = refs[2 * n + 5 : 3 * n + 4], refs[3 * n + 4 :]
    _, row = where_am_i()
    assemble(z, i_ref, pieces, row, 0, z.share)
    assemble(z, g_ref, pieces, row, 2 * z.share, z.channels)
    back_through_second(
        z, i_ref[...], g_ref[...].astype(F32), kernel, q_out, q_send, act_out, pad, line
    )
    rows = z.cells // FOLD
    for d, send in enumerate(sends, 1):
        send[:rows, :] = q_send[...]
        send[rows:, :] = heads[d][...]


def later_backward(z, fs, bs, *refs):
    n = z.parts
    arrivals, mirror, received, kept = refs[:n], refs[n], refs[n + 1 : 2 * n], refs[2 * n]
    nexts, others = refs[2 * n + 1], refs[2 * n + 2 : 3 * n + 1]
    i_before, arrived, kernel = refs[3 * n + 1 : 3 * n + 4]
    q_out, pad, act_out, grad_in, skip_in = refs[3 * n + 4 : 3 * n + 9]
    rows_own, sends = refs[3 * n + 9], refs[3 * n + 10 : 4 * n + 9]
    q_send, i_ref, full, line = refs[4 * n + 9 :]
    s, row = where_am_i()
    w = z.share
    shares = [unfold(z, part) for part in arrivals]
    grad = side_by_side(all_shares(z, shares[0], shares[1:], row))
    grad_in[...] = grad.astype(BF)
    shares = [unfolded(x[: z.cells // FOLD, :], FOLD) for x in received]
    skip = side_by_side(all_shares(z, unfold(z, mirror), shares, row))
    skip_in[...] = skip.astype(BF)
    grad_taken, skip_taken = taken_back(z, bs, s)
    for j in range(n):
        assemble(z, full.at[j], enclosed(z, kept, received, j), row, 0, w)
    g = side_by_side([full[j] for j in range(n)]) + jnp.where(grad_taken, grad, 0.0)
    g = g + jnp.where(skip_taken, skip, 0.0)
    g = g.astype(BF).astype(F32)
    assemble(z, i_ref, enclosed(z, nexts, others, 1), row, 0, w)
    i = jnp.where(fs[0, s] == bs[1, s], i_before[...].astype(F32), i_ref[...].astype(F32))
    back_through_second(z, i, g, kernel, q_out, q_send, act_out, pad, line)
    for d, out in enumerate([rows_own, *sends]):
        at = part_rows(z, target(z, row, d))
        part = folded(side_by_side([i_before[at, :], arrived[at, :]]), 2).astype(BF)
        out[out.shape[0] - part.shape[0] :, :] = part
    for send in sends:
        send[: q_send.shape[0], :] = q_send[...]


def second_convolution(z, encoder, row, own, received, skip, h, kernel, i_out, full, line, pad):
    c0 = own[...]
    for other in received:
        c0 = c0 + unfolded(other[: z.cells // FOLD, :], FOLD)
    i = jnp.where(encoder, c0, skip.astype(F32)).astype(BF)
    i_out[...] = i
    y, _ = normalize(z, i.astype(F32))
    spread_wide(z, y * sigmoid(y), line, pad)
    total = convolve(z, pad, kernel, 1)
    base = h[...].astype(F32) + jnp.where(encoder, 0.0, c0)
    full[...] = total + side_by_side([jnp.where(row == j, base, 0.0) for j in range(z.parts)])


def middle(z, pad):
    return pad[1, z.cols : z.cols + z.cells, :].astype(F32)


def second_forward(z, *refs):
    n = z.parts
    own, received, h, pieces, kernel = refs[0], refs[1:n], refs[n], refs[n + 1 : 2 * n + 1], refs[2 * n + 1]
    i_out, full_out = refs[2 * n + 2 : 2 * n + 4]
    sends = refs[2 * n + 4 : 3 * n + 4]
    skip, full, line, pad = refs[3 * n + 4 :]
    s, row = where_am_i()
    encoder = s < z.sections // 2
    assemble(z, skip, pieces, row, z.share, z.share)
    second_convolution(
        z, encoder, row, own, received, skip[...], h, kernel, i_out, full, line, pad
    )
    full_out[...] = full[...].astype(BF)
    for d in range(n):
        fold(z, sends[d], share_of(z, full[...], target(z, row, d)))


def last_forward(z, fs, *refs):
    n = z.parts
    own, received, h = refs[0], refs[1:n], refs[n]
    lasts, arrived, kernel = refs[n + 1 : n + 4]
    sends = refs[n + 4 : 2 * n + 4]
    i_out, skip, full, line, pad = refs[2 * n + 4 :]
    s, row = where_am_i()
    encoder = s < z.sections // 2
    partner = z.sections - 1 - s
    assemble(z, skip, enclosed(z, lasts, received, 0), row, 0, z.share)
    now = jnp.where(
        fs[0, partner] == fs[1, s], unfold(z, arrived), skip[...].astype(F32)
    )
    second_convolution(z, encoder, row, own, received, now, h, kernel, i_out, full, line, pad)
    for d, send in enumerate(sends):
        at = part_rows(z, target(z, row, d))
        send[...] = side_by_side([full[at, :], i_out[at, :]]).astype(BF)


def joined_shares(z, own, received, row):
    others = [unfolded(other[: z.cells // FOLD, :], FOLD) for other in received]
    return side_by_side(all_shares(z, own[...].astype(F32), others, row))


def back_through_first(z, encoder, row, q, received, g_pad, h, kernel, act_out, pad, line):
    g = middle(z, g_pad)
    whole = joined_shares(z, q, received, row)
    now = jnp.where(encoder, whole, g)
    y, factor = normalize(z, h.astype(F32))
    logistic = sigmoid(y)
    act_out[...] = (y * logistic).astype(BF)
    spread(z, now, line, pad)
    back = norm_back(z, y, factor, logistic, convolve_back(z, pad, kernel, 0, line))
    return share_of(z, g, row) + back, whole


def second_backward(z, *refs):
    n = z.parts
    q, received, g = refs[0], refs[1:n], refs[n]
    heads, others, mirror = refs[n + 1], refs[n + 2 : 2 * n + 1], refs[2 * n + 1]
    grads, kernel = refs[2 * n + 2 : 3 * n + 2], refs[3 * n + 2]
    send, pad, act_out = refs[3 * n + 3 : 3 * n + 6]
    relays, (h, line) = refs[3 * n + 6 : 4 * n + 5], refs[4 * n + 5 :]
    s, row = where_am_i()
    for d, relay in enumerate(relays, 1):
        relay[: z.cells // FOLD, :] = mirror[...]
        relay[z.cells // FOLD :, :] = grads[d][...]
    assemble(z, h, enclosed(z, heads, others, 0), row, 0, z.share)
    value, _ = back_through_first(
        z, s < z.sections // 2, row, q, received, g, h[...], kernel, act_out, pad, line
    )
    fold(z, send, value)


def last_backward(z, fs, bs, *refs):
    n = z.parts
    q, received, g = refs[0], refs[1:n], refs[n]
    heads, others = refs[n + 1], refs[n + 2 : 2 * n + 1]
    h_before, kernel = refs[2 * n + 1 : 2 * n + 3]
    sends = refs[2 * n + 3 : 3 * n + 3]
    pad, act_out, h, value, line = refs[3 * n + 3 :]
    s, row = where_am_i()
    assemble(z, h, enclosed(z, heads, others, 1), row, 0, z.share)
    now = jnp.where(fs[0, s] == bs[1, s], h_before[...], h[...])
    result, _ = back_through_first(
        z, s < z.sections // 2, row, q, received, g, now, kernel, act_out, pad, line
    )
    value[...] = result.astype(BF)
    for d, send in enumerate(sends):
        fold(z, send, value[part_rows(z, target(z, row, d)), :])


def pack_rows(z, *refs):
    n = z.parts
    full, mirror = refs[:2]
    sends, skip = refs[2 : n + 2], refs[n + 2]
    _, row = where_am_i()
    skip[...] = unfold(z, mirror).astype(BF)
    for d, send in enumerate(sends):
        at = part_rows(z, target(z, row, d))
        send[...] = side_by_side([ref[at, :] for ref in (full, skip)]).astype(BF)


def add_rows(z, *refs):
    n = z.parts
    pieces, q, received = refs[:n], refs[n], refs[n + 1 : 2 * n]
    out, mirror, i_rows, whole = refs[2 * n :]
    s, row = where_am_i()
    c = z.channels
    whole[...] = joined_shares(z, q, received, row)
    values = [piece[...].astype(F32) for piece in pieces]
    total = sum(value[:, :c] for value in values)
    out[...] = total.astype(BF)
    mine = whole[part_rows(z, row), :]
    mirror[...] = jnp.where(s < z.sections // 2, total, mine).astype(BF)
    shares = all_shares(z, values[0][:, c:], [value[:, c:] for value in values[1:]], row)
    i_rows[...] = side_by_side(shares).astype(BF)


def write_queues(z, fs, bs, *refs):
    n = z.parts
    fwd, bwd, mir, stash, grad_in, skip_in = refs[:6]
    pieces = refs[6 : n + 6]
    token, outs, held = refs[n + 6], refs[n + 7 : n + 11], refs[n + 11 : n + 15]
    sems = refs[n + 15]
    token[...] = jnp.zeros_like(token)
    s, row = where_am_i()
    w = z.share
    prior, later = jnp.maximum(s - 1, 0), jnp.minimum(s + 1, z.sections - 1)
    partner = z.sections - 1 - s
    f0, f1 = fs[0, s], fs[1, s]
    mine = part_rows(z, row)
    copies = [pltpu.make_async_copy(a, b, sems.at[j]) for j, (a, b) in enumerate(zip(held, outs))]
    for ref, queue in zip(held, (fwd, bwd, mir, stash)):
        ref[...] = queue[...]

    @pl.when(s < z.sections - 1)
    def _():
        held[1][bs[0, later]] = grad_in[mine, :]

    copies[1].start()

    @pl.when(s < z.sections // 2)
    def _():
        held[2][bs[0, partner]] = skip_in[mine, :]

    copies[2].start()
    values = [unfolded(piece[piece.shape[0] - z.local // 2 :, :], 2) for piece in pieces]

    def joined(at):
        shares = [value[:, at : at + w] for value in values]
        return side_by_side(all_shares(z, shares[0], shares[1:], row)).astype(BF)

    fwd_in = joined(w)

    @pl.when(s > 0)
    def _():
        held[0][fs[0, prior]] = fwd_in

    copies[0].start()
    held[3][2 * f0] = fwd[f0]
    held[3][2 * f0 + 1] = joined(0)
    held[3][2 * f1] = fwd[f1]

    @pl.when(jnp.logical_and(s > 0, fs[0, prior] == f1))
    def _():
        held[3][2 * f1] = fwd_in

    copies[3].start()
    for copy in copies:
        copy.wait()


def finish(z, fs, bs, *refs):
    n = z.parts
    out1, i1, fwd1, mir1 = refs[4:8]
    rows0, grads1 = refs[8 : n + 8], refs[n + 8 : 2 * n + 8]
    fwd_out, bwd_out, mir_out, stash_out, emitted = refs[2 * n + 8 : 2 * n + 13]
    out0, skip, grads, sems = refs[2 * n + 13 :]
    s, row = where_am_i()
    c = z.channels
    prior, later = jnp.maximum(s - 1, 0), jnp.minimum(s + 1, z.sections - 1)
    partner = z.sections - 1 - s
    encoder, has_prior, has_later = s < z.sections // 2, s > 0, s < z.sections - 1
    first = jnp.where(encoder, bs[0, partner], fs[0, partner])
    second = jnp.where(encoder, bs[1, partner], fs[1, partner])
    skip_stays = jnp.logical_and(jnp.logical_not(encoder), first != second)

    def put(source, place, j):
        return pltpu.make_async_copy(source, place, sems.at[j])

    always = [
        put(out1, emitted.at[1], 0),
        put(i1, stash_out.at[2 * fs[1, s] + 1], 1),
        put(mir1, mir_out.at[second], 2),
        put(out0, emitted.at[0], 3),
    ]
    for copy in always[:3]:
        copy.start()
    onward, back = put(fwd1, fwd_out.at[fs[1, prior]], 4), put(grads, bwd_out.at[bs[1, later]], 5)
    aside = put(skip, mir_out.at[first], 6)
    pl.when(has_prior)(onward.start)
    pieces = [unfold(z, piece) for piece in grads1]
    grads[...] = side_by_side(all_shares(z, pieces[0], pieces[1:], row)).astype(BF)
    pl.when(has_later)(back.start)
    pieces = [piece[...].astype(F32) for piece in rows0]
    out0[...] = sum(piece[:, :c] for piece in pieces).astype(BF)
    always[3].start()
    shares = [piece[:, c:] for piece in pieces]
    skip[...] = side_by_side(all_shares(z, shares[0], shares[1:], row)).astype(BF)
    pl.when(skip_stays)(aside.start)
    for copy in always:
        copy.wait()
    pl.when(has_prior)(onward.wait)
    pl.when(has_later)(back.wait)
    pl.when(skip_stays)(aside.wait)


def add_taps(z, act, pad, before, store):
    turned = jnp.transpose(act[...].astype(F32)).astype(BF)
    for tap in range(9):
        a, b = divmod(tap, 3)
        at = (2 - a) * z.cols
        moved = pad[2 - b, at : at + z.cells, :]
        store(tap, before(tap) + jnp.dot(turned, moved, preferred_element_type=F32))


def kernel_grads_add(z, start, acc, act, pad, out):
    def store(tap, value):
        out[tap] = value

    add_taps(z, act, pad, lambda tap: acc[start + tap], store)


def kernel_grads_last(z, total, other, act, pad, token, out, held, sems):
    token[...] = jnp.zeros_like(token)
    copies = [pltpu.make_async_copy(other, out.at[9:], sems.at[9])]
    copies[0].start()

    def store(tap, value):
        held[tap] = value
        copies.append(pltpu.make_async_copy(held.at[tap], out.at[tap], sems.at[tap]))
        copies[-1].start()

    add_taps(z, act, pad, lambda tap: total[tap], store)
    for copy in copies:
        copy.wait()


def per_device(fwd_queue, bwd_queue, mirror_queue, stash, weights, grad_acc, fwd_slot, bwd_slot):
    sections, n = lax.axis_size("section"), lax.axis_size("row")
    z = Sizes(fwd_queue[0], sections, n)
    slots = fwd_queue.shape[1]
    c, w, local, cells = z.channels, z.share, z.local, z.cells
    fwd, bwd, mir = (x.reshape(slots, local, c) for x in (fwd_queue, bwd_queue, mirror_queue))
    kept = stash.reshape(2 * slots, local, c)
    kernels = weights.reshape(18 * w, c)
    acc = grad_acc.reshape(18, w, c)
    fs, bs = fwd_slot.T, bwd_slot.T
    fold_shape, wide = (cells // FOLD, FOLD * w), (cells, c)
    half = (cells, w)

    def with_shares(k):
        return ((cells + k * local) // FOLD, FOLD * w)

    padded = (3, cells + 2 * z.cols, c)

    def move(x, d, step):
        route = [
            (s * n + r, step(s) * n + (r + d) % n) for s in range(sections) for r in range(n)
        ]
        return lax.ppermute(x, ("section", "row"), route)

    across = functools.partial(move, step=lambda s: s)
    onward = functools.partial(move, step=lambda s: (s + 1) % sections)
    backward = functools.partial(move, step=lambda s: (s - 1) % sections)
    crossed = functools.partial(move, step=lambda s: (sections - s) % sections)
    mirrored = functools.partial(move, step=lambda s: sections - 1 - s)

    def run(body, scalars, arrays, outs, scratch=(), **options):
        return call(
            functools.partial(body, z), body.__name__, scalars, arrays, outs, scratch, **options
        )

    def exchange(pieces):
        return [pieces[0]] + [across(piece, d) for d, piece in enumerate(pieces[1:], 1)]

    narrow_pad = pad_shapes(z, w)
    wide_line = pltpu.VMEM((cells + 16, c), F32)
    queues = (fwd, bwd, mir, kept)
    rows = (local, c)
    sems = pltpu.SemaphoreType.DMA
    packed = run(
        pack_first,
        (),
        (fs, bs, *queues),
        [((local // FOLD, FOLD * w), BF)] * n
        + [(x.shape, BF) for x in queues],
        [pltpu.SMEM(fs.shape, jnp.int32)] * 2 + [sems((6,))],
        remote=6,
    )
    inputs, held = exchange(packed[:n]), packed[n:]

    packed = run(
        pack_later,
        (),
        (fs, bs, *held),
        [((local, 2 * w + c), BF)] * n
        + [((k * (local // FOLD), FOLD * w), BF) for k in (2, 2, n, 1) for _ in range(n)],
        [pltpu.SMEM(fs.shape, jnp.int32)] * 2 + [sems((2,))],
        remote=2,
        after=(inputs[0],),
    )
    pieces, heads, nexts, grads, lasts = (packed[j * n : (j + 1) * n] for j in range(5))
    first = exchange(held_until(pieces, inputs))

    own, h0, *sends = run(
        first_forward,
        (),
        (*inputs, *heads, kernels),
        [(half, F32), (half, BF)] + [(with_shares(2), BF)] * (n - 1),
        narrow_pad,
    )
    sums = [across(x, d) for d, x in enumerate(sends, 1)]
    q0, q_send, g_pad0, act_i0, *sends = run(
        first_backward,
        (),
        (*first, *nexts, kernels),
        [(half, BF), (fold_shape, BF), (padded, BF), (half, BF)]
        + [(with_shares(2), BF)] * (n - 1),
        [pltpu.VMEM(half, BF), pltpu.VMEM(wide, BF), wide_line],
        after=(own,),
    )
    q_received = [across(x, d) for d, x in enumerate(sends, 1)]
    skip_in = mirrored(q_send, 0)

    def add_grads(start, total, act, pad, after):
        [out] = call(
            functools.partial(kernel_grads_add, z, start),
            f"kernel_grads_add_{start}",
            (),
            (total, act, pad),
            [((9, w, c), F32)],
            after=after,
        )
        return out

    sum_i = add_grads(9, acc, act_i0, g_pad0, (q0,))
    i0, full0, *sends = run(
        second_forward,
        (),
        (own, *sums, h0, *first, kernels),
        [(half, BF), (wide, BF)] + [(fold_shape, BF)] * n,
        [pltpu.VMEM(half, BF), pltpu.VMEM(wide, F32)] + narrow_pad,
        after=(sum_i,),
    )
    fwd_in = [onward(x, d) for d, x in enumerate(sends)]
    dh_send, f_pad0, act_h0, *relays = run(
        second_backward,
        (),
        (q0, *q_received, g_pad0, heads[0], *sums, skip_in, *grads, kernels),
        [(fold_shape, BF), (padded, BF), (half, BF)] + [(with_shares(n), BF)] * (n - 1),
        [pltpu.VMEM(half, BF), wide_line],
        after=(i0,),
    )
    dh_in = [backward(dh_send, d) for d in range(n)]
    relayed = [across(x, d) for d, x in enumerate(relays, 1)]

    own, h1, arrived, turned, *sends = run(
        later_forward,
        (fs,),
        (*fwd_in, nexts[0], *q_received, *lasts, kernels),
        [(half, F32), (half, BF), (half, BF), (fold_shape, BF)]
        + [(with_shares(1), BF)] * (n - 1),
        narrow_pad,
        after=(dh_send,),
    )
    received = [across(x, d) for d, x in enumerate(sends, 1)]
    mir_in = crossed(turned, 0)
    sum_h = add_grads(0, acc, act_h0, f_pad0, (own,))
    q1, g_pad1, act_i1, grad_in, skip_full, rows_own, *sends = run(
        later_backward,
        (fs, bs),
        (*dh_in, skip_in, *relayed, grads[0], nexts[0], *q_received, i0, arrived, kernels),
        [(half, BF), (padded, BF), (half, BF), (wide, BF), (wide, BF), ((local // 2, 4 * w), BF)]
        + [((cells // FOLD + local // 2, FOLD * w), BF)] * (n - 1),
        [pltpu.VMEM(fold_shape, BF), pltpu.VMEM(half, BF), pltpu.VMEM((n, *half), BF), wide_line],
        after=(sum_h,),
    )
    q_received = [across(x, d) for d, x in enumerate(sends, 1)]
    sends = run(
        last_forward,
        (fs,),
        (own, *received, h1, lasts[0], mir_in, kernels),
        [((local, c + w), BF)] * n,
        [pltpu.VMEM(half, BF), pltpu.VMEM(half, BF), pltpu.VMEM(wide, F32)] + narrow_pad,
        after=(q1,),
    )
    rows1 = exchange(sends)
    part_i = add_grads(0, sum_i, act_i1, g_pad1, (sends[0],))
    packed = run(
        pack_rows,
        (),
        (full0, mir_in),
        [((local, c + w), BF)] * n,
        [pltpu.VMEM(half, BF)],
        after=(part_i,),
    )
    token, *written = run(
        write_queues,
        (fs, bs),
        (*held, grad_in, skip_full, rows_own, *q_received),
        [((8, 128), F32)] + [(x.shape, BF) for x in queues],
        [pltpu.VMEM(x.shape, BF) for x in queues] + [sems((4,))],
        far_outs=4,
        after=(packed[0],),
    )
    rows0 = exchange(held_until(packed, (rows1, token)))
    out1, mirror1, i1 = run(
        add_rows,
        (),
        (*rows1, q1, *q_received),
        [(rows, BF)] * 3,
        [pltpu.VMEM(wide, F32)],
        after=(token,),
    )
    fwd1, mir1 = onward(out1, 0), mirrored(mirror1, 0)
    *dh_sends, f_pad1, act_h1 = run(
        last_backward,
        (fs, bs),
        (q1, *q_received, g_pad1, heads[0], *sums, h0, kernels),
        [((local // FOLD, FOLD * w), BF)] * n + [(padded, BF), (half, BF)],
        [pltpu.VMEM(half, BF), pltpu.VMEM(half, BF), wide_line],
        after=(out1,),
    )
    dh1_in = [backward(x, d) for d, x in enumerate(dh_sends)]
    token, grad_total = run(
        kernel_grads_last,
        (),
        (sum_h, part_i, act_h1, f_pad1),
        [((8, 128), F32), ((18, w, c), F32)],
        [pltpu.VMEM((9, w, c), F32), sems((10,))],
        far_outs=1,
    )
    fwd_out, bwd_out, mir_out, stash_out, emitted = run(
        finish,
        (fs, bs),
        (*written, out1, i1, fwd1, mir1, *rows0, *dh1_in),
        [(x.shape, BF) for x in queues] + [((TICKS, local, c), BF)],
        [pltpu.VMEM(rows, BF)] * 3 + [sems((7,))],
        remote=4,
        far_outs=5,
        aliases={j + 2: j for j in range(4)},
        after=(token,),
    )
    return (
        fwd_out.reshape(fwd_queue.shape),
        bwd_out.reshape(bwd_queue.shape),
        mir_out.reshape(mirror_queue.shape),
        stash_out.reshape(stash.shape),
        grad_total.reshape(grad_acc.shape),
        emitted.reshape((1, TICKS) + fwd_queue.shape[2:]),
    )


def solution(mesh):
    return jax.shard_map(
        per_device,
        mesh=mesh,
        in_specs=(
            P("section", None, "row", None, None),
            P("section", None, "row", None, None),
            P("section", None, "row", None, None),
            P("section", None, None, "row", None, None),
            P("section", None, None, None, "row", None),
            P("section", None, None, None, "row", None),
            P(),
            P(),
        ),
        out_specs=(
            P("section", None, "row", None, None),
            P("section", None, "row", None, None),
            P("section", None, "row", None, None),
            P("section", None, None, "row", None, None),
            P("section", None, None, None, "row", None),
            P("section", None, "row", None, None),
        ),
        check_vma=False,
    )
```

```python
import functools

import jax
import jax.numpy as jnp
from jax import lax
from jax.experimental import pallas as pl
from jax.experimental.pallas import tpu as pltpu
from jax.sharding import PartitionSpec as P

GROUPS = 32
TICKS = 2
FOLD = 4
EPSILON = 1e-05
BF, F32 = jnp.bfloat16, jnp.float32
VMEM_LIMIT = 24 * 2**20


class Sizes:
    def __init__(self, queue, sections, rows):
        self.sections, self.parts = sections, rows
        self.cols = queue.shape[2]
        self.channels = queue.shape[3]
        self.local = queue.shape[1] * queue.shape[2]
        self.cells = self.local * rows
        self.share = self.channels // rows
        self.group = self.channels // GROUPS
        self.count = self.cells * self.group


def where_am_i():
    return lax.axis_index("section"), lax.axis_index("row")


def share_of(z, value, part):
    value = value.astype(F32)
    out = value[:, : z.share]
    for j in range(1, z.parts):
        out = jnp.where(part == j, value[:, j * z.share : (j + 1) * z.share], out)
    return out


def all_shares(z, own, others, row):
    out = []
    for j in range(z.parts):
        value = own
        for d in range(1, z.parts):
            value = jnp.where(lax.rem(row + z.parts - d, z.parts) == j, others[d - 1], value)
        out.append(value)
    return out


def side_by_side(values):
    return jnp.concatenate([value.astype(F32) for value in values], axis=1)


def folded(value, blocks):
    rows = value.shape[0] // blocks
    return side_by_side([value[j * rows : (j + 1) * rows] for j in range(blocks)])


def unfolded(value, blocks):
    value, width = value.astype(F32), value.shape[1] // blocks
    return jnp.concatenate([value[:, j * width : (j + 1) * width] for j in range(blocks)], axis=0)


def fold(z, ref, value):
    ref[...] = folded(value, FOLD).astype(BF)


def unfold(z, ref):
    return unfolded(ref[...], FOLD)


def source(z, row, d):
    return lax.rem(row + z.parts - d, z.parts)


def target(z, row, d):
    return lax.rem(row + d, z.parts)


def part_rows(z, part):
    return pl.ds(pl.multiple_of(part * z.local, z.local), z.local)


def assemble(z, ref, pieces, row, start, width):
    for d, piece in enumerate(pieces):
        value = (piece if isinstance(piece, jax.Array) else piece[...]).astype(F32)
        value = value[:, start : start + width]
        ref[part_rows(z, source(z, row, d)), :] = value.astype(BF)


def group_sums(z, first, second):
    width = first.shape[1]
    line = lax.broadcasted_iota(jnp.int32, (8, width), 0)
    both = jnp.where(line == 0, first, jnp.where(line == 1, second, 0.0))
    across = lax.broadcasted_iota(jnp.int32, (width, width), 1).astype(F32)
    down = lax.broadcasted_iota(jnp.int32, (width, width), 0).astype(F32)
    same = jnp.floor((across + 0.5) * (1.0 / z.group)) == jnp.floor((down + 0.5) * (1.0 / z.group))
    sums = jnp.dot(
        both, same.astype(F32), precision=lax.Precision.HIGHEST, preferred_element_type=F32
    )
    return sums[0:1], sums[1:2]


def normalize(z, x):
    total, square = group_sums(
        z, jnp.sum(x, axis=0, keepdims=True), jnp.sum(x * x, axis=0, keepdims=True)
    )
    center = total / z.count
    factor = lax.rsqrt(square / z.count - center * center + EPSILON)
    return (x - center) * factor, factor


def sigmoid(y):
    return 1.0 / (1.0 + jnp.exp(-y))


def norm_back(z, y, factor, logistic, upstream):
    e = upstream * logistic * (1.0 + y * (1.0 - logistic))
    first, second = group_sums(
        z, jnp.sum(e, axis=0, keepdims=True), jnp.sum(e * y, axis=0, keepdims=True)
    )
    return factor * (e - first / z.count - y * (second / z.count))


def spread(z, x, line_ref, pad_ref):
    cells, cols = z.cells, z.cols
    width = x.shape[1]
    line_ref[8 : 8 + cells, :] = x
    column = lax.rem(lax.broadcasted_iota(jnp.int32, (cells, 1), 0), cols)
    edge = jnp.zeros((cols, width), BF)
    for b in range(3):
        pad_ref[b, :cols, :] = edge
        pad_ref[b, cols + cells :, :] = edge
    pad_ref[1, cols : cols + cells, :] = x.astype(BF)
    left = jnp.where(column > 0, line_ref[7 : 7 + cells, :], 0.0)
    pad_ref[0, cols : cols + cells, :] = left.astype(BF)
    right = jnp.where(column < cols - 1, line_ref[9 : 9 + cells, :], 0.0)
    pad_ref[2, cols : cols + cells, :] = right.astype(BF)


def spread_wide(z, x, line_ref, pad_ref):
    cells, cols = z.cells, z.cols
    line_ref[8 : 8 + cells, :] = x
    column = lax.rem(lax.broadcasted_iota(jnp.int32, (cells, 1), 0), cols)
    edge = jnp.zeros((cols, 3 * z.share), BF)
    pad_ref[:cols, :] = edge
    pad_ref[cols + cells :, :] = edge
    left = jnp.where(column > 0, line_ref[7 : 7 + cells, :], 0.0)
    right = jnp.where(column < cols - 1, line_ref[9 : 9 + cells, :], 0.0)
    pad_ref[cols : cols + cells, :] = side_by_side([left, x, right]).astype(BF)


def convolve(z, pad_ref, kernel_ref, which):
    total = None
    for a in range(3):
        first = (9 * which + 3 * a) * z.share
        term = jnp.dot(
            pad_ref[a * z.cols : a * z.cols + z.cells, :],
            kernel_ref[first : first + 3 * z.share, :],
            preferred_element_type=F32,
        )
        total = term if total is None else total + term
    return total


def convolve_back(z, pad_ref, kernel_ref, which):
    total = None
    for a in range(3):
        for b in range(3):
            first = (9 * which + 3 * (2 - a) + 2 - b) * z.share
            term = lax.dot_general(
                pad_ref[b, a * z.cols : a * z.cols + z.cells, :],
                kernel_ref[first : first + z.share, :],
                (((1,), (1,)), ((), ())),
                preferred_element_type=F32,
            )
            total = term if total is None else total + term
    return total


def pad_shapes(z, width):
    return [
        pltpu.VMEM((z.cells + 16, width), F32),
        pltpu.VMEM((z.cells + 2 * z.cols, 3 * width), BF),
    ]


def call(body, name, scalars, arrays, outs, scratch=(), after=(), remote=0, far_outs=0, aliases=None):
    near, far = pl.BlockSpec(memory_space=pltpu.VMEM), pl.BlockSpec(memory_space=pltpu.HBM)

    def inner(*refs):
        given = len(scalars) + len(arrays)
        body(*refs[:given], *refs[given + len(after) :])

    arrays = [
        pltpu.with_memory_space_constraint(x, pltpu.HBM) if j < remote else x
        for j, x in enumerate(arrays)
    ]
    near_outs = len(outs) - far_outs
    return pl.pallas_call(
        inner,
        name=name,
        out_shape=[
            jax.ShapeDtypeStruct(shape, dtype) if j < near_outs else pltpu.HBM(shape, dtype)
            for j, (shape, dtype) in enumerate(outs)
        ],
        in_specs=[pl.BlockSpec(memory_space=pltpu.SMEM)] * len(scalars)
        + [far] * remote
        + [near] * (len(arrays) - remote)
        + [pl.BlockSpec(memory_space=pl.ANY)] * len(after),
        out_specs=[near] * near_outs + [far] * far_outs,
        scratch_shapes=list(scratch),
        input_output_aliases=aliases or {},
        compiler_params=pltpu.CompilerParams(vmem_limit_bytes=VMEM_LIMIT),
        cost_estimate=pl.CostEstimate(flops=1, bytes_accessed=1, transcendentals=0),
    )(*scalars, *arrays, *after)


def held_until(values, earlier):
    return lax.optimization_barrier((tuple(values), earlier))[0]


def fetch(pairs, sems):
    copies = [pltpu.make_async_copy(a, b, sems.at[j]) for j, (a, b) in enumerate(pairs)]
    for copy in copies:
        copy.start()
    for copy in copies:
        copy.wait()


def pack_first(z, fs_far, bs_far, fwd_far, bwd_far, mir_far, stash_far, *refs):
    n = z.parts
    heads = refs[:n]
    fwd, bwd, mir, stash, fs, bs, sems = refs[n:]
    fetch(
        [
            (fs_far, fs),
            (bs_far, bs),
            (fwd_far, fwd),
            (bwd_far, bwd),
            (mir_far, mir),
            (stash_far, stash),
        ],
        sems,
    )
    s, row = where_am_i()
    h = fwd[fs[0, s]]
    for d in range(n):
        fold(z, heads[d], share_of(z, h, target(z, row, d)))


def taken_back(z, bs, s):
    later, partner = jnp.minimum(s + 1, z.sections - 1), z.sections - 1 - s
    return (
        jnp.logical_and(s < z.sections - 1, bs[0, later] == bs[1, s]),
        jnp.logical_and(s < z.sections // 2, bs[0, partner] == bs[1, s]),
    )


def pack_later(z, fs_far, bs_far, fwd, bwd, mir, stash, *refs):
    n = z.parts
    pieces, groups = refs[:n], [refs[j * n : (j + 1) * n] for j in range(1, 5)]
    fs, bs, sems = refs[5 * n :]
    fetch([(fs_far, fs), (bs_far, bs)], sems)
    s, row = where_am_i()
    f1, b1 = fs[1, s], bs[1, s]
    grad_taken, skip_taken = taken_back(z, bs, s)
    skip_kept = jnp.logical_and(s < z.sections // 2, jnp.logical_not(skip_taken))
    kept = jnp.where(grad_taken, 0.0, bwd[b1].astype(F32))
    kept = kept + jnp.where(skip_kept, mir[b1].astype(F32), 0.0)
    f0, b0 = fs[0, s], bs[0, s]
    g = bwd[b0].astype(F32) + jnp.where(s < z.sections // 2, mir[b0].astype(F32), 0.0)
    for d, piece in enumerate(pieces):
        part = target(z, row, d)
        shares = [share_of(z, stash[2 * b0 + 1], part), share_of(z, mir[f0], part)]
        piece[...] = side_by_side(shares + [g]).astype(BF)
    values = [stash[2 * b0], stash[2 * b1], fwd[f1], stash[2 * b1 + 1], mir[f1]]
    rows = z.local // FOLD
    for d in range(n):
        shares = [share_of(z, value, target(z, row, d)) for value in values]
        grads = [kept[:, j * z.share : (j + 1) * z.share] for j in range(n)]
        for outs, parts in zip(groups, (shares[:2], shares[2:4], grads, shares[4:])):
            for j, value in enumerate(parts):
                outs[d][j * rows : (j + 1) * rows, :] = folded(value, FOLD).astype(BF)


def send_partials(z, row, total, own, sends, extra):
    own[...] = share_of(z, total, row)
    for d, send in enumerate(sends, 1):
        part = folded(share_of(z, total, target(z, row, d)), FOLD).astype(BF)
        send[: part.shape[0], :] = part
        send[part.shape[0] :, :] = extra[d][...]


def first_forward(z, *refs):
    n = z.parts
    pieces, extra, kernel = refs[:n], refs[n : 2 * n], refs[2 * n]
    own, h_out = refs[2 * n + 1 : 2 * n + 3]
    sends, (line, pad) = refs[2 * n + 3 : 3 * n + 2], refs[3 * n + 2 :]
    _, row = where_am_i()
    assemble(z, h_out, [unfold(z, piece) for piece in pieces], row, 0, z.share)
    y, _ = normalize(z, h_out[...].astype(F32))
    spread_wide(z, y * sigmoid(y), line, pad)
    send_partials(z, row, convolve(z, pad, kernel, 0), own, sends, extra)


def enclosed(z, own, received, j):
    rows, base = z.local // FOLD, z.cells // FOLD
    at, there = slice(j * rows, (j + 1) * rows), slice(base + j * rows, base + (j + 1) * rows)
    return [unfolded(own[at, :], FOLD)] + [unfolded(x[there, :], FOLD) for x in received]


def later_forward(z, fs, *refs):
    n = z.parts
    arrivals, nexts, received = refs[:n], refs[n], refs[n + 1 : 2 * n]
    lasts, kernel = refs[2 * n : 3 * n], refs[3 * n]
    own, h_out, arrived, onward = refs[3 * n + 1 : 3 * n + 5]
    sends = refs[3 * n + 5 : 4 * n + 4]
    line, pad = refs[4 * n + 4 :]
    s, row = where_am_i()
    total = unfold(z, arrivals[0])
    for other in arrivals[1:]:
        total = total + unfold(z, other)
    total = total.astype(BF).astype(F32)
    arrived[...] = total.astype(BF)
    fold(z, onward, total)
    assemble(z, h_out, enclosed(z, nexts, received, 0), row, 0, z.share)
    prior = jnp.maximum(s - 1, 0)
    taken = jnp.logical_and(s > 0, fs[0, prior] == fs[1, s])
    h = jnp.where(taken, total, h_out[...].astype(F32))
    h_out[...] = h.astype(BF)
    y, _ = normalize(z, h)
    spread_wide(z, y * sigmoid(y), line, pad)
    send_partials(z, row, convolve(z, pad, kernel, 0), own, sends, lasts)


def back_through_second(z, i, g, kernel, q_out, q_send, act_out, pad, line):
    y, factor = normalize(z, i.astype(F32))
    logistic = sigmoid(y)
    act_out[...] = (y * logistic).astype(BF)
    spread(z, g, line, pad)
    q = norm_back(z, y, factor, logistic, convolve_back(z, pad, kernel, 1)).astype(BF)
    q_out[...] = q
    fold(z, q_send, q.astype(F32))


def first_backward(z, *refs):
    n = z.parts
    pieces, heads, kernel = refs[:n], refs[n : 2 * n], refs[2 * n]
    q_out, q_send, pad, act_out = refs[2 * n + 1 : 2 * n + 5]
    sends, (i_ref, g_ref, line) = refs[2 * n + 5 : 3 * n + 4], refs[3 * n + 4 :]
    _, row = where_am_i()
    assemble(z, i_ref, pieces, row, 0, z.share)
    assemble(z, g_ref, pieces, row, 2 * z.share, z.channels)
    back_through_second(
        z, i_ref[...], g_ref[...].astype(F32), kernel, q_out, q_send, act_out, pad, line
    )
    rows = z.cells // FOLD
    for d, send in enumerate(sends, 1):
        send[:rows, :] = q_send[...]
        send[rows:, :] = heads[d][...]


def later_backward(z, fs, bs, *refs):
    n = z.parts
    arrivals, mirror, received, kept = refs[:n], refs[n], refs[n + 1 : 2 * n], refs[2 * n]
    nexts, others = refs[2 * n + 1], refs[2 * n + 2 : 3 * n + 1]
    i_before, arrived, kernel = refs[3 * n + 1 : 3 * n + 4]
    q_out, pad, act_out, grad_in, skip_in = refs[3 * n + 4 : 3 * n + 9]
    rows_own, sends = refs[3 * n + 9], refs[3 * n + 10 : 4 * n + 9]
    q_send, i_ref, full, line = refs[4 * n + 9 :]
    s, row = where_am_i()
    w = z.share
    shares = [unfold(z, part) for part in arrivals]
    grad = side_by_side(all_shares(z, shares[0], shares[1:], row))
    grad_in[...] = grad.astype(BF)
    shares = [unfolded(x[: z.cells // FOLD, :], FOLD) for x in received]
    skip = side_by_side(all_shares(z, unfold(z, mirror), shares, row))
    skip_in[...] = skip.astype(BF)
    grad_taken, skip_taken = taken_back(z, bs, s)
    for j in range(n):
        assemble(z, full.at[j], enclosed(z, kept, received, j), row, 0, w)
    g = side_by_side([full[j] for j in range(n)]) + jnp.where(grad_taken, grad, 0.0)
    g = g + jnp.where(skip_taken, skip, 0.0)
    g = g.astype(BF).astype(F32)
    assemble(z, i_ref, enclosed(z, nexts, others, 1), row, 0, w)
    i = jnp.where(fs[0, s] == bs[1, s], i_before[...].astype(F32), i_ref[...].astype(F32))
    back_through_second(z, i, g, kernel, q_out, q_send, act_out, pad, line)
    for d, out in enumerate([rows_own, *sends]):
        at = part_rows(z, target(z, row, d))
        part = folded(side_by_side([i_before[at, :], arrived[at, :]]), 2).astype(BF)
        out[out.shape[0] - part.shape[0] :, :] = part
    for send in sends:
        send[: q_send.shape[0], :] = q_send[...]


def second_convolution(z, encoder, row, own, received, skip, h, kernel, i_out, full, line, pad):
    c0 = own[...]
    for other in received:
        c0 = c0 + unfolded(other[: z.cells // FOLD, :], FOLD)
    i = jnp.where(encoder, c0, skip.astype(F32)).astype(BF)
    i_out[...] = i
    y, _ = normalize(z, i.astype(F32))
    spread_wide(z, y * sigmoid(y), line, pad)
    total = convolve(z, pad, kernel, 1)
    base = h[...].astype(F32) + jnp.where(encoder, 0.0, c0)
    full[...] = total + side_by_side([jnp.where(row == j, base, 0.0) for j in range(z.parts)])


def middle(z, pad):
    return pad[1, z.cols : z.cols + z.cells, :].astype(F32)


def second_forward(z, *refs):
    n = z.parts
    own, received, h, pieces, kernel = refs[0], refs[1:n], refs[n], refs[n + 1 : 2 * n + 1], refs[2 * n + 1]
    i_out, full_out = refs[2 * n + 2 : 2 * n + 4]
    sends = refs[2 * n + 4 : 3 * n + 4]
    skip, full, line, pad = refs[3 * n + 4 :]
    s, row = where_am_i()
    encoder = s < z.sections // 2
    assemble(z, skip, pieces, row, z.share, z.share)
    second_convolution(
        z, encoder, row, own, received, skip[...], h, kernel, i_out, full, line, pad
    )
    full_out[...] = full[...].astype(BF)
    for d in range(n):
        fold(z, sends[d], share_of(z, full[...], target(z, row, d)))


def last_forward(z, fs, *refs):
    n = z.parts
    own, received, h = refs[0], refs[1:n], refs[n]
    lasts, arrived, kernel = refs[n + 1 : n + 4]
    sends = refs[n + 4 : 2 * n + 4]
    i_out, skip, full, line, pad = refs[2 * n + 4 :]
    s, row = where_am_i()
    encoder = s < z.sections // 2
    partner = z.sections - 1 - s
    assemble(z, skip, enclosed(z, lasts, received, 0), row, 0, z.share)
    now = jnp.where(
        fs[0, partner] == fs[1, s], unfold(z, arrived), skip[...].astype(F32)
    )
    second_convolution(z, encoder, row, own, received, now, h, kernel, i_out, full, line, pad)
    for d, send in enumerate(sends):
        at = part_rows(z, target(z, row, d))
        send[...] = side_by_side([full[at, :], i_out[at, :]]).astype(BF)


def joined_shares(z, own, received, row):
    others = [unfolded(other[: z.cells // FOLD, :], FOLD) for other in received]
    return side_by_side(all_shares(z, own[...].astype(F32), others, row))


def back_through_first(z, encoder, row, q, received, g_pad, h, kernel, act_out, pad, line):
    g = middle(z, g_pad)
    whole = joined_shares(z, q, received, row)
    now = jnp.where(encoder, whole, g)
    y, factor = normalize(z, h.astype(F32))
    logistic = sigmoid(y)
    act_out[...] = (y * logistic).astype(BF)
    spread(z, now, line, pad)
    back = norm_back(z, y, factor, logistic, convolve_back(z, pad, kernel, 0))
    return share_of(z, g, row) + back, whole


def second_backward(z, *refs):
    n = z.parts
    q, received, g = refs[0], refs[1:n], refs[n]
    heads, others, mirror = refs[n + 1], refs[n + 2 : 2 * n + 1], refs[2 * n + 1]
    grads, kernel = refs[2 * n + 2 : 3 * n + 2], refs[3 * n + 2]
    send, pad, act_out = refs[3 * n + 3 : 3 * n + 6]
    relays, (h, line) = refs[3 * n + 6 : 4 * n + 5], refs[4 * n + 5 :]
    s, row = where_am_i()
    for d, relay in enumerate(relays, 1):
        relay[: z.cells // FOLD, :] = mirror[...]
        relay[z.cells // FOLD :, :] = grads[d][...]
    assemble(z, h, enclosed(z, heads, others, 0), row, 0, z.share)
    value, _ = back_through_first(
        z, s < z.sections // 2, row, q, received, g, h[...], kernel, act_out, pad, line
    )
    fold(z, send, value)


def last_backward(z, fs, bs, *refs):
    n = z.parts
    q, received, g = refs[0], refs[1:n], refs[n]
    heads, others = refs[n + 1], refs[n + 2 : 2 * n + 1]
    h_before, kernel = refs[2 * n + 1 : 2 * n + 3]
    sends = refs[2 * n + 3 : 3 * n + 3]
    pad, act_out, h, value, line = refs[3 * n + 3 :]
    s, row = where_am_i()
    assemble(z, h, enclosed(z, heads, others, 1), row, 0, z.share)
    now = jnp.where(fs[0, s] == bs[1, s], h_before[...], h[...])
    result, _ = back_through_first(
        z, s < z.sections // 2, row, q, received, g, now, kernel, act_out, pad, line
    )
    value[...] = result.astype(BF)
    for d, send in enumerate(sends):
        fold(z, send, value[part_rows(z, target(z, row, d)), :])


def pack_rows(z, *refs):
    n = z.parts
    full, mirror = refs[:2]
    sends, skip = refs[2 : n + 2], refs[n + 2]
    _, row = where_am_i()
    skip[...] = unfold(z, mirror).astype(BF)
    for d, send in enumerate(sends):
        at = part_rows(z, target(z, row, d))
        send[...] = side_by_side([ref[at, :] for ref in (full, skip)]).astype(BF)


def add_rows(z, *refs):
    n = z.parts
    pieces, q, received = refs[:n], refs[n], refs[n + 1 : 2 * n]
    out, mirror, i_rows, whole = refs[2 * n :]
    s, row = where_am_i()
    c = z.channels
    whole[...] = joined_shares(z, q, received, row)
    values = [piece[...].astype(F32) for piece in pieces]
    total = sum(value[:, :c] for value in values)
    out[...] = total.astype(BF)
    mine = whole[part_rows(z, row), :]
    mirror[...] = jnp.where(s < z.sections // 2, total, mine).astype(BF)
    shares = all_shares(z, values[0][:, c:], [value[:, c:] for value in values[1:]], row)
    i_rows[...] = side_by_side(shares).astype(BF)


def write_queues(z, fs, bs, *refs):
    n = z.parts
    fwd, bwd, mir, stash, grad_in, skip_in = refs[:6]
    pieces = refs[6 : n + 6]
    token, outs, held = refs[n + 6], refs[n + 7 : n + 11], refs[n + 11 : n + 15]
    sems = refs[n + 15]
    token[...] = jnp.zeros_like(token)
    s, row = where_am_i()
    w = z.share
    prior, later = jnp.maximum(s - 1, 0), jnp.minimum(s + 1, z.sections - 1)
    partner = z.sections - 1 - s
    f0, f1 = fs[0, s], fs[1, s]
    mine = part_rows(z, row)
    copies = [pltpu.make_async_copy(a, b, sems.at[j]) for j, (a, b) in enumerate(zip(held, outs))]
    for ref, queue in zip(held, (fwd, bwd, mir, stash)):
        ref[...] = queue[...]

    @pl.when(s < z.sections - 1)
    def _():
        held[1][bs[0, later]] = grad_in[mine, :]

    copies[1].start()

    @pl.when(s < z.sections // 2)
    def _():
        held[2][bs[0, partner]] = skip_in[mine, :]

    copies[2].start()
    values = [unfolded(piece[piece.shape[0] - z.local // 2 :, :], 2) for piece in pieces]

    def joined(at):
        shares = [value[:, at : at + w] for value in values]
        return side_by_side(all_shares(z, shares[0], shares[1:], row)).astype(BF)

    fwd_in = joined(w)

    @pl.when(s > 0)
    def _():
        held[0][fs[0, prior]] = fwd_in

    copies[0].start()
    held[3][2 * f0] = fwd[f0]
    held[3][2 * f0 + 1] = joined(0)
    held[3][2 * f1] = fwd[f1]

    @pl.when(jnp.logical_and(s > 0, fs[0, prior] == f1))
    def _():
        held[3][2 * f1] = fwd_in

    copies[3].start()
    for copy in copies:
        copy.wait()


def finish(z, fs, bs, *refs):
    n = z.parts
    out1, i1, fwd1, mir1 = refs[4:8]
    rows0, grads1 = refs[8 : n + 8], refs[n + 8 : 2 * n + 8]
    fwd_out, bwd_out, mir_out, stash_out, emitted = refs[2 * n + 8 : 2 * n + 13]
    out0, skip, grads, sems = refs[2 * n + 13 :]
    s, row = where_am_i()
    c = z.channels
    prior, later = jnp.maximum(s - 1, 0), jnp.minimum(s + 1, z.sections - 1)
    partner = z.sections - 1 - s
    encoder, has_prior, has_later = s < z.sections // 2, s > 0, s < z.sections - 1
    first = jnp.where(encoder, bs[0, partner], fs[0, partner])
    second = jnp.where(encoder, bs[1, partner], fs[1, partner])
    skip_stays = jnp.logical_and(jnp.logical_not(encoder), first != second)

    def put(source, place, j):
        return pltpu.make_async_copy(source, place, sems.at[j])

    always = [
        put(out1, emitted.at[1], 0),
        put(i1, stash_out.at[2 * fs[1, s] + 1], 1),
        put(mir1, mir_out.at[second], 2),
        put(out0, emitted.at[0], 3),
    ]
    for copy in always[:3]:
        copy.start()
    onward, back = put(fwd1, fwd_out.at[fs[1, prior]], 4), put(grads, bwd_out.at[bs[1, later]], 5)
    aside = put(skip, mir_out.at[first], 6)
    pl.when(has_prior)(onward.start)
    pieces = [unfold(z, piece) for piece in grads1]
    grads[...] = side_by_side(all_shares(z, pieces[0], pieces[1:], row)).astype(BF)
    pl.when(has_later)(back.start)
    pieces = [piece[...].astype(F32) for piece in rows0]
    out0[...] = sum(piece[:, :c] for piece in pieces).astype(BF)
    always[3].start()
    shares = [piece[:, c:] for piece in pieces]
    skip[...] = side_by_side(all_shares(z, shares[0], shares[1:], row)).astype(BF)
    pl.when(skip_stays)(aside.start)
    for copy in always:
        copy.wait()
    pl.when(has_prior)(onward.wait)
    pl.when(has_later)(back.wait)
    pl.when(skip_stays)(aside.wait)


def add_taps(z, act, pad, before, store):
    turned = jnp.transpose(act[...].astype(F32)).astype(BF)
    for tap in range(9):
        a, b = divmod(tap, 3)
        at = (2 - a) * z.cols
        moved = pad[2 - b, at : at + z.cells, :]
        store(tap, before(tap) + jnp.dot(turned, moved, preferred_element_type=F32))


def kernel_grads_add(z, start, acc, act, pad, out):
    def store(tap, value):
        out[tap] = value

    add_taps(z, act, pad, lambda tap: acc[start + tap], store)


def kernel_grads_last(z, total, other, act, pad, token, out, held, sems):
    token[...] = jnp.zeros_like(token)
    copies = [pltpu.make_async_copy(other, out.at[9:], sems.at[9])]
    copies[0].start()

    def store(tap, value):
        held[tap] = value
        copies.append(pltpu.make_async_copy(held.at[tap], out.at[tap], sems.at[tap]))
        copies[-1].start()

    add_taps(z, act, pad, lambda tap: total[tap], store)
    for copy in copies:
        copy.wait()


def per_device(fwd_queue, bwd_queue, mirror_queue, stash, weights, grad_acc, fwd_slot, bwd_slot):
    sections, n = lax.axis_size("section"), lax.axis_size("row")
    z = Sizes(fwd_queue[0], sections, n)
    slots = fwd_queue.shape[1]
    c, w, local, cells = z.channels, z.share, z.local, z.cells
    fwd, bwd, mir = (x.reshape(slots, local, c) for x in (fwd_queue, bwd_queue, mirror_queue))
    kept = stash.reshape(2 * slots, local, c)
    kernels = weights.reshape(18 * w, c)
    acc = grad_acc.reshape(18, w, c)
    fs, bs = fwd_slot.T, bwd_slot.T
    fold_shape, wide = (cells // FOLD, FOLD * w), (cells, c)
    half = (cells, w)

    def with_shares(k):
        return ((cells + k * local) // FOLD, FOLD * w)

    padded = (3, cells + 2 * z.cols, c)

    def move(x, d, step):
        route = [
            (s * n + r, step(s) * n + (r + d) % n) for s in range(sections) for r in range(n)
        ]
        return lax.ppermute(x, ("section", "row"), route)

    across = functools.partial(move, step=lambda s: s)
    onward = functools.partial(move, step=lambda s: (s + 1) % sections)
    backward = functools.partial(move, step=lambda s: (s - 1) % sections)
    crossed = functools.partial(move, step=lambda s: (sections - s) % sections)
    mirrored = functools.partial(move, step=lambda s: sections - 1 - s)

    def run(body, scalars, arrays, outs, scratch=(), **options):
        return call(
            functools.partial(body, z), body.__name__, scalars, arrays, outs, scratch, **options
        )

    def exchange(pieces):
        return [pieces[0]] + [across(piece, d) for d, piece in enumerate(pieces[1:], 1)]

    narrow_pad = pad_shapes(z, w)
    wide_line = pltpu.VMEM((cells + 16, c), F32)
    queues = (fwd, bwd, mir, kept)
    rows = (local, c)
    sems = pltpu.SemaphoreType.DMA
    packed = run(
        pack_first,
        (),
        (fs, bs, *queues),
        [((local // FOLD, FOLD * w), BF)] * n
        + [(x.shape, BF) for x in queues],
        [pltpu.SMEM(fs.shape, jnp.int32)] * 2 + [sems((6,))],
        remote=6,
    )
    inputs, held = exchange(packed[:n]), packed[n:]

    packed = run(
        pack_later,
        (),
        (fs, bs, *held),
        [((local, 2 * w + c), BF)] * n
        + [((k * (local // FOLD), FOLD * w), BF) for k in (2, 2, n, 1) for _ in range(n)],
        [pltpu.SMEM(fs.shape, jnp.int32)] * 2 + [sems((2,))],
        remote=2,
        after=(inputs[0],),
    )
    pieces, heads, nexts, grads, lasts = (packed[j * n : (j + 1) * n] for j in range(5))
    first = exchange(held_until(pieces, inputs))

    own, h0, *sends = run(
        first_forward,
        (),
        (*inputs, *heads, kernels),
        [(half, F32), (half, BF)] + [(with_shares(2), BF)] * (n - 1),
        narrow_pad,
    )
    sums = [across(x, d) for d, x in enumerate(sends, 1)]
    q0, q_send, g_pad0, act_i0, *sends = run(
        first_backward,
        (),
        (*first, *nexts, kernels),
        [(half, BF), (fold_shape, BF), (padded, BF), (half, BF)]
        + [(with_shares(2), BF)] * (n - 1),
        [pltpu.VMEM(half, BF), pltpu.VMEM(wide, BF), wide_line],
        after=(own,),
    )
    q_received = [across(x, d) for d, x in enumerate(sends, 1)]
    skip_in = mirrored(q_send, 0)

    def add_grads(start, total, act, pad, after):
        [out] = call(
            functools.partial(kernel_grads_add, z, start),
            f"kernel_grads_add_{start}",
            (),
            (total, act, pad),
            [((9, w, c), F32)],
            after=after,
        )
        return out

    sum_i = add_grads(9, acc, act_i0, g_pad0, (q0,))
    i0, full0, *sends = run(
        second_forward,
        (),
        (own, *sums, h0, *first, kernels),
        [(half, BF), (wide, BF)] + [(fold_shape, BF)] * n,
        [pltpu.VMEM(half, BF), pltpu.VMEM(wide, F32)] + narrow_pad,
        after=(sum_i,),
    )
    fwd_in = [onward(x, d) for d, x in enumerate(sends)]
    dh_send, f_pad0, act_h0, *relays = run(
        second_backward,
        (),
        (q0, *q_received, g_pad0, heads[0], *sums, skip_in, *grads, kernels),
        [(fold_shape, BF), (padded, BF), (half, BF)] + [(with_shares(n), BF)] * (n - 1),
        [pltpu.VMEM(half, BF), wide_line],
        after=(i0,),
    )
    dh_in = [backward(dh_send, d) for d in range(n)]
    relayed = [across(x, d) for d, x in enumerate(relays, 1)]

    own, h1, arrived, turned, *sends = run(
        later_forward,
        (fs,),
        (*fwd_in, nexts[0], *q_received, *lasts, kernels),
        [(half, F32), (half, BF), (half, BF), (fold_shape, BF)]
        + [(with_shares(1), BF)] * (n - 1),
        narrow_pad,
        after=(dh_send,),
    )
    received = [across(x, d) for d, x in enumerate(sends, 1)]
    mir_in = crossed(turned, 0)
    sum_h = add_grads(0, acc, act_h0, f_pad0, (own,))
    q1, g_pad1, act_i1, grad_in, skip_full, rows_own, *sends = run(
        later_backward,
        (fs, bs),
        (*dh_in, skip_in, *relayed, grads[0], nexts[0], *q_received, i0, arrived, kernels),
        [(half, BF), (padded, BF), (half, BF), (wide, BF), (wide, BF), ((local // 2, 4 * w), BF)]
        + [((cells // FOLD + local // 2, FOLD * w), BF)] * (n - 1),
        [pltpu.VMEM(fold_shape, BF), pltpu.VMEM(half, BF), pltpu.VMEM((n, *half), BF), wide_line],
        after=(sum_h,),
    )
    q_received = [across(x, d) for d, x in enumerate(sends, 1)]
    sends = run(
        last_forward,
        (fs,),
        (own, *received, h1, lasts[0], mir_in, kernels),
        [((local, c + w), BF)] * n,
        [pltpu.VMEM(half, BF), pltpu.VMEM(half, BF), pltpu.VMEM(wide, F32)] + narrow_pad,
        after=(q1,),
    )
    rows1 = exchange(sends)
    part_i = add_grads(0, sum_i, act_i1, g_pad1, (sends[0],))
    packed = run(
        pack_rows,
        (),
        (full0, mir_in),
        [((local, c + w), BF)] * n,
        [pltpu.VMEM(half, BF)],
        after=(part_i,),
    )
    token, *written = run(
        write_queues,
        (fs, bs),
        (*held, grad_in, skip_full, rows_own, *q_received),
        [((8, 128), F32)] + [(x.shape, BF) for x in queues],
        [pltpu.VMEM(x.shape, BF) for x in queues] + [sems((4,))],
        far_outs=4,
        after=(packed[0],),
    )
    rows0 = exchange(held_until(packed, (rows1, token)))
    out1, mirror1, i1 = run(
        add_rows,
        (),
        (*rows1, q1, *q_received),
        [(rows, BF)] * 3,
        [pltpu.VMEM(wide, F32)],
        after=(token,),
    )
    fwd1, mir1 = onward(out1, 0), mirrored(mirror1, 0)
    *dh_sends, f_pad1, act_h1 = run(
        last_backward,
        (fs, bs),
        (q1, *q_received, g_pad1, heads[0], *sums, h0, kernels),
        [((local // FOLD, FOLD * w), BF)] * n + [(padded, BF), (half, BF)],
        [pltpu.VMEM(half, BF), pltpu.VMEM(half, BF), wide_line],
        after=(out1,),
    )
    dh1_in = [backward(x, d) for d, x in enumerate(dh_sends)]
    token, grad_total = run(
        kernel_grads_last,
        (),
        (sum_h, part_i, act_h1, f_pad1),
        [((8, 128), F32), ((18, w, c), F32)],
        [pltpu.VMEM((9, w, c), F32), sems((10,))],
        far_outs=1,
    )
    fwd_out, bwd_out, mir_out, stash_out, emitted = run(
        finish,
        (fs, bs),
        (*written, out1, i1, fwd1, mir1, *rows0, *dh1_in),
        [(x.shape, BF) for x in queues] + [((TICKS, local, c), BF)],
        [pltpu.VMEM(rows, BF)] * 3 + [sems((7,))],
        remote=4,
        far_outs=5,
        aliases={j + 2: j for j in range(4)},
        after=(token,),
    )
    return (
        fwd_out.reshape(fwd_queue.shape),
        bwd_out.reshape(bwd_queue.shape),
        mir_out.reshape(mirror_queue.shape),
        stash_out.reshape(stash.shape),
        grad_total.reshape(grad_acc.shape),
        emitted.reshape((1, TICKS) + fwd_queue.shape[2:]),
    )


def solution(mesh):
    return jax.shard_map(
        per_device,
        mesh=mesh,
        in_specs=(
            P("section", None, "row", None, None),
            P("section", None, "row", None, None),
            P("section", None, "row", None, None),
            P("section", None, None, "row", None, None),
            P("section", None, None, None, "row", None),
            P("section", None, None, None, "row", None),
            P(),
            P(),
        ),
        out_specs=(
            P("section", None, "row", None, None),
            P("section", None, "row", None, None),
            P("section", None, "row", None, None),
            P("section", None, None, "row", None, None),
            P("section", None, None, None, "row", None),
            P("section", None, "row", None, None),
        ),
        check_vma=False,
    )
```

```python
import functools

import jax
import jax.numpy as jnp
from jax import lax
from jax.experimental import pallas as pl
from jax.experimental.pallas import tpu as pltpu
from jax.sharding import PartitionSpec as P

GROUPS = 32
TICKS = 2
FOLD = 4
EPSILON = 1e-05
BF, F32 = jnp.bfloat16, jnp.float32
VMEM_LIMIT = 24 * 2**20


class Sizes:
    def __init__(self, queue, sections, rows):
        self.sections, self.parts = sections, rows
        self.cols = queue.shape[2]
        self.channels = queue.shape[3]
        self.local = queue.shape[1] * queue.shape[2]
        self.cells = self.local * rows
        self.share = self.channels // rows
        self.group = self.channels // GROUPS
        self.count = self.cells * self.group


def where_am_i():
    return lax.axis_index("section"), lax.axis_index("row")


def share_of(z, value, part):
    value = value.astype(F32)
    out = value[:, : z.share]
    for j in range(1, z.parts):
        out = jnp.where(part == j, value[:, j * z.share : (j + 1) * z.share], out)
    return out


def all_shares(z, own, others, row):
    out = []
    for j in range(z.parts):
        value = own
        for d in range(1, z.parts):
            value = jnp.where(lax.rem(row + z.parts - d, z.parts) == j, others[d - 1], value)
        out.append(value)
    return out


def side_by_side(values):
    return jnp.concatenate([value.astype(F32) for value in values], axis=1)


def folded(value, blocks):
    rows = value.shape[0] // blocks
    return side_by_side([value[j * rows : (j + 1) * rows] for j in range(blocks)])


def unfolded(value, blocks):
    value, width = value.astype(F32), value.shape[1] // blocks
    return jnp.concatenate([value[:, j * width : (j + 1) * width] for j in range(blocks)], axis=0)


def fold(z, ref, value):
    ref[...] = folded(value, FOLD).astype(BF)


def unfold(z, ref):
    return unfolded(ref[...], FOLD)


def source(z, row, d):
    return lax.rem(row + z.parts - d, z.parts)


def target(z, row, d):
    return lax.rem(row + d, z.parts)


def part_rows(z, part):
    return pl.ds(pl.multiple_of(part * z.local, z.local), z.local)


def assemble(z, ref, pieces, row, start, width):
    for d, piece in enumerate(pieces):
        value = (piece if isinstance(piece, jax.Array) else piece[...]).astype(F32)
        value = value[:, start : start + width]
        ref[part_rows(z, source(z, row, d)), :] = value.astype(BF)


def group_sums(z, first, second):
    width = first.shape[1]
    line = lax.broadcasted_iota(jnp.int32, (8, width), 0)
    both = jnp.where(line == 0, first, jnp.where(line == 1, second, 0.0))
    across = lax.broadcasted_iota(jnp.int32, (width, width), 1).astype(F32)
    down = lax.broadcasted_iota(jnp.int32, (width, width), 0).astype(F32)
    same = jnp.floor((across + 0.5) * (1.0 / z.group)) == jnp.floor((down + 0.5) * (1.0 / z.group))
    sums = jnp.dot(
        both, same.astype(F32), precision=lax.Precision.HIGHEST, preferred_element_type=F32
    )
    return sums[0:1], sums[1:2]


def normalize(z, x):
    total, square = group_sums(
        z, jnp.sum(x, axis=0, keepdims=True), jnp.sum(x * x, axis=0, keepdims=True)
    )
    center = total / z.count
    factor = lax.rsqrt(square / z.count - center * center + EPSILON)
    return (x - center) * factor, factor


def sigmoid(y):
    return 1.0 / (1.0 + jnp.exp(-y))


def norm_back(z, y, factor, logistic, upstream):
    e = upstream * logistic * (1.0 + y * (1.0 - logistic))
    first, second = group_sums(
        z, jnp.sum(e, axis=0, keepdims=True), jnp.sum(e * y, axis=0, keepdims=True)
    )
    return factor * (e - first / z.count - y * (second / z.count))


def spread(z, x, line_ref, pad_ref):
    cells, cols = z.cells, z.cols
    width = x.shape[1]
    line_ref[8 : 8 + cells, :] = x
    column = lax.rem(lax.broadcasted_iota(jnp.int32, (cells, 1), 0), cols)
    edge = jnp.zeros((cols, width), BF)
    for b in range(3):
        pad_ref[b, :cols, :] = edge
        pad_ref[b, cols + cells :, :] = edge
    pad_ref[1, cols : cols + cells, :] = x.astype(BF)
    left = jnp.where(column > 0, line_ref[7 : 7 + cells, :], 0.0)
    pad_ref[0, cols : cols + cells, :] = left.astype(BF)
    right = jnp.where(column < cols - 1, line_ref[9 : 9 + cells, :], 0.0)
    pad_ref[2, cols : cols + cells, :] = right.astype(BF)


def spread_wide(z, x, line_ref, pad_ref):
    cells, cols = z.cells, z.cols
    line_ref[8 : 8 + cells, :] = x
    column = lax.rem(lax.broadcasted_iota(jnp.int32, (cells, 1), 0), cols)
    edge = jnp.zeros((cols, 3 * z.share), BF)
    pad_ref[:cols, :] = edge
    pad_ref[cols + cells :, :] = edge
    left = jnp.where(column > 0, line_ref[7 : 7 + cells, :], 0.0)
    right = jnp.where(column < cols - 1, line_ref[9 : 9 + cells, :], 0.0)
    pad_ref[cols : cols + cells, :] = side_by_side([left, x, right]).astype(BF)


def convolve(z, pad_ref, kernel_ref, which):
    total = None
    for a in range(3):
        first = (9 * which + 3 * a) * z.share
        term = jnp.dot(
            pad_ref[a * z.cols : a * z.cols + z.cells, :],
            kernel_ref[first : first + 3 * z.share, :],
            preferred_element_type=F32,
        )
        total = term if total is None else total + term
    return total


def convolve_back(z, pad_ref, kernel_ref, which):
    total = None
    for a in range(3):
        for b in range(3):
            first = (9 * which + 3 * (2 - a) + 2 - b) * z.share
            term = lax.dot_general(
                pad_ref[b, a * z.cols : a * z.cols + z.cells, :],
                kernel_ref[first : first + z.share, :],
                (((1,), (1,)), ((), ())),
                preferred_element_type=F32,
            )
            total = term if total is None else total + term
    return total


def pad_shapes(z, width):
    return [
        pltpu.VMEM((z.cells + 16, width), F32),
        pltpu.VMEM((z.cells + 2 * z.cols, 3 * width), BF),
    ]


def call(body, name, scalars, arrays, outs, scratch=(), after=(), remote=0, far_outs=0, aliases=None):
    near, far = pl.BlockSpec(memory_space=pltpu.VMEM), pl.BlockSpec(memory_space=pltpu.HBM)

    def inner(*refs):
        given = len(scalars) + len(arrays)
        body(*refs[:given], *refs[given + len(after) :])

    arrays = [
        pltpu.with_memory_space_constraint(x, pltpu.HBM) if j < remote else x
        for j, x in enumerate(arrays)
    ]
    near_outs = len(outs) - far_outs
    return pl.pallas_call(
        inner,
        name=name,
        out_shape=[
            jax.ShapeDtypeStruct(shape, dtype) if j < near_outs else pltpu.HBM(shape, dtype)
            for j, (shape, dtype) in enumerate(outs)
        ],
        in_specs=[pl.BlockSpec(memory_space=pltpu.SMEM)] * len(scalars)
        + [far] * remote
        + [near] * (len(arrays) - remote)
        + [pl.BlockSpec(memory_space=pl.ANY)] * len(after),
        out_specs=[near] * near_outs + [far] * far_outs,
        scratch_shapes=list(scratch),
        input_output_aliases=aliases or {},
        compiler_params=pltpu.CompilerParams(vmem_limit_bytes=VMEM_LIMIT),
        cost_estimate=pl.CostEstimate(flops=1, bytes_accessed=1, transcendentals=0),
    )(*scalars, *arrays, *after)


def held_until(values, earlier):
    return lax.optimization_barrier((tuple(values), earlier))[0]


def fetch(pairs, sems):
    copies = [pltpu.make_async_copy(a, b, sems.at[j]) for j, (a, b) in enumerate(pairs)]
    for copy in copies:
        copy.start()
    for copy in copies:
        copy.wait()


def pack_first(z, fs_far, bs_far, fwd_far, bwd_far, mir_far, stash_far, *refs):
    n = z.parts
    heads = refs[:n]
    fwd, bwd, mir, stash, fs, bs, sems = refs[n:]
    fetch(
        [
            (fs_far, fs),
            (bs_far, bs),
            (fwd_far, fwd),
            (bwd_far, bwd),
            (mir_far, mir),
            (stash_far, stash),
        ],
        sems,
    )
    s, row = where_am_i()
    h = fwd[fs[0, s]]
    for d in range(n):
        fold(z, heads[d], share_of(z, h, target(z, row, d)))


def taken_back(z, bs, s):
    later, partner = jnp.minimum(s + 1, z.sections - 1), z.sections - 1 - s
    return (
        jnp.logical_and(s < z.sections - 1, bs[0, later] == bs[1, s]),
        jnp.logical_and(s < z.sections // 2, bs[0, partner] == bs[1, s]),
    )


def pack_later(z, fs_far, bs_far, fwd, bwd, mir, stash, *refs):
    n = z.parts
    pieces, groups = refs[:n], [refs[j * n : (j + 1) * n] for j in range(1, 5)]
    fs, bs, sems = refs[5 * n :]
    fetch([(fs_far, fs), (bs_far, bs)], sems)
    s, row = where_am_i()
    f1, b1 = fs[1, s], bs[1, s]
    grad_taken, skip_taken = taken_back(z, bs, s)
    skip_kept = jnp.logical_and(s < z.sections // 2, jnp.logical_not(skip_taken))
    kept = jnp.where(grad_taken, 0.0, bwd[b1].astype(F32))
    kept = kept + jnp.where(skip_kept, mir[b1].astype(F32), 0.0)
    f0, b0 = fs[0, s], bs[0, s]
    g = bwd[b0].astype(F32) + jnp.where(s < z.sections // 2, mir[b0].astype(F32), 0.0)
    for d, piece in enumerate(pieces):
        part = target(z, row, d)
        shares = [share_of(z, stash[2 * b0 + 1], part), share_of(z, mir[f0], part)]
        piece[...] = side_by_side(shares + [g]).astype(BF)
    values = [stash[2 * b0], stash[2 * b1], fwd[f1], stash[2 * b1 + 1], mir[f1]]
    rows = z.local // FOLD
    for d in range(n):
        shares = [share_of(z, value, target(z, row, d)) for value in values]
        grads = [kept[:, j * z.share : (j + 1) * z.share] for j in range(n)]
        for outs, parts in zip(groups, (shares[:2], shares[2:4], grads, shares[4:])):
            for j, value in enumerate(parts):
                outs[d][j * rows : (j + 1) * rows, :] = folded(value, FOLD).astype(BF)


def send_partials(z, row, total, own, sends, extra):
    own[...] = share_of(z, total, row)
    for d, send in enumerate(sends, 1):
        part = folded(share_of(z, total, target(z, row, d)), FOLD).astype(BF)
        send[: part.shape[0], :] = part
        send[part.shape[0] :, :] = extra[d][...]


def first_forward(z, *refs):
    n = z.parts
    pieces, extra, kernel = refs[:n], refs[n : 2 * n], refs[2 * n]
    own, h_out = refs[2 * n + 1 : 2 * n + 3]
    sends, (line, pad) = refs[2 * n + 3 : 3 * n + 2], refs[3 * n + 2 :]
    _, row = where_am_i()
    assemble(z, h_out, [unfold(z, piece) for piece in pieces], row, 0, z.share)
    y, _ = normalize(z, h_out[...].astype(F32))
    spread_wide(z, y * sigmoid(y), line, pad)
    send_partials(z, row, convolve(z, pad, kernel, 0), own, sends, extra)


def enclosed(z, own, received, j):
    rows, base = z.local // FOLD, z.cells // FOLD
    at, there = slice(j * rows, (j + 1) * rows), slice(base + j * rows, base + (j + 1) * rows)
    return [unfolded(own[at, :], FOLD)] + [unfolded(x[there, :], FOLD) for x in received]


def later_forward(z, fs, *refs):
    n = z.parts
    arrivals, nexts, received = refs[:n], refs[n], refs[n + 1 : 2 * n]
    lasts, kernel = refs[2 * n : 3 * n], refs[3 * n]
    own, h_out, arrived, onward = refs[3 * n + 1 : 3 * n + 5]
    sends = refs[3 * n + 5 : 4 * n + 4]
    line, pad = refs[4 * n + 4 :]
    s, row = where_am_i()
    total = unfold(z, arrivals[0])
    for other in arrivals[1:]:
        total = total + unfold(z, other)
    total = total.astype(BF).astype(F32)
    arrived[...] = total.astype(BF)
    fold(z, onward, total)
    assemble(z, h_out, enclosed(z, nexts, received, 0), row, 0, z.share)
    prior = jnp.maximum(s - 1, 0)
    taken = jnp.logical_and(s > 0, fs[0, prior] == fs[1, s])
    h = jnp.where(taken, total, h_out[...].astype(F32))
    h_out[...] = h.astype(BF)
    y, _ = normalize(z, h)
    spread_wide(z, y * sigmoid(y), line, pad)
    send_partials(z, row, convolve(z, pad, kernel, 0), own, sends, lasts)


def back_through_second(z, i, g, kernel, q_out, q_send, act_out, pad, line):
    y, factor = normalize(z, i.astype(F32))
    logistic = sigmoid(y)
    act_out[...] = (y * logistic).astype(BF)
    spread(z, g, line, pad)
    q = norm_back(z, y, factor, logistic, convolve_back(z, pad, kernel, 1)).astype(BF)
    q_out[...] = q
    fold(z, q_send, q.astype(F32))


def first_backward(z, *refs):
    n = z.parts
    pieces, heads, kernel = refs[:n], refs[n : 2 * n], refs[2 * n]
    q_out, q_send, pad, act_out = refs[2 * n + 1 : 2 * n + 5]
    sends, (i_ref, g_ref, line) = refs[2 * n + 5 : 3 * n + 4], refs[3 * n + 4 :]
    _, row = where_am_i()
    assemble(z, i_ref, pieces, row, 0, z.share)
    assemble(z, g_ref, pieces, row, 2 * z.share, z.channels)
    back_through_second(
        z, i_ref[...], g_ref[...].astype(F32), kernel, q_out, q_send, act_out, pad, line
    )
    rows = z.cells // FOLD
    for d, send in enumerate(sends, 1):
        send[:rows, :] = q_send[...]
        send[rows:, :] = heads[d][...]


def later_backward(z, fs, bs, *refs):
    n = z.parts
    arrivals, mirror, received, kept = refs[:n], refs[n], refs[n + 1 : 2 * n], refs[2 * n]
    nexts, others = refs[2 * n + 1], refs[2 * n + 2 : 3 * n + 1]
    i_before, arrived, kernel = refs[3 * n + 1 : 3 * n + 4]
    q_out, pad, act_out, grad_in, skip_in = refs[3 * n + 4 : 3 * n + 9]
    rows_own, sends = refs[3 * n + 9], refs[3 * n + 10 : 4 * n + 9]
    q_send, i_ref, full, line = refs[4 * n + 9 :]
    s, row = where_am_i()
    w = z.share
    shares = [unfold(z, part) for part in arrivals]
    grad = side_by_side(all_shares(z, shares[0], shares[1:], row))
    grad_in[...] = grad.astype(BF)
    shares = [unfolded(x[: z.cells // FOLD, :], FOLD) for x in received]
    skip = side_by_side(all_shares(z, unfold(z, mirror), shares, row))
    skip_in[...] = skip.astype(BF)
    grad_taken, skip_taken = taken_back(z, bs, s)
    for j in range(n):
        assemble(z, full.at[j], enclosed(z, kept, received, j), row, 0, w)
    g = side_by_side([full[j] for j in range(n)]) + jnp.where(grad_taken, grad, 0.0)
    g = g + jnp.where(skip_taken, skip, 0.0)
    g = g.astype(BF).astype(F32)
    assemble(z, i_ref, enclosed(z, nexts, others, 1), row, 0, w)
    i = jnp.where(fs[0, s] == bs[1, s], i_before[...].astype(F32), i_ref[...].astype(F32))
    back_through_second(z, i, g, kernel, q_out, q_send, act_out, pad, line)
    for d, out in enumerate([rows_own, *sends]):
        at = part_rows(z, target(z, row, d))
        part = folded(side_by_side([i_before[at, :], arrived[at, :]]), 2).astype(BF)
        out[out.shape[0] - part.shape[0] :, :] = part
    for send in sends:
        send[: q_send.shape[0], :] = q_send[...]


def second_convolution(z, encoder, row, own, received, skip, h, kernel, i_out, full, line, pad):
    c0 = own[...]
    for other in received:
        c0 = c0 + unfolded(other[: z.cells // FOLD, :], FOLD)
    i = jnp.where(encoder, c0, skip.astype(F32)).astype(BF)
    i_out[...] = i
    y, _ = normalize(z, i.astype(F32))
    spread_wide(z, y * sigmoid(y), line, pad)
    total = convolve(z, pad, kernel, 1)
    base = h[...].astype(F32) + jnp.where(encoder, 0.0, c0)
    full[...] = total + side_by_side([jnp.where(row == j, base, 0.0) for j in range(z.parts)])


def middle(z, pad):
    return pad[1, z.cols : z.cols + z.cells, :].astype(F32)


def second_forward(z, *refs):
    n = z.parts
    own, received, h, pieces, kernel = refs[0], refs[1:n], refs[n], refs[n + 1 : 2 * n + 1], refs[2 * n + 1]
    i_out, full_out = refs[2 * n + 2 : 2 * n + 4]
    sends = refs[2 * n + 4 : 3 * n + 4]
    skip, full, line, pad = refs[3 * n + 4 :]
    s, row = where_am_i()
    encoder = s < z.sections // 2
    assemble(z, skip, pieces, row, z.share, z.share)
    second_convolution(
        z, encoder, row, own, received, skip[...], h, kernel, i_out, full, line, pad
    )
    full_out[...] = full[...].astype(BF)
    for d in range(n):
        fold(z, sends[d], share_of(z, full[...], target(z, row, d)))


def last_forward(z, fs, *refs):
    n = z.parts
    own, received, h = refs[0], refs[1:n], refs[n]
    lasts, arrived, kernel = refs[n + 1 : n + 4]
    sends = refs[n + 4 : 2 * n + 4]
    i_out, skip, full, line, pad = refs[2 * n + 4 :]
    s, row = where_am_i()
    encoder = s < z.sections // 2
    partner = z.sections - 1 - s
    assemble(z, skip, enclosed(z, lasts, received, 0), row, 0, z.share)
    now = jnp.where(
        fs[0, partner] == fs[1, s], unfold(z, arrived), skip[...].astype(F32)
    )
    second_convolution(z, encoder, row, own, received, now, h, kernel, i_out, full, line, pad)
    for d, send in enumerate(sends):
        at = part_rows(z, target(z, row, d))
        send[...] = side_by_side([full[at, :], i_out[at, :]]).astype(BF)


def joined_shares(z, own, received, row):
    others = [unfolded(other[: z.cells // FOLD, :], FOLD) for other in received]
    return side_by_side(all_shares(z, own[...].astype(F32), others, row))


def back_through_first(z, encoder, row, q, received, g_pad, h, kernel, act_out, pad, line):
    g = middle(z, g_pad)
    whole = joined_shares(z, q, received, row)
    now = jnp.where(encoder, whole, g)
    y, factor = normalize(z, h.astype(F32))
    logistic = sigmoid(y)
    act_out[...] = (y * logistic).astype(BF)
    spread(z, now, line, pad)
    back = norm_back(z, y, factor, logistic, convolve_back(z, pad, kernel, 0))
    return share_of(z, g, row) + back, whole


def second_backward(z, *refs):
    n = z.parts
    q, received, g = refs[0], refs[1:n], refs[n]
    heads, others, mirror = refs[n + 1], refs[n + 2 : 2 * n + 1], refs[2 * n + 1]
    grads, kernel = refs[2 * n + 2 : 3 * n + 2], refs[3 * n + 2]
    send, pad, act_out = refs[3 * n + 3 : 3 * n + 6]
    relays, (h, line) = refs[3 * n + 6 : 4 * n + 5], refs[4 * n + 5 :]
    s, row = where_am_i()
    for d, relay in enumerate(relays, 1):
        relay[: z.cells // FOLD, :] = mirror[...]
        relay[z.cells // FOLD :, :] = grads[d][...]
    assemble(z, h, enclosed(z, heads, others, 0), row, 0, z.share)
    value, _ = back_through_first(
        z, s < z.sections // 2, row, q, received, g, h[...], kernel, act_out, pad, line
    )
    fold(z, send, value)


def last_backward(z, fs, bs, *refs):
    n = z.parts
    q, received, g = refs[0], refs[1:n], refs[n]
    heads, others = refs[n + 1], refs[n + 2 : 2 * n + 1]
    h_before, kernel = refs[2 * n + 1 : 2 * n + 3]
    sends = refs[2 * n + 3 : 3 * n + 3]
    pad, act_out, h, value, line = refs[3 * n + 3 :]
    s, row = where_am_i()
    assemble(z, h, enclosed(z, heads, others, 1), row, 0, z.share)
    now = jnp.where(fs[0, s] == bs[1, s], h_before[...], h[...])
    result, _ = back_through_first(
        z, s < z.sections // 2, row, q, received, g, now, kernel, act_out, pad, line
    )
    value[...] = result.astype(BF)
    for d, send in enumerate(sends):
        fold(z, send, value[part_rows(z, target(z, row, d)), :])


def pack_rows(z, *refs):
    n = z.parts
    full, mirror = refs[:2]
    sends, skip = refs[2 : n + 2], refs[n + 2]
    _, row = where_am_i()
    skip[...] = unfold(z, mirror).astype(BF)
    for d, send in enumerate(sends):
        at = part_rows(z, target(z, row, d))
        send[...] = side_by_side([ref[at, :] for ref in (full, skip)]).astype(BF)


def add_rows(z, *refs):
    n = z.parts
    pieces, q, received = refs[:n], refs[n], refs[n + 1 : 2 * n]
    out, mirror, i_rows, whole = refs[2 * n :]
    s, row = where_am_i()
    c = z.channels
    whole[...] = joined_shares(z, q, received, row)
    values = [piece[...].astype(F32) for piece in pieces]
    total = sum(value[:, :c] for value in values)
    out[...] = total.astype(BF)
    mine = whole[part_rows(z, row), :]
    mirror[...] = jnp.where(s < z.sections // 2, total, mine).astype(BF)
    shares = all_shares(z, values[0][:, c:], [value[:, c:] for value in values[1:]], row)
    i_rows[...] = side_by_side(shares).astype(BF)


def write_queues(z, fs, bs, *refs):
    n = z.parts
    fwd, bwd, mir, stash, grad_in, skip_in = refs[:6]
    pieces = refs[6 : n + 6]
    token, outs, held = refs[n + 6], refs[n + 7 : n + 11], refs[n + 11 : n + 15]
    sems = refs[n + 15]
    token[...] = jnp.zeros_like(token)
    s, row = where_am_i()
    w = z.share
    prior, later = jnp.maximum(s - 1, 0), jnp.minimum(s + 1, z.sections - 1)
    partner = z.sections - 1 - s
    f0, f1 = fs[0, s], fs[1, s]
    mine = part_rows(z, row)
    copies = [pltpu.make_async_copy(a, b, sems.at[j]) for j, (a, b) in enumerate(zip(held, outs))]
    for ref, queue in zip(held, (fwd, bwd, mir, stash)):
        ref[...] = queue[...]

    @pl.when(s < z.sections - 1)
    def _():
        held[1][bs[0, later]] = grad_in[mine, :]

    copies[1].start()

    @pl.when(s < z.sections // 2)
    def _():
        held[2][bs[0, partner]] = skip_in[mine, :]

    copies[2].start()
    values = [unfolded(piece[piece.shape[0] - z.local // 2 :, :], 2) for piece in pieces]

    def joined(at):
        shares = [value[:, at : at + w] for value in values]
        return side_by_side(all_shares(z, shares[0], shares[1:], row)).astype(BF)

    fwd_in = joined(w)

    @pl.when(s > 0)
    def _():
        held[0][fs[0, prior]] = fwd_in

    copies[0].start()
    held[3][2 * f0] = fwd[f0]
    held[3][2 * f0 + 1] = joined(0)
    held[3][2 * f1] = fwd[f1]

    @pl.when(jnp.logical_and(s > 0, fs[0, prior] == f1))
    def _():
        held[3][2 * f1] = fwd_in

    copies[3].start()
    for copy in copies:
        copy.wait()


def finish(z, fs, bs, *refs):
    n = z.parts
    out1, i1, fwd1, mir1 = refs[4:8]
    rows0, grads1 = refs[8 : n + 8], refs[n + 8 : 2 * n + 8]
    fwd_out, bwd_out, mir_out, stash_out, emitted = refs[2 * n + 8 : 2 * n + 13]
    out0, skip, grads, sems = refs[2 * n + 13 :]
    s, row = where_am_i()
    c = z.channels
    prior, later = jnp.maximum(s - 1, 0), jnp.minimum(s + 1, z.sections - 1)
    partner = z.sections - 1 - s
    encoder, has_prior, has_later = s < z.sections // 2, s > 0, s < z.sections - 1
    first = jnp.where(encoder, bs[0, partner], fs[0, partner])
    second = jnp.where(encoder, bs[1, partner], fs[1, partner])
    skip_stays = jnp.logical_and(jnp.logical_not(encoder), first != second)

    def put(source, place, j):
        return pltpu.make_async_copy(source, place, sems.at[j])

    always = [
        put(out1, emitted.at[1], 0),
        put(i1, stash_out.at[2 * fs[1, s] + 1], 1),
        put(mir1, mir_out.at[second], 2),
        put(out0, emitted.at[0], 3),
    ]
    for copy in always[:3]:
        copy.start()
    onward, back = put(fwd1, fwd_out.at[fs[1, prior]], 4), put(grads, bwd_out.at[bs[1, later]], 5)
    aside = put(skip, mir_out.at[first], 6)
    pl.when(has_prior)(onward.start)
    pieces = [unfold(z, piece) for piece in grads1]
    grads[...] = side_by_side(all_shares(z, pieces[0], pieces[1:], row)).astype(BF)
    pl.when(has_later)(back.start)
    pieces = [piece[...].astype(F32) for piece in rows0]
    out0[...] = sum(piece[:, :c] for piece in pieces).astype(BF)
    always[3].start()
    shares = [piece[:, c:] for piece in pieces]
    skip[...] = side_by_side(all_shares(z, shares[0], shares[1:], row)).astype(BF)
    pl.when(skip_stays)(aside.start)
    for copy in always:
        copy.wait()
    pl.when(has_prior)(onward.wait)
    pl.when(has_later)(back.wait)
    pl.when(skip_stays)(aside.wait)


def add_taps(z, act, pad, before, store):
    turned = jnp.transpose(act[...].astype(F32)).astype(BF)
    for tap in range(9):
        a, b = divmod(tap, 3)
        at = (2 - a) * z.cols
        moved = pad[2 - b, at : at + z.cells, :]
        store(tap, before(tap) + jnp.dot(turned, moved, preferred_element_type=F32))


def kernel_grads_add(z, start, acc, act, pad, out):
    def store(tap, value):
        out[tap] = value

    add_taps(z, act, pad, lambda tap: acc[start + tap], store)


def kernel_grads_last(z, total, other, act, pad, token, out, held, sems):
    token[...] = jnp.zeros_like(token)
    copies = [pltpu.make_async_copy(other, out.at[9:], sems.at[9])]
    copies[0].start()

    def store(tap, value):
        held[tap] = value
        copies.append(pltpu.make_async_copy(held.at[tap], out.at[tap], sems.at[tap]))
        copies[-1].start()

    add_taps(z, act, pad, lambda tap: total[tap], store)
    for copy in copies:
        copy.wait()


def per_device(fwd_queue, bwd_queue, mirror_queue, stash, weights, grad_acc, fwd_slot, bwd_slot):
    sections, n = lax.axis_size("section"), lax.axis_size("row")
    z = Sizes(fwd_queue[0], sections, n)
    slots = fwd_queue.shape[1]
    c, w, local, cells = z.channels, z.share, z.local, z.cells
    fwd, bwd, mir = (x.reshape(slots, local, c) for x in (fwd_queue, bwd_queue, mirror_queue))
    kept = stash.reshape(2 * slots, local, c)
    kernels = weights.reshape(18 * w, c)
    acc = grad_acc.reshape(18, w, c)
    fs, bs = fwd_slot.T, bwd_slot.T
    fold_shape, wide = (cells // FOLD, FOLD * w), (cells, c)
    half = (cells, w)

    def with_shares(k):
        return ((cells + k * local) // FOLD, FOLD * w)

    padded = (3, cells + 2 * z.cols, c)

    def move(x, d, step):
        route = [
            (s * n + r, step(s) * n + (r + d) % n) for s in range(sections) for r in range(n)
        ]
        return lax.ppermute(x, ("section", "row"), route)

    across = functools.partial(move, step=lambda s: s)
    onward = functools.partial(move, step=lambda s: (s + 1) % sections)
    backward = functools.partial(move, step=lambda s: (s - 1) % sections)
    crossed = functools.partial(move, step=lambda s: (sections - s) % sections)
    mirrored = functools.partial(move, step=lambda s: sections - 1 - s)

    def run(body, scalars, arrays, outs, scratch=(), **options):
        return call(
            functools.partial(body, z), body.__name__, scalars, arrays, outs, scratch, **options
        )

    def exchange(pieces):
        return [pieces[0]] + [across(piece, d) for d, piece in enumerate(pieces[1:], 1)]

    narrow_pad = pad_shapes(z, w)
    wide_line = pltpu.VMEM((cells + 16, c), F32)
    queues = (fwd, bwd, mir, kept)
    rows = (local, c)
    sems = pltpu.SemaphoreType.DMA
    packed = run(
        pack_first,
        (),
        (fs, bs, *queues),
        [((local // FOLD, FOLD * w), BF)] * n
        + [(x.shape, BF) for x in queues],
        [pltpu.SMEM(fs.shape, jnp.int32)] * 2 + [sems((6,))],
        remote=6,
    )
    inputs, held = exchange(packed[:n]), packed[n:]

    packed = run(
        pack_later,
        (),
        (fs, bs, *held),
        [((local, 2 * w + c), BF)] * n
        + [((k * (local // FOLD), FOLD * w), BF) for k in (2, 2, n, 1) for _ in range(n)],
        [pltpu.SMEM(fs.shape, jnp.int32)] * 2 + [sems((2,))],
        remote=2,
        after=(inputs[0],),
    )
    pieces, heads, nexts, grads, lasts = (packed[j * n : (j + 1) * n] for j in range(5))
    first = exchange(held_until(pieces, inputs))

    own, h0, *sends = run(
        first_forward,
        (),
        (*inputs, *heads, kernels),
        [(half, F32), (half, BF)] + [(with_shares(2), BF)] * (n - 1),
        narrow_pad,
    )
    sums = [across(x, d) for d, x in enumerate(sends, 1)]
    q0, q_send, g_pad0, act_i0, *sends = run(
        first_backward,
        (),
        (*first, *nexts, kernels),
        [(half, BF), (fold_shape, BF), (padded, BF), (half, BF)]
        + [(with_shares(2), BF)] * (n - 1),
        [pltpu.VMEM(half, BF), pltpu.VMEM(wide, BF), wide_line],
        after=(own,),
    )
    q_received = [across(x, d) for d, x in enumerate(sends, 1)]
    skip_in = mirrored(q_send, 0)

    def add_grads(start, total, act, pad, after):
        [out] = call(
            functools.partial(kernel_grads_add, z, start),
            f"kernel_grads_add_{start}",
            (),
            (total, act, pad),
            [((9, w, c), F32)],
            after=after,
        )
        return out

    sum_i = add_grads(9, acc, act_i0, g_pad0, (q0,))
    i0, full0, *sends = run(
        second_forward,
        (),
        (own, *sums, h0, *first, kernels),
        [(half, BF), (wide, BF)] + [(fold_shape, BF)] * n,
        [pltpu.VMEM(half, BF), pltpu.VMEM(wide, F32)] + narrow_pad,
        after=(sum_i,),
    )
    fwd_in = [onward(x, d) for d, x in enumerate(sends)]
    dh_send, f_pad0, act_h0, *relays = run(
        second_backward,
        (),
        (q0, *q_received, g_pad0, heads[0], *sums, skip_in, *grads, kernels),
        [(fold_shape, BF), (padded, BF), (half, BF)] + [(with_shares(n), BF)] * (n - 1),
        [pltpu.VMEM(half, BF), wide_line],
        after=(i0,),
    )
    dh_in = [backward(dh_send, d) for d in range(n)]
    relayed = [across(x, d) for d, x in enumerate(relays, 1)]

    own, h1, arrived, turned, *sends = run(
        later_forward,
        (fs,),
        (*fwd_in, nexts[0], *q_received, *lasts, kernels),
        [(half, F32), (half, BF), (half, BF), (fold_shape, BF)]
        + [(with_shares(1), BF)] * (n - 1),
        narrow_pad,
        after=(dh_send,),
    )
    received = [across(x, d) for d, x in enumerate(sends, 1)]
    mir_in = crossed(turned, 0)
    sum_h = add_grads(0, acc, act_h0, f_pad0, (own,))
    q1, g_pad1, act_i1, grad_in, skip_full, rows_own, *sends = run(
        later_backward,
        (fs, bs),
        (*dh_in, skip_in, *relayed, grads[0], nexts[0], *q_received, i0, arrived, kernels),
        [(half, BF), (padded, BF), (half, BF), (wide, BF), (wide, BF), ((local // 2, 4 * w), BF)]
        + [((cells // FOLD + local // 2, FOLD * w), BF)] * (n - 1),
        [pltpu.VMEM(fold_shape, BF), pltpu.VMEM(half, BF), pltpu.VMEM((n, *half), BF), wide_line],
        after=(sum_h,),
    )
    q_received = [across(x, d) for d, x in enumerate(sends, 1)]
    sends = run(
        last_forward,
        (fs,),
        (own, *received, h1, lasts[0], mir_in, kernels),
        [((local, c + w), BF)] * n,
        [pltpu.VMEM(half, BF), pltpu.VMEM(half, BF), pltpu.VMEM(wide, F32)] + narrow_pad,
        after=(q1,),
    )
    rows1 = exchange(sends)
    part_i = add_grads(0, sum_i, act_i1, g_pad1, (sends[0],))
    *dh_sends, f_pad1, act_h1 = run(
        last_backward,
        (fs, bs),
        (q1, *q_received, g_pad1, heads[0], *sums, h0, kernels),
        [((local // FOLD, FOLD * w), BF)] * n + [(padded, BF), (half, BF)],
        [pltpu.VMEM(half, BF), pltpu.VMEM(half, BF), wide_line],
        after=(part_i,),
    )
    dh1_in = [backward(x, d) for d, x in enumerate(dh_sends)]
    packed = run(
        pack_rows,
        (),
        (full0, mir_in),
        [((local, c + w), BF)] * n,
        [pltpu.VMEM(half, BF)],
        after=(act_h1,),
    )
    token, *written = run(
        write_queues,
        (fs, bs),
        (*held, grad_in, skip_full, rows_own, *q_received),
        [((8, 128), F32)] + [(x.shape, BF) for x in queues],
        [pltpu.VMEM(x.shape, BF) for x in queues] + [sems((4,))],
        far_outs=4,
        after=(packed[0],),
    )
    rows0 = exchange(held_until(packed, (rows1, token)))
    out1, mirror1, i1 = run(
        add_rows,
        (),
        (*rows1, *held_until([q1], dh1_in), *q_received),
        [(rows, BF)] * 3,
        [pltpu.VMEM(wide, F32)],
        after=(token,),
    )
    fwd1, mir1 = onward(out1, 0), mirrored(mirror1, 0)
    token, grad_total = run(
        kernel_grads_last,
        (),
        (sum_h, part_i, act_h1, f_pad1),
        [((8, 128), F32), ((18, w, c), F32)],
        [pltpu.VMEM((9, w, c), F32), sems((10,))],
        far_outs=1,
        after=(out1,),
    )
    fwd_out, bwd_out, mir_out, stash_out, emitted = run(
        finish,
        (fs, bs),
        (*written, out1, i1, fwd1, mir1, *rows0, *dh1_in),
        [(x.shape, BF) for x in queues] + [((TICKS, local, c), BF)],
        [pltpu.VMEM(rows, BF)] * 3 + [sems((7,))],
        remote=4,
        far_outs=5,
        aliases={j + 2: j for j in range(4)},
        after=(token,),
    )
    return (
        fwd_out.reshape(fwd_queue.shape),
        bwd_out.reshape(bwd_queue.shape),
        mir_out.reshape(mirror_queue.shape),
        stash_out.reshape(stash.shape),
        grad_total.reshape(grad_acc.shape),
        emitted.reshape((1, TICKS) + fwd_queue.shape[2:]),
    )


def solution(mesh):
    return jax.shard_map(
        per_device,
        mesh=mesh,
        in_specs=(
            P("section", None, "row", None, None),
            P("section", None, "row", None, None),
            P("section", None, "row", None, None),
            P("section", None, None, "row", None, None),
            P("section", None, None, None, "row", None),
            P("section", None, None, None, "row", None),
            P(),
            P(),
        ),
        out_specs=(
            P("section", None, "row", None, None),
            P("section", None, "row", None, None),
            P("section", None, "row", None, None),
            P("section", None, None, "row", None, None),
            P("section", None, None, None, "row", None),
            P("section", None, "row", None, None),
        ),
        check_vma=False,
    )
```

```python
import functools

import jax
import jax.numpy as jnp
from jax import lax
from jax.experimental import pallas as pl
from jax.experimental.pallas import tpu as pltpu
from jax.sharding import PartitionSpec as P

GROUPS = 32
TICKS = 2
FOLD = 4
EPSILON = 1e-05
BF, F32 = jnp.bfloat16, jnp.float32
VMEM_LIMIT = 24 * 2**20


class Sizes:
    def __init__(self, queue, sections, rows):
        self.sections, self.parts = sections, rows
        self.cols = queue.shape[2]
        self.channels = queue.shape[3]
        self.local = queue.shape[1] * queue.shape[2]
        self.cells = self.local * rows
        self.share = self.channels // rows
        self.group = self.channels // GROUPS
        self.count = self.cells * self.group


def where_am_i():
    return lax.axis_index("section"), lax.axis_index("row")


def share_of(z, value, part):
    value = value.astype(F32)
    out = value[:, : z.share]
    for j in range(1, z.parts):
        out = jnp.where(part == j, value[:, j * z.share : (j + 1) * z.share], out)
    return out


def all_shares(z, own, others, row):
    out = []
    for j in range(z.parts):
        value = own
        for d in range(1, z.parts):
            value = jnp.where(lax.rem(row + z.parts - d, z.parts) == j, others[d - 1], value)
        out.append(value)
    return out


def side_by_side(values):
    return jnp.concatenate([value.astype(F32) for value in values], axis=1)


def folded(value, blocks):
    rows = value.shape[0] // blocks
    return side_by_side([value[j * rows : (j + 1) * rows] for j in range(blocks)])


def unfolded(value, blocks):
    value, width = value.astype(F32), value.shape[1] // blocks
    return jnp.concatenate([value[:, j * width : (j + 1) * width] for j in range(blocks)], axis=0)


def fold(z, ref, value):
    ref[...] = folded(value, FOLD).astype(BF)


def unfold(z, ref):
    return unfolded(ref[...], FOLD)


def source(z, row, d):
    return lax.rem(row + z.parts - d, z.parts)


def target(z, row, d):
    return lax.rem(row + d, z.parts)


def part_rows(z, part):
    return pl.ds(pl.multiple_of(part * z.local, z.local), z.local)


def assemble(z, ref, pieces, row, start, width):
    for d, piece in enumerate(pieces):
        value = (piece if isinstance(piece, jax.Array) else piece[...]).astype(F32)
        value = value[:, start : start + width]
        ref[part_rows(z, source(z, row, d)), :] = value.astype(BF)


def group_sums(z, first, second):
    width = first.shape[1]
    line = lax.broadcasted_iota(jnp.int32, (16, width), 0)
    rows = jnp.zeros((16, width), F32)
    for start, rest in ((0, first), (3, second)):
        for j in range(3):
            piece = rest.astype(BF).astype(F32)
            rows = jnp.where(line == start + j, piece, rows)
            rest = rest - piece
    across = lax.broadcasted_iota(jnp.int32, (width, width), 1).astype(F32)
    down = lax.broadcasted_iota(jnp.int32, (width, width), 0).astype(F32)
    same = jnp.floor((across + 0.5) * (1.0 / z.group)) == jnp.floor((down + 0.5) * (1.0 / z.group))
    ones = jnp.where(same, 1.0, 0.0).astype(BF)
    sums = jnp.dot(rows.astype(BF), ones, preferred_element_type=F32)
    return sums[0:1] + sums[1:2] + sums[2:3], sums[3:4] + sums[4:5] + sums[5:6]


def normalize(z, x):
    total, square = group_sums(
        z, jnp.sum(x, axis=0, keepdims=True), jnp.sum(x * x, axis=0, keepdims=True)
    )
    center = total / z.count
    factor = lax.rsqrt(square / z.count - center * center + EPSILON)
    return (x - center) * factor, factor


def sigmoid(y):
    return 1.0 / (1.0 + jnp.exp(-y))


def norm_back(z, y, factor, logistic, upstream):
    e = upstream * logistic * (1.0 + y * (1.0 - logistic))
    first, second = group_sums(
        z, jnp.sum(e, axis=0, keepdims=True), jnp.sum(e * y, axis=0, keepdims=True)
    )
    return factor * (e - first / z.count - y * (second / z.count))


def spread(z, x, line_ref, pad_ref):
    cells, cols = z.cells, z.cols
    width = x.shape[1]
    line_ref[8 : 8 + cells, :] = x
    column = lax.rem(lax.broadcasted_iota(jnp.int32, (cells, 1), 0), cols)
    edge = jnp.zeros((cols, width), BF)
    for b in range(3):
        pad_ref[b, :cols, :] = edge
        pad_ref[b, cols + cells :, :] = edge
    pad_ref[1, cols : cols + cells, :] = x.astype(BF)
    left = jnp.where(column > 0, line_ref[7 : 7 + cells, :], 0.0)
    pad_ref[0, cols : cols + cells, :] = left.astype(BF)
    right = jnp.where(column < cols - 1, line_ref[9 : 9 + cells, :], 0.0)
    pad_ref[2, cols : cols + cells, :] = right.astype(BF)


def spread_wide(z, x, line_ref, pad_ref):
    cells, cols = z.cells, z.cols
    line_ref[8 : 8 + cells, :] = x
    column = lax.rem(lax.broadcasted_iota(jnp.int32, (cells, 1), 0), cols)
    edge = jnp.zeros((cols, 3 * z.share), BF)
    pad_ref[:cols, :] = edge
    pad_ref[cols + cells :, :] = edge
    left = jnp.where(column > 0, line_ref[7 : 7 + cells, :], 0.0)
    right = jnp.where(column < cols - 1, line_ref[9 : 9 + cells, :], 0.0)
    pad_ref[cols : cols + cells, :] = side_by_side([left, x, right]).astype(BF)


def convolve(z, pad_ref, kernel_ref, which):
    total = None
    for a in range(3):
        first = (9 * which + 3 * a) * z.share
        term = jnp.dot(
            pad_ref[a * z.cols : a * z.cols + z.cells, :],
            kernel_ref[first : first + 3 * z.share, :],
            preferred_element_type=F32,
        )
        total = term if total is None else total + term
    return total


def convolve_back(z, pad_ref, kernel_ref, which):
    total = None
    for a in range(3):
        for b in range(3):
            first = (9 * which + 3 * (2 - a) + 2 - b) * z.share
            term = lax.dot_general(
                pad_ref[b, a * z.cols : a * z.cols + z.cells, :],
                kernel_ref[first : first + z.share, :],
                (((1,), (1,)), ((), ())),
                preferred_element_type=F32,
            )
            total = term if total is None else total + term
    return total


def pad_shapes(z, width):
    return [
        pltpu.VMEM((z.cells + 16, width), F32),
        pltpu.VMEM((z.cells + 2 * z.cols, 3 * width), BF),
    ]


def call(body, name, scalars, arrays, outs, scratch=(), after=(), remote=0, far_outs=0, aliases=None):
    near, far = pl.BlockSpec(memory_space=pltpu.VMEM), pl.BlockSpec(memory_space=pltpu.HBM)

    def inner(*refs):
        given = len(scalars) + len(arrays)
        body(*refs[:given], *refs[given + len(after) :])

    arrays = [
        pltpu.with_memory_space_constraint(x, pltpu.HBM) if j < remote else x
        for j, x in enumerate(arrays)
    ]
    near_outs = len(outs) - far_outs
    return pl.pallas_call(
        inner,
        name=name,
        out_shape=[
            jax.ShapeDtypeStruct(shape, dtype) if j < near_outs else pltpu.HBM(shape, dtype)
            for j, (shape, dtype) in enumerate(outs)
        ],
        in_specs=[pl.BlockSpec(memory_space=pltpu.SMEM)] * len(scalars)
        + [far] * remote
        + [near] * (len(arrays) - remote)
        + [pl.BlockSpec(memory_space=pl.ANY)] * len(after),
        out_specs=[near] * near_outs + [far] * far_outs,
        scratch_shapes=list(scratch),
        input_output_aliases=aliases or {},
        compiler_params=pltpu.CompilerParams(vmem_limit_bytes=VMEM_LIMIT),
        cost_estimate=pl.CostEstimate(flops=1, bytes_accessed=1, transcendentals=0),
    )(*scalars, *arrays, *after)


def held_until(values, earlier):
    return lax.optimization_barrier((tuple(values), earlier))[0]


def fetch(pairs, sems):
    copies = [pltpu.make_async_copy(a, b, sems.at[j]) for j, (a, b) in enumerate(pairs)]
    for copy in copies:
        copy.start()
    for copy in copies:
        copy.wait()


def pack_first(z, fs_far, bs_far, fwd_far, bwd_far, mir_far, stash_far, *refs):
    n = z.parts
    heads = refs[:n]
    fwd, bwd, mir, stash, fs, bs, sems = refs[n:]
    fetch(
        [
            (fs_far, fs),
            (bs_far, bs),
            (fwd_far, fwd),
            (bwd_far, bwd),
            (mir_far, mir),
            (stash_far, stash),
        ],
        sems,
    )
    s, row = where_am_i()
    h = fwd[fs[0, s]]
    for d in range(n):
        fold(z, heads[d], share_of(z, h, target(z, row, d)))


def taken_back(z, bs, s):
    later, partner = jnp.minimum(s + 1, z.sections - 1), z.sections - 1 - s
    return (
        jnp.logical_and(s < z.sections - 1, bs[0, later] == bs[1, s]),
        jnp.logical_and(s < z.sections // 2, bs[0, partner] == bs[1, s]),
    )


def pack_later(z, fs_far, bs_far, fwd, bwd, mir, stash, *refs):
    n = z.parts
    pieces, groups = refs[:n], [refs[j * n : (j + 1) * n] for j in range(1, 5)]
    fs, bs, sems = refs[5 * n :]
    fetch([(fs_far, fs), (bs_far, bs)], sems)
    s, row = where_am_i()
    f1, b1 = fs[1, s], bs[1, s]
    grad_taken, skip_taken = taken_back(z, bs, s)
    skip_kept = jnp.logical_and(s < z.sections // 2, jnp.logical_not(skip_taken))
    kept = jnp.where(grad_taken, 0.0, bwd[b1].astype(F32))
    kept = kept + jnp.where(skip_kept, mir[b1].astype(F32), 0.0)
    f0, b0 = fs[0, s], bs[0, s]
    g = bwd[b0].astype(F32) + jnp.where(s < z.sections // 2, mir[b0].astype(F32), 0.0)
    for d, piece in enumerate(pieces):
        part = target(z, row, d)
        shares = [share_of(z, stash[2 * b0 + 1], part), share_of(z, mir[f0], part)]
        piece[...] = side_by_side(shares + [g]).astype(BF)
    values = [stash[2 * b0], stash[2 * b1], fwd[f1], stash[2 * b1 + 1], mir[f1]]
    rows = z.local // FOLD
    for d in range(n):
        shares = [share_of(z, value, target(z, row, d)) for value in values]
        grads = [kept[:, j * z.share : (j + 1) * z.share] for j in range(n)]
        for outs, parts in zip(groups, (shares[:2], shares[2:4], grads, shares[4:])):
            for j, value in enumerate(parts):
                outs[d][j * rows : (j + 1) * rows, :] = folded(value, FOLD).astype(BF)


def send_partials(z, row, total, own, sends, extra):
    own[...] = share_of(z, total, row)
    for d, send in enumerate(sends, 1):
        part = folded(share_of(z, total, target(z, row, d)), FOLD).astype(BF)
        send[: part.shape[0], :] = part
        send[part.shape[0] :, :] = extra[d][...]


def first_forward(z, *refs):
    n = z.parts
    pieces, extra, kernel = refs[:n], refs[n : 2 * n], refs[2 * n]
    own, h_out = refs[2 * n + 1 : 2 * n + 3]
    sends, (line, pad) = refs[2 * n + 3 : 3 * n + 2], refs[3 * n + 2 :]
    _, row = where_am_i()
    assemble(z, h_out, [unfold(z, piece) for piece in pieces], row, 0, z.share)
    y, _ = normalize(z, h_out[...].astype(F32))
    spread_wide(z, y * sigmoid(y), line, pad)
    send_partials(z, row, convolve(z, pad, kernel, 0), own, sends, extra)


def enclosed(z, own, received, j):
    rows, base = z.local // FOLD, z.cells // FOLD
    at, there = slice(j * rows, (j + 1) * rows), slice(base + j * rows, base + (j + 1) * rows)
    return [unfolded(own[at, :], FOLD)] + [unfolded(x[there, :], FOLD) for x in received]


def later_forward(z, fs, *refs):
    n = z.parts
    arrivals, nexts, received = refs[:n], refs[n], refs[n + 1 : 2 * n]
    lasts, kernel = refs[2 * n : 3 * n], refs[3 * n]
    own, h_out, arrived, onward = refs[3 * n + 1 : 3 * n + 5]
    sends = refs[3 * n + 5 : 4 * n + 4]
    line, pad = refs[4 * n + 4 :]
    s, row = where_am_i()
    total = unfold(z, arrivals[0])
    for other in arrivals[1:]:
        total = total + unfold(z, other)
    total = total.astype(BF).astype(F32)
    arrived[...] = total.astype(BF)
    fold(z, onward, total)
    assemble(z, h_out, enclosed(z, nexts, received, 0), row, 0, z.share)
    prior = jnp.maximum(s - 1, 0)
    taken = jnp.logical_and(s > 0, fs[0, prior] == fs[1, s])
    h = jnp.where(taken, total, h_out[...].astype(F32))
    h_out[...] = h.astype(BF)
    y, _ = normalize(z, h)
    spread_wide(z, y * sigmoid(y), line, pad)
    send_partials(z, row, convolve(z, pad, kernel, 0), own, sends, lasts)


def back_through_second(z, i, g, kernel, q_out, q_send, act_out, pad, line):
    y, factor = normalize(z, i.astype(F32))
    logistic = sigmoid(y)
    act_out[...] = (y * logistic).astype(BF)
    spread(z, g, line, pad)
    q = norm_back(z, y, factor, logistic, convolve_back(z, pad, kernel, 1)).astype(BF)
    q_out[...] = q
    fold(z, q_send, q.astype(F32))


def first_backward(z, *refs):
    n = z.parts
    pieces, heads, kernel = refs[:n], refs[n : 2 * n], refs[2 * n]
    q_out, q_send, pad, act_out = refs[2 * n + 1 : 2 * n + 5]
    sends, (i_ref, g_ref, line) = refs[2 * n + 5 : 3 * n + 4], refs[3 * n + 4 :]
    _, row = where_am_i()
    assemble(z, i_ref, pieces, row, 0, z.share)
    assemble(z, g_ref, pieces, row, 2 * z.share, z.channels)
    back_through_second(
        z, i_ref[...], g_ref[...].astype(F32), kernel, q_out, q_send, act_out, pad, line
    )
    rows = z.cells // FOLD
    for d, send in enumerate(sends, 1):
        send[:rows, :] = q_send[...]
        send[rows:, :] = heads[d][...]


def later_backward(z, fs, bs, *refs):
    n = z.parts
    arrivals, mirror, received, kept = refs[:n], refs[n], refs[n + 1 : 2 * n], refs[2 * n]
    nexts, others = refs[2 * n + 1], refs[2 * n + 2 : 3 * n + 1]
    i_before, arrived, kernel = refs[3 * n + 1 : 3 * n + 4]
    q_out, pad, act_out, grad_in, skip_in = refs[3 * n + 4 : 3 * n + 9]
    rows_own, sends = refs[3 * n + 9], refs[3 * n + 10 : 4 * n + 9]
    q_send, i_ref, full, line = refs[4 * n + 9 :]
    s, row = where_am_i()
    w = z.share
    shares = [unfold(z, part) for part in arrivals]
    grad = side_by_side(all_shares(z, shares[0], shares[1:], row))
    grad_in[...] = grad.astype(BF)
    shares = [unfolded(x[: z.cells // FOLD, :], FOLD) for x in received]
    skip = side_by_side(all_shares(z, unfold(z, mirror), shares, row))
    skip_in[...] = skip.astype(BF)
    grad_taken, skip_taken = taken_back(z, bs, s)
    for j in range(n):
        assemble(z, full.at[j], enclosed(z, kept, received, j), row, 0, w)
    g = side_by_side([full[j] for j in range(n)]) + jnp.where(grad_taken, grad, 0.0)
    g = g + jnp.where(skip_taken, skip, 0.0)
    g = g.astype(BF).astype(F32)
    assemble(z, i_ref, enclosed(z, nexts, others, 1), row, 0, w)
    i = jnp.where(fs[0, s] == bs[1, s], i_before[...].astype(F32), i_ref[...].astype(F32))
    back_through_second(z, i, g, kernel, q_out, q_send, act_out, pad, line)
    for d, out in enumerate([rows_own, *sends]):
        at = part_rows(z, target(z, row, d))
        part = folded(side_by_side([i_before[at, :], arrived[at, :]]), 2).astype(BF)
        out[out.shape[0] - part.shape[0] :, :] = part
    for send in sends:
        send[: q_send.shape[0], :] = q_send[...]


def second_convolution(z, encoder, row, own, received, skip, h, kernel, i_out, full, line, pad):
    c0 = own[...]
    for other in received:
        c0 = c0 + unfolded(other[: z.cells // FOLD, :], FOLD)
    i = jnp.where(encoder, c0, skip.astype(F32)).astype(BF)
    i_out[...] = i
    y, _ = normalize(z, i.astype(F32))
    spread_wide(z, y * sigmoid(y), line, pad)
    total = convolve(z, pad, kernel, 1)
    base = h[...].astype(F32) + jnp.where(encoder, 0.0, c0)
    full[...] = total + side_by_side([jnp.where(row == j, base, 0.0) for j in range(z.parts)])


def middle(z, pad):
    return pad[1, z.cols : z.cols + z.cells, :].astype(F32)


def second_forward(z, *refs):
    n = z.parts
    own, received, h, pieces, kernel = refs[0], refs[1:n], refs[n], refs[n + 1 : 2 * n + 1], refs[2 * n + 1]
    i_out, full_out = refs[2 * n + 2 : 2 * n + 4]
    sends = refs[2 * n + 4 : 3 * n + 4]
    skip, full, line, pad = refs[3 * n + 4 :]
    s, row = where_am_i()
    encoder = s < z.sections // 2
    assemble(z, skip, pieces, row, z.share, z.share)
    second_convolution(
        z, encoder, row, own, received, skip[...], h, kernel, i_out, full, line, pad
    )
    full_out[...] = full[...].astype(BF)
    for d in range(n):
        fold(z, sends[d], share_of(z, full[...], target(z, row, d)))


def last_forward(z, fs, *refs):
    n = z.parts
    own, received, h = refs[0], refs[1:n], refs[n]
    lasts, arrived, kernel = refs[n + 1 : n + 4]
    sends = refs[n + 4 : 2 * n + 4]
    i_out, skip, full, line, pad = refs[2 * n + 4 :]
    s, row = where_am_i()
    encoder = s < z.sections // 2
    partner = z.sections - 1 - s
    assemble(z, skip, enclosed(z, lasts, received, 0), row, 0, z.share)
    now = jnp.where(
        fs[0, partner] == fs[1, s], unfold(z, arrived), skip[...].astype(F32)
    )
    second_convolution(z, encoder, row, own, received, now, h, kernel, i_out, full, line, pad)
    for d, send in enumerate(sends):
        at = part_rows(z, target(z, row, d))
        send[...] = side_by_side([full[at, :], i_out[at, :]]).astype(BF)


def joined_shares(z, own, received, row):
    others = [unfolded(other[: z.cells // FOLD, :], FOLD) for other in received]
    return side_by_side(all_shares(z, own[...].astype(F32), others, row))


def back_through_first(z, encoder, row, q, received, g_pad, h, kernel, act_out, pad, line):
    g = middle(z, g_pad)
    whole = joined_shares(z, q, received, row)
    now = jnp.where(encoder, whole, g)
    y, factor = normalize(z, h.astype(F32))
    logistic = sigmoid(y)
    act_out[...] = (y * logistic).astype(BF)
    spread(z, now, line, pad)
    back = norm_back(z, y, factor, logistic, convolve_back(z, pad, kernel, 0))
    return share_of(z, g, row) + back, whole


def second_backward(z, *refs):
    n = z.parts
    q, received, g = refs[0], refs[1:n], refs[n]
    heads, others, mirror = refs[n + 1], refs[n + 2 : 2 * n + 1], refs[2 * n + 1]
    grads, kernel = refs[2 * n + 2 : 3 * n + 2], refs[3 * n + 2]
    send, pad, act_out = refs[3 * n + 3 : 3 * n + 6]
    relays, (h, line) = refs[3 * n + 6 : 4 * n + 5], refs[4 * n + 5 :]
    s, row = where_am_i()
    for d, relay in enumerate(relays, 1):
        relay[: z.cells // FOLD, :] = mirror[...]
        relay[z.cells // FOLD :, :] = grads[d][...]
    assemble(z, h, enclosed(z, heads, others, 0), row, 0, z.share)
    value, _ = back_through_first(
        z, s < z.sections // 2, row, q, received, g, h[...], kernel, act_out, pad, line
    )
    fold(z, send, value)


def last_backward(z, fs, bs, *refs):
    n = z.parts
    q, received, g = refs[0], refs[1:n], refs[n]
    heads, others = refs[n + 1], refs[n + 2 : 2 * n + 1]
    h_before, kernel = refs[2 * n + 1 : 2 * n + 3]
    sends = refs[2 * n + 3 : 3 * n + 3]
    pad, act_out, h, value, line = refs[3 * n + 3 :]
    s, row = where_am_i()
    assemble(z, h, enclosed(z, heads, others, 1), row, 0, z.share)
    now = jnp.where(fs[0, s] == bs[1, s], h_before[...], h[...])
    result, _ = back_through_first(
        z, s < z.sections // 2, row, q, received, g, now, kernel, act_out, pad, line
    )
    value[...] = result.astype(BF)
    for d, send in enumerate(sends):
        fold(z, send, value[part_rows(z, target(z, row, d)), :])


def pack_rows(z, *refs):
    n = z.parts
    full, mirror = refs[:2]
    sends, skip = refs[2 : n + 2], refs[n + 2]
    _, row = where_am_i()
    skip[...] = unfold(z, mirror).astype(BF)
    for d, send in enumerate(sends):
        at = part_rows(z, target(z, row, d))
        send[...] = side_by_side([ref[at, :] for ref in (full, skip)]).astype(BF)


def add_rows(z, *refs):
    n = z.parts
    pieces, q, received = refs[:n], refs[n], refs[n + 1 : 2 * n]
    out, mirror, i_rows, whole = refs[2 * n :]
    s, row = where_am_i()
    c = z.channels
    whole[...] = joined_shares(z, q, received, row)
    values = [piece[...].astype(F32) for piece in pieces]
    total = sum(value[:, :c] for value in values)
    out[...] = total.astype(BF)
    mine = whole[part_rows(z, row), :]
    mirror[...] = jnp.where(s < z.sections // 2, total, mine).astype(BF)
    shares = all_shares(z, values[0][:, c:], [value[:, c:] for value in values[1:]], row)
    i_rows[...] = side_by_side(shares).astype(BF)


def write_queues(z, fs, bs, *refs):
    n = z.parts
    fwd, bwd, mir, stash, grad_in, skip_in = refs[:6]
    pieces = refs[6 : n + 6]
    token, outs, held = refs[n + 6], refs[n + 7 : n + 11], refs[n + 11 : n + 15]
    sems = refs[n + 15]
    token[...] = jnp.zeros_like(token)
    s, row = where_am_i()
    w = z.share
    prior, later = jnp.maximum(s - 1, 0), jnp.minimum(s + 1, z.sections - 1)
    partner = z.sections - 1 - s
    f0, f1 = fs[0, s], fs[1, s]
    mine = part_rows(z, row)
    copies = [pltpu.make_async_copy(a, b, sems.at[j]) for j, (a, b) in enumerate(zip(held, outs))]
    for ref, queue in zip(held, (fwd, bwd, mir, stash)):
        ref[...] = queue[...]

    @pl.when(s < z.sections - 1)
    def _():
        held[1][bs[0, later]] = grad_in[mine, :]

    copies[1].start()

    @pl.when(s < z.sections // 2)
    def _():
        held[2][bs[0, partner]] = skip_in[mine, :]

    copies[2].start()
    values = [unfolded(piece[piece.shape[0] - z.local // 2 :, :], 2) for piece in pieces]

    def joined(at):
        shares = [value[:, at : at + w] for value in values]
        return side_by_side(all_shares(z, shares[0], shares[1:], row)).astype(BF)

    fwd_in = joined(w)

    @pl.when(s > 0)
    def _():
        held[0][fs[0, prior]] = fwd_in

    copies[0].start()
    held[3][2 * f0] = fwd[f0]
    held[3][2 * f0 + 1] = joined(0)
    held[3][2 * f1] = fwd[f1]

    @pl.when(jnp.logical_and(s > 0, fs[0, prior] == f1))
    def _():
        held[3][2 * f1] = fwd_in

    copies[3].start()
    for copy in copies:
        copy.wait()


def finish(z, fs, bs, *refs):
    n = z.parts
    out1, i1, fwd1, mir1 = refs[4:8]
    rows0, grads1 = refs[8 : n + 8], refs[n + 8 : 2 * n + 8]
    fwd_out, bwd_out, mir_out, stash_out, emitted = refs[2 * n + 8 : 2 * n + 13]
    out0, skip, grads, sems = refs[2 * n + 13 :]
    s, row = where_am_i()
    c = z.channels
    prior, later = jnp.maximum(s - 1, 0), jnp.minimum(s + 1, z.sections - 1)
    partner = z.sections - 1 - s
    encoder, has_prior, has_later = s < z.sections // 2, s > 0, s < z.sections - 1
    first = jnp.where(encoder, bs[0, partner], fs[0, partner])
    second = jnp.where(encoder, bs[1, partner], fs[1, partner])
    skip_stays = jnp.logical_and(jnp.logical_not(encoder), first != second)

    def put(source, place, j):
        return pltpu.make_async_copy(source, place, sems.at[j])

    always = [
        put(out1, emitted.at[1], 0),
        put(i1, stash_out.at[2 * fs[1, s] + 1], 1),
        put(mir1, mir_out.at[second], 2),
        put(out0, emitted.at[0], 3),
    ]
    for copy in always[:3]:
        copy.start()
    onward, back = put(fwd1, fwd_out.at[fs[1, prior]], 4), put(grads, bwd_out.at[bs[1, later]], 5)
    aside = put(skip, mir_out.at[first], 6)
    pl.when(has_prior)(onward.start)
    pieces = [unfold(z, piece) for piece in grads1]
    grads[...] = side_by_side(all_shares(z, pieces[0], pieces[1:], row)).astype(BF)
    pl.when(has_later)(back.start)
    pieces = [piece[...].astype(F32) for piece in rows0]
    out0[...] = sum(piece[:, :c] for piece in pieces).astype(BF)
    always[3].start()
    shares = [piece[:, c:] for piece in pieces]
    skip[...] = side_by_side(all_shares(z, shares[0], shares[1:], row)).astype(BF)
    pl.when(skip_stays)(aside.start)
    for copy in always:
        copy.wait()
    pl.when(has_prior)(onward.wait)
    pl.when(has_later)(back.wait)
    pl.when(skip_stays)(aside.wait)


def add_taps(z, act, pad, before, store):
    turned = jnp.transpose(act[...].astype(F32)).astype(BF)
    for tap in range(9):
        a, b = divmod(tap, 3)
        at = (2 - a) * z.cols
        moved = pad[2 - b, at : at + z.cells, :]
        store(tap, before(tap) + jnp.dot(turned, moved, preferred_element_type=F32))


def kernel_grads_add(z, start, acc, act, pad, out):
    def store(tap, value):
        out[tap] = value

    add_taps(z, act, pad, lambda tap: acc[start + tap], store)


def kernel_grads_last(z, total, other, act, pad, token, out, held, sems):
    token[...] = jnp.zeros_like(token)
    copies = [pltpu.make_async_copy(other, out.at[9:], sems.at[9])]
    copies[0].start()

    def store(tap, value):
        held[tap] = value
        copies.append(pltpu.make_async_copy(held.at[tap], out.at[tap], sems.at[tap]))
        copies[-1].start()

    add_taps(z, act, pad, lambda tap: total[tap], store)
    for copy in copies:
        copy.wait()


def per_device(fwd_queue, bwd_queue, mirror_queue, stash, weights, grad_acc, fwd_slot, bwd_slot):
    sections, n = lax.axis_size("section"), lax.axis_size("row")
    z = Sizes(fwd_queue[0], sections, n)
    slots = fwd_queue.shape[1]
    c, w, local, cells = z.channels, z.share, z.local, z.cells
    fwd, bwd, mir = (x.reshape(slots, local, c) for x in (fwd_queue, bwd_queue, mirror_queue))
    kept = stash.reshape(2 * slots, local, c)
    kernels = weights.reshape(18 * w, c)
    acc = grad_acc.reshape(18, w, c)
    fs, bs = fwd_slot.T, bwd_slot.T
    fold_shape, wide = (cells // FOLD, FOLD * w), (cells, c)
    half = (cells, w)

    def with_shares(k):
        return ((cells + k * local) // FOLD, FOLD * w)

    padded = (3, cells + 2 * z.cols, c)

    def move(x, d, step):
        route = [
            (s * n + r, step(s) * n + (r + d) % n) for s in range(sections) for r in range(n)
        ]
        return lax.ppermute(x, ("section", "row"), route)

    across = functools.partial(move, step=lambda s: s)
    onward = functools.partial(move, step=lambda s: (s + 1) % sections)
    backward = functools.partial(move, step=lambda s: (s - 1) % sections)
    crossed = functools.partial(move, step=lambda s: (sections - s) % sections)
    mirrored = functools.partial(move, step=lambda s: sections - 1 - s)

    def run(body, scalars, arrays, outs, scratch=(), **options):
        return call(
            functools.partial(body, z), body.__name__, scalars, arrays, outs, scratch, **options
        )

    def exchange(pieces):
        return [pieces[0]] + [across(piece, d) for d, piece in enumerate(pieces[1:], 1)]

    narrow_pad = pad_shapes(z, w)
    wide_line = pltpu.VMEM((cells + 16, c), F32)
    queues = (fwd, bwd, mir, kept)
    rows = (local, c)
    sems = pltpu.SemaphoreType.DMA
    packed = run(
        pack_first,
        (),
        (fs, bs, *queues),
        [((local // FOLD, FOLD * w), BF)] * n
        + [(x.shape, BF) for x in queues],
        [pltpu.SMEM(fs.shape, jnp.int32)] * 2 + [sems((6,))],
        remote=6,
    )
    inputs, held = exchange(packed[:n]), packed[n:]

    packed = run(
        pack_later,
        (),
        (fs, bs, *held),
        [((local, 2 * w + c), BF)] * n
        + [((k * (local // FOLD), FOLD * w), BF) for k in (2, 2, n, 1) for _ in range(n)],
        [pltpu.SMEM(fs.shape, jnp.int32)] * 2 + [sems((2,))],
        remote=2,
        after=(inputs[0],),
    )
    pieces, heads, nexts, grads, lasts = (packed[j * n : (j + 1) * n] for j in range(5))
    first = exchange(held_until(pieces, inputs))

    own, h0, *sends = run(
        first_forward,
        (),
        (*inputs, *heads, kernels),
        [(half, F32), (half, BF)] + [(with_shares(2), BF)] * (n - 1),
        narrow_pad,
    )
    sums = [across(x, d) for d, x in enumerate(sends, 1)]
    q0, q_send, g_pad0, act_i0, *sends = run(
        first_backward,
        (),
        (*first, *nexts, kernels),
        [(half, BF), (fold_shape, BF), (padded, BF), (half, BF)]
        + [(with_shares(2), BF)] * (n - 1),
        [pltpu.VMEM(half, BF), pltpu.VMEM(wide, BF), wide_line],
        after=(own,),
    )
    q_received = [across(x, d) for d, x in enumerate(sends, 1)]
    skip_in = mirrored(q_send, 0)

    def add_grads(start, total, act, pad, after):
        [out] = call(
            functools.partial(kernel_grads_add, z, start),
            f"kernel_grads_add_{start}",
            (),
            (total, act, pad),
            [((9, w, c), F32)],
            after=after,
        )
        return out

    sum_i = add_grads(9, acc, act_i0, g_pad0, (q0,))
    i0, full0, *sends = run(
        second_forward,
        (),
        (own, *sums, h0, *first, kernels),
        [(half, BF), (wide, BF)] + [(fold_shape, BF)] * n,
        [pltpu.VMEM(half, BF), pltpu.VMEM(wide, F32)] + narrow_pad,
        after=(sum_i,),
    )
    fwd_in = [onward(x, d) for d, x in enumerate(sends)]
    dh_send, f_pad0, act_h0, *relays = run(
        second_backward,
        (),
        (q0, *q_received, g_pad0, heads[0], *sums, skip_in, *grads, kernels),
        [(fold_shape, BF), (padded, BF), (half, BF)] + [(with_shares(n), BF)] * (n - 1),
        [pltpu.VMEM(half, BF), wide_line],
        after=(i0,),
    )
    dh_in = [backward(dh_send, d) for d in range(n)]
    relayed = [across(x, d) for d, x in enumerate(relays, 1)]

    own, h1, arrived, turned, *sends = run(
        later_forward,
        (fs,),
        (*fwd_in, nexts[0], *q_received, *lasts, kernels),
        [(half, F32), (half, BF), (half, BF), (fold_shape, BF)]
        + [(with_shares(1), BF)] * (n - 1),
        narrow_pad,
        after=(dh_send,),
    )
    received = [across(x, d) for d, x in enumerate(sends, 1)]
    mir_in = crossed(turned, 0)
    sum_h = add_grads(0, acc, act_h0, f_pad0, (own,))
    q1, g_pad1, act_i1, grad_in, skip_full, rows_own, *sends = run(
        later_backward,
        (fs, bs),
        (*dh_in, skip_in, *relayed, grads[0], nexts[0], *q_received, i0, arrived, kernels),
        [(half, BF), (padded, BF), (half, BF), (wide, BF), (wide, BF), ((local // 2, 4 * w), BF)]
        + [((cells // FOLD + local // 2, FOLD * w), BF)] * (n - 1),
        [pltpu.VMEM(fold_shape, BF), pltpu.VMEM(half, BF), pltpu.VMEM((n, *half), BF), wide_line],
        after=(sum_h,),
    )
    q_received = [across(x, d) for d, x in enumerate(sends, 1)]
    sends = run(
        last_forward,
        (fs,),
        (own, *received, h1, lasts[0], mir_in, kernels),
        [((local, c + w), BF)] * n,
        [pltpu.VMEM(half, BF), pltpu.VMEM(half, BF), pltpu.VMEM(wide, F32)] + narrow_pad,
        after=(q1,),
    )
    rows1 = exchange(sends)
    part_i = add_grads(0, sum_i, act_i1, g_pad1, (sends[0],))
    packed = run(
        pack_rows,
        (),
        (full0, mir_in),
        [((local, c + w), BF)] * n,
        [pltpu.VMEM(half, BF)],
        after=(part_i,),
    )
    token, *written = run(
        write_queues,
        (fs, bs),
        (*held, grad_in, skip_full, rows_own, *q_received),
        [((8, 128), F32)] + [(x.shape, BF) for x in queues],
        [pltpu.VMEM(x.shape, BF) for x in queues] + [sems((4,))],
        far_outs=4,
        after=(packed[0],),
    )
    rows0 = exchange(held_until(packed, (rows1, token)))
    out1, mirror1, i1 = run(
        add_rows,
        (),
        (*rows1, q1, *q_received),
        [(rows, BF)] * 3,
        [pltpu.VMEM(wide, F32)],
        after=(token,),
    )
    fwd1, mir1 = onward(out1, 0), mirrored(mirror1, 0)
    *dh_sends, f_pad1, act_h1 = run(
        last_backward,
        (fs, bs),
        (q1, *q_received, g_pad1, heads[0], *sums, h0, kernels),
        [((local // FOLD, FOLD * w), BF)] * n + [(padded, BF), (half, BF)],
        [pltpu.VMEM(half, BF), pltpu.VMEM(half, BF), wide_line],
        after=(out1,),
    )
    dh1_in = [backward(x, d) for d, x in enumerate(dh_sends)]
    token, grad_total = run(
        kernel_grads_last,
        (),
        (sum_h, part_i, act_h1, f_pad1),
        [((8, 128), F32), ((18, w, c), F32)],
        [pltpu.VMEM((9, w, c), F32), sems((10,))],
        far_outs=1,
    )
    fwd_out, bwd_out, mir_out, stash_out, emitted = run(
        finish,
        (fs, bs),
        (*written, out1, i1, fwd1, mir1, *rows0, *dh1_in),
        [(x.shape, BF) for x in queues] + [((TICKS, local, c), BF)],
        [pltpu.VMEM(rows, BF)] * 3 + [sems((7,))],
        remote=4,
        far_outs=5,
        aliases={j + 2: j for j in range(4)},
        after=(token,),
    )
    return (
        fwd_out.reshape(fwd_queue.shape),
        bwd_out.reshape(bwd_queue.shape),
        mir_out.reshape(mirror_queue.shape),
        stash_out.reshape(stash.shape),
        grad_total.reshape(grad_acc.shape),
        emitted.reshape((1, TICKS) + fwd_queue.shape[2:]),
    )


def solution(mesh):
    return jax.shard_map(
        per_device,
        mesh=mesh,
        in_specs=(
            P("section", None, "row", None, None),
            P("section", None, "row", None, None),
            P("section", None, "row", None, None),
            P("section", None, None, "row", None, None),
            P("section", None, None, None, "row", None),
            P("section", None, None, None, "row", None),
            P(),
            P(),
        ),
        out_specs=(
            P("section", None, "row", None, None),
            P("section", None, "row", None, None),
            P("section", None, "row", None, None),
            P("section", None, None, "row", None, None),
            P("section", None, None, None, "row", None),
            P("section", None, "row", None, None),
        ),
        check_vma=False,
    )
```
